32 devices in a mesh: dp: 8 (over z, y), tensor: 4 (over x, core).
Axes of the slice: x: 2, y: 2, z: 4, core: 2. Of those that a mesh axis runs over, the one named last changes fastest.
Arguments:
- tokens_in: float32 [8192, 768], P('dp'), may hold values from -6 to 6
- cotangent: float32 [8192, 768], P('dp')
- segment_ids: int32 [8192], P('dp'), may hold values from -1 to 59, as said below
- long_seq: int32 [8], P('dp'), may hold values from 0 to 1
- weights: float32 [2, 192, 4, 9216], P(None, 'dp', 'tensor')
- left_stats: float32 [2, 192, 4, 9216], P(None, 'dp', 'tensor')
- right_stats: float32 [2, 192, 4, 9216], P(None, 'dp', 'tensor')
- left_roots: float32 [2, 192, 4, 9216], P(None, 'dp', 'tensor')
- right_roots: float32 [2, 192, 4, 9216], P(None, 'dp', 'tensor')
- split_params: float32 [2, 4, 1152], P(None, 'tensor', 'dp'), may hold values from -1 to 1
- shared_params: float32 [2, 6, 768], P(None, None, 'dp')
Outputs:
- block_out: float32 [8192, 768], P('dp')
- input_grad: float32 [8192, 768], P('dp')
- weight_grads: float32 [2, 192, 4, 9216], P(None, 'dp', 'tensor')
- new_weights: float32 [2, 192, 4, 9216], P(None, 'dp', 'tensor')
- new_left_stats: float32 [2, 192, 4, 9216], P(None, 'dp', 'tensor')
- new_right_stats: float32 [2, 192, 4, 9216], P(None, 'dp', 'tensor')
- split_grads: float32 [2, 4, 1152], P(None, 'tensor', 'dp')
- new_split_params: float32 [2, 4, 1152], P(None, 'tensor', 'dp')
- shared_grads: float32 [2, 6, 768], P(None, None, 'dp')
- new_shared_params: float32 [2, 6, 768], P(None, None, 'dp')
- grad_norm: float32 [], replicated
The draws below stay inside these ranges and needn't reach their ends.
Inputs may be any that keep to these rules, and one draw needn't show every extreme that they name: `segment_ids`: within each sequence (1024 slots on indices of dp whose long_seq is 1, 256 otherwise, laid end to end) the ids start at 0, never fall and rise by at most one from a slot to the next; padding (-1) fills only the sequence's last slots, at most a quarter of them.
All inputs are finite; a program needn't handle non-finite values.
Results may differ from the reference program's by a relative error of at most 0.035.
Values may be sent and summed in bfloat16 or wider, within the bound.
A program may use at most 192 MiB of HBM per device.

```python
import math
import jax
import jax.numpy as jnp
from jax import lax

D = 768
HEADS = 12
FF = 3072
HD = 64
B = 96
LAYERS = 2
TOK_DEV = 1024
SEQ_SHORT = 256
SEQ_LONG = 1024
TOKENS = 8192
EMB_DEV = 192
HID_DEV = 768
GROUP = 24
NBL = 192
VS = 1152
NPARAM = 14174208
N_DP = 8
N_TENSOR = 4


def packing_layout(key):
    base_key = jax.random.fold_in(key, 101)
    key_flag, key_mean, key_pad, key_cut = jax.random.split(base_key, 4)
    long_flag = jax.random.randint(key_flag, (N_DP,), 0, 2).astype(jnp.int32)
    slot_count = TOK_DEV // SEQ_SHORT
    slot_mean = jax.random.randint(key_mean, (N_DP, slot_count), SEQ_SHORT // 8, SEQ_SHORT // 2 + 1).astype(jnp.int32)
    slot_pad = jax.random.randint(key_pad, (N_DP, slot_count), 0, 65).astype(jnp.int32)
    seq_length = jnp.where(long_flag > 0, SEQ_LONG, SEQ_SHORT).astype(jnp.int32)[:, None]
    position = jnp.arange(TOK_DEV, dtype=jnp.int32)[None, :]
    group_row = jnp.arange(N_DP, dtype=jnp.int32)[:, None]
    within = position % seq_length
    start_pos = position - within
    start_slot = start_pos // SEQ_SHORT
    image_mean = jnp.take_along_axis(slot_mean, start_slot, axis=1)
    pad_length = jnp.take_along_axis(slot_pad, start_slot, axis=1) * seq_length // 256
    raw_cut = jax.random.randint(key_cut, (N_DP, TOK_DEV), 0, 1 << 20).astype(jnp.int32)
    cut_flags = jnp.where(within == 0, 0, (raw_cut % image_mean == 0).astype(jnp.int32))
    id_cap = min(59, SEQ_SHORT // 4 - 1)
    forced = (group_row == 0) & (start_pos == 0) & (within > 0) & (within % 2 == 0) & (within <= 2 * id_cap)
    cut_flags = jnp.where(forced, 1, cut_flags)
    running = jnp.cumsum(cut_flags, axis=1).astype(jnp.int32)
    image_id = jnp.minimum(running - jnp.take_along_axis(running, start_pos, axis=1), id_cap)
    valid_slot = within < seq_length - pad_length
    segments = jnp.where(valid_slot, image_id, -1).astype(jnp.int32)
    return (long_flag, segments.reshape(N_DP * TOK_DEV))


def draw_segment_ids(key, part):
    return packing_layout(key)[1]


def draw_long_seq(key, part):
    return packing_layout(key)[0]


def draw_weights(key, part):
    base_key = jax.random.fold_in(key, 202)
    full_shape = (LAYERS, NBL, N_TENSOR, B, B)
    noise_draw = jax.random.truncated_normal(base_key, -3.0, 3.0, full_shape)
    qkv_end = 3 * EMB_DEV // B
    up_end = qkv_end + HID_DEV // B
    out_end = up_end + EMB_DEV // B
    within = (jnp.arange(NBL, dtype=jnp.int32) % GROUP)[:, None]
    shard_gain = 0.75 + 0.6 * jnp.arange(N_TENSOR, dtype=jnp.float32)[None, :] / (N_TENSOR - 1)
    scale_map = jnp.where(within < qkv_end, 1.5 / math.sqrt(D) + 0.0 * shard_gain, jnp.where(within < up_end, shard_gain / math.sqrt(D), jnp.where(within < out_end, 0.5 * math.sqrt(SEQ_SHORT) / math.sqrt(D) + 0.0 * shard_gain, shard_gain / math.sqrt(FF))))
    return (noise_draw * scale_map[None, :, :, None, None]).reshape(LAYERS, NBL, N_TENSOR, B * B)


def symmetric_draw(key, salt_value, diag_low, diag_high, spread, level_scale):
    base_key = jax.random.fold_in(key, salt_value)
    key_diag, key_off = jax.random.split(base_key)
    full_shape = (LAYERS, NBL, N_TENSOR, B, B)
    diagonal = jax.random.uniform(key_diag, full_shape[:-1], minval=diag_low, maxval=diag_high)
    raw_draw = jax.random.uniform(key_off, full_shape, minval=-1.0, maxval=1.0)
    mirrored = 0.5 * (raw_draw + jnp.swapaxes(raw_draw, -1, -2))
    identity = jnp.eye(B, dtype=jnp.float32)
    blocks = level_scale * (identity * diagonal[..., None] + (1.0 - identity) * mirrored * spread / math.sqrt(B))
    return blocks.reshape(LAYERS, NBL, N_TENSOR, B * B)


def stat_level():
    return B * 10000.0 / NPARAM


def draw_left_stats(key, part):
    return symmetric_draw(key, 303, 1.0, 4.0, 0.6, stat_level())


def draw_right_stats(key, part):
    return symmetric_draw(key, 304, 1.0, 4.0, 0.6, stat_level())


def draw_left_roots(key, part):
    root_level = stat_level() ** (-0.25) / 3.0
    return symmetric_draw(key, 305, 2.0, 4.0, 2.0, root_level)


def draw_right_roots(key, part):
    root_level = stat_level() ** (-0.25) / 3.0
    return symmetric_draw(key, 306, 2.0, 4.0, 2.0, root_level)


def draw_cotangent(key, part):
    base_key = jax.random.fold_in(key, 404)
    fraction = jnp.arange(D, dtype=jnp.float32) / (D - 1)
    noise_draw = jax.random.truncated_normal(base_key, -4.0, 4.0, (TOKENS, D))
    slope = 0.7 + 0.6 * fraction
    return noise_draw * slope[None, :]


def draw_shared_params(key, part):
    base_key = jax.random.fold_in(key, 505)
    key_gain, key_bias = jax.random.split(base_key)
    fraction = jnp.arange(D, dtype=jnp.float32) / (D - 1)
    row_index = jnp.arange(6, dtype=jnp.int32)[:, None]
    is_gain = (row_index == 0) | (row_index == 2)
    gain_ramp = 0.7 + 0.6 * fraction
    jitter = jax.random.uniform(key_gain, (LAYERS, 6, D), minval=-0.1, maxval=0.1)
    bias_draw = 0.2 * jax.random.truncated_normal(key_bias, -3.0, 3.0, (LAYERS, 6, D))
    return jnp.where(is_gain[None], gain_ramp[None, None, :] * (1.0 + jitter), bias_draw)


def shard_levels(own_key, shape, shards, least, top_value):
    loudness = 1.0
    for axis_at, blocks in shards:
        draws = jax.random.uniform(jax.random.fold_in(jax.random.fold_in(own_key, 6), axis_at), (blocks,), jnp.float32, least / len(shards), top_value / len(shards))
        loudness = loudness * jnp.repeat(jnp.exp(draws), shape[axis_at] // blocks).reshape((-1,) + (1,) * (len(shape) - 1 - axis_at))
    return loudness


def scatter_about(stream_key, shape, deviation, bound, cuts=(), kind=jnp.bfloat16):
    result = deviation * jax.random.normal(stream_key, shape, jnp.float32)
    if cuts:
        result = result * shard_levels(stream_key, shape, cuts, -0.22, 0.18)
    return jnp.clip(result, -bound, bound).astype(kind)


def setup_inputs(seed: int = 0) -> dict:
    splits = jax.random.split(jax.random.key(seed), 12)
    tokens_in = scatter_about(splits[0], (TOKENS, D), 1.0, 6.0, ((0, 8),), jnp.float32)
    cotangent = draw_cotangent(jax.random.fold_in(splits[11], 71), 0)
    segment_ids = draw_segment_ids(jax.random.fold_in(splits[11], 71), 0)
    long_seq = draw_long_seq(jax.random.fold_in(splits[11], 71), 0)
    weights = draw_weights(jax.random.fold_in(splits[11], 71), 0)
    left_stats = draw_left_stats(jax.random.fold_in(splits[11], 71), 0)
    right_stats = draw_right_stats(jax.random.fold_in(splits[11], 71), 0)
    left_roots = draw_left_roots(jax.random.fold_in(splits[11], 71), 0)
    right_roots = draw_right_roots(jax.random.fold_in(splits[11], 71), 0)
    split_params = scatter_about(splits[9], (LAYERS, N_TENSOR, VS), 0.2, 1.0, ((1, 4), (2, 8)), jnp.float32)
    shared_params = draw_shared_params(jax.random.fold_in(splits[11], 71), 0)
    return dict(tokens_in=tokens_in, cotangent=cotangent, segment_ids=segment_ids, long_seq=long_seq, weights=weights, left_stats=left_stats, right_stats=right_stats, left_roots=left_roots, right_roots=right_roots, split_params=split_params, shared_params=shared_params)


clip_limit = 100.0
rate_matrix = 0.06
rate_vector = 0.2
decay = 0.5
eps_norm = 1e-06
eps_layer = 1e-06
big_negative = -1e+30
highest = lax.Precision.HIGHEST

@jax.custom_vjp
def low(v):
    return lax.optimization_barrier(v.astype(jnp.bfloat16)).astype(jnp.float32)

@jax.custom_vjp
def low_back(v):
    return v

def low_keep(v):
    return (low(v), None)

def low_pass(kept, grad):
    return (grad,)

def back_keep(v):
    return (v, None)

def back_low(kept, grad):
    return (low(grad),)
low.defvjp(low_keep, low_pass)
low_back.defvjp(back_keep, back_low)

def layer_norm(hidden, gain_vec, shift_vec):
    row_mean = lax.optimization_barrier(jnp.mean(hidden, axis=-1, keepdims=True))
    centered = hidden - row_mean
    row_var = lax.optimization_barrier(jnp.mean(centered * centered, axis=-1, keepdims=True))
    return centered * lax.rsqrt(row_var + eps_layer) * gain_vec + shift_vec

def gelu_exact(values):
    return jax.nn.gelu(values, approximate=False)

def matmul(left_mat, right_mat):
    return jnp.dot(left_mat, right_mat, precision=highest, preferred_element_type=jnp.float32)

def unpack_layer(blocks, embed_dev, inner_dev):
    row_groups = blocks.shape[0]
    block_size = blocks.shape[2]
    qkv_count = 3 * embed_dev // block_size
    up_count = inner_dev // block_size
    out_count = embed_dev // block_size

    def by_rows(part_blocks):
        block_count = part_blocks.shape[1]
        return jnp.transpose(part_blocks, (0, 2, 1, 3)).reshape(row_groups * block_size, block_count * block_size)

    def by_cols(part_blocks):
        block_count = part_blocks.shape[1]
        return jnp.transpose(part_blocks, (1, 2, 0, 3)).reshape(block_count * block_size, row_groups * block_size)
    qkv_weight = by_rows(blocks[:, :qkv_count])
    up_weight = by_rows(blocks[:, qkv_count:qkv_count + up_count])
    out_weight = by_cols(blocks[:, qkv_count + up_count:qkv_count + up_count + out_count])
    down_weight = by_cols(blocks[:, qkv_count + up_count + out_count:])
    return (qkv_weight, out_weight, up_weight, down_weight)

def attend(queries, key_rows, value_rows, allowed, score_scale):
    scores = jnp.einsum('qhd,khd->hqk', queries, key_rows, precision=highest) * score_scale
    scores = low_back(scores)
    scores = jnp.where(allowed[None], scores, big_negative)
    row_max = lax.optimization_barrier(jnp.max(scores, axis=-1, keepdims=True))
    exponent = jnp.exp(scores - row_max)
    attn_probs = low(exponent / lax.optimization_barrier(jnp.sum(exponent, axis=-1, keepdims=True)))
    return jnp.einsum('hqk,khd->qhd', attn_probs, value_rows, precision=highest)

def group_forward(params, tokens_group, segment_group, long_flag):
    weight_stack, split_stack, shared_stack = params
    embed_dev = D // N_TENSOR
    inner_dev = FF // N_TENSOR
    heads_dev = HEADS // N_TENSOR
    token_count = tokens_group.shape[0]
    score_scale = 1.0 / math.sqrt(HD)
    seq_length = jnp.where(long_flag > 0, SEQ_LONG, SEQ_SHORT)
    positions = jnp.arange(token_count, dtype=jnp.int32)
    seq_index = positions // seq_length
    allowed = (seq_index[:, None] == seq_index[None, :]) & (segment_group[:, None] == segment_group[None, :])
    hidden_state = tokens_group
    for layer_index in range(LAYERS):
        shared = shared_stack[layer_index]
        layer_mats = []
        for shard_index in range(N_TENSOR):
            blocks = low(weight_stack[layer_index, :, shard_index]).reshape(D // B, -1, B, B)
            layer_mats.append(unpack_layer(blocks, embed_dev, inner_dev))
        normed = low(layer_norm(hidden_state, shared[0], shared[1]))
        attn_total = jnp.zeros_like(hidden_state)
        for shard_index in range(N_TENSOR):
            qkv_weight, out_weight, up_weight, down_weight = layer_mats[shard_index]
            bias_table = split_stack[layer_index, shard_index].reshape(embed_dev, 6)
            qkv_bias = jnp.concatenate([bias_table[:, 0], jnp.zeros((embed_dev,), jnp.float32), bias_table[:, 1]])
            projected = low(low_back(matmul(normed, qkv_weight) + qkv_bias))
            queries = projected[:, :embed_dev].reshape(token_count, heads_dev, HD)
            keys_all = projected[:, embed_dev:2 * embed_dev].reshape(token_count, heads_dev, HD)
            values_all = projected[:, 2 * embed_dev:].reshape(token_count, heads_dev, HD)
            attended = attend(queries, keys_all, values_all, allowed, score_scale).reshape(token_count, embed_dev)
            attended = low(low_back(attended))
            attn_total = attn_total + low(matmul(attended, out_weight))
        middle = hidden_state + low_back(attn_total) + shared[4]
        normed_mid = low(layer_norm(middle, shared[2], shared[3]))
        mlp_total = jnp.zeros_like(hidden_state)
        for shard_index in range(N_TENSOR):
            qkv_weight, out_weight, up_weight, down_weight = layer_mats[shard_index]
            bias_table = split_stack[layer_index, shard_index].reshape(embed_dev, 6)
            up_bias = bias_table[:, 2:].reshape(inner_dev)
            pre_act = low_back(matmul(normed_mid, up_weight) + up_bias)
            activation = low(gelu_exact(pre_act))
            mlp_total = mlp_total + low(matmul(activation, down_weight))
        hidden_state = middle + low_back(mlp_total) + shared[5]
    return hidden_state

def reference(tokens_in, cotangent, segment_ids, long_seq, weights, left_stats, right_stats, left_roots, right_roots, split_params, shared_params):
    embed_dev = D // N_TENSOR
    group_tokens = tokens_in.reshape(N_DP, TOK_DEV, D)
    group_segments = segment_ids.reshape(N_DP, TOK_DEV)
    checked = jax.checkpoint(group_forward)

    def forward(weight_stack, split_stack, shared_stack, token_groups):

        def one_group(group_items):
            return checked((weight_stack, split_stack, shared_stack), group_items[0], group_items[1], group_items[2])
        return lax.map(one_group, (token_groups, group_segments, long_seq))
    outputs, pullback = jax.vjp(forward, weights, split_params, shared_params, group_tokens)
    valid_rows = (group_segments >= 0).astype(jnp.float32)
    weight_grad, split_grad, shared_grad, token_grad = pullback(cotangent.reshape(N_DP, TOK_DEV, D) * valid_rows[..., None])
    total_sq = jnp.sum(weight_grad * weight_grad) + jnp.sum(split_grad * split_grad) + jnp.sum(shared_grad * shared_grad)
    grad_norm = jnp.sqrt(total_sq)
    factor = clip_limit / jnp.maximum(grad_norm, clip_limit)
    weight_clip = weight_grad * factor
    split_clip = split_grad * factor
    shared_clip = shared_grad * factor
    block_shape = (LAYERS, NBL, N_TENSOR, B, B)
    grad_mats = weight_clip.reshape(block_shape)
    left_gram = jnp.einsum('...ij,...kj->...ik', grad_mats, grad_mats, precision=highest)
    right_gram = jnp.einsum('...ji,...jk->...ik', grad_mats, grad_mats, precision=highest)
    new_left = decay * left_stats + (1.0 - decay) * left_gram.reshape(left_stats.shape)
    new_right = decay * right_stats + (1.0 - decay) * right_gram.reshape(right_stats.shape)
    direction = jnp.einsum('...ij,...jk->...ik', left_roots.reshape(block_shape), grad_mats, precision=highest)
    direction = jnp.einsum('...ij,...jk->...ik', direction, right_roots.reshape(block_shape), precision=highest)
    mean_sq = lax.optimization_barrier(jnp.mean(direction * direction, axis=(-2, -1), keepdims=True))
    step_mats = direction * lax.rsqrt(mean_sq + eps_norm)
    new_weights = weights - rate_matrix * step_mats.reshape(weights.shape)
    grad_table = split_clip.reshape(LAYERS, N_TENSOR, embed_dev, 6)
    param_table = split_params.reshape(LAYERS, N_TENSOR, embed_dev, 6)
    square_table = grad_table * grad_table
    query_mean = lax.optimization_barrier(jnp.mean(square_table[..., 0], axis=(1, 2)))
    value_mean = lax.optimization_barrier(jnp.mean(square_table[..., 1], axis=(1, 2)))
    up_mean = lax.optimization_barrier(jnp.mean(square_table[..., 2:], axis=(1, 2, 3)))
    column_means = jnp.stack([query_mean, value_mean, up_mean, up_mean, up_mean, up_mean], axis=-1)
    new_table = param_table - rate_vector * grad_table * lax.rsqrt(column_means[:, None, None, :] + eps_norm)
    new_split = new_table.reshape(split_params.shape)
    shared_mean = lax.optimization_barrier(jnp.mean(shared_clip * shared_clip, axis=-1, keepdims=True))
    new_shared = shared_params - rate_vector * shared_clip * lax.rsqrt(shared_mean + eps_norm)
    return (outputs.reshape(TOKENS, D), token_grad.reshape(TOKENS, D), weight_clip, new_weights, new_left, new_right, split_clip, new_split, shared_clip, new_shared, grad_norm)
```

```python
import functools
import math

import jax
import jax.numpy as jnp
from jax import lax
from jax.experimental import pallas as pl
from jax.experimental.pallas import tpu as pltpu
from jax.sharding import PartitionSpec as P

D = 768
HEADS = 12
FF = 3072
HD = 64
B = 96
LAYERS = 2
SEQ_SHORT = 256
SEQ_LONG = 1024


clip_limit = 100.0
rate_matrix = 0.06
rate_vector = 0.2
decay = 0.5
eps_norm = 1e-06
eps_layer = 1e-06
big_negative = -1e30
highest = lax.Precision.HIGHEST


def layer_norm(hidden, gain_vec, shift_vec):
    row_mean = jnp.mean(hidden, axis=-1, keepdims=True)
    centered = hidden - row_mean
    row_var = jnp.mean(centered * centered, axis=-1, keepdims=True)
    return centered * lax.rsqrt(row_var + eps_layer) * gain_vec + shift_vec


def gelu_exact(values):
    return jax.nn.gelu(values, approximate=False)


def matmul_low(left_mat, right_mat):
    return jnp.dot(left_mat, right_mat, preferred_element_type=jnp.float32)


def inner_rows(left_mat, right_mat):
    return lax.dot_general(
        left_mat, right_mat, (((0,), (0,)), ((), ())), preferred_element_type=jnp.float32
    )


def times_trans(left_mat, right_mat):
    return lax.dot_general(
        left_mat, right_mat, (((1,), (1,)), ((), ())), preferred_element_type=jnp.float32
    )


def unpack_layer(blocks, embed_dev, inner_dev):
    row_groups = blocks.shape[0]
    block_size = blocks.shape[2]
    qkv_count = 3 * embed_dev // block_size
    up_count = inner_dev // block_size
    out_count = embed_dev // block_size

    def by_rows(part_blocks):
        block_count = part_blocks.shape[1]
        return jnp.transpose(part_blocks, (0, 2, 1, 3)).reshape(
            row_groups * block_size, block_count * block_size
        )

    def by_cols(part_blocks):
        block_count = part_blocks.shape[1]
        return jnp.transpose(part_blocks, (1, 2, 0, 3)).reshape(
            block_count * block_size, row_groups * block_size
        )

    qkv_weight = by_rows(blocks[:, :qkv_count])
    up_weight = by_rows(blocks[:, qkv_count : qkv_count + up_count])
    out_weight = by_cols(blocks[:, qkv_count + up_count : qkv_count + up_count + out_count])
    down_weight = by_cols(blocks[:, qkv_count + up_count + out_count :])
    return (qkv_weight, out_weight, up_weight, down_weight)


def pack_layer(qkv_grad, out_grad, up_grad, down_grad, block_size):
    row_groups = qkv_grad.shape[0] // block_size

    def from_rows(matrix):
        block_count = matrix.shape[1] // block_size
        return jnp.transpose(
            matrix.reshape(row_groups, block_size, block_count, block_size), (0, 2, 1, 3)
        )

    def from_cols(matrix):
        block_count = matrix.shape[0] // block_size
        return jnp.transpose(
            matrix.reshape(block_count, block_size, row_groups, block_size), (2, 0, 1, 3)
        )

    return jnp.concatenate(
        [from_rows(qkv_grad), from_rows(up_grad), from_cols(out_grad), from_cols(down_grad)], axis=1
    )


def masked_scores(query_block, key_window, query_seq, key_seq, query_seg, key_seg, score_scale):
    scores = (
        jnp.einsum("qhd,khd->hqk", query_block, key_window, preferred_element_type=jnp.float32)
        * score_scale
    )
    allowed = (query_seq[:, None] == key_seq[None, :]) & (query_seg[:, None] == key_seg[None, :])
    return jnp.where(allowed[None], scores, big_negative)


def attention_forward(queries, keys_all, values_all, seq_index, segments, block_rows, score_scale):
    block_count = queries.shape[0] // block_rows

    def one_block(block_index):
        row_start = block_index * block_rows
        query_block = lax.dynamic_slice_in_dim(queries, row_start, block_rows, 0)
        scores = masked_scores(
            query_block,
            keys_all,
            lax.dynamic_slice_in_dim(seq_index, row_start, block_rows, 0),
            seq_index,
            lax.dynamic_slice_in_dim(segments, row_start, block_rows, 0),
            segments,
            score_scale,
        )
        row_max = jnp.max(scores, axis=-1, keepdims=True)
        exponent = jnp.exp(scores - row_max)
        row_total = jnp.sum(exponent, axis=-1, keepdims=True)
        attn_probs = (exponent / row_total).astype(jnp.bfloat16)
        attended = jnp.einsum(
            "hqk,khd->qhd", attn_probs, values_all, preferred_element_type=jnp.float32
        )
        return (attended, (row_max + jnp.log(row_total))[..., 0])

    return lax.map(one_block, jnp.arange(block_count, dtype=jnp.int32))


def attention_backward(
    queries, keys_all, values_all, grad_out, log_total, seq_index, segments, block_rows, score_scale
):
    token_count = queries.shape[0]
    block_count = token_count // block_rows
    zero_grad = jnp.zeros(keys_all.shape, jnp.float32)

    def one_block(carry_pair, block_index):
        key_grad, value_grad = carry_pair
        row_start = block_index * block_rows
        query_block = lax.dynamic_slice_in_dim(queries, row_start, block_rows, 0)
        out_block = lax.dynamic_slice_in_dim(grad_out, row_start, block_rows, 0)
        scores = masked_scores(
            query_block,
            keys_all,
            lax.dynamic_slice_in_dim(seq_index, row_start, block_rows, 0),
            seq_index,
            lax.dynamic_slice_in_dim(segments, row_start, block_rows, 0),
            segments,
            score_scale,
        )
        lse_block = lax.dynamic_index_in_dim(log_total, block_index, 0, keepdims=False)
        attn_probs = jnp.exp(scores - lse_block[..., None])
        prob_grad = jnp.einsum(
            "qhd,khd->hqk", out_block, values_all, preferred_element_type=jnp.float32
        )
        row_delta = jnp.sum(attn_probs * prob_grad, axis=-1, keepdims=True)
        score_grad = (attn_probs * (prob_grad - row_delta)).astype(jnp.bfloat16)
        query_grad = (
            jnp.einsum("hqk,khd->qhd", score_grad, keys_all, preferred_element_type=jnp.float32)
            * score_scale
        )
        key_part = (
            jnp.einsum("hqk,qhd->khd", score_grad, query_block, preferred_element_type=jnp.float32)
            * score_scale
        )
        value_part = jnp.einsum(
            "hqk,qhd->khd",
            attn_probs.astype(jnp.bfloat16),
            out_block,
            preferred_element_type=jnp.float32,
        )
        key_grad = key_grad + key_part
        value_grad = value_grad + value_part
        return ((key_grad, value_grad), query_grad)

    (key_grad, value_grad), query_grad = lax.scan(
        one_block, (zero_grad, zero_grad), jnp.arange(block_count, dtype=jnp.int32)
    )
    return (query_grad.reshape(keys_all.shape), key_grad, value_grad)


def body(
    tokens_in,
    cotangent,
    segment_ids,
    long_seq,
    weights,
    left_stats,
    right_stats,
    left_roots,
    right_roots,
    split_params,
    shared_params,
):
    full_weights, full_split, full_shared = (
        lax.all_gather(weights, "dp", axis=1, tiled=True),
        lax.all_gather(split_params, "dp", axis=2, tiled=True),
        lax.all_gather(shared_params, "dp", axis=2, tiled=True),
    )
    tensor_count = lax.axis_size("tensor")
    embed_dev = D // tensor_count
    inner_dev = FF // tensor_count
    heads_local = HEADS // tensor_count
    token_count = tokens_in.shape[0]
    window = SEQ_LONG
    block_rows = min(512, window)
    score_scale = 1.0 / math.sqrt(HD)
    seq_length = jnp.where(long_seq[0] > 0, SEQ_LONG, SEQ_SHORT)
    positions = jnp.arange(token_count, dtype=jnp.int32)
    seq_index = positions // seq_length
    valid_rows = (segment_ids >= 0).astype(jnp.float32)
    matrices = []
    for layer_index in range(LAYERS):
        blocks = full_weights[layer_index, :, 0].astype(jnp.bfloat16).reshape(D // B, -1, B, B)
        matrices.append(unpack_layer(blocks, embed_dev, inner_dev))
    hidden_state = tokens_in
    kept_state = []
    for layer_index in range(LAYERS):
        qkv_weight, out_weight, up_weight, down_weight = matrices[layer_index]
        shared = full_shared[layer_index]
        bias_table = full_split[layer_index, 0].reshape(embed_dev, 6)
        up_bias = bias_table[:, 2:].reshape(inner_dev)
        normed = layer_norm(hidden_state, shared[0], shared[1]).astype(jnp.bfloat16)
        qkv_bias = jnp.concatenate(
            [bias_table[:, 0], jnp.zeros((embed_dev,), jnp.float32), bias_table[:, 1]]
        )
        projected = (matmul_low(normed, qkv_weight) + qkv_bias).astype(jnp.bfloat16)
        queries = projected[:, :embed_dev].reshape(token_count, heads_local, HD)
        keys_all = projected[:, embed_dev : 2 * embed_dev].reshape(token_count, heads_local, HD)
        values_all = projected[:, 2 * embed_dev :].reshape(token_count, heads_local, HD)
        attended, log_total = attention_forward(
            queries, keys_all, values_all, seq_index, segment_ids, block_rows, score_scale
        )
        attended = attended.reshape(token_count, embed_dev).astype(jnp.bfloat16)
        attn_branch = lax.psum(
            matmul_low(attended, out_weight).astype(jnp.bfloat16), "tensor"
        ).astype(jnp.float32)
        middle = hidden_state + attn_branch + shared[4]
        normed_mid = layer_norm(middle, shared[2], shared[3]).astype(jnp.bfloat16)
        pre_act = matmul_low(normed_mid, up_weight) + up_bias
        activation = gelu_exact(pre_act).astype(jnp.bfloat16)
        mlp_branch = lax.psum(
            matmul_low(activation, down_weight).astype(jnp.bfloat16), "tensor"
        ).astype(jnp.float32)
        kept_state.append(
            (
                hidden_state,
                normed,
                queries,
                keys_all,
                values_all,
                attended,
                log_total,
                middle,
                normed_mid,
                pre_act,
                activation,
            )
        )
        hidden_state = middle + mlp_branch + shared[5]
    grad_state = cotangent * valid_rows[:, None]
    layer_grads = [None] * LAYERS
    for layer_index in reversed(range(LAYERS)):
        (
            hidden_in,
            normed,
            queries,
            keys_all,
            values_all,
            attended,
            log_total,
            middle,
            normed_mid,
            pre_act,
            activation,
        ) = kept_state[layer_index]
        qkv_weight, out_weight, up_weight, down_weight = matrices[layer_index]
        shared = full_shared[layer_index]
        down_bias_grad = jnp.sum(grad_state, axis=0)
        grad_low = grad_state.astype(jnp.bfloat16)
        down_grad = inner_rows(activation, grad_low)
        act_grad = times_trans(grad_low, down_weight)
        gelu_pull = jax.vjp(gelu_exact, pre_act)[1]
        pre_grad = gelu_pull(act_grad)[0].astype(jnp.bfloat16)
        up_bias_grad = jnp.sum(pre_grad, axis=0, dtype=jnp.float32)
        up_grad = inner_rows(normed_mid, pre_grad)
        normed_mid_grad = lax.psum(times_trans(pre_grad, up_weight), "tensor")
        norm_pull = jax.vjp(layer_norm, middle, shared[2], shared[3])[1]
        middle_ln, gain_two_grad, shift_two_grad = norm_pull(normed_mid_grad)
        middle_grad = grad_state + middle_ln
        out_bias_grad = jnp.sum(middle_grad, axis=0)
        middle_low = middle_grad.astype(jnp.bfloat16)
        out_grad = inner_rows(attended, middle_low)
        attended_grad = (
            times_trans(middle_low, out_weight)
            .astype(jnp.bfloat16)
            .reshape(token_count, heads_local, HD)
        )
        query_grad, key_grad, value_grad = attention_backward(
            queries,
            keys_all,
            values_all,
            attended_grad,
            log_total,
            seq_index,
            segment_ids,
            block_rows,
            score_scale,
        )
        proj_grad = jnp.concatenate(
            [
                query_grad.reshape(token_count, embed_dev),
                key_grad.reshape(token_count, embed_dev),
                value_grad.reshape(token_count, embed_dev),
            ],
            axis=1,
        ).astype(jnp.bfloat16)
        query_bias_grad = jnp.sum(proj_grad[:, :embed_dev], axis=0, dtype=jnp.float32)
        value_bias_grad = jnp.sum(proj_grad[:, 2 * embed_dev :], axis=0, dtype=jnp.float32)
        qkv_grad = inner_rows(normed, proj_grad)
        normed_grad = lax.psum(times_trans(proj_grad, qkv_weight), "tensor")
        input_pull = jax.vjp(layer_norm, hidden_in, shared[0], shared[1])[1]
        hidden_ln, gain_one_grad, shift_one_grad = input_pull(normed_grad)
        grad_state = middle_grad + hidden_ln
        block_grads = pack_layer(qkv_grad, out_grad, up_grad, down_grad, B).reshape(-1, 1, B * B)
        split_vec = jnp.concatenate(
            [
                query_bias_grad[:, None],
                value_bias_grad[:, None],
                up_bias_grad.reshape(embed_dev, 4),
            ],
            axis=1,
        ).reshape(1, -1)
        shared_vec = jnp.stack(
            [
                gain_one_grad,
                shift_one_grad,
                gain_two_grad,
                shift_two_grad,
                out_bias_grad,
                down_bias_grad,
            ]
        )
        layer_grads[layer_index] = (block_grads, split_vec, shared_vec)
    weight_grad, split_grad, shared_grad = (
        lax.psum_scatter(
            jnp.stack([entry[0] for entry in layer_grads]), "dp", scatter_dimension=1, tiled=True
        ),
        lax.psum_scatter(
            jnp.stack([entry[1] for entry in layer_grads]), "dp", scatter_dimension=2, tiled=True
        ),
        lax.psum_scatter(
            jnp.stack([entry[2] for entry in layer_grads]), "dp", scatter_dimension=2, tiled=True
        ),
    )
    dp_index = lax.axis_index("dp")
    lead_shard = (lax.axis_index("tensor") == 0).astype(jnp.float32)
    slice_len = split_grad.shape[-1]
    global_pos = dp_index * slice_len + jnp.arange(slice_len, dtype=jnp.int32)
    table_column = global_pos % 6
    segment_of = (table_column >= 1).astype(jnp.int32) + (table_column >= 2).astype(jnp.int32)
    selector = (segment_of[:, None] == jnp.arange(3, dtype=jnp.int32)[None, :]).astype(jnp.float32)
    split_sq = split_grad[:, 0] * split_grad[:, 0]
    split_rows = jnp.dot(split_sq, selector, precision=highest)
    shared_sq = shared_grad * shared_grad
    shared_rows = jnp.sum(shared_sq, axis=-1) * lead_shard
    local_total = (
        jnp.sum(weight_grad * weight_grad) + jnp.sum(split_sq) + lead_shard * jnp.sum(shared_sq)
    )
    total_sq, split_rows, shared_rows = lax.psum(
        (local_total, split_rows, shared_rows), ("dp", "tensor")
    )
    grad_norm = jnp.sqrt(total_sq)
    factor = clip_limit / jnp.maximum(grad_norm, clip_limit)
    squared = factor * factor
    block_shape = weight_grad.shape[:-1] + (B, B)
    left_mats = left_roots.reshape(block_shape)
    right_mats = right_roots.reshape(block_shape)
    clipped = weight_grad * factor
    clipped_mats = clipped.reshape(block_shape)
    new_left = decay * left_stats + (1.0 - decay) * jnp.einsum(
        "...ij,...kj->...ik", clipped_mats, clipped_mats, precision=highest
    ).reshape(left_stats.shape)
    new_right = decay * right_stats + (1.0 - decay) * jnp.einsum(
        "...ji,...jk->...ik", clipped_mats, clipped_mats, precision=highest
    ).reshape(right_stats.shape)
    partial_dir = jnp.einsum("...ij,...jk->...ik", left_mats, clipped_mats, precision=highest)
    direction = jnp.einsum("...ij,...jk->...ik", partial_dir, right_mats, precision=highest)
    mean_sq = jnp.mean(direction * direction, axis=(-2, -1), keepdims=True)
    step_mats = direction * lax.rsqrt(mean_sq + eps_norm)
    new_weights = weights - rate_matrix * step_mats.reshape(weights.shape)
    vector_sizes = jnp.array([D, D, FF], jnp.float32)
    split_mean = jnp.dot(split_rows / vector_sizes[None, :], selector.T, precision=highest)
    split_clip = split_grad * factor
    new_split = split_params - rate_vector * split_clip * lax.rsqrt(
        squared * split_mean[:, None, :] + eps_norm
    )
    shared_clip = shared_grad * factor
    shared_mean = shared_rows / D
    new_shared = shared_params - rate_vector * shared_clip * lax.rsqrt(
        squared * shared_mean[..., None] + eps_norm
    )
    return (
        hidden_state,
        grad_state,
        clipped,
        new_weights,
        new_left,
        new_right,
        split_clip,
        new_split,
        shared_clip,
        new_shared,
        grad_norm,
    )


F32 = jnp.float32
BF16 = jnp.bfloat16
MESH = pl.DeviceIdType.MESH
CHUNKS = 4
HALF = 128
CHUNK = 2 * HALF
ROWS = CHUNKS * CHUNK
HEADS_DEV = 3
GROUPS = D // B
GROUP = 24
PARTS = ((0, 1, 2, 3, 4, 5, 14, 15), tuple(range(6, 14)), tuple(range(16, 24)))
TRANSPOSED = (frozenset((14, 15)), frozenset(), frozenset(range(16, 24)))


def dot_nn(left_mat, right_mat):
    return lax.dot_general(left_mat, right_mat, (((1,), (0,)), ((), ())), preferred_element_type=F32)


def dot_nt(left_mat, right_mat):
    return lax.dot_general(left_mat, right_mat, (((1,), (1,)), ((), ())), preferred_element_type=F32)


def dot_tn(left_mat, right_mat):
    return lax.dot_general(left_mat, right_mat, (((0,), (0,)), ((), ())), preferred_element_type=F32)


def lanes_of(shape):
    return lax.broadcasted_iota(jnp.int32, shape, len(shape) - 1)


def norm_rows(rows):
    mean = jnp.mean(rows, axis=-1, keepdims=True)
    centered = rows - mean
    var = jnp.mean(centered * centered, axis=-1, keepdims=True)
    inv = lax.rsqrt(var + eps_layer)
    return centered * inv, inv


def norm_back(grad, rows, gain):
    hat, inv = norm_rows(rows)
    scaled = grad * gain
    mean_one = jnp.mean(scaled, axis=-1, keepdims=True)
    mean_two = jnp.mean(scaled * hat, axis=-1, keepdims=True)
    d_rows = inv * (scaled - mean_one - hat * mean_two)
    return d_rows, jnp.sum(grad * hat, axis=0, keepdims=True), jnp.sum(grad, axis=0, keepdims=True)


def table_selector(shape):
    row = lax.broadcasted_iota(jnp.int32, shape, 0)
    col = lax.broadcasted_iota(jnp.int32, shape, 1)
    up_row = 6 * (col >> 2) + 2 + (col & 3)
    hit = (col < B) & (row == up_row)
    hit = hit | ((col >= 128) & (col < 152) & (row == 6 * (col - 128)))
    hit = hit | ((col >= 152) & (col < 176) & (row == 6 * (col - 152) + 1))
    return hit.astype(F32)


def flat_to_square(x_zero, x_one, x_two, place):
    lane = lanes_of((24, 128))
    place[pl.ds(0, 24, stride=4), :] = x_zero
    place[pl.ds(1, 24, stride=4), :] = jnp.where(
        lane < 32, pltpu.roll(x_zero, 32, 1), pltpu.roll(x_one, 32, 1)
    )
    place[pl.ds(2, 24, stride=4), :] = jnp.where(
        lane < 64, pltpu.roll(x_one, 64, 1), pltpu.roll(x_two, 64, 1)
    )
    place[pl.ds(3, 24, stride=4), :] = pltpu.roll(x_two, 96, 1)
    return place[...][:, :B]


def square_to_flat(square, place):
    lane = lanes_of((24, 128))
    place[:, 0:B] = square
    m_zero, m_one, m_two, m_three = [place[pl.ds(m, 24, stride=4), :] for m in range(4)]
    one_back = pltpu.roll(m_one, 96, 1)
    two_back = pltpu.roll(m_two, 64, 1)
    return (
        jnp.where(lane < 96, m_zero, one_back),
        jnp.where(lane < 64, one_back, two_back),
        jnp.where(lane < 32, two_back, pltpu.roll(m_three, 32, 1)),
    )


def train_kernel(
    n_y,
    x_hbm,
    ct_hbm,
    seg_ref,
    long_ref,
    w_hbm,
    split_ref,
    shared_ref,
    bo_hbm,
    ig_hbm,
    gb_hbm,
    sg_ref,
    nm_ref,
    wt,
    a_all,
    c_all,
    q_all,
    k_all,
    v_all,
    v_tr,
    o_all,
    lse_all,
    z_all,
    gp_all,
    res,
    y_own,
    y_all,
    g_all,
    du_all,
    dx_all,
    dk_acc,
    dv_acc,
    stage,
    core_in,
    x_in,
    dw,
    rs_one,
    rs_two,
    place,
    g_out,
    x_out,
    kid_col,
    kid_row,
    vecs,
    bias_row,
    gvecs,
    gbias,
    sib_in,
    msg_in,
    gmsg_in,
    gmsg_out,
    nb_out,
    nb_in,
    nd_in,
    g_s,
    g_r,
    c_s,
    c_r,
    x_s,
    x_r,
    a_s,
    a_r,
    p_s,
    p_r,
    t_s,
    t_r,
    load_sem,
    land_sem,
    ct_sem,
    out_sem,
    far_s,
    far_r,
    gout_sem,
    m_s,
    m_r,
    gm_s,
    gm_r,
    sib_s,
    sib_r,
    nb_s,
    nb_r,
    nd_s,
    nd_r,
):
    n_dp = GROUPS
    n_z = n_dp // n_y
    me = lax.axis_index("dp")
    ten = lax.axis_index("tensor")
    my_z, my_y = me // n_y, lax.rem(me, n_y)
    my_x, my_c = ten // 2, lax.rem(ten, 2)
    other_c = 1 - my_c
    sibling = (me, 2 * my_x + other_c)
    across = (me, 2 * (1 - my_x) + my_c)
    scale = 1.0 / math.sqrt(HD)

    def dp_dev(index):
        return (index, ten)

    def z_peer(step):
        return lax.rem(my_z + step, n_z)

    def remote(src, dst, send, recv, dev):
        return pltpu.make_async_remote_copy(
            src_ref=src, dst_ref=dst, send_sem=send, recv_sem=recv, device_id=dev, device_id_type=MESH
        )

    def load_rows(j, which):
        half = my_c if which == 0 else other_c
        return pltpu.make_async_copy(x_hbm.at[j, half], res.at[which, j], load_sem.at[which, j])

    def load_blocks(l):
        return pltpu.make_async_copy(
            w_hbm.at[l], g_out.at[l, :, pl.ds(0, 72)], land_sem.at[l]
        )

    for l in range(LAYERS):
        load_blocks(l).start()
    for j in range(CHUNKS):
        load_rows(j, 0).start()
        load_rows(j, 1).start()

    barrier = pltpu.get_barrier_semaphore()
    for step in range(1, n_dp):
        pl.semaphore_signal(
            barrier, inc=1, device_id=dp_dev(lax.rem(me + step, n_dp)), device_id_type=MESH
        )
    pl.semaphore_signal(barrier, inc=1, device_id=sibling, device_id_type=MESH)
    pl.semaphore_signal(barrier, inc=1, device_id=across, device_id_type=MESH)

    sel = table_selector((144, 256))
    for l in range(LAYERS):
        row = lax.dot_general(
            jnp.broadcast_to(split_ref[l : l + 1, :], (8, 144)),
            sel,
            (((1,), (0,)), ((), ())),
            precision=highest,
            preferred_element_type=F32,
        )
        msg_in[me, 8 * l : 8 * l + 8, :] = row
        msg_in[me, 8 * l : 8 * l + 6, 0:B] = shared_ref[6 * l : 6 * l + 6, :]

    pl.semaphore_wait(barrier, n_dp + 1)

    def msg_copy(step):
        return remote(
            msg_in.at[me], msg_in.at[me], m_s.at[step - 1], m_r.at[me],
            dp_dev(lax.rem(me + step, n_dp)),
        )

    def msg_from(step):
        src = lax.rem(me + step, n_dp)
        return remote(msg_in.at[src], msg_in.at[src], m_s.at[step - 1], m_r.at[src], dp_dev(src))

    for step in range(1, n_dp):
        msg_copy(step).start()

    def gather_send(l, p, slab, k, dev):
        return remote(
            wt.at[l, p, slab], wt.at[l, p, slab], g_s.at[l, p, k], g_r.at[l, p, slab], dp_dev(dev)
        )

    def y_peers():
        return [my_z * n_y + lax.rem(my_y + s, n_y) for s in range(1, n_y)]

    def gather_begin(l, p):
        for s in range(1, n_z):
            gather_send(l, p, me, s - 1, z_peer(s) * n_y + my_y).start()
        gather_send(l, p, me, n_z - 1, y_peers()[0]).start()

    def gather_forward(l, p):
        for s in range(1, n_z):
            slab = z_peer(s) * n_y + my_y
            gather_send(l, p, slab, n_z + s - 1, slab).wait_recv()
            gather_send(l, p, slab, n_z + s - 1, y_peers()[0]).start()

    def gather_finish(l, p):
        for s in range(0, n_z):
            slab = z_peer(s) * n_y + lax.rem(my_y + 1, n_y)
            gather_send(l, p, slab, 0, slab).wait_recv()

    def gather_drain(l, p):
        for k in range(2 * n_z - 1):
            gather_send(l, p, me, k, me).wait_send()

    def relayout(l, p):
        cols = []
        for b in range(8):
            blk = PARTS[p][b]
            xs = [g_out[l, blk, pl.ds(m, 24, stride=3), :] for m in range(3)]
            square = flat_to_square(*xs, place.at[b])
            cols.append(jnp.transpose(square) if blk in TRANSPOSED[p] else square)
        wt[l, p, me] = jnp.concatenate(cols, axis=1).astype(BF16)

    def relayout_layer(l, carry):
        load_blocks(l).wait()
        for p in range(3):
            relayout(l, p)
            gather_begin(l, p)
        return carry

    lax.fori_loop(0, LAYERS, relayout_layer, 0)

    seq_shift = jnp.where(long_ref[0, 0] > 0, 0, 1)
    seg = seg_ref[...]
    pos = lax.broadcasted_iota(jnp.int32, (8, 128), 0) * 128 + lax.broadcasted_iota(
        jnp.int32, (8, 128), 1
    )
    seq = (pos >> 8) * seq_shift
    kid = jnp.where(seg >= 0, seq * 64 + seg, -1 - seq).astype(F32)
    for r in range(8):
        kid_row[r // 2, 0:1, 128 * (r % 2) : 128 * (r % 2) + 128] = kid[r : r + 1, :]
        kid_col[r] = jnp.transpose(
            jnp.broadcast_to(kid[r : r + 1, :], (128, 128))
        )

    gvecs[...] = jnp.zeros_like(gvecs)
    gbias[...] = jnp.zeros_like(gbias)

    for step in range(1, n_dp):
        msg_from(step).wait_recv()
    for l in range(LAYERS):
        vecs[l] = jnp.concatenate(
            [msg_in[s, 8 * l : 8 * l + 8, 0:B] for s in range(n_dp)], axis=1
        )
        rows = [msg_in[s, 8 * l : 8 * l + 8, 128:256] for s in range(n_dp)]
        pad = jnp.zeros((8, D // 4), F32)
        bias_row[l] = jnp.concatenate(
            [r[:, 0:24] for r in rows]
            + [pad]
            + [r[:, 24:48] for r in rows]
            + [jnp.zeros((8, 64), F32)],
            axis=1,
        )

    low_half = lanes_of((CHUNK, 128)) < 64

    def vec(l, k):
        return vecs[l, k : k + 1, :]

    def core_copy(j):
        return remote(stage.at[j, other_c], core_in.at[j], c_s.at[j], c_r.at[j], sibling)

    def x_copy(j, par):
        return remote(stage.at[j, my_c], x_in.at[par, j], x_s.at[par, j], x_r.at[par, j], across)

    def own_copy(ref, j):
        return remote(ref.at[j, my_c], ref.at[j, my_c], a_s.at[j], a_r.at[j], sibling)

    def send_partial(j, value):
        stage[j] = value.astype(BF16).reshape(2, HALF, D)
        core_copy(j).start()

    def pass_on(j, par):
        core_copy(j).wait()
        mine = stage[j, my_c].astype(F32) + core_in[j].astype(F32)
        stage[j, my_c] = mine.astype(BF16)
        x_copy(j, par).start()

    def total(j, par):
        x_copy(j, par).wait()
        return stage[j, my_c].astype(F32) + x_in[par, j].astype(F32)

    def project(l, j):
        rows = a_all[l, j].reshape(CHUNK, D)
        weight = wt[l, 0].reshape(D, D)[:, 0:640]
        out = dot_nn(rows, weight) + bias_row[l, 0:1, :]
        tiles = [out[:, 128 * t : 128 * t + 128] for t in range(5)]
        q_roll = pltpu.roll(tiles[0], 64, 1)
        v_roll = pltpu.roll(tiles[3], 64, 1)
        zero = jnp.zeros((CHUNK, 128), F32)
        q_val = [
            jnp.where(low_half, zero, q_roll),
            jnp.where(low_half, q_roll, pltpu.roll(tiles[1], 64, 1)),
        ]
        k_val = [jnp.where(low_half, zero, tiles[1]), tiles[2]]
        v_val = [
            jnp.where(low_half, zero, v_roll),
            jnp.where(low_half, v_roll, pltpu.roll(tiles[4], 64, 1)),
        ]
        q_all[l, j] = jnp.concatenate(q_val, axis=1).astype(BF16)
        k_all[l, j] = jnp.concatenate(k_val, axis=1).astype(BF16)
        v_mat = jnp.concatenate(v_val, axis=1)
        v_all[l, j] = v_mat.astype(BF16)
        v_tr[:, pl.ds(pl.multiple_of(j * CHUNK, CHUNK), CHUNK)] = jnp.transpose(v_mat).astype(BF16)

    def head_tile(mat, h):
        if h == 0:
            return mat[:, 0:128]
        keep = low_half if h == 1 else jnp.logical_not(low_half)
        return jnp.where(keep, mat[:, 128:256], jnp.zeros((), mat.dtype))

    def tile_of(ref, l, h):
        full = ref[l].reshape(ROWS, 256)
        return full[:, 0:128] if h == 0 else full[:, 128:256]

    def allowed_of(j):
        col = kid_col[...].reshape(ROWS, 128)
        return jnp.concatenate([col, col], axis=1) == kid_row[j, 0:1, :]

    def attend_chunk(l, j):
        allowed = allowed_of(j)
        q_mat = q_all[l, j]
        outs = [jnp.zeros((64, CHUNK), F32)]
        for h in range(HEADS_DEV):
            scores = dot_nt(tile_of(k_all, l, h), head_tile(q_mat, h)) * scale
            scores = jnp.where(allowed, scores, big_negative)
            top = jnp.max(scores, axis=0, keepdims=True)
            expo = jnp.exp(scores - top)
            tot = jnp.sum(expo, axis=0, keepdims=True)
            lse_all[l, j, h : h + 1, :] = top + jnp.log(tot)
            out = dot_nn(v_tr[64 + 64 * h : 128 + 64 * h, :], expo.astype(BF16))
            outs.append(out / tot)
        o_mat = jnp.transpose(jnp.concatenate(outs, axis=0)).astype(BF16)
        o_all[l, j] = o_mat
        send_partial(j, dot_nt(o_mat, wt[l, 0].reshape(D, D)[:, 512:768]))

    def middle(l, j):
        mid = res[2 * l, j] + total(j, 0) + vec(l, 4)
        res[2 * l + 1, j] = mid
        hat, _ = norm_rows(mid)
        c_all[l, j, my_c] = (hat * vec(l, 2) + vec(l, 3)).astype(BF16)
        own_copy(c_all.at[l], j).start()

    def mlp(l, j):
        own_copy(c_all.at[l], j).wait()
        rows = c_all[l, j].reshape(CHUNK, D)
        pre = dot_nn(rows, wt[l, 1].reshape(D, D)) + vec(l, 6)
        cdf = 0.5 * (1.0 + lax.erf(pre * (1.0 / math.sqrt(2.0))))
        pdf = jnp.exp(-0.5 * pre * pre) * (1.0 / math.sqrt(2.0 * math.pi))
        act = (pre * cdf).astype(BF16)
        z_all[l, j] = act
        gp_all[l, j] = (cdf + pre * pdf).astype(BF16)

        @pl.when(jnp.logical_and(l == 0, j == 0))
        def _():
            gather_finish(0, 2)

        send_partial(j, dot_nt(z_all[l, j], wt[l, 2].reshape(D, D)))

    def out_copies(ref, hbm, which, j):
        return (
            pltpu.make_async_copy(ref.at[j], hbm.at[j, my_c], out_sem.at[which, j]),
            remote(ref.at[j], hbm.at[j, my_c], far_s.at[which, j], far_r.at[which, j], sibling),
        )

    def layer_end(l, j):
        new = res[2 * l + 1, j] + total(j, 1) + vec(l, 5)

        @pl.when(l < LAYERS - 1)
        def _():
            res[2 * LAYERS - 2, j] = new
            hat, _ = norm_rows(new)
            a_all[LAYERS - 1, j, my_c] = (hat * vec(LAYERS - 1, 0) + vec(LAYERS - 1, 1)).astype(BF16)
            own_copy(a_all.at[LAYERS - 1], j).start()

        @pl.when(l == LAYERS - 1)
        def _():
            x_out[j] = new
            for copy in out_copies(x_out, bo_hbm, 0, j):
                copy.start()

    def when_chunk(tick, offset, func):
        @pl.when(jnp.logical_and(tick >= offset, tick < offset + CHUNKS))
        def _():
            func(tick - offset)

    def at(cond, func):
        @pl.when(cond)
        def _():
            func()

    def first_norm(j, carry):
        load_rows(j, 0).wait()
        load_rows(j, 1).wait()
        hat, _ = norm_rows(res[0, j])
        a_all[0, j, my_c] = (hat * vec(0, 0) + vec(0, 1)).astype(BF16)
        hat, _ = norm_rows(res[1, j])
        a_all[0, j, other_c] = (hat * vec(0, 0) + vec(0, 1)).astype(BF16)
        return carry

    lax.fori_loop(0, CHUNKS, first_norm, 0)
    gather_forward(0, 0)
    gather_finish(0, 0)

    def first_project(j, carry):
        project(0, j)
        return carry

    lax.fori_loop(0, CHUNKS, first_project, 0)

    def forward_layer(l, carry):
        def step(tick, inner):
            when_chunk(tick, 1, lambda j: pass_on(j, 0))
            when_chunk(tick, 5, lambda j: pass_on(j, 1))
            when_chunk(tick, 3, lambda j: middle(l, j))
            when_chunk(tick, 7, lambda j: layer_end(l, j))
            when_chunk(tick, 0, lambda j: attend_chunk(l, j))

            def next_project(j):
                own_copy(a_all.at[LAYERS - 1], j).wait()
                project(LAYERS - 1, j)

            @pl.when(l == 0)
            def _():
                at(tick == 2, lambda: gather_forward(0, 1))

                @pl.when(tick == 4)
                def _():
                    gather_finish(0, 1)
                    gather_forward(0, 2)

                at(tick == 6, lambda: gather_forward(1, 0))
                at(tick == 8, lambda: gather_finish(1, 0))
                at(tick == 9, lambda: gather_forward(1, 1))

            @pl.when(l == 1)
            def _():
                at(tick == 3, lambda: gather_forward(1, 2))

                @pl.when(tick == 4)
                def _():
                    gather_finish(1, 1)
                    gather_finish(1, 2)

            when_chunk(tick, 4, lambda j: mlp(l, j))

            @pl.when(l == 0)
            def _():
                when_chunk(tick, 8, next_project)

            return inner

        lax.fori_loop(0, 12, step, 0)
        return carry

    lax.fori_loop(0, LAYERS, forward_layer, 0)

    def load_cot(j):
        return pltpu.make_async_copy(ct_hbm.at[j, my_c], y_own.at[j], ct_sem.at[j])

    for j in range(CHUNKS):
        load_cot(j).start()

    def first_grad(j, carry):
        load_cot(j).wait()
        rows = jnp.where(kid_col[2 * j + my_c][:, 0:1] >= 0.0, y_own[j], 0.0)
        y_own[j] = rows
        y_all[j, my_c] = rows.astype(BF16)
        own_copy(y_all, j).start()
        return carry

    lax.fori_loop(0, CHUNKS, first_grad, 0)

    def add_vec(l, k, value):
        gvecs[l, k : k + 1, :] += value

    def mlp_back(l, j):
        own_copy(y_all, j).wait()
        d_act = dot_nn(y_all[j].reshape(CHUNK, D), wt[l, 2].reshape(D, D))
        d_pre = (d_act * gp_all[l, j].astype(F32)).astype(BF16)
        du_all[j] = d_pre
        add_vec(l, 6, jnp.sum(d_pre.astype(F32), axis=0, keepdims=True))
        send_partial(j, dot_nt(du_all[j], wt[l, 1].reshape(D, D)))

    def middle_back(l, j):
        grad = total(j, 0)
        d_rows, d_gain, d_shift = norm_back(grad, res[2 * l + 1, j], vec(l, 2))
        y_rows = y_own[j]
        add_vec(l, 5, jnp.sum(y_rows, axis=0, keepdims=True))
        g_rows = y_rows + d_rows
        add_vec(l, 2, d_gain)
        add_vec(l, 3, d_shift)
        add_vec(l, 4, jnp.sum(g_rows, axis=0, keepdims=True))
        y_own[j] = g_rows
        g_all[j, my_c] = g_rows.astype(BF16)
        own_copy(g_all, j).start()

    def attend_back(l, j):
        own_copy(g_all, j).wait()
        d_out = dot_nn(g_all[j].reshape(CHUNK, D), wt[l, 0].reshape(D, D)[:, 512:768])
        do_mat = d_out.astype(BF16)
        prod = jnp.transpose(do_mat.astype(F32) * o_all[l, j].astype(F32))
        allowed = allowed_of(j)
        q_mat = q_all[l, j]
        dq_parts = []
        for h in range(HEADS_DEV):
            q_h = head_tile(q_mat, h)
            do_h = head_tile(do_mat, h)
            scores = dot_nt(tile_of(k_all, l, h), q_h) * scale
            scores = jnp.where(allowed, scores, big_negative)
            probs = jnp.exp(scores - lse_all[l, j, h : h + 1, :])
            delta = jnp.sum(prod[64 + 64 * h : 128 + 64 * h, :], axis=0, keepdims=True)
            d_probs = dot_nt(tile_of(v_all, l, h), do_h)
            d_scores = (probs * (d_probs - delta)).astype(BF16)
            t = 0 if h == 0 else 128
            dv_acc[:, t : t + 128] += dot_nn(probs.astype(BF16), do_h)
            dk_acc[:, t : t + 128] += dot_nn(d_scores, q_h)
            dq_parts.append(dot_nn(v_tr[64 + 64 * h : 128 + 64 * h, :], d_scores))
        dq_parts.append(jnp.zeros((64, CHUNK), F32))
        dq_mat = jnp.transpose(jnp.concatenate(dq_parts, axis=0) * scale)
        dx_all[j, :, 0:256] = dq_mat.astype(BF16)

    def project_back(l, j):
        rows = pl.ds(pl.multiple_of(j * CHUNK, CHUNK), CHUNK)
        dk_mat = dk_acc[rows, :] * scale
        dv_mat = dv_acc[rows, :]
        zero = jnp.zeros((CHUNK, 128), F32)
        roll_zero = pltpu.roll(dv_mat[:, 0:128], 64, 1)
        roll_one = pltpu.roll(dv_mat[:, 128:256], 64, 1)
        tile_one = jnp.where(low_half, dx_all[j, :, 128:256].astype(F32), dk_mat[:, 0:128])
        dx_all[j, :, 128:640] = jnp.concatenate(
            [
                tile_one,
                dk_mat[:, 128:256],
                jnp.where(low_half, roll_zero, roll_one),
                jnp.where(low_half, roll_one, zero),
            ],
            axis=1,
        ).astype(BF16)
        dx_mat = dx_all[j]
        gbias[l, 0:1, :] += jnp.sum(dx_mat.astype(F32), axis=0, keepdims=True)
        send_partial(j, dot_nt(dx_mat, wt[l, 0].reshape(D, D)[:, 0:640]))

    def layer_begin(l, j):
        grad = total(j, 1)
        d_rows, d_gain, d_shift = norm_back(grad, res[2 * l, j], vec(l, 0))
        add_vec(l, 0, d_gain)
        add_vec(l, 1, d_shift)
        new = y_own[j] + d_rows
        y_own[j] = new

        @pl.when(l > 0)
        def _():
            y_all[j, my_c] = new.astype(BF16)
            own_copy(y_all, j).start()

        @pl.when(l == 0)
        def _():
            for copy in out_copies(y_own, ig_hbm, 1, j):
                copy.start()

    def slab(ref, p, owner):
        return ref.at[p, pl.ds(pl.multiple_of(owner * B, B), B)]

    def pair_copy(l, p, z):
        dest = y_peers()[0]
        return remote(
            slab(dw, p, z * n_y + lax.rem(my_y + 1, n_y)),
            rs_one.at[l, p, z],
            p_s.at[l, p, z],
            p_r.at[l, p, z],
            dp_dev(dest),
        )

    def line_copy(l, p, s):
        dest = z_peer(s)
        return remote(
            slab(dw, p, dest * n_y + my_y),
            rs_two.at[l, p, n_z - 1 - s],
            t_s.at[l, p, s - 1],
            t_r.at[l, p, n_z - 1 - s],
            dp_dev(dest * n_y + my_y),
        )

    def line_from(l, p, s):
        return remote(
            slab(dw, p, me),
            rs_two.at[l, p, s - 1],
            t_s.at[l, p, s - 1],
            t_r.at[l, p, s - 1],
            dp_dev(z_peer(s) * n_y + my_y),
        )

    def scatter_drain(l, p):
        for z in range(n_z):
            pair_copy(l, p, z).wait_send()
        for s in range(1, n_z):
            line_copy(l, p, s).wait_send()

    def scatter_begin(l, p):
        for z in range(n_z):
            pair_copy(l, p, z).start()

    def scatter_middle(l, p):
        for s in list(range(1, n_z)) + [0]:
            z = z_peer(s)
            pair_copy(l, p, z).wait_recv()
            ref = slab(dw, p, z * n_y + my_y)
            ref[...] = (ref[...].astype(F32) + rs_one[l, p, z].astype(F32)).astype(BF16)
            if s:
                line_copy(l, p, s).start()

    def block_copies(l, p):
        runs = ((0, 6), (14, 2)) if p == 0 else ((PARTS[p][0], 8),)
        return [
            pltpu.make_async_copy(
                g_out.at[l, pl.ds(first, count)],
                gb_hbm.at[l, pl.ds(first, count)],
                gout_sem.at[l, p + 3 * k],
            )
            for k, (first, count) in enumerate(runs)
        ]

    def scatter_end(l, p):
        acc = slab(dw, p, me)[...].astype(F32)
        for s in range(1, n_z):
            line_from(l, p, s).wait_recv()
            acc = acc + rs_two[l, p, s - 1].astype(F32)
        nm_ref[0:1, 0:1] += jnp.sum(acc * acc, keepdims=True)
        for b in range(8):
            square = acc[:, B * b : B * b + B]
            blk = PARTS[p][b]
            g_out[l, blk, :, 0:B] = jnp.transpose(square) if blk in TRANSPOSED[p] else square
        for copy in block_copies(l, p):
            copy.start()

    nm_ref[...] = jnp.zeros_like(nm_ref)

    def weight_grad(l, p, func):
        at(l < LAYERS - 1, lambda: scatter_drain(LAYERS - 1, p))

        def piece(m, carry):
            cols = pl.ds(pl.multiple_of(m * 256, 256), 256)
            dw[p, cols, :] = func(cols).astype(BF16)
            return carry

        lax.fori_loop(0, D // 256, piece, 0)
        scatter_begin(l, p)

    def down_grad(l):
        def func(cols):
            return dot_tn(
                y_all[:, :, :, cols].reshape(ROWS, 256), z_all[l].reshape(ROWS, D)
            )

        weight_grad(l, 2, func)

    def up_grad(l):
        def func(cols):
            return dot_tn(
                c_all[l, :, :, :, cols].reshape(ROWS, 256), du_all[...].reshape(ROWS, D)
            )

        weight_grad(l, 1, func)

    def qkv_grad(l):
        def func(cols):
            first = dot_tn(
                a_all[l, :, :, :, cols].reshape(ROWS, 256), dx_all[...].reshape(ROWS, 640)
            )
            second = dot_tn(
                g_all[:, :, :, cols].reshape(ROWS, 256), o_all[l].reshape(ROWS, 256)
            )
            return jnp.concatenate(
                [first[:, 0:512], first[:, 512:640] + second[:, 0:128], second[:, 128:256]], axis=1
            )

        weight_grad(l, 0, func)

    def wait_blocks(l, p):
        for copy in block_copies(l, p):
            copy.wait()

    def backward_layer(n, carry):
        l = LAYERS - 1 - n
        for j in range(CHUNKS):
            v_tr[:, j * CHUNK : j * CHUNK + CHUNK] = jnp.transpose(k_all[l, j].astype(F32)).astype(
                BF16
            )
        dk_acc[...] = jnp.zeros_like(dk_acc)
        dv_acc[...] = jnp.zeros_like(dv_acc)

        def step(tick, inner):
            when_chunk(tick, 1, lambda j: pass_on(j, 0))
            when_chunk(tick, 3, lambda j: middle_back(l, j))
            when_chunk(tick, 0, lambda j: mlp_back(l, j))
            at(tick == 3, lambda: down_grad(l))
            at(tick == 4, lambda: up_grad(l))
            when_chunk(tick, 4, lambda j: attend_back(l, j))
            at(tick == 6, lambda: scatter_middle(l, 2))
            at(tick == 7, lambda: scatter_middle(l, 1))
            return inner

        lax.fori_loop(0, 8, step, 0)

        def step_two(tick, inner):
            when_chunk(tick, 1, lambda j: pass_on(j, 1))
            when_chunk(tick, 3, lambda j: layer_begin(l, j))
            when_chunk(tick, 0, lambda j: project_back(l, j))
            at(tick == 3, lambda: qkv_grad(l))

            at(tick == 5, lambda: scatter_end(l, 2))

            @pl.when(tick == 6)
            def _():
                scatter_end(l, 1)
                scatter_middle(l, 0)

            return inner

        lax.fori_loop(0, 7, step_two, 0)
        scatter_end(l, 0)
        return carry

    lax.fori_loop(0, LAYERS, backward_layer, 0)

    sib = remote(gvecs, sib_in, sib_s.at[0], sib_r.at[0], sibling)
    sib.start()
    sib.wait()
    row_at = lax.broadcasted_iota(jnp.int32, (8, D), 0)
    for l in range(LAYERS):
        mat = gvecs[l] + jnp.where(row_at < 6, sib_in[l], 0.0)
        extra = gbias[l]
        for s in range(n_dp):
            gmsg_out[s, 8 * l : 8 * l + 8, 0:B] = mat[:, B * s : B * s + B]
            gmsg_out[s, 8 * l : 8 * l + 8, 128:152] = extra[:, 24 * s : 24 * s + 24]
            gmsg_out[s, 8 * l : 8 * l + 8, 152:176] = extra[:, 384 + 24 * s : 384 + 24 * s + 24]
            gmsg_out[s, 8 * l : 8 * l + 8, B:128] = jnp.zeros((8, 128 - B), F32)
            gmsg_out[s, 8 * l : 8 * l + 8, 176:256] = jnp.zeros((8, 80), F32)

    def gmsg_copy(step):
        dest = lax.rem(me + step, n_dp)
        return remote(
            gmsg_out.at[dest], gmsg_in.at[me], gm_s.at[step - 1], gm_r.at[me], dp_dev(dest)
        )

    def gmsg_from(step):
        src = lax.rem(me + step, n_dp)
        return remote(gmsg_out.at[src], gmsg_in.at[src], gm_s.at[step - 1], gm_r.at[src], dp_dev(src))

    for step in range(1, n_dp):
        gmsg_copy(step).start()
    gmsg_in[me] = gmsg_out[me]
    for step in range(1, n_dp):
        gmsg_from(step).wait_recv()
    summed = gmsg_in[0]
    for s in range(1, n_dp):
        summed = summed + gmsg_in[s]
    sg_ref[...] = summed

    squares = summed * summed
    lane = lanes_of((1, 128))
    packed = jnp.where(lane == 0, nm_ref[0:1, :], 0.0)
    shared_sums = jnp.zeros((1, 128), F32)
    for l in range(LAYERS):
        base = 8 * l
        up = jnp.sum(squares[base + 6 : base + 7, 0:B], keepdims=True)
        query = jnp.sum(squares[base : base + 1, 128:152], keepdims=True)
        value = jnp.sum(squares[base : base + 1, 152:176], keepdims=True)
        for k, item in enumerate((query, value, up)):
            packed = packed + jnp.where(lane == 1 + 3 * l + k, item, 0.0)
        for r in range(6):
            item = jnp.sum(squares[base + r : base + r + 1, 0:B], keepdims=True)
            shared_sums = shared_sums + jnp.where(lane == 6 * l + r, item, 0.0)

    for hop, dev in enumerate((sibling, across)):
        nb_out[hop] = jnp.broadcast_to(packed, (8, 128))
        swap = remote(nb_out.at[hop], nb_in.at[hop], nb_s.at[hop], nb_r.at[hop], dev)
        swap.start()
        swap.wait()
        packed = packed + nb_in[hop, 0:1, :]
    row8 = lax.broadcasted_iota(jnp.int32, (8, 128), 0)
    nd_in[me] = jnp.where(row8 == 0, packed, jnp.where(row8 == 1, shared_sums, 0.0))

    def nd_copy(step):
        dest = lax.rem(me + step, n_dp)
        return remote(nd_in.at[me], nd_in.at[me], nd_s.at[step - 1], nd_r.at[me], dp_dev(dest))

    def nd_from(step):
        src = lax.rem(me + step, n_dp)
        return remote(nd_in.at[src], nd_in.at[src], nd_s.at[step - 1], nd_r.at[src], dp_dev(src))

    for step in range(1, n_dp):
        nd_copy(step).start()
    for step in range(1, n_dp):
        nd_from(step).wait_recv()
    acc = nd_in[0]
    for s in range(1, n_dp):
        acc = acc + nd_in[s]
    nm_ref[...] = acc

    for p in range(3):
        scatter_drain(0, p)
        for l in range(LAYERS):
            wait_blocks(l, p)
            gather_drain(l, p)
    for step in range(1, n_dp):
        msg_copy(step).wait_send()
        gmsg_copy(step).wait_send()
        nd_copy(step).wait_send()
    for j in range(CHUNKS):
        for which, (ref, hbm) in enumerate(((x_out, bo_hbm), (y_own, ig_hbm))):
            for copy in out_copies(ref, hbm, which, j):
                copy.wait()


def train_call(n_y, x_rows, ct_rows, seg, long_flag, blocks, split, shared):
    hbm = pl.BlockSpec(memory_space=pl.ANY)
    vmem = pl.BlockSpec(memory_space=pltpu.VMEM)
    smem = pl.BlockSpec(memory_space=pltpu.SMEM)
    dma = pltpu.SemaphoreType.DMA
    n_dp = GROUPS
    n_z = n_dp // n_y

    def buf(shape, dtype=BF16):
        return pltpu.VMEM(shape, dtype)

    scratch = [
        buf((LAYERS, 3, n_dp, B, D)),
        buf((LAYERS, CHUNKS, 2, HALF, D)),
        buf((LAYERS, CHUNKS, 2, HALF, D)),
        buf((LAYERS, CHUNKS, CHUNK, 256)),
        buf((LAYERS, CHUNKS, CHUNK, 256)),
        buf((LAYERS, CHUNKS, CHUNK, 256)),
        buf((256, ROWS)),
        buf((LAYERS, CHUNKS, CHUNK, 256)),
        buf((LAYERS, CHUNKS, 8, CHUNK), F32),
        buf((LAYERS, CHUNKS, CHUNK, D)),
        buf((LAYERS, CHUNKS, CHUNK, D)),
        buf((2 * LAYERS, CHUNKS, HALF, D), F32),
        buf((CHUNKS, HALF, D), F32),
        buf((CHUNKS, 2, HALF, D)),
        buf((CHUNKS, 2, HALF, D)),
        buf((CHUNKS, CHUNK, D)),
        buf((CHUNKS, CHUNK, 640)),
        buf((ROWS, 256), F32),
        buf((ROWS, 256), F32),
        buf((CHUNKS, 2, HALF, D)),
        buf((CHUNKS, HALF, D)),
        buf((2, CHUNKS, HALF, D)),
        buf((3, D, D)),
        buf((LAYERS, 3, n_z, B, D)),
        buf((LAYERS, 3, n_z - 1, B, D)),
        buf((8, B, 128), F32),
        buf((LAYERS, GROUP, B, 128), F32),
        buf((CHUNKS, HALF, D), F32),
        buf((8, HALF, 128), F32),
        buf((CHUNKS, 8, CHUNK), F32),
        buf((LAYERS, 8, D), F32),
        buf((LAYERS, 8, 640), F32),
        buf((LAYERS, 8, D), F32),
        buf((LAYERS, 8, 640), F32),
        buf((LAYERS, 8, D), F32),
        buf((n_dp, 16, 256), F32),
        buf((n_dp, 16, 256), F32),
        buf((n_dp, 16, 256), F32),
        buf((2, 8, 128), F32),
        buf((2, 8, 128), F32),
        buf((n_dp, 8, 128), F32),
        dma((LAYERS, 3, 2 * n_z - 1)),
        dma((LAYERS, 3, n_dp)),
        dma((CHUNKS,)),
        dma((CHUNKS,)),
        dma((2, CHUNKS)),
        dma((2, CHUNKS)),
        dma((CHUNKS,)),
        dma((CHUNKS,)),
        dma((LAYERS, 3, n_z)),
        dma((LAYERS, 3, n_z)),
        dma((LAYERS, 3, n_z - 1)),
        dma((LAYERS, 3, n_z - 1)),
        dma((2, CHUNKS)),
        dma((LAYERS,)),
        dma((CHUNKS,)),
        dma((2, CHUNKS)),
        dma((2, CHUNKS)),
        dma((2, CHUNKS)),
        dma((LAYERS, 4)),
        dma((n_dp - 1,)),
        dma((n_dp,)),
        dma((n_dp - 1,)),
        dma((n_dp,)),
        dma((1,)),
        dma((1,)),
        dma((2,)),
        dma((2,)),
        dma((n_dp - 1,)),
        dma((n_dp,)),
    ]
    rows_shape = jax.ShapeDtypeStruct((CHUNKS, 2, HALF, D), F32)
    return pl.pallas_call(
        functools.partial(train_kernel, n_y),
        out_shape=(
            rows_shape,
            rows_shape,
            jax.ShapeDtypeStruct((LAYERS, GROUP, B, 128), F32),
            jax.ShapeDtypeStruct((16, 256), F32),
            jax.ShapeDtypeStruct((8, 128), F32),
        ),
        in_specs=[hbm, hbm, vmem, smem, hbm, vmem, vmem],
        out_specs=(hbm, hbm, hbm, vmem, vmem),
        scratch_shapes=scratch,
        compiler_params=pltpu.CompilerParams(
            collective_id=0, has_side_effects=True, vmem_limit_bytes=60 * 1024 * 1024
        ),
        cost_estimate=pl.CostEstimate(
            flops=30_000_000_000, bytes_accessed=30_000_000, transcendentals=20_000_000
        ),
        name="train",
    )(x_rows, ct_rows, seg, long_flag, blocks, split, shared)


def update_kernel(
    g_ref,
    w_ref,
    l_ref,
    r_ref,
    lr_ref,
    rr_ref,
    sg_ref,
    nm_ref,
    sp_ref,
    sh_ref,
    gout_ref,
    nw_ref,
    nl_ref,
    nr_ref,
    sgo_ref,
    nsp_ref,
    shg_ref,
    nsh_ref,
    norm_ref,
    place,
):
    lane = lanes_of((1, 128))
    row_zero = nm_ref[0:1, :]
    row_one = nm_ref[1:2, :]
    total_sq = jnp.sum(jnp.where(lane < 7, row_zero, 0.0), keepdims=True) + jnp.sum(
        jnp.where(lane < 12, row_one, 0.0), keepdims=True
    )
    norm = jnp.sqrt(total_sq)
    factor = clip_limit / jnp.maximum(norm, clip_limit)
    squared = factor * factor

    for b in range(g_ref.shape[1]):
        grad = g_ref[0, b][:, 0:B]
        low = grad.astype(BF16)
        roots = []
        for k, ref in enumerate((lr_ref, rr_ref)):
            xs = [ref[0, b, pl.ds(m, 24, stride=3), :] for m in range(3)]
            roots.append(flat_to_square(*xs, place.at[6 * b + k]))
        left_gram = dot_nt(low, low)
        right_gram = dot_tn(low, low)
        partial_dir = dot_nn(roots[0].astype(BF16), low)
        direction = dot_nn(partial_dir.astype(BF16), roots[1].astype(BF16)) * factor
        mean_sq = jnp.mean(direction * direction, keepdims=True)
        step = direction * (rate_matrix * lax.rsqrt(mean_sq + eps_norm))
        grad_flat = square_to_flat(grad, place.at[6 * b + 2])
        left_flat = square_to_flat(left_gram, place.at[6 * b + 3])
        right_flat = square_to_flat(right_gram, place.at[6 * b + 4])
        step_flat = square_to_flat(step, place.at[6 * b + 5])
        weight = (1.0 - decay) * squared
        for m in range(3):
            rows = pl.ds(m, 24, stride=3)
            gout_ref[0, b, rows, :] = grad_flat[m] * factor
            nl_ref[0, b, rows, :] = decay * l_ref[0, b, rows, :] + weight * left_flat[m]
            nr_ref[0, b, rows, :] = decay * r_ref[0, b, rows, :] + weight * right_flat[m]
            nw_ref[0, b, rows, :] = w_ref[0, b, rows, :] - step_flat[m]

    @pl.when((pl.program_id(0) == 0) & (pl.program_id(1) == 0))
    def _():
        norm_ref[...] = norm
        sel = table_selector((144, 256))
        col = lax.broadcasted_iota(jnp.int32, (8, 256), 1)
        for l in range(LAYERS):
            sums = [row_zero[:, 1 + 3 * l + k : 2 + 3 * l + k] for k in range(3)]
            means = [sums[0] / D, sums[1] / D, sums[2] / FF]
            scales = [lax.rsqrt(squared * m + eps_norm) for m in means]
            src = sg_ref[8 * l : 8 * l + 8, :]
            line = jnp.where(col[0:1] < 128, src[6:7, :], src[0:1, :]) * factor
            step = line * jnp.where(
                col[0:1] < 128, scales[2], jnp.where(col[0:1] < 152, scales[0], scales[1])
            )
            both = jnp.concatenate([line, step, jnp.zeros((6, 256), F32)], axis=0)
            table = lax.dot_general(
                both, sel, (((1,), (1,)), ((), ())), precision=highest, preferred_element_type=F32
            )
            sgo_ref[l : l + 1, :] = table[0:1, :]
            nsp_ref[l : l + 1, :] = sp_ref[l : l + 1, :] - rate_vector * table[1:2, :]
            for r in range(6):
                mean = row_one[:, 6 * l + r : 6 * l + r + 1] / D
                grad = src[r : r + 1, 0:B] * factor
                shg_ref[6 * l + r : 6 * l + r + 1, :] = grad
                nsh_ref[6 * l + r : 6 * l + r + 1, :] = sh_ref[
                    6 * l + r : 6 * l + r + 1, :
                ] - rate_vector * grad * lax.rsqrt(squared * mean + eps_norm)


def update_call(grads, weights, left, right, left_roots, right_roots, sums, norms, split, shared):
    per = 4
    flat = pl.BlockSpec((1, per, 72, 128), lambda i, j: (i, j, 0, 0))
    square = pl.BlockSpec((1, per, B, 128), lambda i, j: (i, j, 0, 0))

    def whole(shape):
        return pl.BlockSpec(shape, lambda i, j: (0,) * len(shape))

    flat_shape = jax.ShapeDtypeStruct((LAYERS, GROUP, 72, 128), F32)
    return pl.pallas_call(
        update_kernel,
        grid=(LAYERS, GROUP // per),
        out_shape=(
            flat_shape,
            flat_shape,
            flat_shape,
            flat_shape,
            jax.ShapeDtypeStruct((LAYERS, 144), F32),
            jax.ShapeDtypeStruct((LAYERS, 144), F32),
            jax.ShapeDtypeStruct((6 * LAYERS, B), F32),
            jax.ShapeDtypeStruct((6 * LAYERS, B), F32),
            jax.ShapeDtypeStruct((1, 1), F32),
        ),
        in_specs=[square, flat, flat, flat, flat, flat]
        + [whole((16, 256)), whole((8, 128)), whole((LAYERS, 144)), whole((6 * LAYERS, B))],
        out_specs=(
            flat,
            flat,
            flat,
            flat,
            whole((LAYERS, 144)),
            whole((LAYERS, 144)),
            whole((6 * LAYERS, B)),
            whole((6 * LAYERS, B)),
            whole((1, 1)),
        ),
        scratch_shapes=[pltpu.VMEM((6 * per, B, 128), F32)],
        compiler_params=pltpu.CompilerParams(vmem_limit_bytes=32 * 1024 * 1024),
        name="update",
    )(grads, weights, left, right, left_roots, right_roots, sums, norms, split, shared)


def fast_body(
    n_y,
    tokens_in,
    cotangent,
    segment_ids,
    long_seq,
    weights,
    left_stats,
    right_stats,
    left_roots,
    right_roots,
    split_params,
    shared_params,
):
    rows = (CHUNKS, 2, HALF, D)
    flat = (LAYERS, GROUP, 72, 128)
    split = split_params.reshape(LAYERS, 144)
    shared = shared_params.reshape(6 * LAYERS, B)
    blocks = weights.reshape(flat)
    out_rows, in_grad, grads, sums, norms = train_call(
        n_y,
        tokens_in.reshape(rows),
        cotangent.reshape(rows),
        segment_ids.reshape(8, 128),
        long_seq.reshape(1, 1),
        blocks,
        split,
        shared,
    )
    res = update_call(
        grads,
        blocks,
        left_stats.reshape(flat),
        right_stats.reshape(flat),
        left_roots.reshape(flat),
        right_roots.reshape(flat),
        sums,
        norms,
        split,
        shared,
    )
    mats = [r.reshape(weights.shape) for r in res[:4]]
    return (
        out_rows.reshape(tokens_in.shape),
        in_grad.reshape(tokens_in.shape),
        *mats,
        res[4].reshape(split_params.shape),
        res[5].reshape(split_params.shape),
        res[6].reshape(shared_params.shape),
        res[7].reshape(shared_params.shape),
        res[8].reshape(()),
    )


def solution(mesh):
    in_specs = (
        P("dp", None),
        P("dp", None),
        P("dp"),
        P("dp"),
        P(None, "dp", "tensor", None),
        P(None, "dp", "tensor", None),
        P(None, "dp", "tensor", None),
        P(None, "dp", "tensor", None),
        P(None, "dp", "tensor", None),
        P(None, "tensor", "dp"),
        P(None, None, "dp"),
    )
    out_specs = (
        P("dp", None),
        P("dp", None),
        P(None, "dp", "tensor", None),
        P(None, "dp", "tensor", None),
        P(None, "dp", "tensor", None),
        P(None, "dp", "tensor", None),
        P(None, "tensor", "dp"),
        P(None, "tensor", "dp"),
        P(None, None, "dp"),
        P(None, None, "dp"),
        P(),
    )
    plan = body
    if mesh.shape["dp"] == GROUPS and mesh.shape["tensor"] == 4:
        plan = functools.partial(fast_body, 2)
    return jax.shard_map(plan, mesh=mesh, in_specs=in_specs, out_specs=out_specs, check_vma=False)
```

```python
import functools
import math

import jax
import jax.numpy as jnp
from jax import lax
from jax.experimental import pallas as pl
from jax.experimental.pallas import tpu as pltpu
from jax.sharding import PartitionSpec as P

D = 768
HEADS = 12
FF = 3072
HD = 64
B = 96
LAYERS = 2
SEQ_SHORT = 256
SEQ_LONG = 1024


clip_limit = 100.0
rate_matrix = 0.06
rate_vector = 0.2
decay = 0.5
eps_norm = 1e-06
eps_layer = 1e-06
big_negative = -1e30
highest = lax.Precision.HIGHEST


def layer_norm(hidden, gain_vec, shift_vec):
    row_mean = jnp.mean(hidden, axis=-1, keepdims=True)
    centered = hidden - row_mean
    row_var = jnp.mean(centered * centered, axis=-1, keepdims=True)
    return centered * lax.rsqrt(row_var + eps_layer) * gain_vec + shift_vec


def gelu_exact(values):
    return jax.nn.gelu(values, approximate=False)


def matmul_low(left_mat, right_mat):
    return jnp.dot(left_mat, right_mat, preferred_element_type=jnp.float32)


def inner_rows(left_mat, right_mat):
    return lax.dot_general(
        left_mat, right_mat, (((0,), (0,)), ((), ())), preferred_element_type=jnp.float32
    )


def times_trans(left_mat, right_mat):
    return lax.dot_general(
        left_mat, right_mat, (((1,), (1,)), ((), ())), preferred_element_type=jnp.float32
    )


def unpack_layer(blocks, embed_dev, inner_dev):
    row_groups = blocks.shape[0]
    block_size = blocks.shape[2]
    qkv_count = 3 * embed_dev // block_size
    up_count = inner_dev // block_size
    out_count = embed_dev // block_size

    def by_rows(part_blocks):
        block_count = part_blocks.shape[1]
        return jnp.transpose(part_blocks, (0, 2, 1, 3)).reshape(
            row_groups * block_size, block_count * block_size
        )

    def by_cols(part_blocks):
        block_count = part_blocks.shape[1]
        return jnp.transpose(part_blocks, (1, 2, 0, 3)).reshape(
            block_count * block_size, row_groups * block_size
        )

    qkv_weight = by_rows(blocks[:, :qkv_count])
    up_weight = by_rows(blocks[:, qkv_count : qkv_count + up_count])
    out_weight = by_cols(blocks[:, qkv_count + up_count : qkv_count + up_count + out_count])
    down_weight = by_cols(blocks[:, qkv_count + up_count + out_count :])
    return (qkv_weight, out_weight, up_weight, down_weight)


def pack_layer(qkv_grad, out_grad, up_grad, down_grad, block_size):
    row_groups = qkv_grad.shape[0] // block_size

    def from_rows(matrix):
        block_count = matrix.shape[1] // block_size
        return jnp.transpose(
            matrix.reshape(row_groups, block_size, block_count, block_size), (0, 2, 1, 3)
        )

    def from_cols(matrix):
        block_count = matrix.shape[0] // block_size
        return jnp.transpose(
            matrix.reshape(block_count, block_size, row_groups, block_size), (2, 0, 1, 3)
        )

    return jnp.concatenate(
        [from_rows(qkv_grad), from_rows(up_grad), from_cols(out_grad), from_cols(down_grad)], axis=1
    )


def masked_scores(query_block, key_window, query_seq, key_seq, query_seg, key_seg, score_scale):
    scores = (
        jnp.einsum("qhd,khd->hqk", query_block, key_window, preferred_element_type=jnp.float32)
        * score_scale
    )
    allowed = (query_seq[:, None] == key_seq[None, :]) & (query_seg[:, None] == key_seg[None, :])
    return jnp.where(allowed[None], scores, big_negative)


def attention_forward(queries, keys_all, values_all, seq_index, segments, block_rows, score_scale):
    block_count = queries.shape[0] // block_rows

    def one_block(block_index):
        row_start = block_index * block_rows
        query_block = lax.dynamic_slice_in_dim(queries, row_start, block_rows, 0)
        scores = masked_scores(
            query_block,
            keys_all,
            lax.dynamic_slice_in_dim(seq_index, row_start, block_rows, 0),
            seq_index,
            lax.dynamic_slice_in_dim(segments, row_start, block_rows, 0),
            segments,
            score_scale,
        )
        row_max = jnp.max(scores, axis=-1, keepdims=True)
        exponent = jnp.exp(scores - row_max)
        row_total = jnp.sum(exponent, axis=-1, keepdims=True)
        attn_probs = (exponent / row_total).astype(jnp.bfloat16)
        attended = jnp.einsum(
            "hqk,khd->qhd", attn_probs, values_all, preferred_element_type=jnp.float32
        )
        return (attended, (row_max + jnp.log(row_total))[..., 0])

    return lax.map(one_block, jnp.arange(block_count, dtype=jnp.int32))


def attention_backward(
    queries, keys_all, values_all, grad_out, log_total, seq_index, segments, block_rows, score_scale
):
    token_count = queries.shape[0]
    block_count = token_count // block_rows
    zero_grad = jnp.zeros(keys_all.shape, jnp.float32)

    def one_block(carry_pair, block_index):
        key_grad, value_grad = carry_pair
        row_start = block_index * block_rows
        query_block = lax.dynamic_slice_in_dim(queries, row_start, block_rows, 0)
        out_block = lax.dynamic_slice_in_dim(grad_out, row_start, block_rows, 0)
        scores = masked_scores(
            query_block,
            keys_all,
            lax.dynamic_slice_in_dim(seq_index, row_start, block_rows, 0),
            seq_index,
            lax.dynamic_slice_in_dim(segments, row_start, block_rows, 0),
            segments,
            score_scale,
        )
        lse_block = lax.dynamic_index_in_dim(log_total, block_index, 0, keepdims=False)
        attn_probs = jnp.exp(scores - lse_block[..., None])
        prob_grad = jnp.einsum(
            "qhd,khd->hqk", out_block, values_all, preferred_element_type=jnp.float32
        )
        row_delta = jnp.sum(attn_probs * prob_grad, axis=-1, keepdims=True)
        score_grad = (attn_probs * (prob_grad - row_delta)).astype(jnp.bfloat16)
        query_grad = (
            jnp.einsum("hqk,khd->qhd", score_grad, keys_all, preferred_element_type=jnp.float32)
            * score_scale
        )
        key_part = (
            jnp.einsum("hqk,qhd->khd", score_grad, query_block, preferred_element_type=jnp.float32)
            * score_scale
        )
        value_part = jnp.einsum(
            "hqk,qhd->khd",
            attn_probs.astype(jnp.bfloat16),
            out_block,
            preferred_element_type=jnp.float32,
        )
        key_grad = key_grad + key_part
        value_grad = value_grad + value_part
        return ((key_grad, value_grad), query_grad)

    (key_grad, value_grad), query_grad = lax.scan(
        one_block, (zero_grad, zero_grad), jnp.arange(block_count, dtype=jnp.int32)
    )
    return (query_grad.reshape(keys_all.shape), key_grad, value_grad)


def body(
    tokens_in,
    cotangent,
    segment_ids,
    long_seq,
    weights,
    left_stats,
    right_stats,
    left_roots,
    right_roots,
    split_params,
    shared_params,
):
    full_weights, full_split, full_shared = (
        lax.all_gather(weights, "dp", axis=1, tiled=True),
        lax.all_gather(split_params, "dp", axis=2, tiled=True),
        lax.all_gather(shared_params, "dp", axis=2, tiled=True),
    )
    tensor_count = lax.axis_size("tensor")
    embed_dev = D // tensor_count
    inner_dev = FF // tensor_count
    heads_local = HEADS // tensor_count
    token_count = tokens_in.shape[0]
    window = SEQ_LONG
    block_rows = min(512, window)
    score_scale = 1.0 / math.sqrt(HD)
    seq_length = jnp.where(long_seq[0] > 0, SEQ_LONG, SEQ_SHORT)
    positions = jnp.arange(token_count, dtype=jnp.int32)
    seq_index = positions // seq_length
    valid_rows = (segment_ids >= 0).astype(jnp.float32)
    matrices = []
    for layer_index in range(LAYERS):
        blocks = full_weights[layer_index, :, 0].astype(jnp.bfloat16).reshape(D // B, -1, B, B)
        matrices.append(unpack_layer(blocks, embed_dev, inner_dev))
    hidden_state = tokens_in
    kept_state = []
    for layer_index in range(LAYERS):
        qkv_weight, out_weight, up_weight, down_weight = matrices[layer_index]
        shared = full_shared[layer_index]
        bias_table = full_split[layer_index, 0].reshape(embed_dev, 6)
        up_bias = bias_table[:, 2:].reshape(inner_dev)
        normed = layer_norm(hidden_state, shared[0], shared[1]).astype(jnp.bfloat16)
        qkv_bias = jnp.concatenate(
            [bias_table[:, 0], jnp.zeros((embed_dev,), jnp.float32), bias_table[:, 1]]
        )
        projected = (matmul_low(normed, qkv_weight) + qkv_bias).astype(jnp.bfloat16)
        queries = projected[:, :embed_dev].reshape(token_count, heads_local, HD)
        keys_all = projected[:, embed_dev : 2 * embed_dev].reshape(token_count, heads_local, HD)
        values_all = projected[:, 2 * embed_dev :].reshape(token_count, heads_local, HD)
        attended, log_total = attention_forward(
            queries, keys_all, values_all, seq_index, segment_ids, block_rows, score_scale
        )
        attended = attended.reshape(token_count, embed_dev).astype(jnp.bfloat16)
        attn_branch = lax.psum(
            matmul_low(attended, out_weight).astype(jnp.bfloat16), "tensor"
        ).astype(jnp.float32)
        middle = hidden_state + attn_branch + shared[4]
        normed_mid = layer_norm(middle, shared[2], shared[3]).astype(jnp.bfloat16)
        pre_act = matmul_low(normed_mid, up_weight) + up_bias
        activation = gelu_exact(pre_act).astype(jnp.bfloat16)
        mlp_branch = lax.psum(
            matmul_low(activation, down_weight).astype(jnp.bfloat16), "tensor"
        ).astype(jnp.float32)
        kept_state.append(
            (
                hidden_state,
                normed,
                queries,
                keys_all,
                values_all,
                attended,
                log_total,
                middle,
                normed_mid,
                pre_act,
                activation,
            )
        )
        hidden_state = middle + mlp_branch + shared[5]
    grad_state = cotangent * valid_rows[:, None]
    layer_grads = [None] * LAYERS
    for layer_index in reversed(range(LAYERS)):
        (
            hidden_in,
            normed,
            queries,
            keys_all,
            values_all,
            attended,
            log_total,
            middle,
            normed_mid,
            pre_act,
            activation,
        ) = kept_state[layer_index]
        qkv_weight, out_weight, up_weight, down_weight = matrices[layer_index]
        shared = full_shared[layer_index]
        down_bias_grad = jnp.sum(grad_state, axis=0)
        grad_low = grad_state.astype(jnp.bfloat16)
        down_grad = inner_rows(activation, grad_low)
        act_grad = times_trans(grad_low, down_weight)
        gelu_pull = jax.vjp(gelu_exact, pre_act)[1]
        pre_grad = gelu_pull(act_grad)[0].astype(jnp.bfloat16)
        up_bias_grad = jnp.sum(pre_grad, axis=0, dtype=jnp.float32)
        up_grad = inner_rows(normed_mid, pre_grad)
        normed_mid_grad = lax.psum(times_trans(pre_grad, up_weight), "tensor")
        norm_pull = jax.vjp(layer_norm, middle, shared[2], shared[3])[1]
        middle_ln, gain_two_grad, shift_two_grad = norm_pull(normed_mid_grad)
        middle_grad = grad_state + middle_ln
        out_bias_grad = jnp.sum(middle_grad, axis=0)
        middle_low = middle_grad.astype(jnp.bfloat16)
        out_grad = inner_rows(attended, middle_low)
        attended_grad = (
            times_trans(middle_low, out_weight)
            .astype(jnp.bfloat16)
            .reshape(token_count, heads_local, HD)
        )
        query_grad, key_grad, value_grad = attention_backward(
            queries,
            keys_all,
            values_all,
            attended_grad,
            log_total,
            seq_index,
            segment_ids,
            block_rows,
            score_scale,
        )
        proj_grad = jnp.concatenate(
            [
                query_grad.reshape(token_count, embed_dev),
                key_grad.reshape(token_count, embed_dev),
                value_grad.reshape(token_count, embed_dev),
            ],
            axis=1,
        ).astype(jnp.bfloat16)
        query_bias_grad = jnp.sum(proj_grad[:, :embed_dev], axis=0, dtype=jnp.float32)
        value_bias_grad = jnp.sum(proj_grad[:, 2 * embed_dev :], axis=0, dtype=jnp.float32)
        qkv_grad = inner_rows(normed, proj_grad)
        normed_grad = lax.psum(times_trans(proj_grad, qkv_weight), "tensor")
        input_pull = jax.vjp(layer_norm, hidden_in, shared[0], shared[1])[1]
        hidden_ln, gain_one_grad, shift_one_grad = input_pull(normed_grad)
        grad_state = middle_grad + hidden_ln
        block_grads = pack_layer(qkv_grad, out_grad, up_grad, down_grad, B).reshape(-1, 1, B * B)
        split_vec = jnp.concatenate(
            [
                query_bias_grad[:, None],
                value_bias_grad[:, None],
                up_bias_grad.reshape(embed_dev, 4),
            ],
            axis=1,
        ).reshape(1, -1)
        shared_vec = jnp.stack(
            [
                gain_one_grad,
                shift_one_grad,
                gain_two_grad,
                shift_two_grad,
                out_bias_grad,
                down_bias_grad,
            ]
        )
        layer_grads[layer_index] = (block_grads, split_vec, shared_vec)
    weight_grad, split_grad, shared_grad = (
        lax.psum_scatter(
            jnp.stack([entry[0] for entry in layer_grads]), "dp", scatter_dimension=1, tiled=True
        ),
        lax.psum_scatter(
            jnp.stack([entry[1] for entry in layer_grads]), "dp", scatter_dimension=2, tiled=True
        ),
        lax.psum_scatter(
            jnp.stack([entry[2] for entry in layer_grads]), "dp", scatter_dimension=2, tiled=True
        ),
    )
    dp_index = lax.axis_index("dp")
    lead_shard = (lax.axis_index("tensor") == 0).astype(jnp.float32)
    slice_len = split_grad.shape[-1]
    global_pos = dp_index * slice_len + jnp.arange(slice_len, dtype=jnp.int32)
    table_column = global_pos % 6
    segment_of = (table_column >= 1).astype(jnp.int32) + (table_column >= 2).astype(jnp.int32)
    selector = (segment_of[:, None] == jnp.arange(3, dtype=jnp.int32)[None, :]).astype(jnp.float32)
    split_sq = split_grad[:, 0] * split_grad[:, 0]
    split_rows = jnp.dot(split_sq, selector, precision=highest)
    shared_sq = shared_grad * shared_grad
    shared_rows = jnp.sum(shared_sq, axis=-1) * lead_shard
    local_total = (
        jnp.sum(weight_grad * weight_grad) + jnp.sum(split_sq) + lead_shard * jnp.sum(shared_sq)
    )
    total_sq, split_rows, shared_rows = lax.psum(
        (local_total, split_rows, shared_rows), ("dp", "tensor")
    )
    grad_norm = jnp.sqrt(total_sq)
    factor = clip_limit / jnp.maximum(grad_norm, clip_limit)
    squared = factor * factor
    block_shape = weight_grad.shape[:-1] + (B, B)
    left_mats = left_roots.reshape(block_shape)
    right_mats = right_roots.reshape(block_shape)
    clipped = weight_grad * factor
    clipped_mats = clipped.reshape(block_shape)
    new_left = decay * left_stats + (1.0 - decay) * jnp.einsum(
        "...ij,...kj->...ik", clipped_mats, clipped_mats, precision=highest
    ).reshape(left_stats.shape)
    new_right = decay * right_stats + (1.0 - decay) * jnp.einsum(
        "...ji,...jk->...ik", clipped_mats, clipped_mats, precision=highest
    ).reshape(right_stats.shape)
    partial_dir = jnp.einsum("...ij,...jk->...ik", left_mats, clipped_mats, precision=highest)
    direction = jnp.einsum("...ij,...jk->...ik", partial_dir, right_mats, precision=highest)
    mean_sq = jnp.mean(direction * direction, axis=(-2, -1), keepdims=True)
    step_mats = direction * lax.rsqrt(mean_sq + eps_norm)
    new_weights = weights - rate_matrix * step_mats.reshape(weights.shape)
    vector_sizes = jnp.array([D, D, FF], jnp.float32)
    split_mean = jnp.dot(split_rows / vector_sizes[None, :], selector.T, precision=highest)
    split_clip = split_grad * factor
    new_split = split_params - rate_vector * split_clip * lax.rsqrt(
        squared * split_mean[:, None, :] + eps_norm
    )
    shared_clip = shared_grad * factor
    shared_mean = shared_rows / D
    new_shared = shared_params - rate_vector * shared_clip * lax.rsqrt(
        squared * shared_mean[..., None] + eps_norm
    )
    return (
        hidden_state,
        grad_state,
        clipped,
        new_weights,
        new_left,
        new_right,
        split_clip,
        new_split,
        shared_clip,
        new_shared,
        grad_norm,
    )


F32 = jnp.float32
BF16 = jnp.bfloat16
MESH = pl.DeviceIdType.MESH
CHUNKS = 4
HALF = 128
CHUNK = 2 * HALF
ROWS = CHUNKS * CHUNK
HEADS_DEV = 3
GROUPS = D // B
GROUP = 24
PARTS = ((0, 1, 2, 3, 4, 5, 14, 15), tuple(range(6, 14)), tuple(range(16, 24)))
TRANSPOSED = (frozenset((14, 15)), frozenset(), frozenset(range(16, 24)))


def dot_nn(left_mat, right_mat):
    return lax.dot_general(left_mat, right_mat, (((1,), (0,)), ((), ())), preferred_element_type=F32)


def dot_nt(left_mat, right_mat):
    return lax.dot_general(left_mat, right_mat, (((1,), (1,)), ((), ())), preferred_element_type=F32)


def dot_tn(left_mat, right_mat):
    return lax.dot_general(left_mat, right_mat, (((0,), (0,)), ((), ())), preferred_element_type=F32)


def lanes_of(shape):
    return lax.broadcasted_iota(jnp.int32, shape, len(shape) - 1)


def norm_rows(rows):
    mean = jnp.mean(rows, axis=-1, keepdims=True)
    centered = rows - mean
    var = jnp.mean(centered * centered, axis=-1, keepdims=True)
    inv = lax.rsqrt(var + eps_layer)
    return centered * inv, inv


def norm_back(grad, rows, gain):
    hat, inv = norm_rows(rows)
    scaled = grad * gain
    mean_one = jnp.mean(scaled, axis=-1, keepdims=True)
    mean_two = jnp.mean(scaled * hat, axis=-1, keepdims=True)
    d_rows = inv * (scaled - mean_one - hat * mean_two)
    return d_rows, jnp.sum(grad * hat, axis=0, keepdims=True), jnp.sum(grad, axis=0, keepdims=True)


def table_selector(shape):
    row = lax.broadcasted_iota(jnp.int32, shape, 0)
    col = lax.broadcasted_iota(jnp.int32, shape, 1)
    up_row = 6 * (col >> 2) + 2 + (col & 3)
    hit = (col < B) & (row == up_row)
    hit = hit | ((col >= 128) & (col < 152) & (row == 6 * (col - 128)))
    hit = hit | ((col >= 152) & (col < 176) & (row == 6 * (col - 152) + 1))
    return hit.astype(F32)


def flat_rows(ref):
    x_zero, x_one, x_two = [ref[pl.ds(m, 24, stride=3), :] for m in range(3)]
    lane = lanes_of((24, 128))
    x_half = pltpu.roll(x_two, 64, 1)
    return (
        x_zero,
        jnp.where(lane < 32, pltpu.roll(x_zero, 32, 1), pltpu.roll(x_one, 32, 1)),
        jnp.where(lane < 64, pltpu.roll(x_one, 64, 1), x_half),
        pltpu.roll(x_two, 96, 1),
    )


def flat_to_square(ref, place):
    for m, rows in enumerate(flat_rows(ref)):
        place[pl.ds(m, 24, stride=4), :] = rows
    return place[...][:, :B]


def split_rows(square, place):
    place[:, 0:B] = square
    return jnp.concatenate([place[pl.ds(m, 24, stride=4), :] for m in range(4)], axis=0)[:, :B]


def store_flat(ref, stacked):
    lane = lanes_of((24, 128))
    wide = jnp.concatenate([stacked, jnp.zeros((B, 128 - B), F32)], axis=1)
    m_zero, m_one, m_two, m_three = [wide[24 * m : 24 * m + 24] for m in range(4)]
    one_back = pltpu.roll(m_one, 96, 1)
    two_back = pltpu.roll(m_two, 64, 1)
    ref[pl.ds(0, 24, stride=3), :] = jnp.where(lane < 96, m_zero, one_back)
    ref[pl.ds(1, 24, stride=3), :] = jnp.where(lane < 64, one_back, two_back)
    ref[pl.ds(2, 24, stride=3), :] = jnp.where(lane < 32, two_back, pltpu.roll(m_three, 32, 1))


def train_kernel(
    n_y,
    x_hbm,
    ct_hbm,
    seg_ref,
    long_ref,
    w_hbm,
    lr_hbm,
    rr_hbm,
    split_ref,
    shared_ref,
    bo_hbm,
    ig_hbm,
    gf_hbm,
    lf_hbm,
    rf_hbm,
    pf_hbm,
    sg_ref,
    nm_ref,
    wt,
    a_all,
    c_all,
    q_all,
    k_all,
    v_all,
    v_tr,
    o_all,
    lse_all,
    z_all,
    gp_all,
    res,
    y_own,
    y_all,
    g_all,
    du_all,
    dx_all,
    dk_acc,
    dv_acc,
    stage,
    core_in,
    x_in,
    dw,
    rs_one,
    rs_two,
    place,
    flat,
    g_acc,
    x_out,
    kid_col,
    kid_row,
    vecs,
    bias_row,
    gvecs,
    gbias,
    sib_in,
    msg_in,
    gmsg_in,
    gmsg_out,
    nb_out,
    nb_in,
    nd_in,
    g_s,
    g_r,
    c_s,
    c_r,
    x_s,
    x_r,
    a_s,
    a_r,
    p_s,
    p_r,
    t_s,
    t_r,
    load_sem,
    land_sem,
    ct_sem,
    y_s,
    y_r,
    out_sem,
    far_s,
    far_r,
    gout_sem,
    root_sem,
    m_s,
    m_r,
    gm_s,
    gm_r,
    sib_s,
    sib_r,
    nb_s,
    nb_r,
    nd_s,
    nd_r,
):
    n_dp = GROUPS
    n_z = n_dp // n_y
    me = lax.axis_index("dp")
    ten = lax.axis_index("tensor")
    my_z, my_y = me // n_y, lax.rem(me, n_y)
    my_x, my_c = ten // 2, lax.rem(ten, 2)
    other_c = 1 - my_c
    sibling = (me, 2 * my_x + other_c)
    across = (me, 2 * (1 - my_x) + my_c)
    scale = 1.0 / math.sqrt(HD)

    def dp_dev(index):
        return (index, ten)

    def z_peer(step):
        return lax.rem(my_z + step, n_z)

    def remote(src, dst, send, recv, dev):
        return pltpu.make_async_remote_copy(
            src_ref=src, dst_ref=dst, send_sem=send, recv_sem=recv, device_id=dev, device_id_type=MESH
        )

    def at(cond, func):
        @pl.when(cond)
        def _():
            func()

    def load_rows(j, which):
        half = my_c if which == 0 else other_c
        return pltpu.make_async_copy(x_hbm.at[j, half], res.at[which, j], load_sem.at[which, j])

    def load_blocks(l):
        return pltpu.make_async_copy(
            w_hbm.at[l], flat.at[pl.ds(l * GROUP, GROUP)], land_sem.at[l]
        )

    def load_cot(j):
        return pltpu.make_async_copy(ct_hbm.at[j, my_c], y_own.at[j], ct_sem.at[j])

    for l in range(LAYERS):
        load_blocks(l).start()
    for j in range(CHUNKS):
        load_rows(j, 0).start()
        load_rows(j, 1).start()
    for j in range(CHUNKS):
        load_cot(j).start()

    barrier = pltpu.get_barrier_semaphore()
    for step in range(1, n_dp):
        pl.semaphore_signal(
            barrier, inc=1, device_id=dp_dev(lax.rem(me + step, n_dp)), device_id_type=MESH
        )
    pl.semaphore_signal(barrier, inc=1, device_id=sibling, device_id_type=MESH)
    pl.semaphore_signal(barrier, inc=1, device_id=across, device_id_type=MESH)

    sel = table_selector((144, 256))
    for l in range(LAYERS):
        row = lax.dot_general(
            jnp.broadcast_to(split_ref[l], (8, 144)),
            sel,
            (((1,), (0,)), ((), ())),
            precision=highest,
            preferred_element_type=F32,
        )
        msg_in[me, 8 * l : 8 * l + 8, :] = row
        for r in range(6):
            msg_in[me, 8 * l + r : 8 * l + r + 1, 0:B] = shared_ref[r, l : l + 1, :]

    pl.semaphore_wait(barrier, n_dp + 1)

    def msg_copy(step):
        return remote(
            msg_in.at[me], msg_in.at[me], m_s.at[step - 1], m_r.at[me],
            dp_dev(lax.rem(me + step, n_dp)),
        )

    def msg_from(step):
        src = lax.rem(me + step, n_dp)
        return remote(msg_in.at[src], msg_in.at[src], m_s.at[step - 1], m_r.at[src], dp_dev(src))

    for step in range(1, n_dp):
        msg_copy(step).start()

    def gather_send(l, p, slab, k, dev):
        return remote(
            wt.at[l, p, slab], wt.at[l, p, slab], g_s.at[l, p, k], g_r.at[l, p, slab], dp_dev(dev)
        )

    def y_peers():
        return [my_z * n_y + lax.rem(my_y + s, n_y) for s in range(1, n_y)]

    def own_send(l, p):
        @pl.when(my_z < n_z - 1)
        def _():
            gather_send(l, p, me, 0, me + n_y).start()

        @pl.when(my_z > 0)
        def _():
            gather_send(l, p, me, 1, me - n_y).start()

        gather_send(l, p, me, 2, y_peers()[0]).start()

    def wave(l, p, hop):
        @pl.when(my_z >= hop)
        def _():
            slab = me - hop * n_y
            gather_send(l, p, slab, 0, slab).wait_recv()

            @pl.when(my_z < n_z - 1)
            def _():
                gather_send(l, p, slab, 2 + hop, me + n_y).start()

            gather_send(l, p, slab, n_z + 1 + hop, y_peers()[0]).start()

        @pl.when(my_z + hop < n_z)
        def _():
            slab = me + hop * n_y
            gather_send(l, p, slab, 0, slab).wait_recv()

            @pl.when(my_z > 0)
            def _():
                gather_send(l, p, slab, 2 * n_z + hop, me - n_y).start()

            gather_send(l, p, slab, 3 * n_z - 1 + hop, y_peers()[0]).start()

    def gather_finish(l, p):
        for s in range(0, n_z):
            slab = z_peer(s) * n_y + lax.rem(my_y + 1, n_y)
            gather_send(l, p, slab, 0, slab).wait_recv()

    def gather_drain(l, p):
        def sent(k):
            gather_send(l, p, me, k, me).wait_send()

        up, down = my_z < n_z - 1, my_z > 0
        at(up, lambda: sent(0))
        at(down, lambda: sent(1))
        sent(2)
        for hop in range(1, n_z):
            low, high = my_z >= hop, my_z + hop < n_z
            at(jnp.logical_and(low, up), lambda: sent(2 + hop))
            at(low, lambda: sent(n_z + 1 + hop))
            at(jnp.logical_and(high, down), lambda: sent(2 * n_z + hop))
            at(high, lambda: sent(3 * n_z - 1 + hop))

    def relayout(l, p):
        cols = []
        for b in range(8):
            blk = PARTS[p][b]
            square = flat_to_square(flat.at[l * GROUP + blk], place.at[b])
            cols.append(jnp.transpose(square) if blk in TRANSPOSED[p] else square)
        wt[l, p, me] = jnp.concatenate(cols, axis=1).astype(BF16)

    def relayout_layer(l, carry):
        load_blocks(l).wait()
        for p in range(3):
            relayout(l, p)
            if p == 0:
                at(l == 0, lambda: own_send(0, 0))
        return carry

    lax.fori_loop(0, LAYERS, relayout_layer, 0)

    seq_shift = jnp.where(long_ref[0, 0] > 0, 0, 1)
    seg = seg_ref[...]
    pos = lax.broadcasted_iota(jnp.int32, (8, 128), 0) * 128 + lax.broadcasted_iota(
        jnp.int32, (8, 128), 1
    )
    seq = (pos >> 8) * seq_shift
    kid = jnp.where(seg >= 0, seq * 64 + seg, -1 - seq).astype(F32)
    for r in range(8):
        kid_row[r // 2, 0:1, 128 * (r % 2) : 128 * (r % 2) + 128] = kid[r : r + 1, :]
        kid_col[r] = jnp.transpose(
            jnp.broadcast_to(kid[r : r + 1, :], (128, 128))
        )

    gvecs[...] = jnp.zeros_like(gvecs)
    gbias[...] = jnp.zeros_like(gbias)

    for step in range(1, n_dp):
        msg_from(step).wait_recv()
    for l in range(LAYERS):
        vecs[l] = jnp.concatenate(
            [msg_in[s, 8 * l : 8 * l + 8, 0:B] for s in range(n_dp)], axis=1
        )
        rows = [msg_in[s, 8 * l : 8 * l + 8, 128:256] for s in range(n_dp)]
        pad = jnp.zeros((8, D // 4), F32)
        bias_row[l] = jnp.concatenate(
            [r[:, 0:24] for r in rows]
            + [pad]
            + [r[:, 24:48] for r in rows]
            + [jnp.zeros((8, 64), F32)],
            axis=1,
        )

    low_half = lanes_of((CHUNK, 128)) < 64

    def vec(l, k):
        return vecs[l, k : k + 1, :]

    def core_copy(j):
        return remote(stage.at[j, other_c], core_in.at[j], c_s.at[j], c_r.at[j], sibling)

    def x_copy(j, par):
        return remote(stage.at[j, my_c], x_in.at[par, j], x_s.at[par, j], x_r.at[par, j], across)

    def own_copy(ref, j):
        return remote(ref.at[j, my_c], ref.at[j, my_c], a_s.at[j], a_r.at[j], sibling)

    def send_partial(j, value):
        stage[j] = value.astype(BF16).reshape(2, HALF, D)
        core_copy(j).start()

    def pass_on(j, par):
        core_copy(j).wait()
        mine = stage[j, my_c].astype(F32) + core_in[j].astype(F32)
        stage[j, my_c] = mine.astype(BF16)
        x_copy(j, par).start()

    def total(j, par):
        x_copy(j, par).wait()
        return stage[j, my_c].astype(F32) + x_in[par, j].astype(F32)

    def project(l, j):
        rows = a_all[l, j].reshape(CHUNK, D)
        weight = wt[l, 0].reshape(D, D)[:, 0:640]
        out = dot_nn(rows, weight) + bias_row[l, 0:1, :]
        tiles = [out[:, 128 * t : 128 * t + 128] for t in range(5)]
        q_roll = pltpu.roll(tiles[0], 64, 1)
        v_roll = pltpu.roll(tiles[3], 64, 1)
        zero = jnp.zeros((CHUNK, 128), F32)
        q_val = [
            jnp.where(low_half, zero, q_roll),
            jnp.where(low_half, q_roll, pltpu.roll(tiles[1], 64, 1)),
        ]
        k_val = [jnp.where(low_half, zero, tiles[1]), tiles[2]]
        v_val = [
            jnp.where(low_half, zero, v_roll),
            jnp.where(low_half, v_roll, pltpu.roll(tiles[4], 64, 1)),
        ]
        q_all[l, j] = jnp.concatenate(q_val, axis=1).astype(BF16)
        k_all[l, j] = jnp.concatenate(k_val, axis=1).astype(BF16)
        v_mat = jnp.concatenate(v_val, axis=1)
        v_all[l, j] = v_mat.astype(BF16)
        v_tr[:, pl.ds(pl.multiple_of(j * CHUNK, CHUNK), CHUNK)] = jnp.transpose(v_mat).astype(BF16)

    def head_tile(mat, h):
        if h == 0:
            return mat[:, 0:128]
        keep = low_half if h == 1 else jnp.logical_not(low_half)
        return jnp.where(keep, mat[:, 128:256], jnp.zeros((), mat.dtype))

    def tile_of(ref, l, h):
        full = ref[l].reshape(ROWS, 256)
        return full[:, 0:128] if h == 0 else full[:, 128:256]

    def allowed_of(j):
        col = kid_col[...].reshape(ROWS, 128)
        return jnp.concatenate([col, col], axis=1) == kid_row[j, 0:1, :]

    def attend_chunk(l, j):
        allowed = allowed_of(j)
        q_mat = q_all[l, j]
        outs = [jnp.zeros((64, CHUNK), F32)]
        for h in range(HEADS_DEV):
            scores = dot_nt(tile_of(k_all, l, h), head_tile(q_mat, h)) * scale
            scores = jnp.where(allowed, scores, big_negative)
            top = jnp.max(scores, axis=0, keepdims=True)
            expo = jnp.exp(scores - top)
            tot = jnp.sum(expo, axis=0, keepdims=True)
            lse_all[l, j, h : h + 1, :] = top + jnp.log(tot)
            out = dot_nn(v_tr[64 + 64 * h : 128 + 64 * h, :], expo.astype(BF16))
            outs.append(out / tot)
        o_mat = jnp.transpose(jnp.concatenate(outs, axis=0)).astype(BF16)
        o_all[l, j] = o_mat
        send_partial(j, dot_nt(o_mat, wt[l, 0].reshape(D, D)[:, 512:768]))

    def middle(l, j):
        mid = res[2 * l, j] + total(j, 0) + vec(l, 4)
        res[2 * l + 1, j] = mid
        hat, _ = norm_rows(mid)
        c_all[l, j, my_c] = (hat * vec(l, 2) + vec(l, 3)).astype(BF16)
        own_copy(c_all.at[l], j).start()

    def mlp(l, j):
        own_copy(c_all.at[l], j).wait()
        rows = c_all[l, j].reshape(CHUNK, D)
        pre = dot_nn(rows, wt[l, 1].reshape(D, D)) + vec(l, 6)
        cdf = 0.5 * (1.0 + lax.erf(pre * (1.0 / math.sqrt(2.0))))
        pdf = jnp.exp(-0.5 * pre * pre) * (1.0 / math.sqrt(2.0 * math.pi))
        act = (pre * cdf).astype(BF16)
        z_all[l, j] = act
        gp_all[l, j] = (cdf + pre * pdf).astype(BF16)

        @pl.when(jnp.logical_and(l == 0, j == 0))
        def _():
            gather_finish(0, 2)

        send_partial(j, dot_nt(z_all[l, j], wt[l, 2].reshape(D, D)))

    def near_copy(ref, hbm, which, j):
        slot = j if which else lax.rem(j, 2)
        return pltpu.make_async_copy(ref.at[slot], hbm.at[j, my_c], out_sem.at[which, j])

    def far_copy(ref, hbm, which, j):
        slot = j if which else lax.rem(j, 2)
        return remote(ref.at[slot], hbm.at[j, my_c], far_s.at[which, j], far_r.at[which, j], sibling)

    def layer_end(l, j):
        new = res[2 * l + 1, j] + total(j, 1) + vec(l, 5)

        @pl.when(l < LAYERS - 1)
        def _():
            res[2 * LAYERS - 2, j] = new
            hat, _ = norm_rows(new)
            a_all[LAYERS - 1, j, my_c] = (hat * vec(LAYERS - 1, 0) + vec(LAYERS - 1, 1)).astype(BF16)
            own_copy(a_all.at[LAYERS - 1], j).start()

        @pl.when(l == LAYERS - 1)
        def _():
            @pl.when(j >= 2)
            def _():
                near_copy(x_out, bo_hbm, 0, j - 2).wait()
                far_copy(x_out, bo_hbm, 0, j - 2).wait_send()

            x_out[lax.rem(j, 2)] = new
            near_copy(x_out, bo_hbm, 0, j).start()
            far_copy(x_out, bo_hbm, 0, j).start()

    def when_chunk(tick, offset, func):
        @pl.when(jnp.logical_and(tick >= offset, tick < offset + CHUNKS))
        def _():
            func(tick - offset)

    def add_vec(l, k, value):
        gvecs[l, k : k + 1, :] += value

    def mlp_back(l, j):
        d_act = dot_nn(y_all[j].reshape(CHUNK, D), wt[l, 2].reshape(D, D))
        d_pre = (d_act * gp_all[l, j].astype(F32)).astype(BF16)
        du_all[j] = d_pre
        add_vec(l, 6, jnp.sum(d_pre.astype(F32), axis=0, keepdims=True))
        send_partial(j, dot_nt(du_all[j], wt[l, 1].reshape(D, D)))

    def middle_back(l, j):
        grad = total(j, 0)
        d_rows, d_gain, d_shift = norm_back(grad, res[2 * l + 1, j], vec(l, 2))
        y_rows = y_own[j]
        add_vec(l, 5, jnp.sum(y_rows, axis=0, keepdims=True))
        g_rows = y_rows + d_rows
        add_vec(l, 2, d_gain)
        add_vec(l, 3, d_shift)
        add_vec(l, 4, jnp.sum(g_rows, axis=0, keepdims=True))
        y_own[j] = g_rows
        g_all[j, my_c] = g_rows.astype(BF16)
        own_copy(g_all, j).start()

    def attend_back(l, j):
        own_copy(g_all, j).wait()
        d_out = dot_nn(g_all[j].reshape(CHUNK, D), wt[l, 0].reshape(D, D)[:, 512:768])
        do_mat = d_out.astype(BF16)
        prod = jnp.transpose(do_mat.astype(F32) * o_all[l, j].astype(F32))
        allowed = allowed_of(j)
        q_mat = q_all[l, j]
        dq_parts = []
        for h in range(HEADS_DEV):
            q_h = head_tile(q_mat, h)
            do_h = head_tile(do_mat, h)
            scores = dot_nt(tile_of(k_all, l, h), q_h) * scale
            scores = jnp.where(allowed, scores, big_negative)
            probs = jnp.exp(scores - lse_all[l, j, h : h + 1, :])
            delta = jnp.sum(prod[64 + 64 * h : 128 + 64 * h, :], axis=0, keepdims=True)
            d_probs = dot_nt(tile_of(v_all, l, h), do_h)
            d_scores = (probs * (d_probs - delta)).astype(BF16)
            t = 0 if h == 0 else 128
            dv_acc[:, t : t + 128] += dot_nn(probs.astype(BF16), do_h)
            dk_acc[:, t : t + 128] += dot_nn(d_scores, q_h)
            dq_parts.append(dot_nn(v_tr[64 + 64 * h : 128 + 64 * h, :], d_scores))
        dq_parts.append(jnp.zeros((64, CHUNK), F32))
        dq_mat = jnp.transpose(jnp.concatenate(dq_parts, axis=0) * scale)
        dx_all[j, :, 0:256] = dq_mat.astype(BF16)

    def project_back(l, j):
        rows = pl.ds(pl.multiple_of(j * CHUNK, CHUNK), CHUNK)
        dk_mat = dk_acc[rows, :] * scale
        dv_mat = dv_acc[rows, :]
        zero = jnp.zeros((CHUNK, 128), F32)
        roll_zero = pltpu.roll(dv_mat[:, 0:128], 64, 1)
        roll_one = pltpu.roll(dv_mat[:, 128:256], 64, 1)
        tile_one = jnp.where(low_half, dx_all[j, :, 128:256].astype(F32), dk_mat[:, 0:128])
        dx_all[j, :, 128:640] = jnp.concatenate(
            [
                tile_one,
                dk_mat[:, 128:256],
                jnp.where(low_half, roll_zero, roll_one),
                jnp.where(low_half, roll_one, zero),
            ],
            axis=1,
        ).astype(BF16)
        dx_mat = dx_all[j]
        gbias[l, 0:1, :] += jnp.sum(dx_mat.astype(F32), axis=0, keepdims=True)
        send_partial(j, dot_nt(dx_mat, wt[l, 0].reshape(D, D)[:, 0:640]))

    def layer_begin(l, j):
        grad = total(j, 1)
        d_rows, d_gain, d_shift = norm_back(grad, res[2 * l, j], vec(l, 0))
        add_vec(l, 0, d_gain)
        add_vec(l, 1, d_shift)
        new = y_own[j] + d_rows
        y_own[j] = new

        @pl.when(l > 0)
        def _():
            y_all[j, my_c] = new.astype(BF16)
            own_copy(y_all, j).start()

        @pl.when(l == 0)
        def _():
            near_copy(y_own, ig_hbm, 1, j).start()
            far_copy(y_own, ig_hbm, 1, j).start()

    def slab(ref, p, owner):
        return ref.at[p, pl.ds(pl.multiple_of(owner * B, B), B)]

    def pair_copy(l, p, z):
        dest = y_peers()[0]
        return remote(
            slab(dw, p, z * n_y + lax.rem(my_y + 1, n_y)),
            rs_one.at[l, p, z],
            p_s.at[l, p, z],
            p_r.at[l, p, z],
            dp_dev(dest),
        )

    def line_copy(l, p, s):
        dest = z_peer(s)
        return remote(
            slab(dw, p, dest * n_y + my_y),
            rs_two.at[l, p, n_z - 1 - s],
            t_s.at[l, p, s - 1],
            t_r.at[l, p, n_z - 1 - s],
            dp_dev(dest * n_y + my_y),
        )

    def line_from(l, p, s):
        return remote(
            slab(dw, p, me),
            rs_two.at[l, p, s - 1],
            t_s.at[l, p, s - 1],
            t_r.at[l, p, s - 1],
            dp_dev(z_peer(s) * n_y + my_y),
        )

    def scatter_drain(l, p):
        for z in range(n_z):
            pair_copy(l, p, z).wait_send()
        for s in range(1, n_z):
            line_copy(l, p, s).wait_send()

    def scatter_begin(l, p):
        for s in list(range(1, n_z)) + [0]:
            pair_copy(l, p, z_peer(s)).start()

    def scatter_middle(l, p):
        for s in list(range(1, n_z)) + [0]:
            z = z_peer(s)
            pair_copy(l, p, z).wait_recv()
            ref = slab(dw, p, z * n_y + my_y)
            both = (ref[...].astype(F32) + rs_one[l, p, z].astype(F32)).astype(BF16)
            if s:
                ref[...] = both
                line_copy(l, p, s).start()
            else:
                rs_one[l, p, my_z] = both

    def runs_of(p):
        return ((0, 0, 6), (6, 14, 2)) if p == 0 else ((0, PARTS[p][0], 8),)

    def block_copies(l, p):
        return [
            pltpu.make_async_copy(
                flat.at[pl.ds(16 + 8 * k + here, count)],
                hbm.at[l, pl.ds(there, count)],
                gout_sem.at[k, n],
            )
            for k, hbm in enumerate((gf_hbm, lf_hbm, rf_hbm, pf_hbm))
            for n, (here, there, count) in enumerate(runs_of(p))
        ]

    def root_copies(l, p):
        return [
            pltpu.make_async_copy(
                hbm.at[l, pl.ds(there, count)],
                flat.at[pl.ds(8 * k + here, count)],
                root_sem.at[k, n],
            )
            for k, hbm in enumerate((lr_hbm, rr_hbm))
            for n, (here, there, count) in enumerate(runs_of(p))
        ]

    def scatter_end(l, p):
        acc = rs_one[l, p, my_z].astype(F32)
        for s in range(1, n_z):
            line_from(l, p, s).wait_recv()
            acc = acc + rs_two[l, p, s - 1].astype(F32)
        nm_ref[0:1, 0:1] += jnp.sum(acc * acc, keepdims=True)
        g_acc[...] = acc

    def block_update(l, p):
        acc = g_acc[...]
        for copy in root_copies(l, p):
            copy.wait()
        if p < 2:
            for copy in block_copies(l, p + 1):
                copy.wait()
        else:
            @pl.when(l < LAYERS - 1)
            def _():
                for copy in block_copies(LAYERS - 1, 0):
                    copy.wait()

        for b in range(8):
            square = acc[:, B * b : B * b + B]
            turned = jnp.transpose(square)
            if PARTS[p][b] in TRANSPOSED[p]:
                square, turned = turned, square
            slot = 3 * (b % 2)
            low = square.astype(BF16)
            rows = split_rows(square, place.at[slot])
            cols = split_rows(turned, place.at[slot + 1])
            right = flat_to_square(flat.at[8 + b], place.at[slot + 2])
            left = jnp.concatenate(flat_rows(flat.at[b]), axis=0)[:, :B]
            store_flat(flat.at[16 + b], rows)
            store_flat(flat.at[24 + b], dot_nt(rows.astype(BF16), low))
            store_flat(flat.at[32 + b], dot_nn(cols.astype(BF16), low))
            half = dot_nn(left.astype(BF16), low).astype(BF16)
            store_flat(flat.at[40 + b], dot_nn(half, right.astype(BF16)))
        for copy in block_copies(l, p):
            copy.start()
        if p > 0:
            for copy in root_copies(l, p - 1):
                copy.start()
        else:
            @pl.when(l > 0)
            def _():
                for copy in root_copies(0, 2):
                    copy.start()

    nm_ref[...] = jnp.zeros_like(nm_ref)

    def weight_grad(l, p, func):
        at(l < LAYERS - 1, lambda: scatter_drain(LAYERS - 1, p))

        def piece(m, carry):
            cols = pl.ds(pl.multiple_of(m * 256, 256), 256)
            dw[p, cols, :] = func(cols).astype(BF16)
            return carry

        lax.fori_loop(0, D // 256, piece, 0)
        scatter_begin(l, p)

    def down_grad(l):
        def func(cols):
            return dot_tn(
                y_all[:, :, :, cols].reshape(ROWS, 256), z_all[l].reshape(ROWS, D)
            )

        weight_grad(l, 2, func)

    def up_grad(l):
        def func(cols):
            return dot_tn(
                c_all[l, :, :, :, cols].reshape(ROWS, 256), du_all[...].reshape(ROWS, D)
            )

        weight_grad(l, 1, func)

    def qkv_grad(l):
        def func(cols):
            first = dot_tn(
                a_all[l, :, :, :, cols].reshape(ROWS, 256), dx_all[...].reshape(ROWS, 640)
            )
            second = dot_tn(
                g_all[:, :, :, cols].reshape(ROWS, 256), o_all[l].reshape(ROWS, 256)
            )
            return jnp.concatenate(
                [first[:, 0:512], first[:, 512:640] + second[:, 0:128], second[:, 128:256]], axis=1
            )

        weight_grad(l, 0, func)

    def first_norm(j, carry):
        load_rows(j, 0).wait()
        load_rows(j, 1).wait()
        hat, _ = norm_rows(res[0, j])
        a_all[0, j, my_c] = (hat * vec(0, 0) + vec(0, 1)).astype(BF16)
        hat, _ = norm_rows(res[1, j])
        a_all[0, j, other_c] = (hat * vec(0, 0) + vec(0, 1)).astype(BF16)
        return carry

    def y_copy(j):
        return remote(y_all.at[j, my_c], y_all.at[j, my_c], y_s.at[j], y_r.at[j], sibling)

    def first_grad(j, carry):
        load_cot(j).wait()
        rows = jnp.where(kid_col[2 * j + my_c][:, 0:1] >= 0.0, y_own[j], 0.0)
        y_own[j] = rows
        y_all[j, my_c] = rows.astype(BF16)
        y_copy(j).start()
        return carry

    def first_project(j, carry):
        project(0, j)
        return carry

    for copy in root_copies(LAYERS - 1, 2):
        copy.start()
    wave(0, 0, 1)
    own_send(0, 1)
    lax.fori_loop(0, CHUNKS // 2, first_norm, 0)
    wave(0, 0, 2)
    lax.fori_loop(CHUNKS // 2, CHUNKS, first_norm, 0)
    wave(0, 0, 3)
    wave(0, 1, 1)
    lax.fori_loop(0, CHUNKS, first_grad, 0)
    gather_finish(0, 0)
    wave(0, 1, 2)
    own_send(0, 2)
    lax.fori_loop(0, CHUNKS, first_project, 0)

    def prepare_back(l):
        for j in range(CHUNKS):
            v_tr[:, j * CHUNK : j * CHUNK + CHUNK] = jnp.transpose(k_all[l, j].astype(F32)).astype(
                BF16
            )
        dk_acc[...] = jnp.zeros_like(dk_acc)
        dv_acc[...] = jnp.zeros_like(dv_acc)

    def forward_layer(l, carry):
        def step(tick, inner):
            when_chunk(tick, 1, lambda j: pass_on(j, 0))
            when_chunk(tick, 5, lambda j: pass_on(j, 1))

            @pl.when(l == LAYERS - 1)
            def _():
                when_chunk(tick, 9, lambda j: pass_on(j, 0))

            when_chunk(tick, 3, lambda j: middle(l, j))
            when_chunk(tick, 7, lambda j: layer_end(l, j))
            when_chunk(tick, 0, lambda j: attend_chunk(l, j))

            def next_project(j):
                own_copy(a_all.at[LAYERS - 1], j).wait()
                project(LAYERS - 1, j)

            def first_back(j):
                far_copy(x_out, bo_hbm, 0, j).wait_recv()
                y_copy(j).wait()
                mlp_back(LAYERS - 1, j)

            @pl.when(l == 0)
            def _():
                @pl.when(tick == 1)
                def _():
                    wave(0, 1, 3)
                    wave(0, 2, 1)

                @pl.when(tick == 3)
                def _():
                    wave(0, 2, 2)
                    own_send(1, 0)

                @pl.when(tick == 4)
                def _():
                    gather_finish(0, 1)
                    wave(0, 2, 3)
                    wave(1, 0, 1)

                @pl.when(tick == 5)
                def _():
                    wave(1, 0, 2)
                    own_send(1, 1)

                @pl.when(tick == 7)
                def _():
                    wave(1, 0, 3)
                    wave(1, 1, 1)

                at(tick == 8, lambda: gather_finish(1, 0))

                @pl.when(tick == 9)
                def _():
                    wave(1, 1, 2)
                    own_send(1, 2)

                @pl.when(tick == 11)
                def _():
                    wave(1, 1, 3)
                    wave(1, 2, 1)

            @pl.when(l == 1)
            def _():
                at(tick == 0, lambda: wave(1, 2, 2))
                at(tick == 1, lambda: wave(1, 2, 3))

                @pl.when(tick == 4)
                def _():
                    gather_finish(1, 1)
                    gather_finish(1, 2)

            when_chunk(tick, 4, lambda j: mlp(l, j))

            @pl.when(l == 0)
            def _():
                when_chunk(tick, 8, next_project)

            @pl.when(l == LAYERS - 1)
            def _():
                at(tick == 7, lambda: prepare_back(LAYERS - 1))
                when_chunk(tick, 8, first_back)

            return inner

        lax.fori_loop(0, 13, step, 0)
        return carry

    lax.fori_loop(0, LAYERS, forward_layer, 0)

    def finish_part(l, p):
        scatter_end(l, p)
        block_update(l, p)

    def backward_layer(n, carry):
        l = LAYERS - 1 - n
        upper = l == LAYERS - 1
        lower = l < LAYERS - 1
        down_grad(l)

        @pl.when(lower)
        def _():
            scatter_middle(LAYERS - 1, 0)

        def step(tick, inner):
            middle_back(l, tick)
            at(tick == 0, lambda: up_grad(l))

            at(tick == 3, lambda: scatter_middle(l, 2))
            attend_back(l, tick)
            return inner

        lax.fori_loop(0, CHUNKS, step, 0)

        def step_two(tick, inner):
            when_chunk(tick, 1, lambda j: pass_on(j, 1))

            @pl.when(upper)
            def _():
                when_chunk(tick, 6, lambda j: pass_on(j, 0))

            when_chunk(tick, 4, lambda j: layer_begin(l, j))
            when_chunk(tick, 0, lambda j: project_back(l, j))
            at(tick == 3, lambda: qkv_grad(l))

            @pl.when(lower)
            def _():
                at(tick == 4, lambda: finish_part(LAYERS - 1, 1))
                at(tick == 5, lambda: finish_part(LAYERS - 1, 0))

            def next_back(j):
                own_copy(y_all, j).wait()
                mlp_back(l - 1, j)

            @pl.when(upper)
            def _():
                at(tick == 4, lambda: prepare_back(l - 1))
                when_chunk(tick, 5, next_back)

            at(tick == 5, lambda: scatter_middle(l, 1))
            at(tick == 6, lambda: finish_part(l, 2))
            return inner

        lax.fori_loop(0, 10, step_two, 0)
        return carry

    lax.fori_loop(0, LAYERS, backward_layer, 0)

    sib = remote(gvecs, sib_in, sib_s.at[0], sib_r.at[0], sibling)
    sib.start()
    sib.wait()
    row_at = lax.broadcasted_iota(jnp.int32, (8, D), 0)
    for l in range(LAYERS):
        mat = gvecs[l] + jnp.where(row_at < 6, sib_in[l], 0.0)
        extra = gbias[l]
        for s in range(n_dp):
            gmsg_out[s, 8 * l : 8 * l + 8, 0:B] = mat[:, B * s : B * s + B]
            gmsg_out[s, 8 * l : 8 * l + 8, 128:152] = extra[:, 24 * s : 24 * s + 24]
            gmsg_out[s, 8 * l : 8 * l + 8, 152:176] = extra[:, 384 + 24 * s : 384 + 24 * s + 24]
            gmsg_out[s, 8 * l : 8 * l + 8, B:128] = jnp.zeros((8, 128 - B), F32)
            gmsg_out[s, 8 * l : 8 * l + 8, 176:256] = jnp.zeros((8, 80), F32)

    def gmsg_copy(step):
        dest = lax.rem(me + step, n_dp)
        return remote(
            gmsg_out.at[dest], gmsg_in.at[me], gm_s.at[step - 1], gm_r.at[me], dp_dev(dest)
        )

    def gmsg_from(step):
        src = lax.rem(me + step, n_dp)
        return remote(gmsg_out.at[src], gmsg_in.at[src], gm_s.at[step - 1], gm_r.at[src], dp_dev(src))

    for step in range(1, n_dp):
        gmsg_copy(step).start()
    gmsg_in[me] = gmsg_out[me]
    scatter_middle(0, 0)
    finish_part(0, 1)
    for step in range(1, n_dp):
        gmsg_from(step).wait_recv()
    summed = gmsg_in[0]
    for s in range(1, n_dp):
        summed = summed + gmsg_in[s]
    sg_ref[...] = summed

    scatter_end(0, 0)
    squares = summed * summed
    lane = lanes_of((1, 128))
    packed = jnp.where(lane == 0, nm_ref[0:1, :], 0.0)
    shared_sums = jnp.zeros((1, 128), F32)
    for l in range(LAYERS):
        base = 8 * l
        up = jnp.sum(squares[base + 6 : base + 7, 0:B], keepdims=True)
        query = jnp.sum(squares[base : base + 1, 128:152], keepdims=True)
        value = jnp.sum(squares[base : base + 1, 152:176], keepdims=True)
        for k, item in enumerate((query, value, up)):
            packed = packed + jnp.where(lane == 1 + 3 * l + k, item, 0.0)
        for r in range(6):
            item = jnp.sum(squares[base + r : base + r + 1, 0:B], keepdims=True)
            shared_sums = shared_sums + jnp.where(lane == 6 * l + r, item, 0.0)

    for hop, dev in enumerate((sibling, across)):
        nb_out[hop] = jnp.broadcast_to(packed, (8, 128))
        swap = remote(nb_out.at[hop], nb_in.at[hop], nb_s.at[hop], nb_r.at[hop], dev)
        swap.start()
        if hop == 0:
            swap.wait()
        else:
            block_update(0, 0)
            swap.wait()
        packed = packed + nb_in[hop, 0:1, :]
    row8 = lax.broadcasted_iota(jnp.int32, (8, 128), 0)
    nd_in[me] = jnp.where(row8 == 0, packed, jnp.where(row8 == 1, shared_sums, 0.0))

    def nd_copy(step):
        dest = lax.rem(me + step, n_dp)
        return remote(nd_in.at[me], nd_in.at[me], nd_s.at[step - 1], nd_r.at[me], dp_dev(dest))

    def nd_from(step):
        src = lax.rem(me + step, n_dp)
        return remote(nd_in.at[src], nd_in.at[src], nd_s.at[step - 1], nd_r.at[src], dp_dev(src))

    for step in range(1, n_dp):
        nd_copy(step).start()
    for step in range(1, n_dp):
        nd_from(step).wait_recv()
    acc = nd_in[0]
    for s in range(1, n_dp):
        acc = acc + nd_in[s]
    nm_ref[...] = acc

    for p in range(3):
        scatter_drain(0, p)
        for l in range(LAYERS):
            gather_drain(l, p)
    for copy in block_copies(0, 0):
        copy.wait()
    for step in range(1, n_dp):
        msg_copy(step).wait_send()
        gmsg_copy(step).wait_send()
        nd_copy(step).wait_send()
    for j in range(CHUNKS):
        if j >= 2:
            near_copy(x_out, bo_hbm, 0, j).wait()
            far_copy(x_out, bo_hbm, 0, j).wait_send()
        near_copy(y_own, ig_hbm, 1, j).wait()
        far_copy(y_own, ig_hbm, 1, j).wait()


def train_call(n_y, x_rows, ct_rows, seg, long_flag, blocks, left, right, split, shared):
    hbm = pl.BlockSpec(memory_space=pl.ANY)
    vmem = pl.BlockSpec(memory_space=pltpu.VMEM)
    smem = pl.BlockSpec(memory_space=pltpu.SMEM)
    dma = pltpu.SemaphoreType.DMA
    n_dp = GROUPS
    n_z = n_dp // n_y

    def buf(shape, dtype=BF16):
        return pltpu.VMEM(shape, dtype)

    scratch = [
        buf((LAYERS, 3, n_dp, B, D)),
        buf((LAYERS, CHUNKS, 2, HALF, D)),
        buf((LAYERS, CHUNKS, 2, HALF, D)),
        buf((LAYERS, CHUNKS, CHUNK, 256)),
        buf((LAYERS, CHUNKS, CHUNK, 256)),
        buf((LAYERS, CHUNKS, CHUNK, 256)),
        buf((256, ROWS)),
        buf((LAYERS, CHUNKS, CHUNK, 256)),
        buf((LAYERS, CHUNKS, 8, CHUNK), F32),
        buf((LAYERS, CHUNKS, CHUNK, D)),
        buf((LAYERS, CHUNKS, CHUNK, D)),
        buf((2 * LAYERS, CHUNKS, HALF, D), F32),
        buf((CHUNKS, HALF, D), F32),
        buf((CHUNKS, 2, HALF, D)),
        buf((CHUNKS, 2, HALF, D)),
        buf((CHUNKS, CHUNK, D)),
        buf((CHUNKS, CHUNK, 640)),
        buf((ROWS, 256), F32),
        buf((ROWS, 256), F32),
        buf((CHUNKS, 2, HALF, D)),
        buf((CHUNKS, HALF, D)),
        buf((2, CHUNKS, HALF, D)),
        buf((3, D, D)),
        buf((LAYERS, 3, n_z, B, D)),
        buf((LAYERS, 3, n_z - 1, B, D)),
        buf((8, B, 128), F32),
        buf((LAYERS * GROUP, 72, 128), F32),
        buf((B, D), F32),
        buf((2, HALF, D), F32),
        buf((8, HALF, 128), F32),
        buf((CHUNKS, 8, CHUNK), F32),
        buf((LAYERS, 8, D), F32),
        buf((LAYERS, 8, 640), F32),
        buf((LAYERS, 8, D), F32),
        buf((LAYERS, 8, 640), F32),
        buf((LAYERS, 8, D), F32),
        buf((n_dp, 16, 256), F32),
        buf((n_dp, 16, 256), F32),
        buf((n_dp, 16, 256), F32),
        buf((2, 8, 128), F32),
        buf((2, 8, 128), F32),
        buf((n_dp, 8, 128), F32),
        dma((LAYERS, 3, 4 * n_z)),
        dma((LAYERS, 3, n_dp)),
        dma((CHUNKS,)),
        dma((CHUNKS,)),
        dma((2, CHUNKS)),
        dma((2, CHUNKS)),
        dma((CHUNKS,)),
        dma((CHUNKS,)),
        dma((LAYERS, 3, n_z)),
        dma((LAYERS, 3, n_z)),
        dma((LAYERS, 3, n_z - 1)),
        dma((LAYERS, 3, n_z - 1)),
        dma((2, CHUNKS)),
        dma((LAYERS,)),
        dma((CHUNKS,)),
        dma((CHUNKS,)),
        dma((CHUNKS,)),
        dma((2, CHUNKS)),
        dma((2, CHUNKS)),
        dma((2, CHUNKS)),
        dma((4, 2)),
        dma((2, 2)),
        dma((n_dp - 1,)),
        dma((n_dp,)),
        dma((n_dp - 1,)),
        dma((n_dp,)),
        dma((1,)),
        dma((1,)),
        dma((2,)),
        dma((2,)),
        dma((n_dp - 1,)),
        dma((n_dp,)),
    ]
    rows_shape = jax.ShapeDtypeStruct((CHUNKS, 2, HALF, D), F32)
    return pl.pallas_call(
        functools.partial(train_kernel, n_y),
        out_shape=(
            rows_shape,
            rows_shape,
            *[jax.ShapeDtypeStruct((LAYERS, GROUP, 72, 128), F32)] * 4,
            jax.ShapeDtypeStruct((16, 256), F32),
            jax.ShapeDtypeStruct((8, 128), F32),
        ),
        in_specs=[hbm, hbm, vmem, smem, hbm, hbm, hbm, vmem, vmem],
        out_specs=(hbm, hbm, hbm, hbm, hbm, hbm, vmem, vmem),
        scratch_shapes=scratch,
        compiler_params=pltpu.CompilerParams(
            collective_id=0, has_side_effects=True, vmem_limit_bytes=60 * 1024 * 1024
        ),
        cost_estimate=pl.CostEstimate(
            flops=30_000_000_000, bytes_accessed=30_000_000, transcendentals=20_000_000
        ),
        name="train",
    )(x_rows, ct_rows, seg, long_flag, blocks, left, right, split, shared)


def update_kernel(
    g_ref,
    lg_ref,
    rg_ref,
    p_ref,
    w_ref,
    l_ref,
    r_ref,
    sg_ref,
    nm_ref,
    sp_ref,
    sh_ref,
    bo_ref,
    ig_ref,
    gout_ref,
    nw_ref,
    nl_ref,
    nr_ref,
    sgo_ref,
    nsp_ref,
    shg_ref,
    nsh_ref,
    norm_ref,
    bo_out,
    ig_out,
):
    step_at = pl.program_id(0)
    bo_out[...] = bo_ref[...]
    ig_out[...] = ig_ref[...]
    lane = lanes_of((1, 128))
    row_zero = nm_ref[0:1, :]
    row_one = nm_ref[1:2, :]
    total_sq = jnp.sum(jnp.where(lane < 7, row_zero, 0.0), keepdims=True) + jnp.sum(
        jnp.where(lane < 12, row_one, 0.0), keepdims=True
    )
    norm = jnp.sqrt(total_sq)
    factor = clip_limit / jnp.maximum(norm, clip_limit)
    squared = factor * factor
    gram_weight = (1.0 - decay) * squared

    for b in range(g_ref.shape[0]):
        gout_ref[b] = g_ref[b] * factor
        nl_ref[b] = decay * l_ref[b] + gram_weight * lg_ref[b]
        nr_ref[b] = decay * r_ref[b] + gram_weight * rg_ref[b]
        direction = p_ref[b] * factor
        mean_sq = jnp.sum(direction * direction, keepdims=True) / (B * B)
        nw_ref[b] = w_ref[b] - direction * (rate_matrix * lax.rsqrt(mean_sq + eps_norm))

    @pl.when(step_at == 0)
    def _():
        norm_ref[...] = norm
        sel = table_selector((144, 256))
        col = lanes_of((1, 256))
        for l in range(LAYERS):
            sums = [row_zero[:, 1 + 3 * l + k : 2 + 3 * l + k] for k in range(3)]
            means = [sums[0] / D, sums[1] / D, sums[2] / FF]
            scales = [lax.rsqrt(squared * m + eps_norm) for m in means]
            src = sg_ref[8 * l : 8 * l + 8, :]
            line = jnp.where(col < 128, src[6:7, :], src[0:1, :]) * factor
            step = line * jnp.where(col < 128, scales[2], jnp.where(col < 152, scales[0], scales[1]))
            both = jnp.concatenate([line, step, jnp.zeros((6, 256), F32)], axis=0)
            table = lax.dot_general(
                both, sel, (((1,), (1,)), ((), ())), precision=highest, preferred_element_type=F32
            )
            sgo_ref[l] = table[0:1, :]
            nsp_ref[l] = sp_ref[l] - rate_vector * table[1:2, :]
            for r in range(6):
                mean = row_one[:, 6 * l + r : 6 * l + r + 1] / D
                grad = src[r : r + 1, 0:B] * factor
                shg_ref[r, l : l + 1, :] = grad
                nsh_ref[r, l : l + 1, :] = sh_ref[r, l : l + 1, :] - rate_vector * grad * lax.rsqrt(
                    squared * mean + eps_norm
                )


def update_call(grads, lefts, rights, dirs, weights, left, right, sums, norms, split, shared, outs):
    per = 6
    count = LAYERS * GROUP
    flat = pl.BlockSpec((per, 72, 128), lambda i: (i, 0, 0))
    rows = pl.BlockSpec((2 * HALF * CHUNKS * per // count, D), lambda i: (i, 0))

    def whole(shape):
        return pl.BlockSpec(shape, lambda i: (0,) * len(shape))

    flat_shape = jax.ShapeDtypeStruct((count, 72, 128), F32)
    split_shape, shared_shape = (LAYERS, 1, 144), (6, LAYERS, B)
    return pl.pallas_call(
        update_kernel,
        grid=(count // per,),
        out_shape=(
            *[flat_shape] * 4,
            *[jax.ShapeDtypeStruct(split_shape, F32)] * 2,
            *[jax.ShapeDtypeStruct(shared_shape, F32)] * 2,
            jax.ShapeDtypeStruct((1, 1), F32),
            *[jax.ShapeDtypeStruct(o.shape, F32) for o in outs],
        ),
        in_specs=[flat] * 7
        + [whole((16, 256)), whole((8, 128)), whole(split_shape), whole(shared_shape), rows, rows],
        out_specs=(
            *[flat] * 4,
            *[whole(split_shape)] * 2,
            *[whole(shared_shape)] * 2,
            whole((1, 1)),
            rows,
            rows,
        ),
        compiler_params=pltpu.CompilerParams(vmem_limit_bytes=60 * 1024 * 1024),
        name="update",
    )(grads, lefts, rights, dirs, weights, left, right, sums, norms, split, shared, *outs)


def fast_body(
    n_y,
    tokens_in,
    cotangent,
    segment_ids,
    long_seq,
    weights,
    left_stats,
    right_stats,
    left_roots,
    right_roots,
    split_params,
    shared_params,
):
    rows = (CHUNKS, 2, HALF, D)
    flat = (LAYERS, GROUP, 72, 128)
    blocks = (LAYERS * GROUP, 72, 128)
    split = split_params
    shared = jnp.transpose(shared_params, (1, 0, 2))
    out_rows, in_grad, grads, lefts, rights, dirs, sums, norms = train_call(
        n_y,
        tokens_in.reshape(rows),
        cotangent.reshape(rows),
        segment_ids.reshape(8, 128),
        long_seq.reshape(1, 1),
        weights.reshape(flat),
        left_roots.reshape(flat),
        right_roots.reshape(flat),
        split,
        shared,
    )
    res = update_call(
        *[m.reshape(blocks) for m in (grads, lefts, rights, dirs, weights, left_stats, right_stats)],
        sums,
        norms,
        split,
        shared,
        (out_rows.reshape(tokens_in.shape), in_grad.reshape(tokens_in.shape)),
    )
    mats = [r.reshape(weights.shape) for r in res[:4]]
    return (
        res[9],
        res[10],
        *mats,
        res[4],
        res[5],
        jnp.transpose(res[6], (1, 0, 2)),
        jnp.transpose(res[7], (1, 0, 2)),
        res[8].reshape(()),
    )


def solution(mesh):
    in_specs = (
        P("dp", None),
        P("dp", None),
        P("dp"),
        P("dp"),
        P(None, "dp", "tensor", None),
        P(None, "dp", "tensor", None),
        P(None, "dp", "tensor", None),
        P(None, "dp", "tensor", None),
        P(None, "dp", "tensor", None),
        P(None, "tensor", "dp"),
        P(None, None, "dp"),
    )
    out_specs = (
        P("dp", None),
        P("dp", None),
        P(None, "dp", "tensor", None),
        P(None, "dp", "tensor", None),
        P(None, "dp", "tensor", None),
        P(None, "dp", "tensor", None),
        P(None, "tensor", "dp"),
        P(None, "tensor", "dp"),
        P(None, None, "dp"),
        P(None, None, "dp"),
        P(),
    )
    plan = body
    if mesh.shape["dp"] == GROUPS and mesh.shape["tensor"] == 4:
        plan = functools.partial(fast_body, 2)
    return jax.shard_map(plan, mesh=mesh, in_specs=in_specs, out_specs=out_specs, check_vma=False)
```

```python
import functools
import math

import jax
import jax.numpy as jnp
from jax import lax
from jax.experimental import pallas as pl
from jax.experimental.pallas import tpu as pltpu
from jax.sharding import PartitionSpec as P

D = 768
HEADS = 12
FF = 3072
HD = 64
B = 96
LAYERS = 2
SEQ_SHORT = 256
SEQ_LONG = 1024


clip_limit = 100.0
rate_matrix = 0.06
rate_vector = 0.2
decay = 0.5
eps_norm = 1e-06
eps_layer = 1e-06
big_negative = -1e30
highest = lax.Precision.HIGHEST


def layer_norm(hidden, gain_vec, shift_vec):
    row_mean = jnp.mean(hidden, axis=-1, keepdims=True)
    centered = hidden - row_mean
    row_var = jnp.mean(centered * centered, axis=-1, keepdims=True)
    return centered * lax.rsqrt(row_var + eps_layer) * gain_vec + shift_vec


def gelu_exact(values):
    return jax.nn.gelu(values, approximate=False)


def matmul_low(left_mat, right_mat):
    return jnp.dot(left_mat, right_mat, preferred_element_type=jnp.float32)


def inner_rows(left_mat, right_mat):
    return lax.dot_general(
        left_mat, right_mat, (((0,), (0,)), ((), ())), preferred_element_type=jnp.float32
    )


def times_trans(left_mat, right_mat):
    return lax.dot_general(
        left_mat, right_mat, (((1,), (1,)), ((), ())), preferred_element_type=jnp.float32
    )


def unpack_layer(blocks, embed_dev, inner_dev):
    row_groups = blocks.shape[0]
    block_size = blocks.shape[2]
    qkv_count = 3 * embed_dev // block_size
    up_count = inner_dev // block_size
    out_count = embed_dev // block_size

    def by_rows(part_blocks):
        block_count = part_blocks.shape[1]
        return jnp.transpose(part_blocks, (0, 2, 1, 3)).reshape(
            row_groups * block_size, block_count * block_size
        )

    def by_cols(part_blocks):
        block_count = part_blocks.shape[1]
        return jnp.transpose(part_blocks, (1, 2, 0, 3)).reshape(
            block_count * block_size, row_groups * block_size
        )

    qkv_weight = by_rows(blocks[:, :qkv_count])
    up_weight = by_rows(blocks[:, qkv_count : qkv_count + up_count])
    out_weight = by_cols(blocks[:, qkv_count + up_count : qkv_count + up_count + out_count])
    down_weight = by_cols(blocks[:, qkv_count + up_count + out_count :])
    return (qkv_weight, out_weight, up_weight, down_weight)


def pack_layer(qkv_grad, out_grad, up_grad, down_grad, block_size):
    row_groups = qkv_grad.shape[0] // block_size

    def from_rows(matrix):
        block_count = matrix.shape[1] // block_size
        return jnp.transpose(
            matrix.reshape(row_groups, block_size, block_count, block_size), (0, 2, 1, 3)
        )

    def from_cols(matrix):
        block_count = matrix.shape[0] // block_size
        return jnp.transpose(
            matrix.reshape(block_count, block_size, row_groups, block_size), (2, 0, 1, 3)
        )

    return jnp.concatenate(
        [from_rows(qkv_grad), from_rows(up_grad), from_cols(out_grad), from_cols(down_grad)], axis=1
    )


def masked_scores(query_block, key_window, query_seq, key_seq, query_seg, key_seg, score_scale):
    scores = (
        jnp.einsum("qhd,khd->hqk", query_block, key_window, preferred_element_type=jnp.float32)
        * score_scale
    )
    allowed = (query_seq[:, None] == key_seq[None, :]) & (query_seg[:, None] == key_seg[None, :])
    return jnp.where(allowed[None], scores, big_negative)


def attention_forward(queries, keys_all, values_all, seq_index, segments, block_rows, score_scale):
    block_count = queries.shape[0] // block_rows

    def one_block(block_index):
        row_start = block_index * block_rows
        query_block = lax.dynamic_slice_in_dim(queries, row_start, block_rows, 0)
        scores = masked_scores(
            query_block,
            keys_all,
            lax.dynamic_slice_in_dim(seq_index, row_start, block_rows, 0),
            seq_index,
            lax.dynamic_slice_in_dim(segments, row_start, block_rows, 0),
            segments,
            score_scale,
        )
        row_max = jnp.max(scores, axis=-1, keepdims=True)
        exponent = jnp.exp(scores - row_max)
        row_total = jnp.sum(exponent, axis=-1, keepdims=True)
        attn_probs = (exponent / row_total).astype(jnp.bfloat16)
        attended = jnp.einsum(
            "hqk,khd->qhd", attn_probs, values_all, preferred_element_type=jnp.float32
        )
        return (attended, (row_max + jnp.log(row_total))[..., 0])

    return lax.map(one_block, jnp.arange(block_count, dtype=jnp.int32))


def attention_backward(
    queries, keys_all, values_all, grad_out, log_total, seq_index, segments, block_rows, score_scale
):
    token_count = queries.shape[0]
    block_count = token_count // block_rows
    zero_grad = jnp.zeros(keys_all.shape, jnp.float32)

    def one_block(carry_pair, block_index):
        key_grad, value_grad = carry_pair
        row_start = block_index * block_rows
        query_block = lax.dynamic_slice_in_dim(queries, row_start, block_rows, 0)
        out_block = lax.dynamic_slice_in_dim(grad_out, row_start, block_rows, 0)
        scores = masked_scores(
            query_block,
            keys_all,
            lax.dynamic_slice_in_dim(seq_index, row_start, block_rows, 0),
            seq_index,
            lax.dynamic_slice_in_dim(segments, row_start, block_rows, 0),
            segments,
            score_scale,
        )
        lse_block = lax.dynamic_index_in_dim(log_total, block_index, 0, keepdims=False)
        attn_probs = jnp.exp(scores - lse_block[..., None])
        prob_grad = jnp.einsum(
            "qhd,khd->hqk", out_block, values_all, preferred_element_type=jnp.float32
        )
        row_delta = jnp.sum(attn_probs * prob_grad, axis=-1, keepdims=True)
        score_grad = (attn_probs * (prob_grad - row_delta)).astype(jnp.bfloat16)
        query_grad = (
            jnp.einsum("hqk,khd->qhd", score_grad, keys_all, preferred_element_type=jnp.float32)
            * score_scale
        )
        key_part = (
            jnp.einsum("hqk,qhd->khd", score_grad, query_block, preferred_element_type=jnp.float32)
            * score_scale
        )
        value_part = jnp.einsum(
            "hqk,qhd->khd",
            attn_probs.astype(jnp.bfloat16),
            out_block,
            preferred_element_type=jnp.float32,
        )
        key_grad = key_grad + key_part
        value_grad = value_grad + value_part
        return ((key_grad, value_grad), query_grad)

    (key_grad, value_grad), query_grad = lax.scan(
        one_block, (zero_grad, zero_grad), jnp.arange(block_count, dtype=jnp.int32)
    )
    return (query_grad.reshape(keys_all.shape), key_grad, value_grad)


def body(
    tokens_in,
    cotangent,
    segment_ids,
    long_seq,
    weights,
    left_stats,
    right_stats,
    left_roots,
    right_roots,
    split_params,
    shared_params,
):
    full_weights, full_split, full_shared = (
        lax.all_gather(weights, "dp", axis=1, tiled=True),
        lax.all_gather(split_params, "dp", axis=2, tiled=True),
        lax.all_gather(shared_params, "dp", axis=2, tiled=True),
    )
    tensor_count = lax.axis_size("tensor")
    embed_dev = D // tensor_count
    inner_dev = FF // tensor_count
    heads_local = HEADS // tensor_count
    token_count = tokens_in.shape[0]
    window = SEQ_LONG
    block_rows = min(512, window)
    score_scale = 1.0 / math.sqrt(HD)
    seq_length = jnp.where(long_seq[0] > 0, SEQ_LONG, SEQ_SHORT)
    positions = jnp.arange(token_count, dtype=jnp.int32)
    seq_index = positions // seq_length
    valid_rows = (segment_ids >= 0).astype(jnp.float32)
    matrices = []
    for layer_index in range(LAYERS):
        blocks = full_weights[layer_index, :, 0].astype(jnp.bfloat16).reshape(D // B, -1, B, B)
        matrices.append(unpack_layer(blocks, embed_dev, inner_dev))
    hidden_state = tokens_in
    kept_state = []
    for layer_index in range(LAYERS):
        qkv_weight, out_weight, up_weight, down_weight = matrices[layer_index]
        shared = full_shared[layer_index]
        bias_table = full_split[layer_index, 0].reshape(embed_dev, 6)
        up_bias = bias_table[:, 2:].reshape(inner_dev)
        normed = layer_norm(hidden_state, shared[0], shared[1]).astype(jnp.bfloat16)
        qkv_bias = jnp.concatenate(
            [bias_table[:, 0], jnp.zeros((embed_dev,), jnp.float32), bias_table[:, 1]]
        )
        projected = (matmul_low(normed, qkv_weight) + qkv_bias).astype(jnp.bfloat16)
        queries = projected[:, :embed_dev].reshape(token_count, heads_local, HD)
        keys_all = projected[:, embed_dev : 2 * embed_dev].reshape(token_count, heads_local, HD)
        values_all = projected[:, 2 * embed_dev :].reshape(token_count, heads_local, HD)
        attended, log_total = attention_forward(
            queries, keys_all, values_all, seq_index, segment_ids, block_rows, score_scale
        )
        attended = attended.reshape(token_count, embed_dev).astype(jnp.bfloat16)
        attn_branch = lax.psum(
            matmul_low(attended, out_weight).astype(jnp.bfloat16), "tensor"
        ).astype(jnp.float32)
        middle = hidden_state + attn_branch + shared[4]
        normed_mid = layer_norm(middle, shared[2], shared[3]).astype(jnp.bfloat16)
        pre_act = matmul_low(normed_mid, up_weight) + up_bias
        activation = gelu_exact(pre_act).astype(jnp.bfloat16)
        mlp_branch = lax.psum(
            matmul_low(activation, down_weight).astype(jnp.bfloat16), "tensor"
        ).astype(jnp.float32)
        kept_state.append(
            (
                hidden_state,
                normed,
                queries,
                keys_all,
                values_all,
                attended,
                log_total,
                middle,
                normed_mid,
                pre_act,
                activation,
            )
        )
        hidden_state = middle + mlp_branch + shared[5]
    grad_state = cotangent * valid_rows[:, None]
    layer_grads = [None] * LAYERS
    for layer_index in reversed(range(LAYERS)):
        (
            hidden_in,
            normed,
            queries,
            keys_all,
            values_all,
            attended,
            log_total,
            middle,
            normed_mid,
            pre_act,
            activation,
        ) = kept_state[layer_index]
        qkv_weight, out_weight, up_weight, down_weight = matrices[layer_index]
        shared = full_shared[layer_index]
        down_bias_grad = jnp.sum(grad_state, axis=0)
        grad_low = grad_state.astype(jnp.bfloat16)
        down_grad = inner_rows(activation, grad_low)
        act_grad = times_trans(grad_low, down_weight)
        gelu_pull = jax.vjp(gelu_exact, pre_act)[1]
        pre_grad = gelu_pull(act_grad)[0].astype(jnp.bfloat16)
        up_bias_grad = jnp.sum(pre_grad, axis=0, dtype=jnp.float32)
        up_grad = inner_rows(normed_mid, pre_grad)
        normed_mid_grad = lax.psum(times_trans(pre_grad, up_weight), "tensor")
        norm_pull = jax.vjp(layer_norm, middle, shared[2], shared[3])[1]
        middle_ln, gain_two_grad, shift_two_grad = norm_pull(normed_mid_grad)
        middle_grad = grad_state + middle_ln
        out_bias_grad = jnp.sum(middle_grad, axis=0)
        middle_low = middle_grad.astype(jnp.bfloat16)
        out_grad = inner_rows(attended, middle_low)
        attended_grad = (
            times_trans(middle_low, out_weight)
            .astype(jnp.bfloat16)
            .reshape(token_count, heads_local, HD)
        )
        query_grad, key_grad, value_grad = attention_backward(
            queries,
            keys_all,
            values_all,
            attended_grad,
            log_total,
            seq_index,
            segment_ids,
            block_rows,
            score_scale,
        )
        proj_grad = jnp.concatenate(
            [
                query_grad.reshape(token_count, embed_dev),
                key_grad.reshape(token_count, embed_dev),
                value_grad.reshape(token_count, embed_dev),
            ],
            axis=1,
        ).astype(jnp.bfloat16)
        query_bias_grad = jnp.sum(proj_grad[:, :embed_dev], axis=0, dtype=jnp.float32)
        value_bias_grad = jnp.sum(proj_grad[:, 2 * embed_dev :], axis=0, dtype=jnp.float32)
        qkv_grad = inner_rows(normed, proj_grad)
        normed_grad = lax.psum(times_trans(proj_grad, qkv_weight), "tensor")
        input_pull = jax.vjp(layer_norm, hidden_in, shared[0], shared[1])[1]
        hidden_ln, gain_one_grad, shift_one_grad = input_pull(normed_grad)
        grad_state = middle_grad + hidden_ln
        block_grads = pack_layer(qkv_grad, out_grad, up_grad, down_grad, B).reshape(-1, 1, B * B)
        split_vec = jnp.concatenate(
            [
                query_bias_grad[:, None],
                value_bias_grad[:, None],
                up_bias_grad.reshape(embed_dev, 4),
            ],
            axis=1,
        ).reshape(1, -1)
        shared_vec = jnp.stack(
            [
                gain_one_grad,
                shift_one_grad,
                gain_two_grad,
                shift_two_grad,
                out_bias_grad,
                down_bias_grad,
            ]
        )
        layer_grads[layer_index] = (block_grads, split_vec, shared_vec)
    weight_grad, split_grad, shared_grad = (
        lax.psum_scatter(
            jnp.stack([entry[0] for entry in layer_grads]), "dp", scatter_dimension=1, tiled=True
        ),
        lax.psum_scatter(
            jnp.stack([entry[1] for entry in layer_grads]), "dp", scatter_dimension=2, tiled=True
        ),
        lax.psum_scatter(
            jnp.stack([entry[2] for entry in layer_grads]), "dp", scatter_dimension=2, tiled=True
        ),
    )
    dp_index = lax.axis_index("dp")
    lead_shard = (lax.axis_index("tensor") == 0).astype(jnp.float32)
    slice_len = split_grad.shape[-1]
    global_pos = dp_index * slice_len + jnp.arange(slice_len, dtype=jnp.int32)
    table_column = global_pos % 6
    segment_of = (table_column >= 1).astype(jnp.int32) + (table_column >= 2).astype(jnp.int32)
    selector = (segment_of[:, None] == jnp.arange(3, dtype=jnp.int32)[None, :]).astype(jnp.float32)
    split_sq = split_grad[:, 0] * split_grad[:, 0]
    split_rows = jnp.dot(split_sq, selector, precision=highest)
    shared_sq = shared_grad * shared_grad
    shared_rows = jnp.sum(shared_sq, axis=-1) * lead_shard
    local_total = (
        jnp.sum(weight_grad * weight_grad) + jnp.sum(split_sq) + lead_shard * jnp.sum(shared_sq)
    )
    total_sq, split_rows, shared_rows = lax.psum(
        (local_total, split_rows, shared_rows), ("dp", "tensor")
    )
    grad_norm = jnp.sqrt(total_sq)
    factor = clip_limit / jnp.maximum(grad_norm, clip_limit)
    squared = factor * factor
    block_shape = weight_grad.shape[:-1] + (B, B)
    left_mats = left_roots.reshape(block_shape)
    right_mats = right_roots.reshape(block_shape)
    clipped = weight_grad * factor
    clipped_mats = clipped.reshape(block_shape)
    new_left = decay * left_stats + (1.0 - decay) * jnp.einsum(
        "...ij,...kj->...ik", clipped_mats, clipped_mats, precision=highest
    ).reshape(left_stats.shape)
    new_right = decay * right_stats + (1.0 - decay) * jnp.einsum(
        "...ji,...jk->...ik", clipped_mats, clipped_mats, precision=highest
    ).reshape(right_stats.shape)
    partial_dir = jnp.einsum("...ij,...jk->...ik", left_mats, clipped_mats, precision=highest)
    direction = jnp.einsum("...ij,...jk->...ik", partial_dir, right_mats, precision=highest)
    mean_sq = jnp.mean(direction * direction, axis=(-2, -1), keepdims=True)
    step_mats = direction * lax.rsqrt(mean_sq + eps_norm)
    new_weights = weights - rate_matrix * step_mats.reshape(weights.shape)
    vector_sizes = jnp.array([D, D, FF], jnp.float32)
    split_mean = jnp.dot(split_rows / vector_sizes[None, :], selector.T, precision=highest)
    split_clip = split_grad * factor
    new_split = split_params - rate_vector * split_clip * lax.rsqrt(
        squared * split_mean[:, None, :] + eps_norm
    )
    shared_clip = shared_grad * factor
    shared_mean = shared_rows / D
    new_shared = shared_params - rate_vector * shared_clip * lax.rsqrt(
        squared * shared_mean[..., None] + eps_norm
    )
    return (
        hidden_state,
        grad_state,
        clipped,
        new_weights,
        new_left,
        new_right,
        split_clip,
        new_split,
        shared_clip,
        new_shared,
        grad_norm,
    )


F32 = jnp.float32
BF16 = jnp.bfloat16
MESH = pl.DeviceIdType.MESH
CHUNKS = 4
HALF = 128
CHUNK = 2 * HALF
ROWS = CHUNKS * CHUNK
HEADS_DEV = 3
GROUPS = D // B
GROUP = 24
PARTS = ((0, 1, 2, 3, 4, 5, 14, 15), tuple(range(6, 14)), tuple(range(16, 24)))
TRANSPOSED = (frozenset((14, 15)), frozenset(), frozenset(range(16, 24)))


def dot_nn(left_mat, right_mat):
    return lax.dot_general(left_mat, right_mat, (((1,), (0,)), ((), ())), preferred_element_type=F32)


def dot_nt(left_mat, right_mat):
    return lax.dot_general(left_mat, right_mat, (((1,), (1,)), ((), ())), preferred_element_type=F32)


def dot_tn(left_mat, right_mat):
    return lax.dot_general(left_mat, right_mat, (((0,), (0,)), ((), ())), preferred_element_type=F32)


def lanes_of(shape):
    return lax.broadcasted_iota(jnp.int32, shape, len(shape) - 1)


def norm_rows(rows):
    mean = jnp.mean(rows, axis=-1, keepdims=True)
    centered = rows - mean
    var = jnp.mean(centered * centered, axis=-1, keepdims=True)
    inv = lax.rsqrt(var + eps_layer)
    return centered * inv, inv


def norm_back(grad, rows, gain):
    hat, inv = norm_rows(rows)
    scaled = grad * gain
    mean_one = jnp.mean(scaled, axis=-1, keepdims=True)
    mean_two = jnp.mean(scaled * hat, axis=-1, keepdims=True)
    d_rows = inv * (scaled - mean_one - hat * mean_two)
    return d_rows, jnp.sum(grad * hat, axis=0, keepdims=True), jnp.sum(grad, axis=0, keepdims=True)


def table_selector(shape):
    row = lax.broadcasted_iota(jnp.int32, shape, 0)
    col = lax.broadcasted_iota(jnp.int32, shape, 1)
    up_row = 6 * (col >> 2) + 2 + (col & 3)
    hit = (col < B) & (row == up_row)
    hit = hit | ((col >= 128) & (col < 152) & (row == 6 * (col - 128)))
    hit = hit | ((col >= 152) & (col < 176) & (row == 6 * (col - 152) + 1))
    return hit.astype(F32)


def flat_rows(ref):
    x_zero, x_one, x_two = [ref[pl.ds(m, 24, stride=3), :] for m in range(3)]
    lane = lanes_of((24, 128))
    x_half = pltpu.roll(x_two, 64, 1)
    return (
        x_zero,
        jnp.where(lane < 32, pltpu.roll(x_zero, 32, 1), pltpu.roll(x_one, 32, 1)),
        jnp.where(lane < 64, pltpu.roll(x_one, 64, 1), x_half),
        pltpu.roll(x_two, 96, 1),
    )


def flat_to_square(ref, place):
    for m, rows in enumerate(flat_rows(ref)):
        place[pl.ds(m, 24, stride=4), :] = rows
    return place[...][:, :B]


def split_rows(square, place):
    place[:, 0:B] = square
    return jnp.concatenate([place[pl.ds(m, 24, stride=4), :] for m in range(4)], axis=0)[:, :B]


def store_flat(ref, stacked):
    lane = lanes_of((24, 128))
    wide = jnp.concatenate([stacked, jnp.zeros((B, 128 - B), F32)], axis=1)
    m_zero, m_one, m_two, m_three = [wide[24 * m : 24 * m + 24] for m in range(4)]
    one_back = pltpu.roll(m_one, 96, 1)
    two_back = pltpu.roll(m_two, 64, 1)
    ref[pl.ds(0, 24, stride=3), :] = jnp.where(lane < 96, m_zero, one_back)
    ref[pl.ds(1, 24, stride=3), :] = jnp.where(lane < 64, one_back, two_back)
    ref[pl.ds(2, 24, stride=3), :] = jnp.where(lane < 32, two_back, pltpu.roll(m_three, 32, 1))


def train_kernel(
    n_y,
    x_hbm,
    ct_hbm,
    seg_ref,
    long_ref,
    w_hbm,
    lr_hbm,
    rr_hbm,
    split_ref,
    shared_ref,
    bo_hbm,
    ig_hbm,
    gf_hbm,
    lf_hbm,
    rf_hbm,
    pf_hbm,
    sg_ref,
    nm_ref,
    wt,
    a_all,
    c_all,
    q_all,
    k_all,
    v_all,
    v_tr,
    o_all,
    lse_all,
    z_all,
    gp_all,
    res,
    y_own,
    y_all,
    g_all,
    du_all,
    dx_all,
    dk_acc,
    dv_acc,
    stage,
    core_in,
    x_in,
    side_in,
    dw,
    rs_one,
    rs_two,
    place,
    flat,
    g_acc,
    kid_col,
    kid_row,
    vecs,
    bias_row,
    gvecs,
    gbias,
    sib_in,
    msg_in,
    gmsg_out,
    nb_out,
    nb_in,
    nd_in,
    g_s,
    g_r,
    c_s,
    c_r,
    x_s,
    x_r,
    a_s,
    a_r,
    p_s,
    p_r,
    t_s,
    t_r,
    load_sem,
    land_sem,
    ct_sem,
    y_s,
    y_r,
    out_sem,
    far_s,
    far_r,
    gout_sem,
    root_sem,
    m_s,
    m_r,
    gm_s,
    gm_r,
    sib_s,
    sib_r,
    nb_s,
    nb_r,
    nd_s,
    nd_r,
):
    n_dp = GROUPS
    n_z = n_dp // n_y
    me = lax.axis_index("dp")
    ten = lax.axis_index("tensor")
    my_z, my_y = me // n_y, lax.rem(me, n_y)
    my_x, my_c = ten // 2, lax.rem(ten, 2)
    other_c = 1 - my_c
    sibling = (me, 2 * my_x + other_c)
    across = (me, 2 * (1 - my_x) + my_c)
    scale = 1.0 / math.sqrt(HD)

    def dp_dev(index):
        return (index, ten)

    def z_peer(step):
        return lax.rem(my_z + step, n_z)

    def remote(src, dst, send, recv, dev):
        return pltpu.make_async_remote_copy(
            src_ref=src, dst_ref=dst, send_sem=send, recv_sem=recv, device_id=dev, device_id_type=MESH
        )

    def at(cond, func):
        @pl.when(cond)
        def _():
            func()

    def load_rows(j, which):
        half = my_c if which == 0 else other_c
        return pltpu.make_async_copy(x_hbm.at[j, half], res.at[which, j], load_sem.at[which, j])

    def load_blocks(l):
        return pltpu.make_async_copy(
            w_hbm.at[l], flat.at[pl.ds(l * GROUP, GROUP)], land_sem.at[l]
        )

    def load_cot(j):
        return pltpu.make_async_copy(ct_hbm.at[j, my_c], y_own.at[j], ct_sem.at[j])

    for l in range(LAYERS):
        load_blocks(l).start()
    for j in range(CHUNKS):
        load_rows(j, 0).start()
        load_rows(j, 1).start()
    for j in range(CHUNKS):
        load_cot(j).start()

    barrier = pltpu.get_barrier_semaphore()
    for step in range(1, n_dp):
        pl.semaphore_signal(
            barrier, inc=1, device_id=dp_dev(lax.rem(me + step, n_dp)), device_id_type=MESH
        )
    pl.semaphore_signal(barrier, inc=1, device_id=sibling, device_id_type=MESH)
    pl.semaphore_signal(barrier, inc=1, device_id=across, device_id_type=MESH)

    sel = table_selector((144, 256))
    for l in range(LAYERS):
        row = lax.dot_general(
            jnp.broadcast_to(split_ref[l], (8, 144)),
            sel,
            (((1,), (0,)), ((), ())),
            precision=highest,
            preferred_element_type=F32,
        )
        msg_in[me, 8 * l : 8 * l + 8, :] = row
        for r in range(6):
            msg_in[me, 8 * l + r : 8 * l + r + 1, 0:B] = shared_ref[r, l : l + 1, :]

    pl.semaphore_wait(barrier, n_dp + 1)

    def msg_copy(step):
        return remote(
            msg_in.at[me], msg_in.at[me], m_s.at[step - 1], m_r.at[me],
            dp_dev(lax.rem(me + step, n_dp)),
        )

    def msg_from(step):
        src = lax.rem(me + step, n_dp)
        return remote(msg_in.at[src], msg_in.at[src], m_s.at[step - 1], m_r.at[src], dp_dev(src))

    for step in range(1, n_dp):
        msg_copy(step).start()

    def gather_send(l, p, slab, k, dev):
        return remote(
            wt.at[l, p, slab], wt.at[l, p, slab], g_s.at[l, p, k], g_r.at[l, p, slab], dp_dev(dev)
        )

    def y_peers():
        return [my_z * n_y + lax.rem(my_y + s, n_y) for s in range(1, n_y)]

    def own_send(l, p):
        @pl.when(my_z < n_z - 1)
        def _():
            gather_send(l, p, me, 0, me + n_y).start()

        @pl.when(my_z > 0)
        def _():
            gather_send(l, p, me, 1, me - n_y).start()

        gather_send(l, p, me, 2, y_peers()[0]).start()

    def wave(l, p, hop):
        @pl.when(my_z >= hop)
        def _():
            slab = me - hop * n_y
            gather_send(l, p, slab, 0, slab).wait_recv()

            @pl.when(my_z < n_z - 1)
            def _():
                gather_send(l, p, slab, 2 + hop, me + n_y).start()

            gather_send(l, p, slab, n_z + 1 + hop, y_peers()[0]).start()

        @pl.when(my_z + hop < n_z)
        def _():
            slab = me + hop * n_y
            gather_send(l, p, slab, 0, slab).wait_recv()

            @pl.when(my_z > 0)
            def _():
                gather_send(l, p, slab, 2 * n_z + hop, me - n_y).start()

            gather_send(l, p, slab, 3 * n_z - 1 + hop, y_peers()[0]).start()

    def gather_finish(l, p):
        for s in range(0, n_z):
            slab = z_peer(s) * n_y + lax.rem(my_y + 1, n_y)
            gather_send(l, p, slab, 0, slab).wait_recv()

    def gather_drain(l, p):
        def sent(k):
            gather_send(l, p, me, k, me).wait_send()

        up, down = my_z < n_z - 1, my_z > 0
        at(up, lambda: sent(0))
        at(down, lambda: sent(1))
        sent(2)
        for hop in range(1, n_z):
            low, high = my_z >= hop, my_z + hop < n_z
            at(jnp.logical_and(low, up), lambda: sent(2 + hop))
            at(low, lambda: sent(n_z + 1 + hop))
            at(jnp.logical_and(high, down), lambda: sent(2 * n_z + hop))
            at(high, lambda: sent(3 * n_z - 1 + hop))

    def relayout(l, p):
        cols = []
        for b in range(8):
            blk = PARTS[p][b]
            square = flat_to_square(flat.at[l * GROUP + blk], place.at[b % 6])
            cols.append(jnp.transpose(square) if blk in TRANSPOSED[p] else square)
        wt[l, p, me] = jnp.concatenate(cols, axis=1).astype(BF16)

    def relayout_layer(l, carry):
        load_blocks(l).wait()
        for p in range(3):
            relayout(l, p)
            if p == 0:
                at(l == 0, lambda: own_send(0, 0))
        return carry

    lax.fori_loop(0, LAYERS, relayout_layer, 0)

    seq_shift = jnp.where(long_ref[0, 0] > 0, 0, 1)
    seg = seg_ref[...]
    pos = lax.broadcasted_iota(jnp.int32, (8, 128), 0) * 128 + lax.broadcasted_iota(
        jnp.int32, (8, 128), 1
    )
    seq = (pos >> 8) * seq_shift
    kid = jnp.where(seg >= 0, seq * 64 + seg, -1 - seq).astype(F32)
    for r in range(8):
        kid_row[r // 2, 0:1, 128 * (r % 2) : 128 * (r % 2) + 128] = kid[r : r + 1, :]
        kid_col[r] = jnp.transpose(
            jnp.broadcast_to(kid[r : r + 1, :], (128, 128))
        )

    gvecs[...] = jnp.zeros_like(gvecs)
    gbias[...] = jnp.zeros_like(gbias)

    for step in range(1, n_dp):
        msg_from(step).wait_recv()
    for l in range(LAYERS):
        vecs[l] = jnp.concatenate(
            [msg_in[s, 8 * l : 8 * l + 8, 0:B] for s in range(n_dp)], axis=1
        )
        rows = [msg_in[s, 8 * l : 8 * l + 8, 128:256] for s in range(n_dp)]
        pad = jnp.zeros((8, D // 4), F32)
        bias_row[l] = jnp.concatenate(
            [r[:, 0:24] for r in rows]
            + [pad]
            + [r[:, 24:48] for r in rows]
            + [jnp.zeros((8, 64), F32)],
            axis=1,
        )

    low_half = lanes_of((CHUNK, 128)) < 64

    def vec(l, k):
        return vecs[l, k : k + 1, :]

    def core_copy(j):
        return remote(stage.at[j, other_c], core_in.at[j], c_s.at[j], c_r.at[j], sibling)

    def x_copy(j, par):
        if par == 2:
            return remote(stage.at[j, my_c], side_in.at[j], x_s.at[2, j], x_r.at[2, j], across)
        return remote(stage.at[j, my_c], x_in.at[par, j], x_s.at[par, j], x_r.at[par, j], across)

    def own_copy(ref, j):
        return remote(ref.at[j, my_c], ref.at[j, my_c], a_s.at[j], a_r.at[j], sibling)

    def send_partial(j, value):
        stage[j] = value.astype(BF16).reshape(2, HALF, D)
        core_copy(j).start()

    def pass_on(j, par):
        core_copy(j).wait()
        mine = stage[j, my_c].astype(F32) + core_in[j].astype(F32)
        stage[j, my_c] = mine.astype(BF16)
        x_copy(j, par).start()

    def total(j, par):
        x_copy(j, par).wait()
        came = side_in[j] if par == 2 else x_in[par, j]
        return stage[j, my_c].astype(F32) + came.astype(F32)

    def project(l, j):
        rows = a_all[l, j].reshape(CHUNK, D)
        weight = wt[l, 0].reshape(D, D)[:, 0:640]
        out = dot_nn(rows, weight) + bias_row[l, 0:1, :]
        tiles = [out[:, 128 * t : 128 * t + 128] for t in range(5)]
        q_roll = pltpu.roll(tiles[0], 64, 1)
        v_roll = pltpu.roll(tiles[3], 64, 1)
        zero = jnp.zeros((CHUNK, 128), F32)
        q_val = [
            jnp.where(low_half, zero, q_roll),
            jnp.where(low_half, q_roll, pltpu.roll(tiles[1], 64, 1)),
        ]
        k_val = [jnp.where(low_half, zero, tiles[1]), tiles[2]]
        v_val = [
            jnp.where(low_half, zero, v_roll),
            jnp.where(low_half, v_roll, pltpu.roll(tiles[4], 64, 1)),
        ]
        q_all[l, j] = jnp.concatenate(q_val, axis=1).astype(BF16)
        k_all[l, j] = jnp.concatenate(k_val, axis=1).astype(BF16)
        v_mat = jnp.concatenate(v_val, axis=1)
        v_all[l, j] = v_mat.astype(BF16)
        v_tr[:, pl.ds(pl.multiple_of(j * CHUNK, CHUNK), CHUNK)] = jnp.transpose(v_mat).astype(BF16)

    def head_tile(mat, h):
        if h == 0:
            return mat[:, 0:128]
        keep = low_half if h == 1 else jnp.logical_not(low_half)
        return jnp.where(keep, mat[:, 128:256], jnp.zeros((), mat.dtype))

    def tile_of(ref, l, h):
        full = ref[l].reshape(ROWS, 256)
        return full[:, 0:128] if h == 0 else full[:, 128:256]

    def allowed_of(j):
        col = kid_col[...].reshape(ROWS, 128)
        return jnp.concatenate([col, col], axis=1) == kid_row[j, 0:1, :]

    def attend_chunk(l, j):
        allowed = allowed_of(j)
        q_mat = q_all[l, j]
        outs = [jnp.zeros((64, CHUNK), F32)]
        for h in range(HEADS_DEV):
            scores = dot_nt(tile_of(k_all, l, h), head_tile(q_mat, h)) * scale
            scores = jnp.where(allowed, scores, big_negative)
            top = jnp.max(scores, axis=0, keepdims=True)
            expo = jnp.exp(scores - top)
            tot = jnp.sum(expo, axis=0, keepdims=True)
            lse_all[l, j, h : h + 1, :] = top + jnp.log(tot)
            out = dot_nn(v_tr[64 + 64 * h : 128 + 64 * h, :], expo.astype(BF16))
            outs.append(out / tot)
        o_mat = jnp.transpose(jnp.concatenate(outs, axis=0)).astype(BF16)
        o_all[l, j] = o_mat
        send_partial(j, dot_nt(o_mat, wt[l, 0].reshape(D, D)[:, 512:768]))

    def middle(l, j):
        mid = res[2 * l, j] + total(j, 0) + vec(l, 4)
        res[2 * l + 1, j] = mid
        hat, _ = norm_rows(mid)
        c_all[l, j, my_c] = (hat * vec(l, 2) + vec(l, 3)).astype(BF16)
        own_copy(c_all.at[l], j).start()

    def mlp(l, j):
        own_copy(c_all.at[l], j).wait()
        rows = c_all[l, j].reshape(CHUNK, D)
        pre = dot_nn(rows, wt[l, 1].reshape(D, D)) + vec(l, 6)
        cdf = 0.5 * (1.0 + lax.erf(pre * (1.0 / math.sqrt(2.0))))
        pdf = jnp.exp(-0.5 * pre * pre) * (1.0 / math.sqrt(2.0 * math.pi))
        act = (pre * cdf).astype(BF16)
        z_all[l, j] = act
        gp_all[l, j] = (cdf + pre * pdf).astype(BF16)

        @pl.when(l < LAYERS - 1)
        def _():
            at(j == 0, lambda: gather_finish(0, 2))
            send_partial(j, dot_nt(z_all[l, j], wt[l, 2].reshape(D, D)))

        @pl.when(l == LAYERS - 1)
        def _():
            y_copy(j).wait()
            mlp_back(LAYERS - 1, j)

    def y_copy(j):
        return remote(y_all.at[j, my_c], y_all.at[j, my_c], y_s.at[j], y_r.at[j], sibling)

    def near_copy(ref, hbm, which, j):
        return pltpu.make_async_copy(ref.at[j], hbm.at[j, my_c], out_sem.at[which, j])

    def far_copy(ref, hbm, which, j):
        return remote(ref.at[j], hbm.at[j, my_c], far_s.at[which, j], far_r.at[which, j], sibling)

    def layer_end(l, j):
        new = res[2 * l + 1, j] + total(j, 1) + vec(l, 5)
        res[2 * l + 2, j] = new
        hat, _ = norm_rows(new)
        a_all[l + 1, j, my_c] = (hat * vec(l + 1, 0) + vec(l + 1, 1)).astype(BF16)
        own_copy(a_all.at[l + 1], j).start()

    def last_send(slot, j):
        send_partial(slot, dot_nt(z_all[LAYERS - 1, j], wt[LAYERS - 1, 2].reshape(D, D)))

    def last_end(slot, j):
        last = res.at[2 * LAYERS - 1]
        last[j] = last[j] + total(slot, 2) + vec(LAYERS - 1, 5)
        near_copy(last, bo_hbm, 0, j).start()
        far_copy(last, bo_hbm, 0, j).start()

    def when_chunk(tick, offset, func):
        @pl.when(jnp.logical_and(tick >= offset, tick < offset + CHUNKS))
        def _():
            func(tick - offset)

    def add_vec(l, k, value):
        gvecs[l, k : k + 1, :] += value

    def mlp_back(l, j):
        d_act = dot_nn(y_all[j].reshape(CHUNK, D), wt[l, 2].reshape(D, D))
        d_pre = (d_act * gp_all[l, j].astype(F32)).astype(BF16)
        du_all[j] = d_pre
        add_vec(l, 6, jnp.sum(d_pre.astype(F32), axis=0, keepdims=True))
        send_partial(j, dot_nt(du_all[j], wt[l, 1].reshape(D, D)))

    def middle_back(l, j):
        grad = total(j, 1)
        d_rows, d_gain, d_shift = norm_back(grad, res[2 * l + 1, j], vec(l, 2))
        y_rows = y_own[j]
        add_vec(l, 5, jnp.sum(y_rows, axis=0, keepdims=True))
        g_rows = y_rows + d_rows
        add_vec(l, 2, d_gain)
        add_vec(l, 3, d_shift)
        add_vec(l, 4, jnp.sum(g_rows, axis=0, keepdims=True))
        y_own[j] = g_rows
        g_all[j, my_c] = g_rows.astype(BF16)
        own_copy(g_all, j).start()

    def attend_back(l, j):
        own_copy(g_all, j).wait()
        d_out = dot_nn(g_all[j].reshape(CHUNK, D), wt[l, 0].reshape(D, D)[:, 512:768])
        do_mat = d_out.astype(BF16)
        prod = jnp.transpose(do_mat.astype(F32) * o_all[l, j].astype(F32))
        allowed = allowed_of(j)
        q_mat = q_all[l, j]
        dq_parts = []
        for h in range(HEADS_DEV):
            q_h = head_tile(q_mat, h)
            do_h = head_tile(do_mat, h)
            scores = dot_nt(tile_of(k_all, l, h), q_h) * scale
            scores = jnp.where(allowed, scores, big_negative)
            probs = jnp.exp(scores - lse_all[l, j, h : h + 1, :])
            delta = jnp.sum(prod[64 + 64 * h : 128 + 64 * h, :], axis=0, keepdims=True)
            d_probs = dot_nt(tile_of(v_all, l, h), do_h)
            d_scores = (probs * (d_probs - delta)).astype(BF16)
            t = 0 if h == 0 else 128
            dv_acc[:, t : t + 128] += dot_nn(probs.astype(BF16), do_h)
            dk_acc[:, t : t + 128] += dot_nn(d_scores, q_h)
            dq_parts.append(dot_nn(v_tr[64 + 64 * h : 128 + 64 * h, :], d_scores))
        dq_parts.append(jnp.zeros((64, CHUNK), F32))
        dq_mat = jnp.transpose(jnp.concatenate(dq_parts, axis=0) * scale)
        dx_all[j, :, 0:256] = dq_mat.astype(BF16)

    def project_back(l, j):
        rows = pl.ds(pl.multiple_of(j * CHUNK, CHUNK), CHUNK)
        dk_mat = dk_acc[rows, :] * scale
        dv_mat = dv_acc[rows, :]
        zero = jnp.zeros((CHUNK, 128), F32)
        roll_zero = pltpu.roll(dv_mat[:, 0:128], 64, 1)
        roll_one = pltpu.roll(dv_mat[:, 128:256], 64, 1)
        tile_one = jnp.where(low_half, dx_all[j, :, 128:256].astype(F32), dk_mat[:, 0:128])
        dx_all[j, :, 128:640] = jnp.concatenate(
            [
                tile_one,
                dk_mat[:, 128:256],
                jnp.where(low_half, roll_zero, roll_one),
                jnp.where(low_half, roll_one, zero),
            ],
            axis=1,
        ).astype(BF16)
        dx_mat = dx_all[j]
        gbias[l, 0:1, :] += jnp.sum(dx_mat.astype(F32), axis=0, keepdims=True)
        send_partial(j, dot_nt(dx_mat, wt[l, 0].reshape(D, D)[:, 0:640]))

    def layer_begin(l, j):
        grad = total(j, 0)
        d_rows, d_gain, d_shift = norm_back(grad, res[2 * l, j], vec(l, 0))
        add_vec(l, 0, d_gain)
        add_vec(l, 1, d_shift)
        new = y_own[j] + d_rows
        y_own[j] = new

        @pl.when(l > 0)
        def _():
            y_all[j, my_c] = new.astype(BF16)
            own_copy(y_all, j).start()

        @pl.when(l == 0)
        def _():
            near_copy(y_own, ig_hbm, 1, j).start()
            far_copy(y_own, ig_hbm, 1, j).start()

    def slab(ref, p, owner):
        return ref.at[p, pl.ds(pl.multiple_of(owner * B, B), B)]

    def pair_copy(l, p, z):
        dest = y_peers()[0]
        return remote(
            slab(dw, p, z * n_y + lax.rem(my_y + 1, n_y)),
            rs_one.at[l, p, z],
            p_s.at[l, p, z],
            p_r.at[l, p, z],
            dp_dev(dest),
        )

    def line_copy(l, p, s):
        dest = z_peer(s)
        return remote(
            slab(dw, p, dest * n_y + my_y),
            rs_two.at[l, p, n_z - 1 - s],
            t_s.at[l, p, s - 1],
            t_r.at[l, p, n_z - 1 - s],
            dp_dev(dest * n_y + my_y),
        )

    def line_from(l, p, s):
        return remote(
            slab(dw, p, me),
            rs_two.at[l, p, s - 1],
            t_s.at[l, p, s - 1],
            t_r.at[l, p, s - 1],
            dp_dev(z_peer(s) * n_y + my_y),
        )

    def scatter_drain(l, p):
        for z in range(n_z):
            pair_copy(l, p, z).wait_send()
        for s in range(1, n_z):
            line_copy(l, p, s).wait_send()

    def scatter_begin(l, p):
        for s in list(range(1, n_z)) + [0]:
            pair_copy(l, p, z_peer(s)).start()

    def scatter_middle(l, p):
        for s in list(range(1, n_z)) + [0]:
            z = z_peer(s)
            pair_copy(l, p, z).wait_recv()
            ref = slab(dw, p, z * n_y + my_y)
            both = (ref[...].astype(F32) + rs_one[l, p, z].astype(F32)).astype(BF16)
            if s:
                ref[...] = both
                line_copy(l, p, s).start()
            else:
                rs_one[l, p, my_z] = both

    def runs_of(p):
        return ((0, 0, 6), (6, 14, 2)) if p == 0 else ((0, PARTS[p][0], 8),)

    def block_copies(l, p):
        return [
            pltpu.make_async_copy(
                flat.at[pl.ds(16 + 8 * k + here, count)],
                hbm.at[l, pl.ds(there, count)],
                gout_sem.at[k, n],
            )
            for k, hbm in enumerate((gf_hbm, lf_hbm, rf_hbm, pf_hbm))
            for n, (here, there, count) in enumerate(runs_of(p))
        ]

    def root_copies(l, p):
        return [
            pltpu.make_async_copy(
                hbm.at[l, pl.ds(there, count)],
                flat.at[pl.ds(8 * k + here, count)],
                root_sem.at[k, n],
            )
            for k, hbm in enumerate((lr_hbm, rr_hbm))
            for n, (here, there, count) in enumerate(runs_of(p))
        ]

    def scatter_end(l, p):
        acc = rs_one[l, p, my_z].astype(F32)
        for s in range(1, n_z):
            line_from(l, p, s).wait_recv()
            acc = acc + rs_two[l, p, s - 1].astype(F32)
        nm_ref[0:1, 0:1] += jnp.sum(acc * acc, keepdims=True)
        g_acc[...] = acc

    def block_update(l, p):
        acc = g_acc[...]
        for copy in root_copies(l, p):
            copy.wait()
        if p < 2:
            for copy in block_copies(l, p + 1):
                copy.wait()
        else:
            @pl.when(l < LAYERS - 1)
            def _():
                for copy in block_copies(LAYERS - 1, 0):
                    copy.wait()

        for b in range(8):
            square = acc[:, B * b : B * b + B]
            turned = jnp.transpose(square)
            if PARTS[p][b] in TRANSPOSED[p]:
                square, turned = turned, square
            slot = 3 * (b % 2)
            low = square.astype(BF16)
            rows = split_rows(square, place.at[slot])
            cols = split_rows(turned, place.at[slot + 1])
            right = flat_to_square(flat.at[8 + b], place.at[slot + 2])
            left = jnp.concatenate(flat_rows(flat.at[b]), axis=0)[:, :B]
            store_flat(flat.at[16 + b], rows)
            store_flat(flat.at[24 + b], dot_nt(rows.astype(BF16), low))
            store_flat(flat.at[32 + b], dot_nn(cols.astype(BF16), low))
            half = dot_nn(left.astype(BF16), low).astype(BF16)
            store_flat(flat.at[40 + b], dot_nn(half, right.astype(BF16)))
        for copy in block_copies(l, p):
            copy.start()
        if p > 0:
            for copy in root_copies(l, p - 1):
                copy.start()
        else:
            @pl.when(l > 0)
            def _():
                for copy in root_copies(0, 2):
                    copy.start()

    nm_ref[...] = jnp.zeros_like(nm_ref)

    def weight_grad(l, p, func):
        at(l < LAYERS - 1, lambda: scatter_drain(LAYERS - 1, p))

        def piece(m, carry):
            cols = pl.ds(pl.multiple_of(m * 256, 256), 256)
            dw[p, cols, :] = func(cols).astype(BF16)
            return carry

        lax.fori_loop(0, D // 256, piece, 0)
        scatter_begin(l, p)

    def down_grad(l):
        def func(cols):
            return dot_tn(
                y_all[:, :, :, cols].reshape(ROWS, 256), z_all[l].reshape(ROWS, D)
            )

        weight_grad(l, 2, func)

    def up_grad(l):
        def func(cols):
            return dot_tn(
                c_all[l, :, :, :, cols].reshape(ROWS, 256), du_all[...].reshape(ROWS, D)
            )

        weight_grad(l, 1, func)

    def qkv_grad(l):
        def func(cols):
            first = dot_tn(
                a_all[l, :, :, :, cols].reshape(ROWS, 256), dx_all[...].reshape(ROWS, 640)
            )
            second = dot_tn(
                g_all[:, :, :, cols].reshape(ROWS, 256), o_all[l].reshape(ROWS, 256)
            )
            return jnp.concatenate(
                [first[:, 0:512], first[:, 512:640] + second[:, 0:128], second[:, 128:256]], axis=1
            )

        weight_grad(l, 0, func)

    def first_norm(j, carry):
        load_rows(j, 0).wait()
        load_rows(j, 1).wait()
        hat, _ = norm_rows(res[0, j])
        a_all[0, j, my_c] = (hat * vec(0, 0) + vec(0, 1)).astype(BF16)
        hat, _ = norm_rows(res[1, j])
        a_all[0, j, other_c] = (hat * vec(0, 0) + vec(0, 1)).astype(BF16)
        return carry

    def first_grad(j, carry):
        load_cot(j).wait()
        rows = jnp.where(kid_col[2 * j + my_c][:, 0:1] >= 0.0, y_own[j], 0.0)
        y_own[j] = rows
        y_all[j, my_c] = rows.astype(BF16)
        y_copy(j).start()
        return carry

    def first_project(j, carry):
        project(0, j)
        return carry

    for copy in root_copies(LAYERS - 1, 2):
        copy.start()
    wave(0, 0, 1)
    own_send(0, 1)
    lax.fori_loop(0, CHUNKS // 2, first_norm, 0)
    wave(0, 0, 2)
    lax.fori_loop(CHUNKS // 2, CHUNKS, first_norm, 0)
    wave(0, 0, 3)
    wave(0, 1, 1)
    lax.fori_loop(0, CHUNKS, first_grad, 0)
    gather_finish(0, 0)
    wave(0, 1, 2)
    own_send(0, 2)
    lax.fori_loop(0, CHUNKS, first_project, 0)

    def prepare_back(l):
        for j in range(CHUNKS):
            v_tr[:, j * CHUNK : j * CHUNK + CHUNK] = jnp.transpose(k_all[l, j].astype(F32)).astype(
                BF16
            )
        dk_acc[...] = jnp.zeros_like(dk_acc)
        dv_acc[...] = jnp.zeros_like(dv_acc)

    def forward_layer(l, carry):
        def step(tick, inner):
            when_chunk(tick, 1, lambda j: pass_on(j, 0))
            when_chunk(tick, 5, lambda j: pass_on(j, 1))

            when_chunk(tick, 3, lambda j: middle(l, j))

            @pl.when(l < LAYERS - 1)
            def _():
                when_chunk(tick, 7, lambda j: layer_end(0, j))

            when_chunk(tick, 0, lambda j: attend_chunk(l, j))

            def next_project(j):
                own_copy(a_all.at[LAYERS - 1], j).wait()
                project(LAYERS - 1, j)

            @pl.when(l == 0)
            def _():
                @pl.when(tick == 1)
                def _():
                    wave(0, 1, 3)
                    wave(0, 2, 1)

                @pl.when(tick == 3)
                def _():
                    wave(0, 2, 2)
                    own_send(1, 0)

                @pl.when(tick == 4)
                def _():
                    gather_finish(0, 1)
                    wave(0, 2, 3)
                    wave(1, 0, 1)

                @pl.when(tick == 5)
                def _():
                    wave(1, 0, 2)
                    own_send(1, 1)

                @pl.when(tick == 7)
                def _():
                    wave(1, 0, 3)
                    wave(1, 1, 1)

                at(tick == 8, lambda: gather_finish(1, 0))

                @pl.when(tick == 9)
                def _():
                    wave(1, 1, 2)
                    own_send(1, 2)

                @pl.when(tick == 11)
                def _():
                    wave(1, 1, 3)
                    wave(1, 2, 1)

            @pl.when(l == 1)
            def _():
                at(tick == 0, lambda: wave(1, 2, 2))
                at(tick == 1, lambda: wave(1, 2, 3))

                @pl.when(tick == 4)
                def _():
                    gather_finish(1, 1)
                    gather_finish(1, 2)

            when_chunk(tick, 4, lambda j: mlp(l, j))

            @pl.when(l == 0)
            def _():
                when_chunk(tick, 8, next_project)

            at(jnp.logical_and(l == LAYERS - 1, tick == 8), lambda: prepare_back(LAYERS - 1))
            return inner

        lax.fori_loop(0, 12, step, 0)
        return carry

    lax.fori_loop(0, LAYERS, forward_layer, 0)
    for step in range(1, n_dp):
        msg_copy(step).wait_send()

    def finish_part(l, p):
        scatter_end(l, p)
        block_update(l, p)

    def backward_layer(n, carry):
        l = LAYERS - 1 - n
        upper = l == LAYERS - 1
        lower = l < LAYERS - 1
        down_grad(l)

        @pl.when(lower)
        def _():
            scatter_middle(LAYERS - 1, 0)

        def step(tick, inner):
            at(tick == 1, lambda: last_send(0, 2 * n))

            @pl.when(tick == 2)
            def _():
                last_send(1, 2 * n + 1)
                pass_on(0, 2)

            at(tick == 3, lambda: pass_on(1, 2))
            middle_back(l, tick)
            at(tick == 0, lambda: up_grad(l))

            at(tick == 3, lambda: scatter_middle(l, 2))
            attend_back(l, tick)
            return inner

        lax.fori_loop(0, CHUNKS, step, 0)

        def step_two(tick, inner):
            when_chunk(tick, 1, lambda j: pass_on(j, 0))

            @pl.when(upper)
            def _():
                when_chunk(tick, 6, lambda j: pass_on(j, 1))

            when_chunk(tick, 4, lambda j: layer_begin(l, j))
            at(tick < 2, lambda: last_end(tick, 2 * n + tick))
            when_chunk(tick, 0, lambda j: project_back(l, j))
            at(tick == 3, lambda: qkv_grad(l))

            @pl.when(lower)
            def _():
                at(tick == 4, lambda: finish_part(LAYERS - 1, 1))
                at(tick == 5, lambda: finish_part(LAYERS - 1, 0))

            def next_back(j):
                own_copy(y_all, j).wait()
                mlp_back(l - 1, j)

            @pl.when(upper)
            def _():
                at(tick == 4, lambda: prepare_back(l - 1))
                when_chunk(tick, 5, next_back)

            at(tick == 5, lambda: scatter_middle(l, 1))
            at(tick == 6, lambda: finish_part(l, 2))
            return inner

        lax.fori_loop(0, 10, step_two, 0)
        return carry

    lax.fori_loop(0, LAYERS, backward_layer, 0)

    sib = remote(gvecs, sib_in, sib_s.at[0], sib_r.at[0], sibling)
    sib.start()
    sib.wait()
    row_at = lax.broadcasted_iota(jnp.int32, (8, D), 0)
    for l in range(LAYERS):
        mat = gvecs[l] + jnp.where(row_at < 6, sib_in[l], 0.0)
        extra = gbias[l]
        for s in range(n_dp):
            gmsg_out[s, 8 * l : 8 * l + 8, 0:B] = mat[:, B * s : B * s + B]
            gmsg_out[s, 8 * l : 8 * l + 8, 128:152] = extra[:, 24 * s : 24 * s + 24]
            gmsg_out[s, 8 * l : 8 * l + 8, 152:176] = extra[:, 384 + 24 * s : 384 + 24 * s + 24]
            gmsg_out[s, 8 * l : 8 * l + 8, B:128] = jnp.zeros((8, 128 - B), F32)
            gmsg_out[s, 8 * l : 8 * l + 8, 176:256] = jnp.zeros((8, 80), F32)

    def gmsg_copy(step):
        dest = lax.rem(me + step, n_dp)
        return remote(
            gmsg_out.at[dest], msg_in.at[me], gm_s.at[step - 1], gm_r.at[me], dp_dev(dest)
        )

    def gmsg_from(step):
        src = lax.rem(me + step, n_dp)
        return remote(gmsg_out.at[src], msg_in.at[src], gm_s.at[step - 1], gm_r.at[src], dp_dev(src))

    for step in range(1, n_dp):
        gmsg_copy(step).start()
    msg_in[me] = gmsg_out[me]
    scatter_middle(0, 0)
    finish_part(0, 1)
    for step in range(1, n_dp):
        gmsg_from(step).wait_recv()
    summed = msg_in[0]
    for s in range(1, n_dp):
        summed = summed + msg_in[s]
    sg_ref[...] = summed

    scatter_end(0, 0)
    squares = summed * summed
    lane = lanes_of((1, 128))
    packed = jnp.where(lane == 0, nm_ref[0:1, :], 0.0)
    shared_sums = jnp.zeros((1, 128), F32)
    for l in range(LAYERS):
        base = 8 * l
        up = jnp.sum(squares[base + 6 : base + 7, 0:B], keepdims=True)
        query = jnp.sum(squares[base : base + 1, 128:152], keepdims=True)
        value = jnp.sum(squares[base : base + 1, 152:176], keepdims=True)
        for k, item in enumerate((query, value, up)):
            packed = packed + jnp.where(lane == 1 + 3 * l + k, item, 0.0)
        for r in range(6):
            item = jnp.sum(squares[base + r : base + r + 1, 0:B], keepdims=True)
            shared_sums = shared_sums + jnp.where(lane == 6 * l + r, item, 0.0)

    for hop, dev in enumerate((sibling, across)):
        nb_out[hop] = jnp.broadcast_to(packed, (8, 128))
        swap = remote(nb_out.at[hop], nb_in.at[hop], nb_s.at[hop], nb_r.at[hop], dev)
        swap.start()
        if hop == 0:
            swap.wait()
        else:
            block_update(0, 0)
            swap.wait()
        packed = packed + nb_in[hop, 0:1, :]
    row8 = lax.broadcasted_iota(jnp.int32, (8, 128), 0)
    nd_in[me] = jnp.where(row8 == 0, packed, jnp.where(row8 == 1, shared_sums, 0.0))

    def nd_copy(step):
        dest = lax.rem(me + step, n_dp)
        return remote(nd_in.at[me], nd_in.at[me], nd_s.at[step - 1], nd_r.at[me], dp_dev(dest))

    def nd_from(step):
        src = lax.rem(me + step, n_dp)
        return remote(nd_in.at[src], nd_in.at[src], nd_s.at[step - 1], nd_r.at[src], dp_dev(src))

    for step in range(1, n_dp):
        nd_copy(step).start()
    for step in range(1, n_dp):
        nd_from(step).wait_recv()
    acc = nd_in[0]
    for s in range(1, n_dp):
        acc = acc + nd_in[s]
    nm_ref[...] = acc

    for p in range(3):
        scatter_drain(0, p)
        for l in range(LAYERS):
            gather_drain(l, p)
    for copy in block_copies(0, 0):
        copy.wait()
    for step in range(1, n_dp):
        gmsg_copy(step).wait_send()
        nd_copy(step).wait_send()
    for j in range(CHUNKS):
        near_copy(res.at[2 * LAYERS - 1], bo_hbm, 0, j).wait()
        far_copy(res.at[2 * LAYERS - 1], bo_hbm, 0, j).wait()
        near_copy(y_own, ig_hbm, 1, j).wait()
        far_copy(y_own, ig_hbm, 1, j).wait()


def train_call(n_y, x_rows, ct_rows, seg, long_flag, blocks, left, right, split, shared):
    hbm = pl.BlockSpec(memory_space=pl.ANY)
    vmem = pl.BlockSpec(memory_space=pltpu.VMEM)
    smem = pl.BlockSpec(memory_space=pltpu.SMEM)
    dma = pltpu.SemaphoreType.DMA
    n_dp = GROUPS
    n_z = n_dp // n_y

    def buf(shape, dtype=BF16):
        return pltpu.VMEM(shape, dtype)

    scratch = [
        buf((LAYERS, 3, n_dp, B, D)),
        buf((LAYERS, CHUNKS, 2, HALF, D)),
        buf((LAYERS, CHUNKS, 2, HALF, D)),
        buf((LAYERS, CHUNKS, CHUNK, 256)),
        buf((LAYERS, CHUNKS, CHUNK, 256)),
        buf((LAYERS, CHUNKS, CHUNK, 256)),
        buf((256, ROWS)),
        buf((LAYERS, CHUNKS, CHUNK, 256)),
        buf((LAYERS, CHUNKS, 8, CHUNK), F32),
        buf((LAYERS, CHUNKS, CHUNK, D)),
        buf((LAYERS, CHUNKS, CHUNK, D)),
        buf((2 * LAYERS, CHUNKS, HALF, D), F32),
        buf((CHUNKS, HALF, D), F32),
        buf((CHUNKS, 2, HALF, D)),
        buf((CHUNKS, 2, HALF, D)),
        buf((CHUNKS, CHUNK, D)),
        buf((CHUNKS, CHUNK, 640)),
        buf((ROWS, 256), F32),
        buf((ROWS, 256), F32),
        buf((CHUNKS, 2, HALF, D)),
        buf((CHUNKS, HALF, D)),
        buf((2, CHUNKS, HALF, D)),
        buf((2, HALF, D)),
        buf((3, D, D)),
        buf((LAYERS, 3, n_z, B, D)),
        buf((LAYERS, 3, n_z - 1, B, D)),
        buf((6, B, 128), F32),
        buf((LAYERS * GROUP, 72, 128), F32),
        buf((B, D), F32),
        buf((8, HALF, 128), F32),
        buf((CHUNKS, 8, CHUNK), F32),
        buf((LAYERS, 8, D), F32),
        buf((LAYERS, 8, 640), F32),
        buf((LAYERS, 8, D), F32),
        buf((LAYERS, 8, 640), F32),
        buf((LAYERS, 8, D), F32),
        buf((n_dp, 16, 256), F32),
        buf((n_dp, 16, 256), F32),
        buf((2, 8, 128), F32),
        buf((2, 8, 128), F32),
        buf((n_dp, 8, 128), F32),
        dma((LAYERS, 3, 4 * n_z)),
        dma((LAYERS, 3, n_dp)),
        dma((CHUNKS,)),
        dma((CHUNKS,)),
        dma((3, CHUNKS)),
        dma((3, CHUNKS)),
        dma((CHUNKS,)),
        dma((CHUNKS,)),
        dma((LAYERS, 3, n_z)),
        dma((LAYERS, 3, n_z)),
        dma((LAYERS, 3, n_z - 1)),
        dma((LAYERS, 3, n_z - 1)),
        dma((2, CHUNKS)),
        dma((LAYERS,)),
        dma((CHUNKS,)),
        dma((CHUNKS,)),
        dma((CHUNKS,)),
        dma((2, CHUNKS)),
        dma((2, CHUNKS)),
        dma((2, CHUNKS)),
        dma((4, 2)),
        dma((2, 2)),
        dma((n_dp - 1,)),
        dma((n_dp,)),
        dma((n_dp - 1,)),
        dma((n_dp,)),
        dma((1,)),
        dma((1,)),
        dma((2,)),
        dma((2,)),
        dma((n_dp - 1,)),
        dma((n_dp,)),
    ]
    rows_shape = jax.ShapeDtypeStruct((CHUNKS, 2, HALF, D), F32)
    return pl.pallas_call(
        functools.partial(train_kernel, n_y),
        out_shape=(
            rows_shape,
            rows_shape,
            *[jax.ShapeDtypeStruct((LAYERS, GROUP, 72, 128), F32)] * 4,
            jax.ShapeDtypeStruct((16, 256), F32),
            jax.ShapeDtypeStruct((8, 128), F32),
        ),
        in_specs=[hbm, hbm, vmem, smem, hbm, hbm, hbm, vmem, vmem],
        out_specs=(hbm, hbm, hbm, hbm, hbm, hbm, vmem, vmem),
        scratch_shapes=scratch,
        compiler_params=pltpu.CompilerParams(
            collective_id=0, has_side_effects=True, vmem_limit_bytes=61 * 1024 * 1024
        ),
        cost_estimate=pl.CostEstimate(
            flops=30_000_000_000, bytes_accessed=30_000_000, transcendentals=20_000_000
        ),
        name="train",
    )(x_rows, ct_rows, seg, long_flag, blocks, left, right, split, shared)


def update_kernel(
    g_ref,
    lg_ref,
    rg_ref,
    p_ref,
    w_ref,
    l_ref,
    r_ref,
    sg_ref,
    nm_ref,
    sp_ref,
    sh_ref,
    bo_ref,
    ig_ref,
    gout_ref,
    nw_ref,
    nl_ref,
    nr_ref,
    sgo_ref,
    nsp_ref,
    shg_ref,
    nsh_ref,
    norm_ref,
    bo_out,
    ig_out,
):
    step_at = pl.program_id(0)
    bo_out[...] = bo_ref[...]
    ig_out[...] = ig_ref[...]
    lane = lanes_of((1, 128))
    row_zero = nm_ref[0:1, :]
    row_one = nm_ref[1:2, :]
    total_sq = jnp.sum(jnp.where(lane < 7, row_zero, 0.0), keepdims=True) + jnp.sum(
        jnp.where(lane < 12, row_one, 0.0), keepdims=True
    )
    norm = jnp.sqrt(total_sq)
    factor = clip_limit / jnp.maximum(norm, clip_limit)
    squared = factor * factor
    gram_weight = (1.0 - decay) * squared

    for b in range(g_ref.shape[0]):
        gout_ref[b] = g_ref[b] * factor
        nl_ref[b] = decay * l_ref[b] + gram_weight * lg_ref[b]
        nr_ref[b] = decay * r_ref[b] + gram_weight * rg_ref[b]
        direction = p_ref[b] * factor
        mean_sq = jnp.sum(direction * direction, keepdims=True) / (B * B)
        nw_ref[b] = w_ref[b] - direction * (rate_matrix * lax.rsqrt(mean_sq + eps_norm))

    @pl.when(step_at == 0)
    def _():
        norm_ref[...] = norm
        sel = table_selector((144, 256))
        col = lanes_of((1, 256))
        for l in range(LAYERS):
            sums = [row_zero[:, 1 + 3 * l + k : 2 + 3 * l + k] for k in range(3)]
            means = [sums[0] / D, sums[1] / D, sums[2] / FF]
            scales = [lax.rsqrt(squared * m + eps_norm) for m in means]
            src = sg_ref[8 * l : 8 * l + 8, :]
            line = jnp.where(col < 128, src[6:7, :], src[0:1, :]) * factor
            step = line * jnp.where(col < 128, scales[2], jnp.where(col < 152, scales[0], scales[1]))
            both = jnp.concatenate([line, step, jnp.zeros((6, 256), F32)], axis=0)
            table = lax.dot_general(
                both, sel, (((1,), (1,)), ((), ())), precision=highest, preferred_element_type=F32
            )
            sgo_ref[l] = table[0:1, :]
            nsp_ref[l] = sp_ref[l] - rate_vector * table[1:2, :]
            for r in range(6):
                mean = row_one[:, 6 * l + r : 6 * l + r + 1] / D
                grad = src[r : r + 1, 0:B] * factor
                shg_ref[r, l : l + 1, :] = grad
                nsh_ref[r, l : l + 1, :] = sh_ref[r, l : l + 1, :] - rate_vector * grad * lax.rsqrt(
                    squared * mean + eps_norm
                )


def update_call(grads, lefts, rights, dirs, weights, left, right, sums, norms, split, shared, outs):
    per = GROUP
    count = LAYERS * GROUP
    flat = pl.BlockSpec((per, 72, 128), lambda i: (i, 0, 0))
    rows = pl.BlockSpec((2 * HALF * CHUNKS * per // count, D), lambda i: (i, 0))

    def whole(shape):
        return pl.BlockSpec(shape, lambda i: (0,) * len(shape))

    flat_shape = jax.ShapeDtypeStruct((count, 72, 128), F32)
    split_shape, shared_shape = (LAYERS, 1, 144), (6, LAYERS, B)
    return pl.pallas_call(
        update_kernel,
        grid=(count // per,),
        out_shape=(
            *[flat_shape] * 4,
            *[jax.ShapeDtypeStruct(split_shape, F32)] * 2,
            *[jax.ShapeDtypeStruct(shared_shape, F32)] * 2,
            jax.ShapeDtypeStruct((1, 1), F32),
            *[jax.ShapeDtypeStruct(o.shape, F32) for o in outs],
        ),
        in_specs=[flat] * 7
        + [whole((16, 256)), whole((8, 128)), whole(split_shape), whole(shared_shape), rows, rows],
        out_specs=(
            *[flat] * 4,
            *[whole(split_shape)] * 2,
            *[whole(shared_shape)] * 2,
            whole((1, 1)),
            rows,
            rows,
        ),
        compiler_params=pltpu.CompilerParams(vmem_limit_bytes=60 * 1024 * 1024),
        name="update",
    )(grads, lefts, rights, dirs, weights, left, right, sums, norms, split, shared, *outs)


def fast_body(
    n_y,
    tokens_in,
    cotangent,
    segment_ids,
    long_seq,
    weights,
    left_stats,
    right_stats,
    left_roots,
    right_roots,
    split_params,
    shared_params,
):
    rows = (CHUNKS, 2, HALF, D)
    flat = (LAYERS, GROUP, 72, 128)
    blocks = (LAYERS * GROUP, 72, 128)
    split = split_params
    shared = jnp.transpose(shared_params, (1, 0, 2))
    out_rows, in_grad, grads, lefts, rights, dirs, sums, norms = train_call(
        n_y,
        tokens_in.reshape(rows),
        cotangent.reshape(rows),
        segment_ids.reshape(8, 128),
        long_seq.reshape(1, 1),
        weights.reshape(flat),
        left_roots.reshape(flat),
        right_roots.reshape(flat),
        split,
        shared,
    )
    res = update_call(
        *[m.reshape(blocks) for m in (grads, lefts, rights, dirs, weights, left_stats, right_stats)],
        sums,
        norms,
        split,
        shared,
        (out_rows.reshape(tokens_in.shape), in_grad.reshape(tokens_in.shape)),
    )
    mats = [r.reshape(weights.shape) for r in res[:4]]
    return (
        res[9],
        res[10],
        *mats,
        res[4],
        res[5],
        jnp.transpose(res[6], (1, 0, 2)),
        jnp.transpose(res[7], (1, 0, 2)),
        res[8].reshape(()),
    )


def solution(mesh):
    in_specs = (
        P("dp", None),
        P("dp", None),
        P("dp"),
        P("dp"),
        P(None, "dp", "tensor", None),
        P(None, "dp", "tensor", None),
        P(None, "dp", "tensor", None),
        P(None, "dp", "tensor", None),
        P(None, "dp", "tensor", None),
        P(None, "tensor", "dp"),
        P(None, None, "dp"),
    )
    out_specs = (
        P("dp", None),
        P("dp", None),
        P(None, "dp", "tensor", None),
        P(None, "dp", "tensor", None),
        P(None, "dp", "tensor", None),
        P(None, "dp", "tensor", None),
        P(None, "tensor", "dp"),
        P(None, "tensor", "dp"),
        P(None, None, "dp"),
        P(None, None, "dp"),
        P(),
    )
    plan = body
    if mesh.shape["dp"] == GROUPS and mesh.shape["tensor"] == 4:
        plan = functools.partial(fast_body, 2)
    return jax.shard_map(plan, mesh=mesh, in_specs=in_specs, out_specs=out_specs, check_vma=False)
```

```python
import functools
import math

import jax
import jax.numpy as jnp
from jax import lax
from jax.experimental import pallas as pl
from jax.experimental.pallas import tpu as pltpu
from jax.sharding import PartitionSpec as P

D = 768
HEADS = 12
FF = 3072
HD = 64
B = 96
LAYERS = 2
SEQ_SHORT = 256
SEQ_LONG = 1024


clip_limit = 100.0
rate_matrix = 0.06
rate_vector = 0.2
decay = 0.5
eps_norm = 1e-06
eps_layer = 1e-06
big_negative = -1e30
highest = lax.Precision.HIGHEST


def layer_norm(hidden, gain_vec, shift_vec):
    row_mean = jnp.mean(hidden, axis=-1, keepdims=True)
    centered = hidden - row_mean
    row_var = jnp.mean(centered * centered, axis=-1, keepdims=True)
    return centered * lax.rsqrt(row_var + eps_layer) * gain_vec + shift_vec


def gelu_exact(values):
    return jax.nn.gelu(values, approximate=False)


def matmul_low(left_mat, right_mat):
    return jnp.dot(left_mat, right_mat, preferred_element_type=jnp.float32)


def inner_rows(left_mat, right_mat):
    return lax.dot_general(
        left_mat, right_mat, (((0,), (0,)), ((), ())), preferred_element_type=jnp.float32
    )


def times_trans(left_mat, right_mat):
    return lax.dot_general(
        left_mat, right_mat, (((1,), (1,)), ((), ())), preferred_element_type=jnp.float32
    )


def unpack_layer(blocks, embed_dev, inner_dev):
    row_groups = blocks.shape[0]
    block_size = blocks.shape[2]
    qkv_count = 3 * embed_dev // block_size
    up_count = inner_dev // block_size
    out_count = embed_dev // block_size

    def by_rows(part_blocks):
        block_count = part_blocks.shape[1]
        return jnp.transpose(part_blocks, (0, 2, 1, 3)).reshape(
            row_groups * block_size, block_count * block_size
        )

    def by_cols(part_blocks):
        block_count = part_blocks.shape[1]
        return jnp.transpose(part_blocks, (1, 2, 0, 3)).reshape(
            block_count * block_size, row_groups * block_size
        )

    qkv_weight = by_rows(blocks[:, :qkv_count])
    up_weight = by_rows(blocks[:, qkv_count : qkv_count + up_count])
    out_weight = by_cols(blocks[:, qkv_count + up_count : qkv_count + up_count + out_count])
    down_weight = by_cols(blocks[:, qkv_count + up_count + out_count :])
    return (qkv_weight, out_weight, up_weight, down_weight)


def pack_layer(qkv_grad, out_grad, up_grad, down_grad, block_size):
    row_groups = qkv_grad.shape[0] // block_size

    def from_rows(matrix):
        block_count = matrix.shape[1] // block_size
        return jnp.transpose(
            matrix.reshape(row_groups, block_size, block_count, block_size), (0, 2, 1, 3)
        )

    def from_cols(matrix):
        block_count = matrix.shape[0] // block_size
        return jnp.transpose(
            matrix.reshape(block_count, block_size, row_groups, block_size), (2, 0, 1, 3)
        )

    return jnp.concatenate(
        [from_rows(qkv_grad), from_rows(up_grad), from_cols(out_grad), from_cols(down_grad)], axis=1
    )


def masked_scores(query_block, key_window, query_seq, key_seq, query_seg, key_seg, score_scale):
    scores = (
        jnp.einsum("qhd,khd->hqk", query_block, key_window, preferred_element_type=jnp.float32)
        * score_scale
    )
    allowed = (query_seq[:, None] == key_seq[None, :]) & (query_seg[:, None] == key_seg[None, :])
    return jnp.where(allowed[None], scores, big_negative)


def attention_forward(queries, keys_all, values_all, seq_index, segments, block_rows, score_scale):
    block_count = queries.shape[0] // block_rows

    def one_block(block_index):
        row_start = block_index * block_rows
        query_block = lax.dynamic_slice_in_dim(queries, row_start, block_rows, 0)
        scores = masked_scores(
            query_block,
            keys_all,
            lax.dynamic_slice_in_dim(seq_index, row_start, block_rows, 0),
            seq_index,
            lax.dynamic_slice_in_dim(segments, row_start, block_rows, 0),
            segments,
            score_scale,
        )
        row_max = jnp.max(scores, axis=-1, keepdims=True)
        exponent = jnp.exp(scores - row_max)
        row_total = jnp.sum(exponent, axis=-1, keepdims=True)
        attn_probs = (exponent / row_total).astype(jnp.bfloat16)
        attended = jnp.einsum(
            "hqk,khd->qhd", attn_probs, values_all, preferred_element_type=jnp.float32
        )
        return (attended, (row_max + jnp.log(row_total))[..., 0])

    return lax.map(one_block, jnp.arange(block_count, dtype=jnp.int32))


def attention_backward(
    queries, keys_all, values_all, grad_out, log_total, seq_index, segments, block_rows, score_scale
):
    token_count = queries.shape[0]
    block_count = token_count // block_rows
    zero_grad = jnp.zeros(keys_all.shape, jnp.float32)

    def one_block(carry_pair, block_index):
        key_grad, value_grad = carry_pair
        row_start = block_index * block_rows
        query_block = lax.dynamic_slice_in_dim(queries, row_start, block_rows, 0)
        out_block = lax.dynamic_slice_in_dim(grad_out, row_start, block_rows, 0)
        scores = masked_scores(
            query_block,
            keys_all,
            lax.dynamic_slice_in_dim(seq_index, row_start, block_rows, 0),
            seq_index,
            lax.dynamic_slice_in_dim(segments, row_start, block_rows, 0),
            segments,
            score_scale,
        )
        lse_block = lax.dynamic_index_in_dim(log_total, block_index, 0, keepdims=False)
        attn_probs = jnp.exp(scores - lse_block[..., None])
        prob_grad = jnp.einsum(
            "qhd,khd->hqk", out_block, values_all, preferred_element_type=jnp.float32
        )
        row_delta = jnp.sum(attn_probs * prob_grad, axis=-1, keepdims=True)
        score_grad = (attn_probs * (prob_grad - row_delta)).astype(jnp.bfloat16)
        query_grad = (
            jnp.einsum("hqk,khd->qhd", score_grad, keys_all, preferred_element_type=jnp.float32)
            * score_scale
        )
        key_part = (
            jnp.einsum("hqk,qhd->khd", score_grad, query_block, preferred_element_type=jnp.float32)
            * score_scale
        )
        value_part = jnp.einsum(
            "hqk,qhd->khd",
            attn_probs.astype(jnp.bfloat16),
            out_block,
            preferred_element_type=jnp.float32,
        )
        key_grad = key_grad + key_part
        value_grad = value_grad + value_part
        return ((key_grad, value_grad), query_grad)

    (key_grad, value_grad), query_grad = lax.scan(
        one_block, (zero_grad, zero_grad), jnp.arange(block_count, dtype=jnp.int32)
    )
    return (query_grad.reshape(keys_all.shape), key_grad, value_grad)


def body(
    tokens_in,
    cotangent,
    segment_ids,
    long_seq,
    weights,
    left_stats,
    right_stats,
    left_roots,
    right_roots,
    split_params,
    shared_params,
):
    full_weights, full_split, full_shared = (
        lax.all_gather(weights, "dp", axis=1, tiled=True),
        lax.all_gather(split_params, "dp", axis=2, tiled=True),
        lax.all_gather(shared_params, "dp", axis=2, tiled=True),
    )
    tensor_count = lax.axis_size("tensor")
    embed_dev = D // tensor_count
    inner_dev = FF // tensor_count
    heads_local = HEADS // tensor_count
    token_count = tokens_in.shape[0]
    window = SEQ_LONG
    block_rows = min(512, window)
    score_scale = 1.0 / math.sqrt(HD)
    seq_length = jnp.where(long_seq[0] > 0, SEQ_LONG, SEQ_SHORT)
    positions = jnp.arange(token_count, dtype=jnp.int32)
    seq_index = positions // seq_length
    valid_rows = (segment_ids >= 0).astype(jnp.float32)
    matrices = []
    for layer_index in range(LAYERS):
        blocks = full_weights[layer_index, :, 0].astype(jnp.bfloat16).reshape(D // B, -1, B, B)
        matrices.append(unpack_layer(blocks, embed_dev, inner_dev))
    hidden_state = tokens_in
    kept_state = []
    for layer_index in range(LAYERS):
        qkv_weight, out_weight, up_weight, down_weight = matrices[layer_index]
        shared = full_shared[layer_index]
        bias_table = full_split[layer_index, 0].reshape(embed_dev, 6)
        up_bias = bias_table[:, 2:].reshape(inner_dev)
        normed = layer_norm(hidden_state, shared[0], shared[1]).astype(jnp.bfloat16)
        qkv_bias = jnp.concatenate(
            [bias_table[:, 0], jnp.zeros((embed_dev,), jnp.float32), bias_table[:, 1]]
        )
        projected = (matmul_low(normed, qkv_weight) + qkv_bias).astype(jnp.bfloat16)
        queries = projected[:, :embed_dev].reshape(token_count, heads_local, HD)
        keys_all = projected[:, embed_dev : 2 * embed_dev].reshape(token_count, heads_local, HD)
        values_all = projected[:, 2 * embed_dev :].reshape(token_count, heads_local, HD)
        attended, log_total = attention_forward(
            queries, keys_all, values_all, seq_index, segment_ids, block_rows, score_scale
        )
        attended = attended.reshape(token_count, embed_dev).astype(jnp.bfloat16)
        attn_branch = lax.psum(
            matmul_low(attended, out_weight).astype(jnp.bfloat16), "tensor"
        ).astype(jnp.float32)
        middle = hidden_state + attn_branch + shared[4]
        normed_mid = layer_norm(middle, shared[2], shared[3]).astype(jnp.bfloat16)
        pre_act = matmul_low(normed_mid, up_weight) + up_bias
        activation = gelu_exact(pre_act).astype(jnp.bfloat16)
        mlp_branch = lax.psum(
            matmul_low(activation, down_weight).astype(jnp.bfloat16), "tensor"
        ).astype(jnp.float32)
        kept_state.append(
            (
                hidden_state,
                normed,
                queries,
                keys_all,
                values_all,
                attended,
                log_total,
                middle,
                normed_mid,
                pre_act,
                activation,
            )
        )
        hidden_state = middle + mlp_branch + shared[5]
    grad_state = cotangent * valid_rows[:, None]
    layer_grads = [None] * LAYERS
    for layer_index in reversed(range(LAYERS)):
        (
            hidden_in,
            normed,
            queries,
            keys_all,
            values_all,
            attended,
            log_total,
            middle,
            normed_mid,
            pre_act,
            activation,
        ) = kept_state[layer_index]
        qkv_weight, out_weight, up_weight, down_weight = matrices[layer_index]
        shared = full_shared[layer_index]
        down_bias_grad = jnp.sum(grad_state, axis=0)
        grad_low = grad_state.astype(jnp.bfloat16)
        down_grad = inner_rows(activation, grad_low)
        act_grad = times_trans(grad_low, down_weight)
        gelu_pull = jax.vjp(gelu_exact, pre_act)[1]
        pre_grad = gelu_pull(act_grad)[0].astype(jnp.bfloat16)
        up_bias_grad = jnp.sum(pre_grad, axis=0, dtype=jnp.float32)
        up_grad = inner_rows(normed_mid, pre_grad)
        normed_mid_grad = lax.psum(times_trans(pre_grad, up_weight), "tensor")
        norm_pull = jax.vjp(layer_norm, middle, shared[2], shared[3])[1]
        middle_ln, gain_two_grad, shift_two_grad = norm_pull(normed_mid_grad)
        middle_grad = grad_state + middle_ln
        out_bias_grad = jnp.sum(middle_grad, axis=0)
        middle_low = middle_grad.astype(jnp.bfloat16)
        out_grad = inner_rows(attended, middle_low)
        attended_grad = (
            times_trans(middle_low, out_weight)
            .astype(jnp.bfloat16)
            .reshape(token_count, heads_local, HD)
        )
        query_grad, key_grad, value_grad = attention_backward(
            queries,
            keys_all,
            values_all,
            attended_grad,
            log_total,
            seq_index,
            segment_ids,
            block_rows,
            score_scale,
        )
        proj_grad = jnp.concatenate(
            [
                query_grad.reshape(token_count, embed_dev),
                key_grad.reshape(token_count, embed_dev),
                value_grad.reshape(token_count, embed_dev),
            ],
            axis=1,
        ).astype(jnp.bfloat16)
        query_bias_grad = jnp.sum(proj_grad[:, :embed_dev], axis=0, dtype=jnp.float32)
        value_bias_grad = jnp.sum(proj_grad[:, 2 * embed_dev :], axis=0, dtype=jnp.float32)
        qkv_grad = inner_rows(normed, proj_grad)
        normed_grad = lax.psum(times_trans(proj_grad, qkv_weight), "tensor")
        input_pull = jax.vjp(layer_norm, hidden_in, shared[0], shared[1])[1]
        hidden_ln, gain_one_grad, shift_one_grad = input_pull(normed_grad)
        grad_state = middle_grad + hidden_ln
        block_grads = pack_layer(qkv_grad, out_grad, up_grad, down_grad, B).reshape(-1, 1, B * B)
        split_vec = jnp.concatenate(
            [
                query_bias_grad[:, None],
                value_bias_grad[:, None],
                up_bias_grad.reshape(embed_dev, 4),
            ],
            axis=1,
        ).reshape(1, -1)
        shared_vec = jnp.stack(
            [
                gain_one_grad,
                shift_one_grad,
                gain_two_grad,
                shift_two_grad,
                out_bias_grad,
                down_bias_grad,
            ]
        )
        layer_grads[layer_index] = (block_grads, split_vec, shared_vec)
    weight_grad, split_grad, shared_grad = (
        lax.psum_scatter(
            jnp.stack([entry[0] for entry in layer_grads]), "dp", scatter_dimension=1, tiled=True
        ),
        lax.psum_scatter(
            jnp.stack([entry[1] for entry in layer_grads]), "dp", scatter_dimension=2, tiled=True
        ),
        lax.psum_scatter(
            jnp.stack([entry[2] for entry in layer_grads]), "dp", scatter_dimension=2, tiled=True
        ),
    )
    dp_index = lax.axis_index("dp")
    lead_shard = (lax.axis_index("tensor") == 0).astype(jnp.float32)
    slice_len = split_grad.shape[-1]
    global_pos = dp_index * slice_len + jnp.arange(slice_len, dtype=jnp.int32)
    table_column = global_pos % 6
    segment_of = (table_column >= 1).astype(jnp.int32) + (table_column >= 2).astype(jnp.int32)
    selector = (segment_of[:, None] == jnp.arange(3, dtype=jnp.int32)[None, :]).astype(jnp.float32)
    split_sq = split_grad[:, 0] * split_grad[:, 0]
    split_rows = jnp.dot(split_sq, selector, precision=highest)
    shared_sq = shared_grad * shared_grad
    shared_rows = jnp.sum(shared_sq, axis=-1) * lead_shard
    local_total = (
        jnp.sum(weight_grad * weight_grad) + jnp.sum(split_sq) + lead_shard * jnp.sum(shared_sq)
    )
    total_sq, split_rows, shared_rows = lax.psum(
        (local_total, split_rows, shared_rows), ("dp", "tensor")
    )
    grad_norm = jnp.sqrt(total_sq)
    factor = clip_limit / jnp.maximum(grad_norm, clip_limit)
    squared = factor * factor
    block_shape = weight_grad.shape[:-1] + (B, B)
    left_mats = left_roots.reshape(block_shape)
    right_mats = right_roots.reshape(block_shape)
    clipped = weight_grad * factor
    clipped_mats = clipped.reshape(block_shape)
    new_left = decay * left_stats + (1.0 - decay) * jnp.einsum(
        "...ij,...kj->...ik", clipped_mats, clipped_mats, precision=highest
    ).reshape(left_stats.shape)
    new_right = decay * right_stats + (1.0 - decay) * jnp.einsum(
        "...ji,...jk->...ik", clipped_mats, clipped_mats, precision=highest
    ).reshape(right_stats.shape)
    partial_dir = jnp.einsum("...ij,...jk->...ik", left_mats, clipped_mats, precision=highest)
    direction = jnp.einsum("...ij,...jk->...ik", partial_dir, right_mats, precision=highest)
    mean_sq = jnp.mean(direction * direction, axis=(-2, -1), keepdims=True)
    step_mats = direction * lax.rsqrt(mean_sq + eps_norm)
    new_weights = weights - rate_matrix * step_mats.reshape(weights.shape)
    vector_sizes = jnp.array([D, D, FF], jnp.float32)
    split_mean = jnp.dot(split_rows / vector_sizes[None, :], selector.T, precision=highest)
    split_clip = split_grad * factor
    new_split = split_params - rate_vector * split_clip * lax.rsqrt(
        squared * split_mean[:, None, :] + eps_norm
    )
    shared_clip = shared_grad * factor
    shared_mean = shared_rows / D
    new_shared = shared_params - rate_vector * shared_clip * lax.rsqrt(
        squared * shared_mean[..., None] + eps_norm
    )
    return (
        hidden_state,
        grad_state,
        clipped,
        new_weights,
        new_left,
        new_right,
        split_clip,
        new_split,
        shared_clip,
        new_shared,
        grad_norm,
    )


F32 = jnp.float32
BF16 = jnp.bfloat16
MESH = pl.DeviceIdType.MESH
CHUNKS = 4
HALF = 128
CHUNK = 2 * HALF
ROWS = CHUNKS * CHUNK
HEADS_DEV = 3
GROUPS = D // B
GROUP = 24
PARTS = ((0, 1, 2, 3, 4, 5, 14, 15), tuple(range(6, 14)), tuple(range(16, 24)))
TRANSPOSED = (frozenset((14, 15)), frozenset(), frozenset(range(16, 24)))


def dot_nn(left_mat, right_mat):
    return lax.dot_general(left_mat, right_mat, (((1,), (0,)), ((), ())), preferred_element_type=F32)


def dot_nt(left_mat, right_mat):
    return lax.dot_general(left_mat, right_mat, (((1,), (1,)), ((), ())), preferred_element_type=F32)


def dot_tn(left_mat, right_mat):
    return lax.dot_general(left_mat, right_mat, (((0,), (0,)), ((), ())), preferred_element_type=F32)


def lanes_of(shape):
    return lax.broadcasted_iota(jnp.int32, shape, len(shape) - 1)


def norm_rows(rows):
    mean = jnp.mean(rows, axis=-1, keepdims=True)
    centered = rows - mean
    var = jnp.mean(centered * centered, axis=-1, keepdims=True)
    inv = lax.rsqrt(var + eps_layer)
    return centered * inv, inv


def norm_back(grad, rows, gain):
    hat, inv = norm_rows(rows)
    scaled = grad * gain
    mean_one = jnp.mean(scaled, axis=-1, keepdims=True)
    mean_two = jnp.mean(scaled * hat, axis=-1, keepdims=True)
    d_rows = inv * (scaled - mean_one - hat * mean_two)
    return d_rows, jnp.sum(grad * hat, axis=0, keepdims=True), jnp.sum(grad, axis=0, keepdims=True)


def table_selector(shape):
    row = lax.broadcasted_iota(jnp.int32, shape, 0)
    col = lax.broadcasted_iota(jnp.int32, shape, 1)
    up_row = 6 * (col >> 2) + 2 + (col & 3)
    hit = (col < B) & (row == up_row)
    hit = hit | ((col >= 128) & (col < 152) & (row == 6 * (col - 128)))
    hit = hit | ((col >= 152) & (col < 176) & (row == 6 * (col - 152) + 1))
    return hit.astype(F32)


def flat_rows(ref):
    x_zero, x_one, x_two = [ref[pl.ds(m, 24, stride=3), :] for m in range(3)]
    lane = lanes_of((24, 128))
    x_half = pltpu.roll(x_two, 64, 1)
    return (
        x_zero,
        jnp.where(lane < 32, pltpu.roll(x_zero, 32, 1), pltpu.roll(x_one, 32, 1)),
        jnp.where(lane < 64, pltpu.roll(x_one, 64, 1), x_half),
        pltpu.roll(x_two, 96, 1),
    )


def flat_to_square(ref, place):
    for m, rows in enumerate(flat_rows(ref)):
        place[pl.ds(m, 24, stride=4), :] = rows
    return place[...][:, :B]


def split_rows(square, place):
    place[:, 0:B] = square
    return jnp.concatenate([place[pl.ds(m, 24, stride=4), :] for m in range(4)], axis=0)[:, :B]


def store_flat(ref, stacked):
    lane = lanes_of((24, 128))
    wide = jnp.concatenate([stacked, jnp.zeros((B, 128 - B), F32)], axis=1)
    m_zero, m_one, m_two, m_three = [wide[24 * m : 24 * m + 24] for m in range(4)]
    one_back = pltpu.roll(m_one, 96, 1)
    two_back = pltpu.roll(m_two, 64, 1)
    ref[pl.ds(0, 24, stride=3), :] = jnp.where(lane < 96, m_zero, one_back)
    ref[pl.ds(1, 24, stride=3), :] = jnp.where(lane < 64, one_back, two_back)
    ref[pl.ds(2, 24, stride=3), :] = jnp.where(lane < 32, two_back, pltpu.roll(m_three, 32, 1))


def train_kernel(
    n_y,
    x_hbm,
    ct_hbm,
    seg_ref,
    long_ref,
    w_hbm,
    lr_hbm,
    rr_hbm,
    split_ref,
    shared_ref,
    bo_hbm,
    ig_hbm,
    gf_hbm,
    lf_hbm,
    rf_hbm,
    pf_hbm,
    sg_ref,
    nm_ref,
    wt,
    a_all,
    c_all,
    q_all,
    k_all,
    v_all,
    v_tr,
    o_all,
    lse_all,
    z_all,
    gp_all,
    res,
    y_own,
    y_all,
    g_all,
    du_all,
    dx_all,
    dk_acc,
    dv_acc,
    stage,
    core_in,
    x_in,
    side_in,
    dw,
    rs_one,
    rs_two,
    place,
    flat,
    g_acc,
    kid_col,
    kid_row,
    vecs,
    bias_row,
    gvecs,
    gbias,
    sib_in,
    msg_in,
    gmsg_out,
    nb_out,
    nb_in,
    nd_in,
    g_s,
    g_r,
    c_s,
    c_r,
    x_s,
    x_r,
    a_s,
    a_r,
    p_s,
    p_r,
    t_s,
    t_r,
    load_sem,
    land_sem,
    ct_sem,
    y_s,
    y_r,
    out_sem,
    far_s,
    far_r,
    gout_sem,
    root_sem,
    m_s,
    m_r,
    gm_s,
    gm_r,
    sib_s,
    sib_r,
    nb_s,
    nb_r,
    nd_s,
    nd_r,
):
    n_dp = GROUPS
    n_z = n_dp // n_y
    me = lax.axis_index("dp")
    ten = lax.axis_index("tensor")
    my_z, my_y = me // n_y, lax.rem(me, n_y)
    my_x, my_c = ten // 2, lax.rem(ten, 2)
    other_c = 1 - my_c
    sibling = (me, 2 * my_x + other_c)
    across = (me, 2 * (1 - my_x) + my_c)
    scale = 1.0 / math.sqrt(HD)

    def dp_dev(index):
        return (index, ten)

    def z_peer(step):
        return lax.rem(my_z + step, n_z)

    def remote(src, dst, send, recv, dev):
        return pltpu.make_async_remote_copy(
            src_ref=src, dst_ref=dst, send_sem=send, recv_sem=recv, device_id=dev, device_id_type=MESH
        )

    def at(cond, func):
        @pl.when(cond)
        def _():
            func()

    def load_rows(j, which):
        half = my_c if which == 0 else other_c
        return pltpu.make_async_copy(x_hbm.at[j, half], res.at[which, j], load_sem.at[which, j])

    def load_blocks(l):
        return pltpu.make_async_copy(
            w_hbm.at[l], flat.at[pl.ds(l * GROUP, GROUP)], land_sem.at[l]
        )

    def load_cot(j):
        return pltpu.make_async_copy(ct_hbm.at[j, my_c], y_own.at[j], ct_sem.at[j])

    for l in range(LAYERS):
        load_blocks(l).start()
    for j in range(CHUNKS):
        load_rows(j, 0).start()
        load_rows(j, 1).start()
    for j in range(CHUNKS):
        load_cot(j).start()

    barrier = pltpu.get_barrier_semaphore()
    for step in range(1, n_dp):
        pl.semaphore_signal(
            barrier, inc=1, device_id=dp_dev(lax.rem(me + step, n_dp)), device_id_type=MESH
        )
    pl.semaphore_signal(barrier, inc=1, device_id=sibling, device_id_type=MESH)
    pl.semaphore_signal(barrier, inc=1, device_id=across, device_id_type=MESH)

    sel = table_selector((144, 256))
    for l in range(LAYERS):
        row = lax.dot_general(
            jnp.broadcast_to(split_ref[l], (8, 144)),
            sel,
            (((1,), (0,)), ((), ())),
            precision=highest,
            preferred_element_type=F32,
        )
        msg_in[me, 8 * l : 8 * l + 8, :] = row
        for r in range(6):
            msg_in[me, 8 * l + r : 8 * l + r + 1, 0:B] = shared_ref[r, l : l + 1, :]

    pl.semaphore_wait(barrier, n_dp + 1)

    def msg_copy(step):
        return remote(
            msg_in.at[me], msg_in.at[me], m_s.at[step - 1], m_r.at[me],
            dp_dev(lax.rem(me + step, n_dp)),
        )

    def msg_from(step):
        src = lax.rem(me + step, n_dp)
        return remote(msg_in.at[src], msg_in.at[src], m_s.at[step - 1], m_r.at[src], dp_dev(src))

    for step in range(1, n_dp):
        msg_copy(step).start()

    def gather_send(l, p, slab, k, dev):
        return remote(
            wt.at[l, p, slab], wt.at[l, p, slab], g_s.at[l, p, k], g_r.at[l, p, slab], dp_dev(dev)
        )

    def y_peers():
        return [my_z * n_y + lax.rem(my_y + s, n_y) for s in range(1, n_y)]

    def own_send(l, p):
        @pl.when(my_z < n_z - 1)
        def _():
            gather_send(l, p, me, 0, me + n_y).start()

        @pl.when(my_z > 0)
        def _():
            gather_send(l, p, me, 1, me - n_y).start()

    def own_beside(l, p):
        gather_send(l, p, me, 2, y_peers()[0]).start()

    def wave(l, p, hop):
        @pl.when(my_z >= hop)
        def _():
            slab = me - hop * n_y
            gather_send(l, p, slab, 0, slab).wait_recv()

            @pl.when(my_z < n_z - 1)
            def _():
                gather_send(l, p, slab, 2 + hop, me + n_y).start()

            gather_send(l, p, slab, n_z + 1 + hop, y_peers()[0]).start()

        @pl.when(my_z + hop < n_z)
        def _():
            slab = me + hop * n_y
            gather_send(l, p, slab, 0, slab).wait_recv()

            @pl.when(my_z > 0)
            def _():
                gather_send(l, p, slab, 2 * n_z + hop, me - n_y).start()

            gather_send(l, p, slab, 3 * n_z - 1 + hop, y_peers()[0]).start()

    def gather_finish(l, p):
        for s in range(0, n_z):
            slab = z_peer(s) * n_y + lax.rem(my_y + 1, n_y)
            gather_send(l, p, slab, 0, slab).wait_recv()

    def gather_drain(l, p):
        def sent(k):
            gather_send(l, p, me, k, me).wait_send()

        up, down = my_z < n_z - 1, my_z > 0
        at(up, lambda: sent(0))
        at(down, lambda: sent(1))
        sent(2)
        for hop in range(1, n_z):
            low, high = my_z >= hop, my_z + hop < n_z
            at(jnp.logical_and(low, up), lambda: sent(2 + hop))
            at(low, lambda: sent(n_z + 1 + hop))
            at(jnp.logical_and(high, down), lambda: sent(2 * n_z + hop))
            at(high, lambda: sent(3 * n_z - 1 + hop))

    def relayout(l, p):
        cols = []
        for b in range(8):
            blk = PARTS[p][b]
            square = flat_to_square(flat.at[l * GROUP + blk], place.at[b % 6])
            cols.append(jnp.transpose(square) if blk in TRANSPOSED[p] else square)
        wt[l, p, me] = jnp.concatenate(cols, axis=1).astype(BF16)

    def relayout_layer(l, carry):
        load_blocks(l).wait()
        for p in range(3):
            relayout(l, p)
            if p < 2:

                @pl.when(l == 0)
                def _():
                    if p == 0:
                        own_send(0, 0)
                    own_beside(0, p)

        return carry

    lax.fori_loop(0, LAYERS, relayout_layer, 0)

    seq_shift = jnp.where(long_ref[0, 0] > 0, 0, 1)
    seg = seg_ref[...]
    pos = lax.broadcasted_iota(jnp.int32, (8, 128), 0) * 128 + lax.broadcasted_iota(
        jnp.int32, (8, 128), 1
    )
    seq = (pos >> 8) * seq_shift
    kid = jnp.where(seg >= 0, seq * 64 + seg, -1 - seq).astype(F32)
    for r in range(8):
        kid_row[r // 2, 0:1, 128 * (r % 2) : 128 * (r % 2) + 128] = kid[r : r + 1, :]
        kid_col[r] = jnp.transpose(
            jnp.broadcast_to(kid[r : r + 1, :], (128, 128))
        )

    gvecs[...] = jnp.zeros_like(gvecs)
    gbias[...] = jnp.zeros_like(gbias)

    for step in range(1, n_dp):
        msg_from(step).wait_recv()
    for l in range(LAYERS):
        vecs[l] = jnp.concatenate(
            [msg_in[s, 8 * l : 8 * l + 8, 0:B] for s in range(n_dp)], axis=1
        )
        rows = [msg_in[s, 8 * l : 8 * l + 8, 128:256] for s in range(n_dp)]
        pad = jnp.zeros((8, D // 4), F32)
        bias_row[l] = jnp.concatenate(
            [r[:, 0:24] for r in rows]
            + [pad]
            + [r[:, 24:48] for r in rows]
            + [jnp.zeros((8, 64), F32)],
            axis=1,
        )

    low_half = lanes_of((CHUNK, 128)) < 64

    def vec(l, k):
        return vecs[l, k : k + 1, :]

    def core_copy(j):
        return remote(stage.at[j, other_c], core_in.at[j], c_s.at[j], c_r.at[j], sibling)

    def x_copy(j, par):
        if par == 2:
            return remote(stage.at[j, my_c], side_in.at[j], x_s.at[2, j], x_r.at[2, j], across)
        return remote(stage.at[j, my_c], x_in.at[par, j], x_s.at[par, j], x_r.at[par, j], across)

    def own_copy(ref, j):
        return remote(ref.at[j, my_c], ref.at[j, my_c], a_s.at[j], a_r.at[j], sibling)

    def send_partial(j, value):
        stage[j] = value.astype(BF16).reshape(2, HALF, D)
        core_copy(j).start()

    def pass_on(j, par):
        core_copy(j).wait()
        mine = stage[j, my_c].astype(F32) + core_in[j].astype(F32)
        stage[j, my_c] = mine.astype(BF16)
        x_copy(j, par).start()

    def total(j, par):
        x_copy(j, par).wait()
        came = side_in[j] if par == 2 else x_in[par, j]
        return stage[j, my_c].astype(F32) + came.astype(F32)

    def project(l, j):
        rows = a_all[l, j].reshape(CHUNK, D)
        weight = wt[l, 0].reshape(D, D)[:, 0:640]
        out = dot_nn(rows, weight) + bias_row[l, 0:1, :]
        tiles = [out[:, 128 * t : 128 * t + 128] for t in range(5)]
        q_roll = pltpu.roll(tiles[0], 64, 1)
        v_roll = pltpu.roll(tiles[3], 64, 1)
        zero = jnp.zeros((CHUNK, 128), F32)
        q_val = [
            jnp.where(low_half, zero, q_roll),
            jnp.where(low_half, q_roll, pltpu.roll(tiles[1], 64, 1)),
        ]
        k_val = [jnp.where(low_half, zero, tiles[1]), tiles[2]]
        v_val = [
            jnp.where(low_half, zero, v_roll),
            jnp.where(low_half, v_roll, pltpu.roll(tiles[4], 64, 1)),
        ]
        q_all[l, j] = jnp.concatenate(q_val, axis=1).astype(BF16)
        k_all[l, j] = jnp.concatenate(k_val, axis=1).astype(BF16)
        v_mat = jnp.concatenate(v_val, axis=1)
        v_all[l, j] = v_mat.astype(BF16)
        v_tr[:, pl.ds(pl.multiple_of(j * CHUNK, CHUNK), CHUNK)] = jnp.transpose(v_mat).astype(BF16)

    def head_tile(mat, h):
        if h == 0:
            return mat[:, 0:128]
        keep = low_half if h == 1 else jnp.logical_not(low_half)
        return jnp.where(keep, mat[:, 128:256], jnp.zeros((), mat.dtype))

    def tile_of(ref, l, h):
        full = ref[l].reshape(ROWS, 256)
        return full[:, 0:128] if h == 0 else full[:, 128:256]

    def allowed_of(j):
        col = kid_col[...].reshape(ROWS, 128)
        return jnp.concatenate([col, col], axis=1) == kid_row[j, 0:1, :]

    def attend_chunk(l, j):
        allowed = allowed_of(j)
        q_mat = q_all[l, j]
        outs = [jnp.zeros((64, CHUNK), F32)]
        for h in range(HEADS_DEV):
            scores = dot_nt(tile_of(k_all, l, h), head_tile(q_mat, h)) * scale
            scores = jnp.where(allowed, scores, big_negative)
            top = jnp.max(scores, axis=0, keepdims=True)
            expo = jnp.exp(scores - top)
            tot = jnp.sum(expo, axis=0, keepdims=True)
            lse_all[l, j, h : h + 1, :] = top + jnp.log(tot)
            out = dot_nn(v_tr[64 + 64 * h : 128 + 64 * h, :], expo.astype(BF16))
            outs.append(out / tot)
        o_mat = jnp.transpose(jnp.concatenate(outs, axis=0)).astype(BF16)
        o_all[l, j] = o_mat
        send_partial(j, dot_nt(o_mat, wt[l, 0].reshape(D, D)[:, 512:768]))

    def middle(l, j):
        mid = res[2 * l, j] + total(j, 0) + vec(l, 4)
        res[2 * l + 1, j] = mid
        hat, _ = norm_rows(mid)
        c_all[l, j, my_c] = (hat * vec(l, 2) + vec(l, 3)).astype(BF16)
        own_copy(c_all.at[l], j).start()

    def mlp(l, j):
        own_copy(c_all.at[l], j).wait()
        rows = c_all[l, j].reshape(CHUNK, D)
        pre = dot_nn(rows, wt[l, 1].reshape(D, D)) + vec(l, 6)
        cdf = 0.5 * (1.0 + lax.erf(pre * (1.0 / math.sqrt(2.0))))
        pdf = jnp.exp(-0.5 * pre * pre) * (1.0 / math.sqrt(2.0 * math.pi))
        act = (pre * cdf).astype(BF16)
        z_all[l, j] = act
        gp_all[l, j] = (cdf + pre * pdf).astype(BF16)

        @pl.when(l < LAYERS - 1)
        def _():
            at(j == 0, lambda: gather_finish(0, 2))
            send_partial(j, dot_nt(z_all[l, j], wt[l, 2].reshape(D, D)))

        @pl.when(l == LAYERS - 1)
        def _():
            y_copy(j).wait()
            mlp_back(LAYERS - 1, j)

    def y_copy(j):
        return remote(y_all.at[j, my_c], y_all.at[j, my_c], y_s.at[j], y_r.at[j], sibling)

    def near_copy(ref, hbm, which, j):
        return pltpu.make_async_copy(ref.at[j], hbm.at[j, my_c], out_sem.at[which, j])

    def far_copy(ref, hbm, which, j):
        return remote(ref.at[j], hbm.at[j, my_c], far_s.at[which, j], far_r.at[which, j], sibling)

    def layer_end(l, j):
        new = res[2 * l + 1, j] + total(j, 1) + vec(l, 5)
        res[2 * l + 2, j] = new
        hat, _ = norm_rows(new)
        a_all[l + 1, j, my_c] = (hat * vec(l + 1, 0) + vec(l + 1, 1)).astype(BF16)
        own_copy(a_all.at[l + 1], j).start()

    def last_send(slot, j):
        send_partial(slot, dot_nt(z_all[LAYERS - 1, j], wt[LAYERS - 1, 2].reshape(D, D)))

    def last_end(slot, j):
        last = res.at[2 * LAYERS - 1]
        last[j] = last[j] + total(slot, 2) + vec(LAYERS - 1, 5)
        near_copy(last, bo_hbm, 0, j).start()
        far_copy(last, bo_hbm, 0, j).start()

    def when_chunk(tick, offset, func):
        @pl.when(jnp.logical_and(tick >= offset, tick < offset + CHUNKS))
        def _():
            func(tick - offset)

    def add_vec(l, k, value):
        gvecs[l, k : k + 1, :] += value

    def mlp_back(l, j):
        d_act = dot_nn(y_all[j].reshape(CHUNK, D), wt[l, 2].reshape(D, D))
        d_pre = (d_act * gp_all[l, j].astype(F32)).astype(BF16)
        du_all[j] = d_pre
        add_vec(l, 6, jnp.sum(d_pre.astype(F32), axis=0, keepdims=True))
        send_partial(j, dot_nt(du_all[j], wt[l, 1].reshape(D, D)))

    def middle_back(l, j):
        grad = total(j, 1)
        d_rows, d_gain, d_shift = norm_back(grad, res[2 * l + 1, j], vec(l, 2))
        y_rows = y_own[j]
        add_vec(l, 5, jnp.sum(y_rows, axis=0, keepdims=True))
        g_rows = y_rows + d_rows
        add_vec(l, 2, d_gain)
        add_vec(l, 3, d_shift)
        add_vec(l, 4, jnp.sum(g_rows, axis=0, keepdims=True))
        y_own[j] = g_rows
        g_all[j, my_c] = g_rows.astype(BF16)
        own_copy(g_all, j).start()

    def attend_back(l, j):
        own_copy(g_all, j).wait()
        d_out = dot_nn(g_all[j].reshape(CHUNK, D), wt[l, 0].reshape(D, D)[:, 512:768])
        do_mat = d_out.astype(BF16)
        prod = jnp.transpose(do_mat.astype(F32) * o_all[l, j].astype(F32))
        allowed = allowed_of(j)
        q_mat = q_all[l, j]
        dq_parts = []
        for h in range(HEADS_DEV):
            q_h = head_tile(q_mat, h)
            do_h = head_tile(do_mat, h)
            scores = dot_nt(tile_of(k_all, l, h), q_h) * scale
            scores = jnp.where(allowed, scores, big_negative)
            probs = jnp.exp(scores - lse_all[l, j, h : h + 1, :])
            delta = jnp.sum(prod[64 + 64 * h : 128 + 64 * h, :], axis=0, keepdims=True)
            d_probs = dot_nt(tile_of(v_all, l, h), do_h)
            d_scores = (probs * (d_probs - delta)).astype(BF16)
            t = 0 if h == 0 else 128
            dv_acc[:, t : t + 128] += dot_nn(probs.astype(BF16), do_h)
            dk_acc[:, t : t + 128] += dot_nn(d_scores, q_h)
            dq_parts.append(dot_nn(v_tr[64 + 64 * h : 128 + 64 * h, :], d_scores))
        dq_parts.append(jnp.zeros((64, CHUNK), F32))
        dq_mat = jnp.transpose(jnp.concatenate(dq_parts, axis=0) * scale)
        dx_all[j, :, 0:256] = dq_mat.astype(BF16)

    def project_back(l, j):
        rows = pl.ds(pl.multiple_of(j * CHUNK, CHUNK), CHUNK)
        dk_mat = dk_acc[rows, :] * scale
        dv_mat = dv_acc[rows, :]
        zero = jnp.zeros((CHUNK, 128), F32)
        roll_zero = pltpu.roll(dv_mat[:, 0:128], 64, 1)
        roll_one = pltpu.roll(dv_mat[:, 128:256], 64, 1)
        tile_one = jnp.where(low_half, dx_all[j, :, 128:256].astype(F32), dk_mat[:, 0:128])
        dx_all[j, :, 128:640] = jnp.concatenate(
            [
                tile_one,
                dk_mat[:, 128:256],
                jnp.where(low_half, roll_zero, roll_one),
                jnp.where(low_half, roll_one, zero),
            ],
            axis=1,
        ).astype(BF16)
        dx_mat = dx_all[j]
        gbias[l, 0:1, :] += jnp.sum(dx_mat.astype(F32), axis=0, keepdims=True)
        send_partial(j, dot_nt(dx_mat, wt[l, 0].reshape(D, D)[:, 0:640]))

    def layer_begin(l, j):
        grad = total(j, 0)
        d_rows, d_gain, d_shift = norm_back(grad, res[2 * l, j], vec(l, 0))
        add_vec(l, 0, d_gain)
        add_vec(l, 1, d_shift)
        new = y_own[j] + d_rows
        y_own[j] = new

        @pl.when(l > 0)
        def _():
            y_all[j, my_c] = new.astype(BF16)
            own_copy(y_all, j).start()

        @pl.when(l == 0)
        def _():
            near_copy(y_own, ig_hbm, 1, j).start()
            far_copy(y_own, ig_hbm, 1, j).start()

    def slab(ref, p, owner):
        return ref.at[p, pl.ds(pl.multiple_of(owner * B, B), B)]

    def pair_copy(l, p, z):
        dest = y_peers()[0]
        return remote(
            slab(dw, p, z * n_y + lax.rem(my_y + 1, n_y)),
            rs_one.at[l, p, z],
            p_s.at[l, p, z],
            p_r.at[l, p, z],
            dp_dev(dest),
        )

    def line_copy(l, p, s):
        dest = z_peer(s)
        return remote(
            slab(dw, p, dest * n_y + my_y),
            rs_two.at[l, p, n_z - 1 - s],
            t_s.at[l, p, s - 1],
            t_r.at[l, p, n_z - 1 - s],
            dp_dev(dest * n_y + my_y),
        )

    def line_from(l, p, s):
        return remote(
            slab(dw, p, me),
            rs_two.at[l, p, s - 1],
            t_s.at[l, p, s - 1],
            t_r.at[l, p, s - 1],
            dp_dev(z_peer(s) * n_y + my_y),
        )

    def scatter_drain(l, p):
        for z in range(n_z):
            pair_copy(l, p, z).wait_send()
        for s in range(1, n_z):
            line_copy(l, p, s).wait_send()

    def scatter_begin(l, p):
        for s in list(range(1, n_z)) + [0]:
            pair_copy(l, p, z_peer(s)).start()

    def scatter_middle(l, p, steps=(1, 2, 3, 0)):
        for s in steps:
            z = z_peer(s)
            pair_copy(l, p, z).wait_recv()
            ref = slab(dw, p, z * n_y + my_y)
            both = (ref[...].astype(F32) + rs_one[l, p, z].astype(F32)).astype(BF16)
            if s:
                ref[...] = both
                line_copy(l, p, s).start()
            else:
                rs_one[l, p, my_z] = both

    def runs_of(p):
        return ((0, 0, 6), (6, 14, 2)) if p == 0 else ((0, PARTS[p][0], 8),)

    def block_copies(l, p):
        return [
            pltpu.make_async_copy(
                flat.at[pl.ds(16 + 8 * k + here, count)],
                hbm.at[l, pl.ds(there, count)],
                gout_sem.at[k, n],
            )
            for k, hbm in enumerate((gf_hbm, lf_hbm, rf_hbm, pf_hbm))
            for n, (here, there, count) in enumerate(runs_of(p))
        ]

    def root_copies(l, p):
        return [
            pltpu.make_async_copy(
                hbm.at[l, pl.ds(there, count)],
                flat.at[pl.ds(8 * k + here, count)],
                root_sem.at[k, n],
            )
            for k, hbm in enumerate((lr_hbm, rr_hbm))
            for n, (here, there, count) in enumerate(runs_of(p))
        ]

    def scatter_end(l, p):
        acc = rs_one[l, p, my_z].astype(F32)
        for s in range(1, n_z):
            line_from(l, p, s).wait_recv()
            acc = acc + rs_two[l, p, s - 1].astype(F32)
        nm_ref[0:1, 0:1] += jnp.sum(acc * acc, keepdims=True)
        g_acc[...] = acc

    def block_update(l, p):
        acc = g_acc[...]
        for copy in root_copies(l, p):
            copy.wait()
        if p < 2:
            for copy in block_copies(l, p + 1):
                copy.wait()
        else:
            @pl.when(l < LAYERS - 1)
            def _():
                for copy in block_copies(LAYERS - 1, 0):
                    copy.wait()

        for b in range(8):
            square = acc[:, B * b : B * b + B]
            turned = jnp.transpose(square)
            if PARTS[p][b] in TRANSPOSED[p]:
                square, turned = turned, square
            slot = 3 * (b % 2)
            low = square.astype(BF16)
            rows = split_rows(square, place.at[slot])
            cols = split_rows(turned, place.at[slot + 1])
            right = flat_to_square(flat.at[8 + b], place.at[slot + 2])
            left = jnp.concatenate(flat_rows(flat.at[b]), axis=0)[:, :B]
            store_flat(flat.at[16 + b], rows)
            store_flat(flat.at[24 + b], dot_nt(rows.astype(BF16), low))
            store_flat(flat.at[32 + b], dot_nn(cols.astype(BF16), low))
            half = dot_nn(left.astype(BF16), low).astype(BF16)
            store_flat(flat.at[40 + b], dot_nn(half, right.astype(BF16)))
        for copy in block_copies(l, p):
            copy.start()
        if p > 0:
            for copy in root_copies(l, p - 1):
                copy.start()
        else:
            @pl.when(l > 0)
            def _():
                for copy in root_copies(0, 2):
                    copy.start()

    nm_ref[...] = jnp.zeros_like(nm_ref)

    def weight_grad(l, p, func):
        at(l < LAYERS - 1, lambda: scatter_drain(LAYERS - 1, p))

        def piece(m, carry):
            cols = pl.ds(pl.multiple_of(m * 256, 256), 256)
            dw[p, cols, :] = func(cols).astype(BF16)
            return carry

        lax.fori_loop(0, D // 256, piece, 0)
        scatter_begin(l, p)

    def down_grad(l):
        def func(cols):
            return dot_tn(
                y_all[:, :, :, cols].reshape(ROWS, 256), z_all[l].reshape(ROWS, D)
            )

        weight_grad(l, 2, func)

    def up_grad(l):
        def func(cols):
            return dot_tn(
                c_all[l, :, :, :, cols].reshape(ROWS, 256), du_all[...].reshape(ROWS, D)
            )

        weight_grad(l, 1, func)

    def qkv_grad(l):
        def func(cols):
            first = dot_tn(
                a_all[l, :, :, :, cols].reshape(ROWS, 256), dx_all[...].reshape(ROWS, 640)
            )
            second = dot_tn(
                g_all[:, :, :, cols].reshape(ROWS, 256), o_all[l].reshape(ROWS, 256)
            )
            return jnp.concatenate(
                [first[:, 0:512], first[:, 512:640] + second[:, 0:128], second[:, 128:256]], axis=1
            )

        weight_grad(l, 0, func)

    def first_norm(j, carry):
        load_rows(j, 0).wait()
        load_rows(j, 1).wait()
        hat, _ = norm_rows(res[0, j])
        a_all[0, j, my_c] = (hat * vec(0, 0) + vec(0, 1)).astype(BF16)
        hat, _ = norm_rows(res[1, j])
        a_all[0, j, other_c] = (hat * vec(0, 0) + vec(0, 1)).astype(BF16)
        return carry

    def first_grad(j, carry):
        load_cot(j).wait()
        rows = jnp.where(kid_col[2 * j + my_c][:, 0:1] >= 0.0, y_own[j], 0.0)
        y_own[j] = rows
        y_all[j, my_c] = rows.astype(BF16)
        y_copy(j).start()
        return carry

    def first_project(j, carry):
        project(0, j)
        return carry

    for copy in root_copies(LAYERS - 1, 2):
        copy.start()
    wave(0, 0, 1)
    own_send(0, 1)
    own_beside(0, 2)
    lax.fori_loop(0, CHUNKS // 2, first_norm, 0)
    wave(0, 0, 2)
    lax.fori_loop(CHUNKS // 2, CHUNKS, first_norm, 0)
    wave(0, 0, 3)
    wave(0, 1, 1)
    lax.fori_loop(0, CHUNKS, first_grad, 0)
    own_send(0, 2)
    gather_finish(0, 0)
    wave(0, 1, 2)
    own_beside(1, 0)
    lax.fori_loop(0, CHUNKS, first_project, 0)

    def prepare_back(l):
        for j in range(CHUNKS):
            v_tr[:, j * CHUNK : j * CHUNK + CHUNK] = jnp.transpose(k_all[l, j].astype(F32)).astype(
                BF16
            )
        dk_acc[...] = jnp.zeros_like(dk_acc)
        dv_acc[...] = jnp.zeros_like(dv_acc)

    def forward_layer(l, carry):
        def step(tick, inner):
            when_chunk(tick, 1, lambda j: pass_on(j, 0))
            when_chunk(tick, 5, lambda j: pass_on(j, 1))

            when_chunk(tick, 3, lambda j: middle(l, j))

            @pl.when(l < LAYERS - 1)
            def _():
                when_chunk(tick, 7, lambda j: layer_end(0, j))

            @pl.when(l == 0)
            def _():
                @pl.when(tick == 1)
                def _():
                    wave(0, 1, 3)
                    wave(0, 2, 1)

                @pl.when(tick == 2)
                def _():
                    wave(0, 2, 2)
                    own_send(1, 0)
                    own_beside(1, 1)

                @pl.when(tick == 4)
                def _():
                    gather_finish(0, 1)
                    wave(0, 2, 3)
                    wave(1, 0, 1)

                @pl.when(tick == 5)
                def _():
                    wave(1, 0, 2)
                    own_send(1, 1)
                    own_beside(1, 2)

                @pl.when(tick == 6)
                def _():
                    wave(1, 0, 3)
                    wave(1, 1, 1)

                @pl.when(tick == 7)
                def _():
                    wave(1, 1, 2)
                    own_send(1, 2)

                @pl.when(tick == 8)
                def _():
                    gather_finish(1, 0)

                @pl.when(tick == 9)
                def _():
                    wave(1, 1, 3)
                    wave(1, 2, 1)

                @pl.when(tick == 10)
                def _():
                    wave(1, 2, 2)

                @pl.when(tick == 11)
                def _():
                    wave(1, 2, 3)

            @pl.when(l == 1)
            def _():
                @pl.when(tick == 4)
                def _():
                    gather_finish(1, 1)
                    gather_finish(1, 2)

            when_chunk(tick, 0, lambda j: attend_chunk(l, j))

            def next_project(j):
                own_copy(a_all.at[LAYERS - 1], j).wait()
                project(LAYERS - 1, j)

            when_chunk(tick, 4, lambda j: mlp(l, j))

            @pl.when(l == 0)
            def _():
                when_chunk(tick, 8, next_project)

            at(jnp.logical_and(l == LAYERS - 1, tick == 8), lambda: prepare_back(LAYERS - 1))
            return inner

        lax.fori_loop(0, 12, step, 0)
        return carry

    lax.fori_loop(0, LAYERS, forward_layer, 0)
    for step in range(1, n_dp):
        msg_copy(step).wait_send()

    def finish_part(l, p):
        scatter_end(l, p)
        block_update(l, p)

    def backward_layer(n, carry):
        l = LAYERS - 1 - n
        upper = l == LAYERS - 1
        lower = l < LAYERS - 1
        down_grad(l)

        @pl.when(lower)
        def _():
            scatter_middle(LAYERS - 1, 0)

        def step(tick, inner):
            at(tick == 1, lambda: last_send(0, 2 * n))

            @pl.when(tick == 2)
            def _():
                last_send(1, 2 * n + 1)
                pass_on(0, 2)

            at(tick == 3, lambda: pass_on(1, 2))
            middle_back(l, tick)
            at(tick == 2, lambda: up_grad(l))

            at(tick == 3, lambda: scatter_middle(l, 2))
            attend_back(l, tick)
            return inner

        lax.fori_loop(0, CHUNKS, step, 0)

        def step_two(tick, inner):
            when_chunk(tick, 1, lambda j: pass_on(j, 0))

            @pl.when(upper)
            def _():
                when_chunk(tick, 6, lambda j: pass_on(j, 1))

            when_chunk(tick, 4, lambda j: layer_begin(l, j))
            at(tick < 2, lambda: last_end(tick, 2 * n + tick))
            when_chunk(tick, 0, lambda j: project_back(l, j))
            at(tick == 3, lambda: qkv_grad(l))

            @pl.when(lower)
            def _():
                @pl.when(tick == 4)
                def _():
                    scatter_middle(0, 1)
                    finish_part(LAYERS - 1, 1)

                at(tick == 5, lambda: scatter_middle(0, 0, (1,)))
                at(tick == 6, lambda: scatter_middle(0, 0, (2,)))
                at(tick == 7, lambda: scatter_middle(0, 0, (3,)))

            def next_back(j):
                own_copy(y_all, j).wait()
                mlp_back(l - 1, j)

            @pl.when(upper)
            def _():
                at(tick == 4, lambda: prepare_back(l - 1))
                when_chunk(tick, 5, next_back)

            @pl.when(upper)
            def _():
                at(tick == 5, lambda: scatter_middle(l, 1))
                at(tick == 6, lambda: finish_part(l, 2))

            return inner

        lax.fori_loop(0, 10, step_two, 0)
        return carry

    lax.fori_loop(0, LAYERS, backward_layer, 0)

    sib = remote(gvecs, sib_in, sib_s.at[0], sib_r.at[0], sibling)
    sib.start()
    sib.wait()
    row_at = lax.broadcasted_iota(jnp.int32, (8, D), 0)
    for l in range(LAYERS):
        mat = gvecs[l] + jnp.where(row_at < 6, sib_in[l], 0.0)
        extra = gbias[l]
        for s in range(n_dp):
            gmsg_out[s, 8 * l : 8 * l + 8, 0:B] = mat[:, B * s : B * s + B]
            gmsg_out[s, 8 * l : 8 * l + 8, 128:152] = extra[:, 24 * s : 24 * s + 24]
            gmsg_out[s, 8 * l : 8 * l + 8, 152:176] = extra[:, 384 + 24 * s : 384 + 24 * s + 24]
            gmsg_out[s, 8 * l : 8 * l + 8, B:128] = jnp.zeros((8, 128 - B), F32)
            gmsg_out[s, 8 * l : 8 * l + 8, 176:256] = jnp.zeros((8, 80), F32)

    def gmsg_copy(step):
        dest = lax.rem(me + step, n_dp)
        return remote(
            gmsg_out.at[dest], msg_in.at[me], gm_s.at[step - 1], gm_r.at[me], dp_dev(dest)
        )

    def gmsg_from(step):
        src = lax.rem(me + step, n_dp)
        return remote(gmsg_out.at[src], msg_in.at[src], gm_s.at[step - 1], gm_r.at[src], dp_dev(src))

    for step in range(1, n_dp):
        gmsg_copy(step).start()
    msg_in[me] = gmsg_out[me]
    scatter_middle(0, 0, (0,))
    finish_part(LAYERS - 1, 0)
    finish_part(0, 2)
    finish_part(0, 1)
    for step in range(1, n_dp):
        gmsg_from(step).wait_recv()
    summed = msg_in[0]
    for s in range(1, n_dp):
        summed = summed + msg_in[s]
    sg_ref[...] = summed

    scatter_end(0, 0)
    squares = summed * summed
    lane = lanes_of((1, 128))
    packed = jnp.where(lane == 0, nm_ref[0:1, :], 0.0)
    shared_sums = jnp.zeros((1, 128), F32)
    for l in range(LAYERS):
        base = 8 * l
        up = jnp.sum(squares[base + 6 : base + 7, 0:B], keepdims=True)
        query = jnp.sum(squares[base : base + 1, 128:152], keepdims=True)
        value = jnp.sum(squares[base : base + 1, 152:176], keepdims=True)
        for k, item in enumerate((query, value, up)):
            packed = packed + jnp.where(lane == 1 + 3 * l + k, item, 0.0)
        for r in range(6):
            item = jnp.sum(squares[base + r : base + r + 1, 0:B], keepdims=True)
            shared_sums = shared_sums + jnp.where(lane == 6 * l + r, item, 0.0)

    for hop, dev in enumerate((sibling, across)):
        nb_out[hop] = jnp.broadcast_to(packed, (8, 128))
        swap = remote(nb_out.at[hop], nb_in.at[hop], nb_s.at[hop], nb_r.at[hop], dev)
        swap.start()
        swap.wait()
        packed = packed + nb_in[hop, 0:1, :]
    row8 = lax.broadcasted_iota(jnp.int32, (8, 128), 0)
    nd_in[me] = jnp.where(row8 == 0, packed, jnp.where(row8 == 1, shared_sums, 0.0))

    def nd_copy(step):
        dest = lax.rem(me + step, n_dp)
        return remote(nd_in.at[me], nd_in.at[me], nd_s.at[step - 1], nd_r.at[me], dp_dev(dest))

    def nd_from(step):
        src = lax.rem(me + step, n_dp)
        return remote(nd_in.at[src], nd_in.at[src], nd_s.at[step - 1], nd_r.at[src], dp_dev(src))

    for step in range(1, n_dp):
        nd_copy(step).start()
    block_update(0, 0)
    for step in range(1, n_dp):
        nd_from(step).wait_recv()
    acc = nd_in[0]
    for s in range(1, n_dp):
        acc = acc + nd_in[s]
    nm_ref[...] = acc

    for p in range(3):
        scatter_drain(0, p)
        for l in range(LAYERS):
            gather_drain(l, p)
    for copy in block_copies(0, 0):
        copy.wait()
    for step in range(1, n_dp):
        gmsg_copy(step).wait_send()
        nd_copy(step).wait_send()
    for j in range(CHUNKS):
        near_copy(res.at[2 * LAYERS - 1], bo_hbm, 0, j).wait()
        far_copy(res.at[2 * LAYERS - 1], bo_hbm, 0, j).wait()
        near_copy(y_own, ig_hbm, 1, j).wait()
        far_copy(y_own, ig_hbm, 1, j).wait()


def train_call(n_y, x_rows, ct_rows, seg, long_flag, blocks, left, right, split, shared):
    hbm = pl.BlockSpec(memory_space=pl.ANY)
    vmem = pl.BlockSpec(memory_space=pltpu.VMEM)
    smem = pl.BlockSpec(memory_space=pltpu.SMEM)
    dma = pltpu.SemaphoreType.DMA
    n_dp = GROUPS
    n_z = n_dp // n_y

    def buf(shape, dtype=BF16):
        return pltpu.VMEM(shape, dtype)

    scratch = [
        buf((LAYERS, 3, n_dp, B, D)),
        buf((LAYERS, CHUNKS, 2, HALF, D)),
        buf((LAYERS, CHUNKS, 2, HALF, D)),
        buf((LAYERS, CHUNKS, CHUNK, 256)),
        buf((LAYERS, CHUNKS, CHUNK, 256)),
        buf((LAYERS, CHUNKS, CHUNK, 256)),
        buf((256, ROWS)),
        buf((LAYERS, CHUNKS, CHUNK, 256)),
        buf((LAYERS, CHUNKS, 8, CHUNK), F32),
        buf((LAYERS, CHUNKS, CHUNK, D)),
        buf((LAYERS, CHUNKS, CHUNK, D)),
        buf((2 * LAYERS, CHUNKS, HALF, D), F32),
        buf((CHUNKS, HALF, D), F32),
        buf((CHUNKS, 2, HALF, D)),
        buf((CHUNKS, 2, HALF, D)),
        buf((CHUNKS, CHUNK, D)),
        buf((CHUNKS, CHUNK, 640)),
        buf((ROWS, 256), F32),
        buf((ROWS, 256), F32),
        buf((CHUNKS, 2, HALF, D)),
        buf((CHUNKS, HALF, D)),
        buf((2, CHUNKS, HALF, D)),
        buf((2, HALF, D)),
        buf((3, D, D)),
        buf((LAYERS, 3, n_z, B, D)),
        buf((LAYERS, 3, n_z - 1, B, D)),
        buf((6, B, 128), F32),
        buf((LAYERS * GROUP, 72, 128), F32),
        buf((B, D), F32),
        buf((8, HALF, 128), F32),
        buf((CHUNKS, 8, CHUNK), F32),
        buf((LAYERS, 8, D), F32),
        buf((LAYERS, 8, 640), F32),
        buf((LAYERS, 8, D), F32),
        buf((LAYERS, 8, 640), F32),
        buf((LAYERS, 8, D), F32),
        buf((n_dp, 16, 256), F32),
        buf((n_dp, 16, 256), F32),
        buf((2, 8, 128), F32),
        buf((2, 8, 128), F32),
        buf((n_dp, 8, 128), F32),
        dma((LAYERS, 3, 4 * n_z)),
        dma((LAYERS, 3, n_dp)),
        dma((CHUNKS,)),
        dma((CHUNKS,)),
        dma((3, CHUNKS)),
        dma((3, CHUNKS)),
        dma((CHUNKS,)),
        dma((CHUNKS,)),
        dma((LAYERS, 3, n_z)),
        dma((LAYERS, 3, n_z)),
        dma((LAYERS, 3, n_z - 1)),
        dma((LAYERS, 3, n_z - 1)),
        dma((2, CHUNKS)),
        dma((LAYERS,)),
        dma((CHUNKS,)),
        dma((CHUNKS,)),
        dma((CHUNKS,)),
        dma((2, CHUNKS)),
        dma((2, CHUNKS)),
        dma((2, CHUNKS)),
        dma((4, 2)),
        dma((2, 2)),
        dma((n_dp - 1,)),
        dma((n_dp,)),
        dma((n_dp - 1,)),
        dma((n_dp,)),
        dma((1,)),
        dma((1,)),
        dma((2,)),
        dma((2,)),
        dma((n_dp - 1,)),
        dma((n_dp,)),
    ]
    rows_shape = jax.ShapeDtypeStruct((CHUNKS, 2, HALF, D), F32)
    return pl.pallas_call(
        functools.partial(train_kernel, n_y),
        out_shape=(
            rows_shape,
            rows_shape,
            *[jax.ShapeDtypeStruct((LAYERS, GROUP, 72, 128), F32)] * 4,
            jax.ShapeDtypeStruct((16, 256), F32),
            jax.ShapeDtypeStruct((8, 128), F32),
        ),
        in_specs=[hbm, hbm, vmem, smem, hbm, hbm, hbm, vmem, vmem],
        out_specs=(hbm, hbm, hbm, hbm, hbm, hbm, vmem, vmem),
        scratch_shapes=scratch,
        compiler_params=pltpu.CompilerParams(
            collective_id=0, has_side_effects=True, vmem_limit_bytes=61 * 1024 * 1024
        ),
        cost_estimate=pl.CostEstimate(
            flops=30_000_000_000, bytes_accessed=30_000_000, transcendentals=20_000_000
        ),
        name="train",
    )(x_rows, ct_rows, seg, long_flag, blocks, left, right, split, shared)


def update_kernel(
    g_ref,
    lg_ref,
    rg_ref,
    p_ref,
    w_ref,
    l_ref,
    r_ref,
    sg_ref,
    nm_ref,
    sp_ref,
    sh_ref,
    bo_ref,
    ig_ref,
    gout_ref,
    nw_ref,
    nl_ref,
    nr_ref,
    sgo_ref,
    nsp_ref,
    shg_ref,
    nsh_ref,
    norm_ref,
    bo_out,
    ig_out,
):
    step_at = pl.program_id(0)
    bo_out[...] = bo_ref[...]
    ig_out[...] = ig_ref[...]
    lane = lanes_of((1, 128))
    row_zero = nm_ref[0:1, :]
    row_one = nm_ref[1:2, :]
    total_sq = jnp.sum(jnp.where(lane < 7, row_zero, 0.0), keepdims=True) + jnp.sum(
        jnp.where(lane < 12, row_one, 0.0), keepdims=True
    )
    norm = jnp.sqrt(total_sq)
    factor = clip_limit / jnp.maximum(norm, clip_limit)
    squared = factor * factor
    gram_weight = (1.0 - decay) * squared

    for b in range(g_ref.shape[0]):
        gout_ref[b] = g_ref[b] * factor
        nl_ref[b] = decay * l_ref[b] + gram_weight * lg_ref[b]
        nr_ref[b] = decay * r_ref[b] + gram_weight * rg_ref[b]
        direction = p_ref[b] * factor
        mean_sq = jnp.sum(direction * direction, keepdims=True) / (B * B)
        nw_ref[b] = w_ref[b] - direction * (rate_matrix * lax.rsqrt(mean_sq + eps_norm))

    @pl.when(step_at == 0)
    def _():
        norm_ref[...] = norm
        sel = table_selector((144, 256))
        col = lanes_of((1, 256))
        for l in range(LAYERS):
            sums = [row_zero[:, 1 + 3 * l + k : 2 + 3 * l + k] for k in range(3)]
            means = [sums[0] / D, sums[1] / D, sums[2] / FF]
            scales = [lax.rsqrt(squared * m + eps_norm) for m in means]
            src = sg_ref[8 * l : 8 * l + 8, :]
            line = jnp.where(col < 128, src[6:7, :], src[0:1, :]) * factor
            step = line * jnp.where(col < 128, scales[2], jnp.where(col < 152, scales[0], scales[1]))
            both = jnp.concatenate([line, step, jnp.zeros((6, 256), F32)], axis=0)
            table = lax.dot_general(
                both, sel, (((1,), (1,)), ((), ())), precision=highest, preferred_element_type=F32
            )
            sgo_ref[l] = table[0:1, :]
            nsp_ref[l] = sp_ref[l] - rate_vector * table[1:2, :]
            for r in range(6):
                mean = row_one[:, 6 * l + r : 6 * l + r + 1] / D
                grad = src[r : r + 1, 0:B] * factor
                shg_ref[r, l : l + 1, :] = grad
                nsh_ref[r, l : l + 1, :] = sh_ref[r, l : l + 1, :] - rate_vector * grad * lax.rsqrt(
                    squared * mean + eps_norm
                )


def update_call(grads, lefts, rights, dirs, weights, left, right, sums, norms, split, shared, outs):
    per = GROUP
    count = LAYERS * GROUP
    flat = pl.BlockSpec((per, 72, 128), lambda i: (i, 0, 0))
    rows = pl.BlockSpec((2 * HALF * CHUNKS * per // count, D), lambda i: (i, 0))

    def whole(shape):
        return pl.BlockSpec(shape, lambda i: (0,) * len(shape))

    flat_shape = jax.ShapeDtypeStruct((count, 72, 128), F32)
    split_shape, shared_shape = (LAYERS, 1, 144), (6, LAYERS, B)
    return pl.pallas_call(
        update_kernel,
        grid=(count // per,),
        out_shape=(
            *[flat_shape] * 4,
            *[jax.ShapeDtypeStruct(split_shape, F32)] * 2,
            *[jax.ShapeDtypeStruct(shared_shape, F32)] * 2,
            jax.ShapeDtypeStruct((1, 1), F32),
            *[jax.ShapeDtypeStruct(o.shape, F32) for o in outs],
        ),
        in_specs=[flat] * 7
        + [whole((16, 256)), whole((8, 128)), whole(split_shape), whole(shared_shape), rows, rows],
        out_specs=(
            *[flat] * 4,
            *[whole(split_shape)] * 2,
            *[whole(shared_shape)] * 2,
            whole((1, 1)),
            rows,
            rows,
        ),
        compiler_params=pltpu.CompilerParams(vmem_limit_bytes=60 * 1024 * 1024),
        name="update",
    )(grads, lefts, rights, dirs, weights, left, right, sums, norms, split, shared, *outs)


def fast_body(
    n_y,
    tokens_in,
    cotangent,
    segment_ids,
    long_seq,
    weights,
    left_stats,
    right_stats,
    left_roots,
    right_roots,
    split_params,
    shared_params,
):
    rows = (CHUNKS, 2, HALF, D)
    flat = (LAYERS, GROUP, 72, 128)
    blocks = (LAYERS * GROUP, 72, 128)
    split = split_params
    shared = jnp.transpose(shared_params, (1, 0, 2))
    out_rows, in_grad, grads, lefts, rights, dirs, sums, norms = train_call(
        n_y,
        tokens_in.reshape(rows),
        cotangent.reshape(rows),
        segment_ids.reshape(8, 128),
        long_seq.reshape(1, 1),
        weights.reshape(flat),
        left_roots.reshape(flat),
        right_roots.reshape(flat),
        split,
        shared,
    )
    res = update_call(
        *[m.reshape(blocks) for m in (grads, lefts, rights, dirs, weights, left_stats, right_stats)],
        sums,
        norms,
        split,
        shared,
        (out_rows.reshape(tokens_in.shape), in_grad.reshape(tokens_in.shape)),
    )
    mats = [r.reshape(weights.shape) for r in res[:4]]
    return (
        res[9],
        res[10],
        *mats,
        res[4],
        res[5],
        jnp.transpose(res[6], (1, 0, 2)),
        jnp.transpose(res[7], (1, 0, 2)),
        res[8].reshape(()),
    )


def solution(mesh):
    in_specs = (
        P("dp", None),
        P("dp", None),
        P("dp"),
        P("dp"),
        P(None, "dp", "tensor", None),
        P(None, "dp", "tensor", None),
        P(None, "dp", "tensor", None),
        P(None, "dp", "tensor", None),
        P(None, "dp", "tensor", None),
        P(None, "tensor", "dp"),
        P(None, None, "dp"),
    )
    out_specs = (
        P("dp", None),
        P("dp", None),
        P(None, "dp", "tensor", None),
        P(None, "dp", "tensor", None),
        P(None, "dp", "tensor", None),
        P(None, "dp", "tensor", None),
        P(None, "tensor", "dp"),
        P(None, "tensor", "dp"),
        P(None, None, "dp"),
        P(None, None, "dp"),
        P(),
    )
    plan = body
    if mesh.shape["dp"] == GROUPS and mesh.shape["tensor"] == 4:
        plan = functools.partial(fast_body, 2)
    return jax.shard_map(plan, mesh=mesh, in_specs=in_specs, out_specs=out_specs, check_vma=False)
```

```python
import functools
import math

import jax
import jax.numpy as jnp
from jax import lax
from jax.experimental import pallas as pl
from jax.experimental.pallas import tpu as pltpu
from jax.sharding import PartitionSpec as P

D = 768
HEADS = 12
FF = 3072
HD = 64
B = 96
LAYERS = 2
SEQ_SHORT = 256
SEQ_LONG = 1024


clip_limit = 100.0
rate_matrix = 0.06
rate_vector = 0.2
decay = 0.5
eps_norm = 1e-06
eps_layer = 1e-06
big_negative = -1e30
highest = lax.Precision.HIGHEST


def layer_norm(hidden, gain_vec, shift_vec):
    row_mean = jnp.mean(hidden, axis=-1, keepdims=True)
    centered = hidden - row_mean
    row_var = jnp.mean(centered * centered, axis=-1, keepdims=True)
    return centered * lax.rsqrt(row_var + eps_layer) * gain_vec + shift_vec


def gelu_exact(values):
    return jax.nn.gelu(values, approximate=False)


def matmul_low(left_mat, right_mat):
    return jnp.dot(left_mat, right_mat, preferred_element_type=jnp.float32)


def inner_rows(left_mat, right_mat):
    return lax.dot_general(
        left_mat, right_mat, (((0,), (0,)), ((), ())), preferred_element_type=jnp.float32
    )


def times_trans(left_mat, right_mat):
    return lax.dot_general(
        left_mat, right_mat, (((1,), (1,)), ((), ())), preferred_element_type=jnp.float32
    )


def unpack_layer(blocks, embed_dev, inner_dev):
    row_groups = blocks.shape[0]
    block_size = blocks.shape[2]
    qkv_count = 3 * embed_dev // block_size
    up_count = inner_dev // block_size
    out_count = embed_dev // block_size

    def by_rows(part_blocks):
        block_count = part_blocks.shape[1]
        return jnp.transpose(part_blocks, (0, 2, 1, 3)).reshape(
            row_groups * block_size, block_count * block_size
        )

    def by_cols(part_blocks):
        block_count = part_blocks.shape[1]
        return jnp.transpose(part_blocks, (1, 2, 0, 3)).reshape(
            block_count * block_size, row_groups * block_size
        )

    qkv_weight = by_rows(blocks[:, :qkv_count])
    up_weight = by_rows(blocks[:, qkv_count : qkv_count + up_count])
    out_weight = by_cols(blocks[:, qkv_count + up_count : qkv_count + up_count + out_count])
    down_weight = by_cols(blocks[:, qkv_count + up_count + out_count :])
    return (qkv_weight, out_weight, up_weight, down_weight)


def pack_layer(qkv_grad, out_grad, up_grad, down_grad, block_size):
    row_groups = qkv_grad.shape[0] // block_size

    def from_rows(matrix):
        block_count = matrix.shape[1] // block_size
        return jnp.transpose(
            matrix.reshape(row_groups, block_size, block_count, block_size), (0, 2, 1, 3)
        )

    def from_cols(matrix):
        block_count = matrix.shape[0] // block_size
        return jnp.transpose(
            matrix.reshape(block_count, block_size, row_groups, block_size), (2, 0, 1, 3)
        )

    return jnp.concatenate(
        [from_rows(qkv_grad), from_rows(up_grad), from_cols(out_grad), from_cols(down_grad)], axis=1
    )


def masked_scores(query_block, key_window, query_seq, key_seq, query_seg, key_seg, score_scale):
    scores = (
        jnp.einsum("qhd,khd->hqk", query_block, key_window, preferred_element_type=jnp.float32)
        * score_scale
    )
    allowed = (query_seq[:, None] == key_seq[None, :]) & (query_seg[:, None] == key_seg[None, :])
    return jnp.where(allowed[None], scores, big_negative)


def attention_forward(queries, keys_all, values_all, seq_index, segments, block_rows, score_scale):
    block_count = queries.shape[0] // block_rows

    def one_block(block_index):
        row_start = block_index * block_rows
        query_block = lax.dynamic_slice_in_dim(queries, row_start, block_rows, 0)
        scores = masked_scores(
            query_block,
            keys_all,
            lax.dynamic_slice_in_dim(seq_index, row_start, block_rows, 0),
            seq_index,
            lax.dynamic_slice_in_dim(segments, row_start, block_rows, 0),
            segments,
            score_scale,
        )
        row_max = jnp.max(scores, axis=-1, keepdims=True)
        exponent = jnp.exp(scores - row_max)
        row_total = jnp.sum(exponent, axis=-1, keepdims=True)
        attn_probs = (exponent / row_total).astype(jnp.bfloat16)
        attended = jnp.einsum(
            "hqk,khd->qhd", attn_probs, values_all, preferred_element_type=jnp.float32
        )
        return (attended, (row_max + jnp.log(row_total))[..., 0])

    return lax.map(one_block, jnp.arange(block_count, dtype=jnp.int32))


def attention_backward(
    queries, keys_all, values_all, grad_out, log_total, seq_index, segments, block_rows, score_scale
):
    token_count = queries.shape[0]
    block_count = token_count // block_rows
    zero_grad = jnp.zeros(keys_all.shape, jnp.float32)

    def one_block(carry_pair, block_index):
        key_grad, value_grad = carry_pair
        row_start = block_index * block_rows
        query_block = lax.dynamic_slice_in_dim(queries, row_start, block_rows, 0)
        out_block = lax.dynamic_slice_in_dim(grad_out, row_start, block_rows, 0)
        scores = masked_scores(
            query_block,
            keys_all,
            lax.dynamic_slice_in_dim(seq_index, row_start, block_rows, 0),
            seq_index,
            lax.dynamic_slice_in_dim(segments, row_start, block_rows, 0),
            segments,
            score_scale,
        )
        lse_block = lax.dynamic_index_in_dim(log_total, block_index, 0, keepdims=False)
        attn_probs = jnp.exp(scores - lse_block[..., None])
        prob_grad = jnp.einsum(
            "qhd,khd->hqk", out_block, values_all, preferred_element_type=jnp.float32
        )
        row_delta = jnp.sum(attn_probs * prob_grad, axis=-1, keepdims=True)
        score_grad = (attn_probs * (prob_grad - row_delta)).astype(jnp.bfloat16)
        query_grad = (
            jnp.einsum("hqk,khd->qhd", score_grad, keys_all, preferred_element_type=jnp.float32)
            * score_scale
        )
        key_part = (
            jnp.einsum("hqk,qhd->khd", score_grad, query_block, preferred_element_type=jnp.float32)
            * score_scale
        )
        value_part = jnp.einsum(
            "hqk,qhd->khd",
            attn_probs.astype(jnp.bfloat16),
            out_block,
            preferred_element_type=jnp.float32,
        )
        key_grad = key_grad + key_part
        value_grad = value_grad + value_part
        return ((key_grad, value_grad), query_grad)

    (key_grad, value_grad), query_grad = lax.scan(
        one_block, (zero_grad, zero_grad), jnp.arange(block_count, dtype=jnp.int32)
    )
    return (query_grad.reshape(keys_all.shape), key_grad, value_grad)


def body(
    tokens_in,
    cotangent,
    segment_ids,
    long_seq,
    weights,
    left_stats,
    right_stats,
    left_roots,
    right_roots,
    split_params,
    shared_params,
):
    full_weights, full_split, full_shared = (
        lax.all_gather(weights, "dp", axis=1, tiled=True),
        lax.all_gather(split_params, "dp", axis=2, tiled=True),
        lax.all_gather(shared_params, "dp", axis=2, tiled=True),
    )
    tensor_count = lax.axis_size("tensor")
    embed_dev = D // tensor_count
    inner_dev = FF // tensor_count
    heads_local = HEADS // tensor_count
    token_count = tokens_in.shape[0]
    window = SEQ_LONG
    block_rows = min(512, window)
    score_scale = 1.0 / math.sqrt(HD)
    seq_length = jnp.where(long_seq[0] > 0, SEQ_LONG, SEQ_SHORT)
    positions = jnp.arange(token_count, dtype=jnp.int32)
    seq_index = positions // seq_length
    valid_rows = (segment_ids >= 0).astype(jnp.float32)
    matrices = []
    for layer_index in range(LAYERS):
        blocks = full_weights[layer_index, :, 0].astype(jnp.bfloat16).reshape(D // B, -1, B, B)
        matrices.append(unpack_layer(blocks, embed_dev, inner_dev))
    hidden_state = tokens_in
    kept_state = []
    for layer_index in range(LAYERS):
        qkv_weight, out_weight, up_weight, down_weight = matrices[layer_index]
        shared = full_shared[layer_index]
        bias_table = full_split[layer_index, 0].reshape(embed_dev, 6)
        up_bias = bias_table[:, 2:].reshape(inner_dev)
        normed = layer_norm(hidden_state, shared[0], shared[1]).astype(jnp.bfloat16)
        qkv_bias = jnp.concatenate(
            [bias_table[:, 0], jnp.zeros((embed_dev,), jnp.float32), bias_table[:, 1]]
        )
        projected = (matmul_low(normed, qkv_weight) + qkv_bias).astype(jnp.bfloat16)
        queries = projected[:, :embed_dev].reshape(token_count, heads_local, HD)
        keys_all = projected[:, embed_dev : 2 * embed_dev].reshape(token_count, heads_local, HD)
        values_all = projected[:, 2 * embed_dev :].reshape(token_count, heads_local, HD)
        attended, log_total = attention_forward(
            queries, keys_all, values_all, seq_index, segment_ids, block_rows, score_scale
        )
        attended = attended.reshape(token_count, embed_dev).astype(jnp.bfloat16)
        attn_branch = lax.psum(
            matmul_low(attended, out_weight).astype(jnp.bfloat16), "tensor"
        ).astype(jnp.float32)
        middle = hidden_state + attn_branch + shared[4]
        normed_mid = layer_norm(middle, shared[2], shared[3]).astype(jnp.bfloat16)
        pre_act = matmul_low(normed_mid, up_weight) + up_bias
        activation = gelu_exact(pre_act).astype(jnp.bfloat16)
        mlp_branch = lax.psum(
            matmul_low(activation, down_weight).astype(jnp.bfloat16), "tensor"
        ).astype(jnp.float32)
        kept_state.append(
            (
                hidden_state,
                normed,
                queries,
                keys_all,
                values_all,
                attended,
                log_total,
                middle,
                normed_mid,
                pre_act,
                activation,
            )
        )
        hidden_state = middle + mlp_branch + shared[5]
    grad_state = cotangent * valid_rows[:, None]
    layer_grads = [None] * LAYERS
    for layer_index in reversed(range(LAYERS)):
        (
            hidden_in,
            normed,
            queries,
            keys_all,
            values_all,
            attended,
            log_total,
            middle,
            normed_mid,
            pre_act,
            activation,
        ) = kept_state[layer_index]
        qkv_weight, out_weight, up_weight, down_weight = matrices[layer_index]
        shared = full_shared[layer_index]
        down_bias_grad = jnp.sum(grad_state, axis=0)
        grad_low = grad_state.astype(jnp.bfloat16)
        down_grad = inner_rows(activation, grad_low)
        act_grad = times_trans(grad_low, down_weight)
        gelu_pull = jax.vjp(gelu_exact, pre_act)[1]
        pre_grad = gelu_pull(act_grad)[0].astype(jnp.bfloat16)
        up_bias_grad = jnp.sum(pre_grad, axis=0, dtype=jnp.float32)
        up_grad = inner_rows(normed_mid, pre_grad)
        normed_mid_grad = lax.psum(times_trans(pre_grad, up_weight), "tensor")
        norm_pull = jax.vjp(layer_norm, middle, shared[2], shared[3])[1]
        middle_ln, gain_two_grad, shift_two_grad = norm_pull(normed_mid_grad)
        middle_grad = grad_state + middle_ln
        out_bias_grad = jnp.sum(middle_grad, axis=0)
        middle_low = middle_grad.astype(jnp.bfloat16)
        out_grad = inner_rows(attended, middle_low)
        attended_grad = (
            times_trans(middle_low, out_weight)
            .astype(jnp.bfloat16)
            .reshape(token_count, heads_local, HD)
        )
        query_grad, key_grad, value_grad = attention_backward(
            queries,
            keys_all,
            values_all,
            attended_grad,
            log_total,
            seq_index,
            segment_ids,
            block_rows,
            score_scale,
        )
        proj_grad = jnp.concatenate(
            [
                query_grad.reshape(token_count, embed_dev),
                key_grad.reshape(token_count, embed_dev),
                value_grad.reshape(token_count, embed_dev),
            ],
            axis=1,
        ).astype(jnp.bfloat16)
        query_bias_grad = jnp.sum(proj_grad[:, :embed_dev], axis=0, dtype=jnp.float32)
        value_bias_grad = jnp.sum(proj_grad[:, 2 * embed_dev :], axis=0, dtype=jnp.float32)
        qkv_grad = inner_rows(normed, proj_grad)
        normed_grad = lax.psum(times_trans(proj_grad, qkv_weight), "tensor")
        input_pull = jax.vjp(layer_norm, hidden_in, shared[0], shared[1])[1]
        hidden_ln, gain_one_grad, shift_one_grad = input_pull(normed_grad)
        grad_state = middle_grad + hidden_ln
        block_grads = pack_layer(qkv_grad, out_grad, up_grad, down_grad, B).reshape(-1, 1, B * B)
        split_vec = jnp.concatenate(
            [
                query_bias_grad[:, None],
                value_bias_grad[:, None],
                up_bias_grad.reshape(embed_dev, 4),
            ],
            axis=1,
        ).reshape(1, -1)
        shared_vec = jnp.stack(
            [
                gain_one_grad,
                shift_one_grad,
                gain_two_grad,
                shift_two_grad,
                out_bias_grad,
                down_bias_grad,
            ]
        )
        layer_grads[layer_index] = (block_grads, split_vec, shared_vec)
    weight_grad, split_grad, shared_grad = (
        lax.psum_scatter(
            jnp.stack([entry[0] for entry in layer_grads]), "dp", scatter_dimension=1, tiled=True
        ),
        lax.psum_scatter(
            jnp.stack([entry[1] for entry in layer_grads]), "dp", scatter_dimension=2, tiled=True
        ),
        lax.psum_scatter(
            jnp.stack([entry[2] for entry in layer_grads]), "dp", scatter_dimension=2, tiled=True
        ),
    )
    dp_index = lax.axis_index("dp")
    lead_shard = (lax.axis_index("tensor") == 0).astype(jnp.float32)
    slice_len = split_grad.shape[-1]
    global_pos = dp_index * slice_len + jnp.arange(slice_len, dtype=jnp.int32)
    table_column = global_pos % 6
    segment_of = (table_column >= 1).astype(jnp.int32) + (table_column >= 2).astype(jnp.int32)
    selector = (segment_of[:, None] == jnp.arange(3, dtype=jnp.int32)[None, :]).astype(jnp.float32)
    split_sq = split_grad[:, 0] * split_grad[:, 0]
    split_rows = jnp.dot(split_sq, selector, precision=highest)
    shared_sq = shared_grad * shared_grad
    shared_rows = jnp.sum(shared_sq, axis=-1) * lead_shard
    local_total = (
        jnp.sum(weight_grad * weight_grad) + jnp.sum(split_sq) + lead_shard * jnp.sum(shared_sq)
    )
    total_sq, split_rows, shared_rows = lax.psum(
        (local_total, split_rows, shared_rows), ("dp", "tensor")
    )
    grad_norm = jnp.sqrt(total_sq)
    factor = clip_limit / jnp.maximum(grad_norm, clip_limit)
    squared = factor * factor
    block_shape = weight_grad.shape[:-1] + (B, B)
    left_mats = left_roots.reshape(block_shape)
    right_mats = right_roots.reshape(block_shape)
    clipped = weight_grad * factor
    clipped_mats = clipped.reshape(block_shape)
    new_left = decay * left_stats + (1.0 - decay) * jnp.einsum(
        "...ij,...kj->...ik", clipped_mats, clipped_mats, precision=highest
    ).reshape(left_stats.shape)
    new_right = decay * right_stats + (1.0 - decay) * jnp.einsum(
        "...ji,...jk->...ik", clipped_mats, clipped_mats, precision=highest
    ).reshape(right_stats.shape)
    partial_dir = jnp.einsum("...ij,...jk->...ik", left_mats, clipped_mats, precision=highest)
    direction = jnp.einsum("...ij,...jk->...ik", partial_dir, right_mats, precision=highest)
    mean_sq = jnp.mean(direction * direction, axis=(-2, -1), keepdims=True)
    step_mats = direction * lax.rsqrt(mean_sq + eps_norm)
    new_weights = weights - rate_matrix * step_mats.reshape(weights.shape)
    vector_sizes = jnp.array([D, D, FF], jnp.float32)
    split_mean = jnp.dot(split_rows / vector_sizes[None, :], selector.T, precision=highest)
    split_clip = split_grad * factor
    new_split = split_params - rate_vector * split_clip * lax.rsqrt(
        squared * split_mean[:, None, :] + eps_norm
    )
    shared_clip = shared_grad * factor
    shared_mean = shared_rows / D
    new_shared = shared_params - rate_vector * shared_clip * lax.rsqrt(
        squared * shared_mean[..., None] + eps_norm
    )
    return (
        hidden_state,
        grad_state,
        clipped,
        new_weights,
        new_left,
        new_right,
        split_clip,
        new_split,
        shared_clip,
        new_shared,
        grad_norm,
    )


F32 = jnp.float32
BF16 = jnp.bfloat16
MESH = pl.DeviceIdType.MESH
CHUNKS = 4
HALF = 128
CHUNK = 2 * HALF
ROWS = CHUNKS * CHUNK
HEADS_DEV = 3
GROUPS = D // B
GROUP = 24
PARTS = ((0, 1, 2, 3, 4, 5, 14, 15), tuple(range(6, 14)), tuple(range(16, 24)))
TRANSPOSED = (frozenset((14, 15)), frozenset(), frozenset(range(16, 24)))


def dot_nn(left_mat, right_mat):
    return lax.dot_general(left_mat, right_mat, (((1,), (0,)), ((), ())), preferred_element_type=F32)


def dot_nt(left_mat, right_mat):
    return lax.dot_general(left_mat, right_mat, (((1,), (1,)), ((), ())), preferred_element_type=F32)


def dot_tn(left_mat, right_mat):
    return lax.dot_general(left_mat, right_mat, (((0,), (0,)), ((), ())), preferred_element_type=F32)


def lanes_of(shape):
    return lax.broadcasted_iota(jnp.int32, shape, len(shape) - 1)


def norm_rows(rows):
    mean = jnp.mean(rows, axis=-1, keepdims=True)
    centered = rows - mean
    var = jnp.mean(centered * centered, axis=-1, keepdims=True)
    inv = lax.rsqrt(var + eps_layer)
    return centered * inv, inv


def norm_back(grad, rows, gain):
    hat, inv = norm_rows(rows)
    scaled = grad * gain
    mean_one = jnp.mean(scaled, axis=-1, keepdims=True)
    mean_two = jnp.mean(scaled * hat, axis=-1, keepdims=True)
    d_rows = inv * (scaled - mean_one - hat * mean_two)
    return d_rows, jnp.sum(grad * hat, axis=0, keepdims=True), jnp.sum(grad, axis=0, keepdims=True)


def table_selector(shape):
    row = lax.broadcasted_iota(jnp.int32, shape, 0)
    col = lax.broadcasted_iota(jnp.int32, shape, 1)
    up_row = 6 * (col >> 2) + 2 + (col & 3)
    hit = (col < B) & (row == up_row)
    hit = hit | ((col >= 128) & (col < 152) & (row == 6 * (col - 128)))
    hit = hit | ((col >= 152) & (col < 176) & (row == 6 * (col - 152) + 1))
    return hit.astype(F32)


def flat_rows(ref):
    x_zero, x_one, x_two = [ref[pl.ds(m, 24, stride=3), :] for m in range(3)]
    lane = lanes_of((24, 128))
    x_half = pltpu.roll(x_two, 64, 1)
    return (
        x_zero,
        jnp.where(lane < 32, pltpu.roll(x_zero, 32, 1), pltpu.roll(x_one, 32, 1)),
        jnp.where(lane < 64, pltpu.roll(x_one, 64, 1), x_half),
        pltpu.roll(x_two, 96, 1),
    )


def flat_to_square(ref, place):
    for m, rows in enumerate(flat_rows(ref)):
        place[pl.ds(m, 24, stride=4), :] = rows
    return place[...][:, :B]


def split_rows(square, place):
    place[:, 0:B] = square
    return jnp.concatenate([place[pl.ds(m, 24, stride=4), :] for m in range(4)], axis=0)[:, :B]


def store_flat(ref, stacked):
    lane = lanes_of((24, 128))
    wide = jnp.concatenate([stacked, jnp.zeros((B, 128 - B), F32)], axis=1)
    m_zero, m_one, m_two, m_three = [wide[24 * m : 24 * m + 24] for m in range(4)]
    one_back = pltpu.roll(m_one, 96, 1)
    two_back = pltpu.roll(m_two, 64, 1)
    ref[pl.ds(0, 24, stride=3), :] = jnp.where(lane < 96, m_zero, one_back)
    ref[pl.ds(1, 24, stride=3), :] = jnp.where(lane < 64, one_back, two_back)
    ref[pl.ds(2, 24, stride=3), :] = jnp.where(lane < 32, two_back, pltpu.roll(m_three, 32, 1))


def train_kernel(
    n_y,
    x_hbm,
    ct_hbm,
    seg_ref,
    long_ref,
    w_hbm,
    lr_hbm,
    rr_hbm,
    split_ref,
    shared_ref,
    bo_hbm,
    ig_hbm,
    gf_hbm,
    lf_hbm,
    rf_hbm,
    pf_hbm,
    sg_ref,
    nm_ref,
    wt,
    a_all,
    c_all,
    q_all,
    k_all,
    v_all,
    v_tr,
    o_all,
    lse_all,
    z_all,
    gp_all,
    res,
    y_own,
    y_all,
    g_all,
    du_all,
    dx_all,
    dk_acc,
    dv_acc,
    stage,
    core_in,
    x_in,
    side_in,
    dw,
    rs_one,
    rs_two,
    place,
    flat,
    g_acc,
    kid_col,
    kid_row,
    vecs,
    bias_row,
    gvecs,
    gbias,
    sib_in,
    msg_in,
    gmsg_out,
    nb_out,
    nb_in,
    nd_in,
    g_s,
    g_r,
    c_s,
    c_r,
    x_s,
    x_r,
    a_s,
    a_r,
    p_s,
    p_r,
    t_s,
    t_r,
    load_sem,
    land_sem,
    ct_sem,
    y_s,
    y_r,
    out_sem,
    far_s,
    far_r,
    gout_sem,
    root_sem,
    m_s,
    m_r,
    gm_s,
    gm_r,
    sib_s,
    sib_r,
    nb_s,
    nb_r,
    nd_s,
    nd_r,
):
    n_dp = GROUPS
    n_z = n_dp // n_y
    me = lax.axis_index("dp")
    ten = lax.axis_index("tensor")
    my_z, my_y = me // n_y, lax.rem(me, n_y)
    my_x, my_c = ten // 2, lax.rem(ten, 2)
    other_c = 1 - my_c
    sibling = (me, 2 * my_x + other_c)
    across = (me, 2 * (1 - my_x) + my_c)
    scale = 1.0 / math.sqrt(HD)

    def dp_dev(index):
        return (index, ten)

    def z_peer(step):
        return lax.rem(my_z + step, n_z)

    def remote(src, dst, send, recv, dev):
        return pltpu.make_async_remote_copy(
            src_ref=src, dst_ref=dst, send_sem=send, recv_sem=recv, device_id=dev, device_id_type=MESH
        )

    def at(cond, func):
        @pl.when(cond)
        def _():
            func()

    def load_rows(j, which):
        half = my_c if which == 0 else other_c
        return pltpu.make_async_copy(x_hbm.at[j, half], res.at[which, j], load_sem.at[which, j])

    def load_blocks(l):
        return pltpu.make_async_copy(
            w_hbm.at[l], flat.at[pl.ds(l * GROUP, GROUP)], land_sem.at[l]
        )

    def load_cot(j):
        return pltpu.make_async_copy(ct_hbm.at[j, my_c], y_own.at[j], ct_sem.at[j])

    for l in range(LAYERS):
        load_blocks(l).start()
    for j in range(CHUNKS):
        load_rows(j, 0).start()
        load_rows(j, 1).start()
    for j in range(CHUNKS):
        load_cot(j).start()

    barrier = pltpu.get_barrier_semaphore()
    for step in range(1, n_dp):
        pl.semaphore_signal(
            barrier, inc=1, device_id=dp_dev(lax.rem(me + step, n_dp)), device_id_type=MESH
        )
    pl.semaphore_signal(barrier, inc=1, device_id=sibling, device_id_type=MESH)
    pl.semaphore_signal(barrier, inc=1, device_id=across, device_id_type=MESH)

    sel = table_selector((144, 256))
    for l in range(LAYERS):
        row = lax.dot_general(
            jnp.broadcast_to(split_ref[l], (8, 144)),
            sel,
            (((1,), (0,)), ((), ())),
            precision=highest,
            preferred_element_type=F32,
        )
        msg_in[me, 8 * l : 8 * l + 8, :] = row
        for r in range(6):
            msg_in[me, 8 * l + r : 8 * l + r + 1, 0:B] = shared_ref[r, l : l + 1, :]

    pl.semaphore_wait(barrier, n_dp + 1)

    def msg_copy(step):
        return remote(
            msg_in.at[me], msg_in.at[me], m_s.at[step - 1], m_r.at[me],
            dp_dev(lax.rem(me + step, n_dp)),
        )

    def msg_from(step):
        src = lax.rem(me + step, n_dp)
        return remote(msg_in.at[src], msg_in.at[src], m_s.at[step - 1], m_r.at[src], dp_dev(src))

    for step in range(1, n_dp):
        msg_copy(step).start()

    def gather_send(l, p, slab, k, dev):
        return remote(
            wt.at[l, p, slab], wt.at[l, p, slab], g_s.at[l, p, k], g_r.at[l, p, slab], dp_dev(dev)
        )

    def y_peers():
        return [my_z * n_y + lax.rem(my_y + s, n_y) for s in range(1, n_y)]

    def own_send(l, p):
        @pl.when(my_z < n_z - 1)
        def _():
            gather_send(l, p, me, 0, me + n_y).start()

        @pl.when(my_z > 0)
        def _():
            gather_send(l, p, me, 1, me - n_y).start()

    def own_beside(l, p):
        gather_send(l, p, me, 2, y_peers()[0]).start()

    def wave(l, p, hop):
        @pl.when(my_z >= hop)
        def _():
            slab = me - hop * n_y
            gather_send(l, p, slab, 0, slab).wait_recv()

            @pl.when(my_z < n_z - 1)
            def _():
                gather_send(l, p, slab, 2 + hop, me + n_y).start()

            gather_send(l, p, slab, n_z + 1 + hop, y_peers()[0]).start()

        @pl.when(my_z + hop < n_z)
        def _():
            slab = me + hop * n_y
            gather_send(l, p, slab, 0, slab).wait_recv()

            @pl.when(my_z > 0)
            def _():
                gather_send(l, p, slab, 2 * n_z + hop, me - n_y).start()

            gather_send(l, p, slab, 3 * n_z - 1 + hop, y_peers()[0]).start()

    def gather_finish(l, p):
        for s in range(0, n_z):
            slab = z_peer(s) * n_y + lax.rem(my_y + 1, n_y)
            gather_send(l, p, slab, 0, slab).wait_recv()

    def gather_drain(l, p):
        def sent(k):
            gather_send(l, p, me, k, me).wait_send()

        up, down = my_z < n_z - 1, my_z > 0
        at(up, lambda: sent(0))
        at(down, lambda: sent(1))
        sent(2)
        for hop in range(1, n_z):
            low, high = my_z >= hop, my_z + hop < n_z
            at(jnp.logical_and(low, up), lambda: sent(2 + hop))
            at(low, lambda: sent(n_z + 1 + hop))
            at(jnp.logical_and(high, down), lambda: sent(2 * n_z + hop))
            at(high, lambda: sent(3 * n_z - 1 + hop))

    def relayout(l, p):
        cols = []
        for b in range(8):
            blk = PARTS[p][b]
            square = flat_to_square(flat.at[l * GROUP + blk], place.at[b % 6])
            cols.append(jnp.transpose(square) if blk in TRANSPOSED[p] else square)
        wt[l, p, me] = jnp.concatenate(cols, axis=1).astype(BF16)

    def relayout_layer(l, carry):
        load_blocks(l).wait()
        for p in range(3):
            relayout(l, p)
            if p < 2:

                @pl.when(l == 0)
                def _():
                    if p == 0:
                        own_send(0, 0)
                    own_beside(0, p)

        return carry

    lax.fori_loop(0, LAYERS, relayout_layer, 0)

    seq_shift = jnp.where(long_ref[0, 0] > 0, 0, 1)
    seg = seg_ref[...]
    pos = lax.broadcasted_iota(jnp.int32, (8, 128), 0) * 128 + lax.broadcasted_iota(
        jnp.int32, (8, 128), 1
    )
    seq = (pos >> 8) * seq_shift
    kid = jnp.where(seg >= 0, seq * 64 + seg, -1 - seq).astype(F32)
    for r in range(8):
        kid_row[r // 2, 0:1, 128 * (r % 2) : 128 * (r % 2) + 128] = kid[r : r + 1, :]
        kid_col[r] = jnp.transpose(
            jnp.broadcast_to(kid[r : r + 1, :], (128, 128))
        )

    gvecs[...] = jnp.zeros_like(gvecs)
    gbias[...] = jnp.zeros_like(gbias)

    for step in range(1, n_dp):
        msg_from(step).wait_recv()
    for l in range(LAYERS):
        vecs[l] = jnp.concatenate(
            [msg_in[s, 8 * l : 8 * l + 8, 0:B] for s in range(n_dp)], axis=1
        )
        rows = [msg_in[s, 8 * l : 8 * l + 8, 128:256] for s in range(n_dp)]
        pad = jnp.zeros((8, D // 4), F32)
        bias_row[l] = jnp.concatenate(
            [r[:, 0:24] for r in rows]
            + [pad]
            + [r[:, 24:48] for r in rows]
            + [jnp.zeros((8, 64), F32)],
            axis=1,
        )

    low_half = lanes_of((CHUNK, 128)) < 64

    def vec(l, k):
        return vecs[l, k : k + 1, :]

    def core_copy(j):
        return remote(stage.at[j, other_c], core_in.at[j], c_s.at[j], c_r.at[j], sibling)

    def x_copy(j, par):
        if par == 2:
            return remote(stage.at[j, my_c], side_in.at[j], x_s.at[2, j], x_r.at[2, j], across)
        return remote(stage.at[j, my_c], x_in.at[par, j], x_s.at[par, j], x_r.at[par, j], across)

    def own_copy(ref, j):
        return remote(ref.at[j, my_c], ref.at[j, my_c], a_s.at[j], a_r.at[j], sibling)

    def send_partial(j, value):
        stage[j] = value.astype(BF16).reshape(2, HALF, D)
        core_copy(j).start()

    def pass_on(j, par):
        core_copy(j).wait()
        mine = stage[j, my_c].astype(F32) + core_in[j].astype(F32)
        stage[j, my_c] = mine.astype(BF16)
        x_copy(j, par).start()

    def total(j, par):
        x_copy(j, par).wait()
        came = side_in[j] if par == 2 else x_in[par, j]
        return stage[j, my_c].astype(F32) + came.astype(F32)

    def project(l, j):
        rows = a_all[l, j].reshape(CHUNK, D)
        weight = wt[l, 0].reshape(D, D)[:, 0:640]
        out = dot_nn(rows, weight) + bias_row[l, 0:1, :]
        tiles = [out[:, 128 * t : 128 * t + 128] for t in range(5)]
        q_roll = pltpu.roll(tiles[0], 64, 1)
        v_roll = pltpu.roll(tiles[3], 64, 1)
        zero = jnp.zeros((CHUNK, 128), F32)
        q_val = [
            jnp.where(low_half, zero, q_roll),
            jnp.where(low_half, q_roll, pltpu.roll(tiles[1], 64, 1)),
        ]
        k_val = [jnp.where(low_half, zero, tiles[1]), tiles[2]]
        v_val = [
            jnp.where(low_half, zero, v_roll),
            jnp.where(low_half, v_roll, pltpu.roll(tiles[4], 64, 1)),
        ]
        q_all[l, j] = jnp.concatenate(q_val, axis=1).astype(BF16)
        k_all[l, j] = jnp.concatenate(k_val, axis=1).astype(BF16)
        v_mat = jnp.concatenate(v_val, axis=1)
        v_all[l, j] = v_mat.astype(BF16)
        v_tr[:, pl.ds(pl.multiple_of(j * CHUNK, CHUNK), CHUNK)] = jnp.transpose(v_mat).astype(BF16)

    def head_tile(mat, h):
        if h == 0:
            return mat[:, 0:128]
        keep = low_half if h == 1 else jnp.logical_not(low_half)
        return jnp.where(keep, mat[:, 128:256], jnp.zeros((), mat.dtype))

    def tile_of(ref, l, h):
        full = ref[l].reshape(ROWS, 256)
        return full[:, 0:128] if h == 0 else full[:, 128:256]

    def allowed_of(j):
        col = kid_col[...].reshape(ROWS, 128)
        return jnp.concatenate([col, col], axis=1) == kid_row[j, 0:1, :]

    def attend_chunk(l, j):
        allowed = allowed_of(j)
        q_mat = q_all[l, j]
        outs = [jnp.zeros((64, CHUNK), F32)]
        for h in range(HEADS_DEV):
            scores = dot_nt(tile_of(k_all, l, h), head_tile(q_mat, h)) * scale
            scores = jnp.where(allowed, scores, big_negative)
            top = jnp.max(scores, axis=0, keepdims=True)
            expo = jnp.exp(scores - top)
            tot = jnp.sum(expo, axis=0, keepdims=True)
            lse_all[l, j, h : h + 1, :] = top + jnp.log(tot)
            out = dot_nn(v_tr[64 + 64 * h : 128 + 64 * h, :], expo.astype(BF16))
            outs.append(out / tot)
        o_mat = jnp.transpose(jnp.concatenate(outs, axis=0)).astype(BF16)
        o_all[l, j] = o_mat
        send_partial(j, dot_nt(o_mat, wt[l, 0].reshape(D, D)[:, 512:768]))

    def middle(l, j):
        mid = res[2 * l, j] + total(j, 0) + vec(l, 4)
        res[2 * l + 1, j] = mid
        hat, _ = norm_rows(mid)
        c_all[l, j, my_c] = (hat * vec(l, 2) + vec(l, 3)).astype(BF16)
        own_copy(c_all.at[l], j).start()

    def mlp(l, j):
        own_copy(c_all.at[l], j).wait()
        rows = c_all[l, j].reshape(CHUNK, D)
        pre = dot_nn(rows, wt[l, 1].reshape(D, D)) + vec(l, 6)
        cdf = 0.5 * (1.0 + lax.erf(pre * (1.0 / math.sqrt(2.0))))
        pdf = jnp.exp(-0.5 * pre * pre) * (1.0 / math.sqrt(2.0 * math.pi))
        act = (pre * cdf).astype(BF16)
        z_all[l, j] = act
        gp_all[l, j] = (cdf + pre * pdf).astype(BF16)

        @pl.when(l < LAYERS - 1)
        def _():
            at(j == 0, lambda: gather_finish(0, 2))
            send_partial(j, dot_nt(z_all[l, j], wt[l, 2].reshape(D, D)))

        @pl.when(l == LAYERS - 1)
        def _():
            y_copy(j).wait()
            mlp_back(LAYERS - 1, j)

    def y_copy(j):
        return remote(y_all.at[j, my_c], y_all.at[j, my_c], y_s.at[j], y_r.at[j], sibling)

    def near_copy(ref, hbm, which, j):
        return pltpu.make_async_copy(ref.at[j], hbm.at[j, my_c], out_sem.at[which, j])

    def far_copy(ref, hbm, which, j):
        return remote(ref.at[j], hbm.at[j, my_c], far_s.at[which, j], far_r.at[which, j], sibling)

    def layer_end(l, j):
        new = res[2 * l + 1, j] + total(j, 1) + vec(l, 5)
        res[2 * l + 2, j] = new
        hat, _ = norm_rows(new)
        a_all[l + 1, j, my_c] = (hat * vec(l + 1, 0) + vec(l + 1, 1)).astype(BF16)
        own_copy(a_all.at[l + 1], j).start()

    def last_send(slot, j):
        send_partial(slot, dot_nt(z_all[LAYERS - 1, j], wt[LAYERS - 1, 2].reshape(D, D)))

    def last_end(slot, j):
        last = res.at[2 * LAYERS - 1]
        last[j] = last[j] + total(slot, 2) + vec(LAYERS - 1, 5)
        near_copy(last, bo_hbm, 0, j).start()
        far_copy(last, bo_hbm, 0, j).start()

    def when_chunk(tick, offset, func):
        @pl.when(jnp.logical_and(tick >= offset, tick < offset + CHUNKS))
        def _():
            func(tick - offset)

    def add_vec(l, k, value):
        gvecs[l, k : k + 1, :] += value

    def mlp_back(l, j):
        d_act = dot_nn(y_all[j].reshape(CHUNK, D), wt[l, 2].reshape(D, D))
        d_pre = (d_act * gp_all[l, j].astype(F32)).astype(BF16)
        du_all[j] = d_pre
        add_vec(l, 6, jnp.sum(d_pre.astype(F32), axis=0, keepdims=True))
        send_partial(j, dot_nt(du_all[j], wt[l, 1].reshape(D, D)))

    def middle_back(l, j):
        grad = total(j, 1)
        d_rows, d_gain, d_shift = norm_back(grad, res[2 * l + 1, j], vec(l, 2))
        y_rows = y_own[j]
        add_vec(l, 5, jnp.sum(y_rows, axis=0, keepdims=True))
        g_rows = y_rows + d_rows
        add_vec(l, 2, d_gain)
        add_vec(l, 3, d_shift)
        add_vec(l, 4, jnp.sum(g_rows, axis=0, keepdims=True))
        y_own[j] = g_rows
        g_all[j, my_c] = g_rows.astype(BF16)
        own_copy(g_all, j).start()

    def attend_back(l, j):
        own_copy(g_all, j).wait()
        d_out = dot_nn(g_all[j].reshape(CHUNK, D), wt[l, 0].reshape(D, D)[:, 512:768])
        do_mat = d_out.astype(BF16)
        prod = jnp.transpose(do_mat.astype(F32) * o_all[l, j].astype(F32))
        allowed = allowed_of(j)
        q_mat = q_all[l, j]
        dq_parts = []
        for h in range(HEADS_DEV):
            q_h = head_tile(q_mat, h)
            do_h = head_tile(do_mat, h)
            scores = dot_nt(tile_of(k_all, l, h), q_h) * scale
            scores = jnp.where(allowed, scores, big_negative)
            probs = jnp.exp(scores - lse_all[l, j, h : h + 1, :])
            delta = jnp.sum(prod[64 + 64 * h : 128 + 64 * h, :], axis=0, keepdims=True)
            d_probs = dot_nt(tile_of(v_all, l, h), do_h)
            d_scores = (probs * (d_probs - delta)).astype(BF16)
            t = 0 if h == 0 else 128
            dv_acc[:, t : t + 128] += dot_nn(probs.astype(BF16), do_h)
            dk_acc[:, t : t + 128] += dot_nn(d_scores, q_h)
            dq_parts.append(dot_nn(v_tr[64 + 64 * h : 128 + 64 * h, :], d_scores))
        dq_parts.append(jnp.zeros((64, CHUNK), F32))
        dq_mat = jnp.transpose(jnp.concatenate(dq_parts, axis=0) * scale)
        dx_all[j, :, 0:256] = dq_mat.astype(BF16)

    def project_back(l, j):
        rows = pl.ds(pl.multiple_of(j * CHUNK, CHUNK), CHUNK)
        dk_mat = dk_acc[rows, :] * scale
        dv_mat = dv_acc[rows, :]
        zero = jnp.zeros((CHUNK, 128), F32)
        roll_zero = pltpu.roll(dv_mat[:, 0:128], 64, 1)
        roll_one = pltpu.roll(dv_mat[:, 128:256], 64, 1)
        tile_one = jnp.where(low_half, dx_all[j, :, 128:256].astype(F32), dk_mat[:, 0:128])
        dx_all[j, :, 128:640] = jnp.concatenate(
            [
                tile_one,
                dk_mat[:, 128:256],
                jnp.where(low_half, roll_zero, roll_one),
                jnp.where(low_half, roll_one, zero),
            ],
            axis=1,
        ).astype(BF16)
        dx_mat = dx_all[j]
        gbias[l, 0:1, :] += jnp.sum(dx_mat.astype(F32), axis=0, keepdims=True)
        send_partial(j, dot_nt(dx_mat, wt[l, 0].reshape(D, D)[:, 0:640]))

    def layer_begin(l, j):
        grad = total(j, 0)
        d_rows, d_gain, d_shift = norm_back(grad, res[2 * l, j], vec(l, 0))
        add_vec(l, 0, d_gain)
        add_vec(l, 1, d_shift)
        new = y_own[j] + d_rows
        y_own[j] = new

        @pl.when(l > 0)
        def _():
            y_all[j, my_c] = new.astype(BF16)
            own_copy(y_all, j).start()

        @pl.when(l == 0)
        def _():
            near_copy(y_own, ig_hbm, 1, j).start()
            far_copy(y_own, ig_hbm, 1, j).start()

    def slab(ref, p, owner):
        return ref.at[p, pl.ds(pl.multiple_of(owner * B, B), B)]

    def pair_copy(l, p, z):
        dest = y_peers()[0]
        return remote(
            slab(dw, p, z * n_y + lax.rem(my_y + 1, n_y)),
            rs_one.at[l, p, z],
            p_s.at[l, p, z],
            p_r.at[l, p, z],
            dp_dev(dest),
        )

    def line_copy(l, p, s):
        dest = z_peer(s)
        return remote(
            slab(dw, p, dest * n_y + my_y),
            rs_two.at[l, p, n_z - 1 - s],
            t_s.at[l, p, s - 1],
            t_r.at[l, p, n_z - 1 - s],
            dp_dev(dest * n_y + my_y),
        )

    def line_from(l, p, s):
        return remote(
            slab(dw, p, me),
            rs_two.at[l, p, s - 1],
            t_s.at[l, p, s - 1],
            t_r.at[l, p, s - 1],
            dp_dev(z_peer(s) * n_y + my_y),
        )

    def scatter_drain(l, p):
        for z in range(n_z):
            pair_copy(l, p, z).wait_send()
        for s in range(1, n_z):
            line_copy(l, p, s).wait_send()

    def scatter_begin(l, p):
        for s in list(range(1, n_z)) + [0]:
            pair_copy(l, p, z_peer(s)).start()

    def scatter_middle(l, p, steps=(1, 2, 3, 0)):
        for s in steps:
            z = z_peer(s)
            pair_copy(l, p, z).wait_recv()
            ref = slab(dw, p, z * n_y + my_y)
            both = (ref[...].astype(F32) + rs_one[l, p, z].astype(F32)).astype(BF16)
            if s:
                ref[...] = both
                line_copy(l, p, s).start()
            else:
                rs_one[l, p, my_z] = both

    def runs_of(p):
        return ((0, 0, 6), (6, 14, 2)) if p == 0 else ((0, PARTS[p][0], 8),)

    def block_copies(l, p):
        return [
            pltpu.make_async_copy(
                flat.at[pl.ds(16 + 8 * k + here, count)],
                hbm.at[l, pl.ds(there, count)],
                gout_sem.at[k, n],
            )
            for k, hbm in enumerate((gf_hbm, lf_hbm, rf_hbm, pf_hbm))
            for n, (here, there, count) in enumerate(runs_of(p))
        ]

    def root_copies(l, p):
        return [
            pltpu.make_async_copy(
                hbm.at[l, pl.ds(there, count)],
                flat.at[pl.ds(8 * k + here, count)],
                root_sem.at[k, n],
            )
            for k, hbm in enumerate((lr_hbm, rr_hbm))
            for n, (here, there, count) in enumerate(runs_of(p))
        ]

    def scatter_end(l, p):
        acc = rs_one[l, p, my_z].astype(F32)
        for s in range(1, n_z):
            line_from(l, p, s).wait_recv()
            acc = acc + rs_two[l, p, s - 1].astype(F32)
        nm_ref[0:1, 0:1] += jnp.sum(acc * acc, keepdims=True)
        g_acc[...] = acc

    def block_update(l, p):
        acc = g_acc[...]
        for copy in root_copies(l, p):
            copy.wait()
        if p < 2:
            for copy in block_copies(l, p + 1):
                copy.wait()
        else:
            @pl.when(l < LAYERS - 1)
            def _():
                for copy in block_copies(LAYERS - 1, 0):
                    copy.wait()

        for b in range(8):
            square = acc[:, B * b : B * b + B]
            turned = jnp.transpose(square)
            if PARTS[p][b] in TRANSPOSED[p]:
                square, turned = turned, square
            slot = 3 * (b % 2)
            low = square.astype(BF16)
            rows = split_rows(square, place.at[slot])
            cols = split_rows(turned, place.at[slot + 1])
            right = flat_to_square(flat.at[8 + b], place.at[slot + 2])
            left = jnp.concatenate(flat_rows(flat.at[b]), axis=0)[:, :B]
            store_flat(flat.at[16 + b], rows)
            store_flat(flat.at[24 + b], dot_nt(rows.astype(BF16), low))
            store_flat(flat.at[32 + b], dot_nn(cols.astype(BF16), low))
            half = dot_nn(left.astype(BF16), low).astype(BF16)
            store_flat(flat.at[40 + b], dot_nn(half, right.astype(BF16)))
        for copy in block_copies(l, p):
            copy.start()
        if p > 0:
            for copy in root_copies(l, p - 1):
                copy.start()
        else:
            @pl.when(l > 0)
            def _():
                for copy in root_copies(0, 2):
                    copy.start()

    nm_ref[...] = jnp.zeros_like(nm_ref)

    def weight_grad(l, p, func):
        at(l < LAYERS - 1, lambda: scatter_drain(LAYERS - 1, p))

        def piece(m, carry):
            cols = pl.ds(pl.multiple_of(m * 256, 256), 256)
            dw[p, cols, :] = func(cols).astype(BF16)
            return carry

        lax.fori_loop(0, D // 256, piece, 0)
        scatter_begin(l, p)

    def down_grad(l):
        def func(cols):
            return dot_tn(
                y_all[:, :, :, cols].reshape(ROWS, 256), z_all[l].reshape(ROWS, D)
            )

        weight_grad(l, 2, func)

    def up_grad(l):
        def func(cols):
            return dot_tn(
                c_all[l, :, :, :, cols].reshape(ROWS, 256), du_all[...].reshape(ROWS, D)
            )

        weight_grad(l, 1, func)

    def qkv_grad(l):
        def func(cols):
            first = dot_tn(
                a_all[l, :, :, :, cols].reshape(ROWS, 256), dx_all[...].reshape(ROWS, 640)
            )
            second = dot_tn(
                g_all[:, :, :, cols].reshape(ROWS, 256), o_all[l].reshape(ROWS, 256)
            )
            return jnp.concatenate(
                [first[:, 0:512], first[:, 512:640] + second[:, 0:128], second[:, 128:256]], axis=1
            )

        weight_grad(l, 0, func)

    def first_norm(j, carry):
        load_rows(j, 0).wait()
        load_rows(j, 1).wait()
        hat, _ = norm_rows(res[0, j])
        a_all[0, j, my_c] = (hat * vec(0, 0) + vec(0, 1)).astype(BF16)
        hat, _ = norm_rows(res[1, j])
        a_all[0, j, other_c] = (hat * vec(0, 0) + vec(0, 1)).astype(BF16)
        return carry

    def first_grad(j, carry):
        load_cot(j).wait()
        rows = jnp.where(kid_col[2 * j + my_c][:, 0:1] >= 0.0, y_own[j], 0.0)
        y_own[j] = rows
        y_all[j, my_c] = rows.astype(BF16)
        y_copy(j).start()
        return carry

    def first_project(j, carry):
        project(0, j)
        return carry

    for copy in root_copies(LAYERS - 1, 2):
        copy.start()
    wave(0, 0, 1)
    own_send(0, 1)
    own_beside(0, 2)
    lax.fori_loop(0, CHUNKS // 2, first_norm, 0)
    wave(0, 0, 2)
    lax.fori_loop(CHUNKS // 2, CHUNKS, first_norm, 0)
    wave(0, 0, 3)
    wave(0, 1, 1)
    lax.fori_loop(0, CHUNKS, first_grad, 0)
    own_send(0, 2)
    gather_finish(0, 0)
    wave(0, 1, 2)
    own_beside(1, 0)
    lax.fori_loop(0, CHUNKS, first_project, 0)

    def prepare_back(l):
        for j in range(CHUNKS):
            v_tr[:, j * CHUNK : j * CHUNK + CHUNK] = jnp.transpose(k_all[l, j].astype(F32)).astype(
                BF16
            )
        dk_acc[...] = jnp.zeros_like(dk_acc)
        dv_acc[...] = jnp.zeros_like(dv_acc)

    def forward_layer(l, carry):
        def step(tick, inner):
            when_chunk(tick, 1, lambda j: pass_on(j, 0))
            when_chunk(tick, 5, lambda j: pass_on(j, 1))

            when_chunk(tick, 3, lambda j: middle(l, j))

            @pl.when(l < LAYERS - 1)
            def _():
                when_chunk(tick, 7, lambda j: layer_end(0, j))

            @pl.when(l == 0)
            def _():
                @pl.when(tick == 0)
                def _():
                    wave(0, 1, 3)

                @pl.when(tick == 1)
                def _():
                    wave(0, 2, 1)

                @pl.when(tick == 2)
                def _():
                    wave(0, 2, 2)
                    own_send(1, 0)
                    own_beside(1, 1)

                @pl.when(tick == 3)
                def _():
                    wave(0, 2, 3)

                @pl.when(tick == 4)
                def _():
                    gather_finish(0, 1)
                    wave(1, 0, 1)

                @pl.when(tick == 5)
                def _():
                    wave(1, 0, 2)
                    own_send(1, 1)
                    own_beside(1, 2)

                @pl.when(tick == 6)
                def _():
                    wave(1, 0, 3)
                    wave(1, 1, 1)

                @pl.when(tick == 7)
                def _():
                    wave(1, 1, 2)
                    own_send(1, 2)

                @pl.when(tick == 8)
                def _():
                    gather_finish(1, 0)
                    wave(1, 1, 3)
                    wave(1, 2, 1)

                @pl.when(tick == 9)
                def _():
                    wave(1, 2, 2)

                @pl.when(tick == 10)
                def _():
                    wave(1, 2, 3)

            @pl.when(l == 1)
            def _():
                @pl.when(tick == 4)
                def _():
                    gather_finish(1, 1)
                    gather_finish(1, 2)

            when_chunk(tick, 0, lambda j: attend_chunk(l, j))

            def next_project(j):
                own_copy(a_all.at[LAYERS - 1], j).wait()
                project(LAYERS - 1, j)

            when_chunk(tick, 4, lambda j: mlp(l, j))

            @pl.when(l == 0)
            def _():
                when_chunk(tick, 8, next_project)

            at(jnp.logical_and(l == LAYERS - 1, tick == 8), lambda: prepare_back(LAYERS - 1))
            return inner

        lax.fori_loop(0, 12, step, 0)
        return carry

    lax.fori_loop(0, LAYERS, forward_layer, 0)
    for step in range(1, n_dp):
        msg_copy(step).wait_send()

    def finish_part(l, p):
        scatter_end(l, p)
        block_update(l, p)

    def backward_layer(n, carry):
        l = LAYERS - 1 - n
        upper = l == LAYERS - 1
        lower = l < LAYERS - 1
        down_grad(l)

        @pl.when(lower)
        def _():
            scatter_middle(LAYERS - 1, 0)

        def step(tick, inner):
            @pl.when(upper)
            def _():
                at(tick == 1, lambda: last_send(0, 0))

                @pl.when(tick == 2)
                def _():
                    last_send(1, 1)
                    pass_on(0, 2)

                at(tick == 3, lambda: pass_on(1, 2))

            middle_back(l, tick)
            at(tick == 2, lambda: up_grad(l))

            at(tick == 3, lambda: scatter_middle(l, 2))
            attend_back(l, tick)
            return inner

        lax.fori_loop(0, CHUNKS, step, 0)

        def step_two(tick, inner):
            when_chunk(tick, 1, lambda j: pass_on(j, 0))

            @pl.when(upper)
            def _():
                when_chunk(tick, 6, lambda j: pass_on(j, 1))

            when_chunk(tick, 4, lambda j: layer_begin(l, j))
            at(jnp.logical_and(upper, tick < 2), lambda: last_end(tick, tick))
            when_chunk(tick, 0, lambda j: project_back(l, j))
            at(tick == 3, lambda: qkv_grad(l))

            @pl.when(lower)
            def _():
                @pl.when(tick == 5)
                def _():
                    far_copy(y_own, ig_hbm, 1, 0).wait_recv()
                    last_send(0, 2)

                @pl.when(tick == 6)
                def _():
                    pass_on(0, 2)
                    far_copy(y_own, ig_hbm, 1, 1).wait_recv()
                    last_send(1, 3)

                at(tick == 7, lambda: pass_on(1, 2))

                @pl.when(tick == 4)
                def _():
                    scatter_middle(0, 1)
                    finish_part(LAYERS - 1, 1)

                at(tick == 5, lambda: scatter_middle(0, 0, (1,)))
                at(tick == 6, lambda: scatter_middle(0, 0, (2,)))
                at(tick == 7, lambda: scatter_middle(0, 0, (3,)))

            def next_back(j):
                own_copy(y_all, j).wait()
                mlp_back(l - 1, j)

            @pl.when(upper)
            def _():
                at(tick == 4, lambda: prepare_back(l - 1))
                when_chunk(tick, 5, next_back)

            @pl.when(upper)
            def _():
                at(tick == 5, lambda: scatter_middle(l, 1))
                at(tick == 6, lambda: finish_part(l, 2))

            return inner

        lax.fori_loop(0, 10, step_two, 0)
        return carry

    lax.fori_loop(0, LAYERS, backward_layer, 0)

    sib = remote(gvecs, sib_in, sib_s.at[0], sib_r.at[0], sibling)
    sib.start()
    sib.wait()
    row_at = lax.broadcasted_iota(jnp.int32, (8, D), 0)
    for l in range(LAYERS):
        mat = gvecs[l] + jnp.where(row_at < 6, sib_in[l], 0.0)
        extra = gbias[l]
        for s in range(n_dp):
            gmsg_out[s, 8 * l : 8 * l + 8, 0:B] = mat[:, B * s : B * s + B]
            gmsg_out[s, 8 * l : 8 * l + 8, 128:152] = extra[:, 24 * s : 24 * s + 24]
            gmsg_out[s, 8 * l : 8 * l + 8, 152:176] = extra[:, 384 + 24 * s : 384 + 24 * s + 24]
            gmsg_out[s, 8 * l : 8 * l + 8, B:128] = jnp.zeros((8, 128 - B), F32)
            gmsg_out[s, 8 * l : 8 * l + 8, 176:256] = jnp.zeros((8, 80), F32)

    def gmsg_copy(step):
        dest = lax.rem(me + step, n_dp)
        return remote(
            gmsg_out.at[dest], msg_in.at[me], gm_s.at[step - 1], gm_r.at[me], dp_dev(dest)
        )

    def gmsg_from(step):
        src = lax.rem(me + step, n_dp)
        return remote(gmsg_out.at[src], msg_in.at[src], gm_s.at[step - 1], gm_r.at[src], dp_dev(src))

    for step in range(1, n_dp):
        gmsg_copy(step).start()
    msg_in[me] = gmsg_out[me]
    scatter_middle(0, 0, (0,))
    finish_part(LAYERS - 1, 0)
    finish_part(0, 2)
    finish_part(0, 1)
    for step in range(1, n_dp):
        gmsg_from(step).wait_recv()
    summed = msg_in[0]
    for s in range(1, n_dp):
        summed = summed + msg_in[s]
    sg_ref[...] = summed

    scatter_end(0, 0)
    squares = summed * summed
    lane = lanes_of((1, 128))
    packed = jnp.where(lane == 0, nm_ref[0:1, :], 0.0)
    shared_sums = jnp.zeros((1, 128), F32)
    for l in range(LAYERS):
        base = 8 * l
        up = jnp.sum(squares[base + 6 : base + 7, 0:B], keepdims=True)
        query = jnp.sum(squares[base : base + 1, 128:152], keepdims=True)
        value = jnp.sum(squares[base : base + 1, 152:176], keepdims=True)
        for k, item in enumerate((query, value, up)):
            packed = packed + jnp.where(lane == 1 + 3 * l + k, item, 0.0)
        for r in range(6):
            item = jnp.sum(squares[base + r : base + r + 1, 0:B], keepdims=True)
            shared_sums = shared_sums + jnp.where(lane == 6 * l + r, item, 0.0)

    for hop, dev in enumerate((sibling, across)):
        nb_out[hop] = jnp.broadcast_to(packed, (8, 128))
        swap = remote(nb_out.at[hop], nb_in.at[hop], nb_s.at[hop], nb_r.at[hop], dev)
        swap.start()
        swap.wait()
        packed = packed + nb_in[hop, 0:1, :]
    row8 = lax.broadcasted_iota(jnp.int32, (8, 128), 0)
    nd_in[me] = jnp.where(row8 == 0, packed, jnp.where(row8 == 1, shared_sums, 0.0))

    def nd_copy(step):
        dest = lax.rem(me + step, n_dp)
        return remote(nd_in.at[me], nd_in.at[me], nd_s.at[step - 1], nd_r.at[me], dp_dev(dest))

    def nd_from(step):
        src = lax.rem(me + step, n_dp)
        return remote(nd_in.at[src], nd_in.at[src], nd_s.at[step - 1], nd_r.at[src], dp_dev(src))

    for step in range(1, n_dp):
        nd_copy(step).start()
    last_end(0, 2)
    last_end(1, 3)
    block_update(0, 0)
    for step in range(1, n_dp):
        nd_from(step).wait_recv()
    acc = nd_in[0]
    for s in range(1, n_dp):
        acc = acc + nd_in[s]
    nm_ref[...] = acc

    for p in range(3):
        scatter_drain(0, p)
        for l in range(LAYERS):
            gather_drain(l, p)
    for copy in block_copies(0, 0):
        copy.wait()
    for step in range(1, n_dp):
        gmsg_copy(step).wait_send()
        nd_copy(step).wait_send()
    for j in range(CHUNKS):
        near_copy(res.at[2 * LAYERS - 1], bo_hbm, 0, j).wait()
        far_copy(res.at[2 * LAYERS - 1], bo_hbm, 0, j).wait()
        near_copy(y_own, ig_hbm, 1, j).wait()
        if j < 2:
            far_copy(y_own, ig_hbm, 1, j).wait_send()
        else:
            far_copy(y_own, ig_hbm, 1, j).wait()


def train_call(n_y, x_rows, ct_rows, seg, long_flag, blocks, left, right, split, shared):
    hbm = pl.BlockSpec(memory_space=pl.ANY)
    vmem = pl.BlockSpec(memory_space=pltpu.VMEM)
    smem = pl.BlockSpec(memory_space=pltpu.SMEM)
    dma = pltpu.SemaphoreType.DMA
    n_dp = GROUPS
    n_z = n_dp // n_y

    def buf(shape, dtype=BF16):
        return pltpu.VMEM(shape, dtype)

    scratch = [
        buf((LAYERS, 3, n_dp, B, D)),
        buf((LAYERS, CHUNKS, 2, HALF, D)),
        buf((LAYERS, CHUNKS, 2, HALF, D)),
        buf((LAYERS, CHUNKS, CHUNK, 256)),
        buf((LAYERS, CHUNKS, CHUNK, 256)),
        buf((LAYERS, CHUNKS, CHUNK, 256)),
        buf((256, ROWS)),
        buf((LAYERS, CHUNKS, CHUNK, 256)),
        buf((LAYERS, CHUNKS, 8, CHUNK), F32),
        buf((LAYERS, CHUNKS, CHUNK, D)),
        buf((LAYERS, CHUNKS, CHUNK, D)),
        buf((2 * LAYERS, CHUNKS, HALF, D), F32),
        buf((CHUNKS, HALF, D), F32),
        buf((CHUNKS, 2, HALF, D)),
        buf((CHUNKS, 2, HALF, D)),
        buf((CHUNKS, CHUNK, D)),
        buf((CHUNKS, CHUNK, 640)),
        buf((ROWS, 256), F32),
        buf((ROWS, 256), F32),
        buf((CHUNKS, 2, HALF, D)),
        buf((CHUNKS, HALF, D)),
        buf((2, CHUNKS, HALF, D)),
        buf((2, HALF, D)),
        buf((3, D, D)),
        buf((LAYERS, 3, n_z, B, D)),
        buf((LAYERS, 3, n_z - 1, B, D)),
        buf((6, B, 128), F32),
        buf((LAYERS * GROUP, 72, 128), F32),
        buf((B, D), F32),
        buf((8, HALF, 128), F32),
        buf((CHUNKS, 8, CHUNK), F32),
        buf((LAYERS, 8, D), F32),
        buf((LAYERS, 8, 640), F32),
        buf((LAYERS, 8, D), F32),
        buf((LAYERS, 8, 640), F32),
        buf((LAYERS, 8, D), F32),
        buf((n_dp, 16, 256), F32),
        buf((n_dp, 16, 256), F32),
        buf((2, 8, 128), F32),
        buf((2, 8, 128), F32),
        buf((n_dp, 8, 128), F32),
        dma((LAYERS, 3, 4 * n_z)),
        dma((LAYERS, 3, n_dp)),
        dma((CHUNKS,)),
        dma((CHUNKS,)),
        dma((3, CHUNKS)),
        dma((3, CHUNKS)),
        dma((CHUNKS,)),
        dma((CHUNKS,)),
        dma((LAYERS, 3, n_z)),
        dma((LAYERS, 3, n_z)),
        dma((LAYERS, 3, n_z - 1)),
        dma((LAYERS, 3, n_z - 1)),
        dma((2, CHUNKS)),
        dma((LAYERS,)),
        dma((CHUNKS,)),
        dma((CHUNKS,)),
        dma((CHUNKS,)),
        dma((2, CHUNKS)),
        dma((2, CHUNKS)),
        dma((2, CHUNKS)),
        dma((4, 2)),
        dma((2, 2)),
        dma((n_dp - 1,)),
        dma((n_dp,)),
        dma((n_dp - 1,)),
        dma((n_dp,)),
        dma((1,)),
        dma((1,)),
        dma((2,)),
        dma((2,)),
        dma((n_dp - 1,)),
        dma((n_dp,)),
    ]
    rows_shape = jax.ShapeDtypeStruct((CHUNKS, 2, HALF, D), F32)
    return pl.pallas_call(
        functools.partial(train_kernel, n_y),
        out_shape=(
            rows_shape,
            rows_shape,
            *[jax.ShapeDtypeStruct((LAYERS, GROUP, 72, 128), F32)] * 4,
            jax.ShapeDtypeStruct((16, 256), F32),
            jax.ShapeDtypeStruct((8, 128), F32),
        ),
        in_specs=[hbm, hbm, vmem, smem, hbm, hbm, hbm, vmem, vmem],
        out_specs=(hbm, hbm, hbm, hbm, hbm, hbm, vmem, vmem),
        scratch_shapes=scratch,
        compiler_params=pltpu.CompilerParams(
            collective_id=0, has_side_effects=True, vmem_limit_bytes=61 * 1024 * 1024
        ),
        cost_estimate=pl.CostEstimate(
            flops=30_000_000_000, bytes_accessed=30_000_000, transcendentals=20_000_000
        ),
        name="train",
    )(x_rows, ct_rows, seg, long_flag, blocks, left, right, split, shared)


def update_kernel(
    g_ref,
    lg_ref,
    rg_ref,
    p_ref,
    w_ref,
    l_ref,
    r_ref,
    sg_ref,
    nm_ref,
    sp_ref,
    sh_ref,
    bo_ref,
    ig_ref,
    gout_ref,
    nw_ref,
    nl_ref,
    nr_ref,
    sgo_ref,
    nsp_ref,
    shg_ref,
    nsh_ref,
    norm_ref,
    bo_out,
    ig_out,
):
    step_at = pl.program_id(0)
    bo_out[...] = bo_ref[...]
    ig_out[...] = ig_ref[...]
    lane = lanes_of((1, 128))
    row_zero = nm_ref[0:1, :]
    row_one = nm_ref[1:2, :]
    total_sq = jnp.sum(jnp.where(lane < 7, row_zero, 0.0), keepdims=True) + jnp.sum(
        jnp.where(lane < 12, row_one, 0.0), keepdims=True
    )
    norm = jnp.sqrt(total_sq)
    factor = clip_limit / jnp.maximum(norm, clip_limit)
    squared = factor * factor
    gram_weight = (1.0 - decay) * squared

    for b in range(g_ref.shape[0]):
        gout_ref[b] = g_ref[b] * factor
        nl_ref[b] = decay * l_ref[b] + gram_weight * lg_ref[b]
        nr_ref[b] = decay * r_ref[b] + gram_weight * rg_ref[b]
        direction = p_ref[b] * factor
        mean_sq = jnp.sum(direction * direction, keepdims=True) / (B * B)
        nw_ref[b] = w_ref[b] - direction * (rate_matrix * lax.rsqrt(mean_sq + eps_norm))

    @pl.when(step_at == 0)
    def _():
        norm_ref[...] = norm
        sel = table_selector((144, 256))
        col = lanes_of((1, 256))
        for l in range(LAYERS):
            sums = [row_zero[:, 1 + 3 * l + k : 2 + 3 * l + k] for k in range(3)]
            means = [sums[0] / D, sums[1] / D, sums[2] / FF]
            scales = [lax.rsqrt(squared * m + eps_norm) for m in means]
            src = sg_ref[8 * l : 8 * l + 8, :]
            line = jnp.where(col < 128, src[6:7, :], src[0:1, :]) * factor
            step = line * jnp.where(col < 128, scales[2], jnp.where(col < 152, scales[0], scales[1]))
            both = jnp.concatenate([line, step, jnp.zeros((6, 256), F32)], axis=0)
            table = lax.dot_general(
                both, sel, (((1,), (1,)), ((), ())), precision=highest, preferred_element_type=F32
            )
            sgo_ref[l] = table[0:1, :]
            nsp_ref[l] = sp_ref[l] - rate_vector * table[1:2, :]
            for r in range(6):
                mean = row_one[:, 6 * l + r : 6 * l + r + 1] / D
                grad = src[r : r + 1, 0:B] * factor
                shg_ref[r, l : l + 1, :] = grad
                nsh_ref[r, l : l + 1, :] = sh_ref[r, l : l + 1, :] - rate_vector * grad * lax.rsqrt(
                    squared * mean + eps_norm
                )


def update_call(grads, lefts, rights, dirs, weights, left, right, sums, norms, split, shared, outs):
    per = GROUP
    count = LAYERS * GROUP
    flat = pl.BlockSpec((per, 72, 128), lambda i: (i, 0, 0))
    rows = pl.BlockSpec((2 * HALF * CHUNKS * per // count, D), lambda i: (i, 0))

    def whole(shape):
        return pl.BlockSpec(shape, lambda i: (0,) * len(shape))

    flat_shape = jax.ShapeDtypeStruct((count, 72, 128), F32)
    split_shape, shared_shape = (LAYERS, 1, 144), (6, LAYERS, B)
    return pl.pallas_call(
        update_kernel,
        grid=(count // per,),
        out_shape=(
            *[flat_shape] * 4,
            *[jax.ShapeDtypeStruct(split_shape, F32)] * 2,
            *[jax.ShapeDtypeStruct(shared_shape, F32)] * 2,
            jax.ShapeDtypeStruct((1, 1), F32),
            *[jax.ShapeDtypeStruct(o.shape, F32) for o in outs],
        ),
        in_specs=[flat] * 7
        + [whole((16, 256)), whole((8, 128)), whole(split_shape), whole(shared_shape), rows, rows],
        out_specs=(
            *[flat] * 4,
            *[whole(split_shape)] * 2,
            *[whole(shared_shape)] * 2,
            whole((1, 1)),
            rows,
            rows,
        ),
        compiler_params=pltpu.CompilerParams(vmem_limit_bytes=60 * 1024 * 1024),
        name="update",
    )(grads, lefts, rights, dirs, weights, left, right, sums, norms, split, shared, *outs)


def fast_body(
    n_y,
    tokens_in,
    cotangent,
    segment_ids,
    long_seq,
    weights,
    left_stats,
    right_stats,
    left_roots,
    right_roots,
    split_params,
    shared_params,
):
    rows = (CHUNKS, 2, HALF, D)
    flat = (LAYERS, GROUP, 72, 128)
    blocks = (LAYERS * GROUP, 72, 128)
    split = split_params
    shared = jnp.transpose(shared_params, (1, 0, 2))
    out_rows, in_grad, grads, lefts, rights, dirs, sums, norms = train_call(
        n_y,
        tokens_in.reshape(rows),
        cotangent.reshape(rows),
        segment_ids.reshape(8, 128),
        long_seq.reshape(1, 1),
        weights.reshape(flat),
        left_roots.reshape(flat),
        right_roots.reshape(flat),
        split,
        shared,
    )
    res = update_call(
        *[m.reshape(blocks) for m in (grads, lefts, rights, dirs, weights, left_stats, right_stats)],
        sums,
        norms,
        split,
        shared,
        (out_rows.reshape(tokens_in.shape), in_grad.reshape(tokens_in.shape)),
    )
    mats = [r.reshape(weights.shape) for r in res[:4]]
    return (
        res[9],
        res[10],
        *mats,
        res[4],
        res[5],
        jnp.transpose(res[6], (1, 0, 2)),
        jnp.transpose(res[7], (1, 0, 2)),
        res[8].reshape(()),
    )


def solution(mesh):
    in_specs = (
        P("dp", None),
        P("dp", None),
        P("dp"),
        P("dp"),
        P(None, "dp", "tensor", None),
        P(None, "dp", "tensor", None),
        P(None, "dp", "tensor", None),
        P(None, "dp", "tensor", None),
        P(None, "dp", "tensor", None),
        P(None, "tensor", "dp"),
        P(None, None, "dp"),
    )
    out_specs = (
        P("dp", None),
        P("dp", None),
        P(None, "dp", "tensor", None),
        P(None, "dp", "tensor", None),
        P(None, "dp", "tensor", None),
        P(None, "dp", "tensor", None),
        P(None, "tensor", "dp"),
        P(None, "tensor", "dp"),
        P(None, None, "dp"),
        P(None, None, "dp"),
        P(),
    )
    plan = body
    if mesh.shape["dp"] == GROUPS and mesh.shape["tensor"] == 4:
        plan = functools.partial(fast_body, 2)
    return jax.shard_map(plan, mesh=mesh, in_specs=in_specs, out_specs=out_specs, check_vma=False)
```

```python
import functools
import math

import jax
import jax.numpy as jnp
from jax import lax
from jax.experimental import pallas as pl
from jax.experimental.pallas import tpu as pltpu
from jax.sharding import PartitionSpec as P

D = 768
HEADS = 12
FF = 3072
HD = 64
B = 96
LAYERS = 2
SEQ_SHORT = 256
SEQ_LONG = 1024


clip_limit = 100.0
rate_matrix = 0.06
rate_vector = 0.2
decay = 0.5
eps_norm = 1e-06
eps_layer = 1e-06
big_negative = -1e30
highest = lax.Precision.HIGHEST


def layer_norm(hidden, gain_vec, shift_vec):
    row_mean = jnp.mean(hidden, axis=-1, keepdims=True)
    centered = hidden - row_mean
    row_var = jnp.mean(centered * centered, axis=-1, keepdims=True)
    return centered * lax.rsqrt(row_var + eps_layer) * gain_vec + shift_vec


def gelu_exact(values):
    return jax.nn.gelu(values, approximate=False)


def matmul_low(left_mat, right_mat):
    return jnp.dot(left_mat, right_mat, preferred_element_type=jnp.float32)


def inner_rows(left_mat, right_mat):
    return lax.dot_general(
        left_mat, right_mat, (((0,), (0,)), ((), ())), preferred_element_type=jnp.float32
    )


def times_trans(left_mat, right_mat):
    return lax.dot_general(
        left_mat, right_mat, (((1,), (1,)), ((), ())), preferred_element_type=jnp.float32
    )


def unpack_layer(blocks, embed_dev, inner_dev):
    row_groups = blocks.shape[0]
    block_size = blocks.shape[2]
    qkv_count = 3 * embed_dev // block_size
    up_count = inner_dev // block_size
    out_count = embed_dev // block_size

    def by_rows(part_blocks):
        block_count = part_blocks.shape[1]
        return jnp.transpose(part_blocks, (0, 2, 1, 3)).reshape(
            row_groups * block_size, block_count * block_size
        )

    def by_cols(part_blocks):
        block_count = part_blocks.shape[1]
        return jnp.transpose(part_blocks, (1, 2, 0, 3)).reshape(
            block_count * block_size, row_groups * block_size
        )

    qkv_weight = by_rows(blocks[:, :qkv_count])
    up_weight = by_rows(blocks[:, qkv_count : qkv_count + up_count])
    out_weight = by_cols(blocks[:, qkv_count + up_count : qkv_count + up_count + out_count])
    down_weight = by_cols(blocks[:, qkv_count + up_count + out_count :])
    return (qkv_weight, out_weight, up_weight, down_weight)


def pack_layer(qkv_grad, out_grad, up_grad, down_grad, block_size):
    row_groups = qkv_grad.shape[0] // block_size

    def from_rows(matrix):
        block_count = matrix.shape[1] // block_size
        return jnp.transpose(
            matrix.reshape(row_groups, block_size, block_count, block_size), (0, 2, 1, 3)
        )

    def from_cols(matrix):
        block_count = matrix.shape[0] // block_size
        return jnp.transpose(
            matrix.reshape(block_count, block_size, row_groups, block_size), (2, 0, 1, 3)
        )

    return jnp.concatenate(
        [from_rows(qkv_grad), from_rows(up_grad), from_cols(out_grad), from_cols(down_grad)], axis=1
    )


def masked_scores(query_block, key_window, query_seq, key_seq, query_seg, key_seg, score_scale):
    scores = (
        jnp.einsum("qhd,khd->hqk", query_block, key_window, preferred_element_type=jnp.float32)
        * score_scale
    )
    allowed = (query_seq[:, None] == key_seq[None, :]) & (query_seg[:, None] == key_seg[None, :])
    return jnp.where(allowed[None], scores, big_negative)


def attention_forward(queries, keys_all, values_all, seq_index, segments, block_rows, score_scale):
    block_count = queries.shape[0] // block_rows

    def one_block(block_index):
        row_start = block_index * block_rows
        query_block = lax.dynamic_slice_in_dim(queries, row_start, block_rows, 0)
        scores = masked_scores(
            query_block,
            keys_all,
            lax.dynamic_slice_in_dim(seq_index, row_start, block_rows, 0),
            seq_index,
            lax.dynamic_slice_in_dim(segments, row_start, block_rows, 0),
            segments,
            score_scale,
        )
        row_max = jnp.max(scores, axis=-1, keepdims=True)
        exponent = jnp.exp(scores - row_max)
        row_total = jnp.sum(exponent, axis=-1, keepdims=True)
        attn_probs = (exponent / row_total).astype(jnp.bfloat16)
        attended = jnp.einsum(
            "hqk,khd->qhd", attn_probs, values_all, preferred_element_type=jnp.float32
        )
        return (attended, (row_max + jnp.log(row_total))[..., 0])

    return lax.map(one_block, jnp.arange(block_count, dtype=jnp.int32))


def attention_backward(
    queries, keys_all, values_all, grad_out, log_total, seq_index, segments, block_rows, score_scale
):
    token_count = queries.shape[0]
    block_count = token_count // block_rows
    zero_grad = jnp.zeros(keys_all.shape, jnp.float32)

    def one_block(carry_pair, block_index):
        key_grad, value_grad = carry_pair
        row_start = block_index * block_rows
        query_block = lax.dynamic_slice_in_dim(queries, row_start, block_rows, 0)
        out_block = lax.dynamic_slice_in_dim(grad_out, row_start, block_rows, 0)
        scores = masked_scores(
            query_block,
            keys_all,
            lax.dynamic_slice_in_dim(seq_index, row_start, block_rows, 0),
            seq_index,
            lax.dynamic_slice_in_dim(segments, row_start, block_rows, 0),
            segments,
            score_scale,
        )
        lse_block = lax.dynamic_index_in_dim(log_total, block_index, 0, keepdims=False)
        attn_probs = jnp.exp(scores - lse_block[..., None])
        prob_grad = jnp.einsum(
            "qhd,khd->hqk", out_block, values_all, preferred_element_type=jnp.float32
        )
        row_delta = jnp.sum(attn_probs * prob_grad, axis=-1, keepdims=True)
        score_grad = (attn_probs * (prob_grad - row_delta)).astype(jnp.bfloat16)
        query_grad = (
            jnp.einsum("hqk,khd->qhd", score_grad, keys_all, preferred_element_type=jnp.float32)
            * score_scale
        )
        key_part = (
            jnp.einsum("hqk,qhd->khd", score_grad, query_block, preferred_element_type=jnp.float32)
            * score_scale
        )
        value_part = jnp.einsum(
            "hqk,qhd->khd",
            attn_probs.astype(jnp.bfloat16),
            out_block,
            preferred_element_type=jnp.float32,
        )
        key_grad = key_grad + key_part
        value_grad = value_grad + value_part
        return ((key_grad, value_grad), query_grad)

    (key_grad, value_grad), query_grad = lax.scan(
        one_block, (zero_grad, zero_grad), jnp.arange(block_count, dtype=jnp.int32)
    )
    return (query_grad.reshape(keys_all.shape), key_grad, value_grad)


def body(
    tokens_in,
    cotangent,
    segment_ids,
    long_seq,
    weights,
    left_stats,
    right_stats,
    left_roots,
    right_roots,
    split_params,
    shared_params,
):
    full_weights, full_split, full_shared = (
        lax.all_gather(weights, "dp", axis=1, tiled=True),
        lax.all_gather(split_params, "dp", axis=2, tiled=True),
        lax.all_gather(shared_params, "dp", axis=2, tiled=True),
    )
    tensor_count = lax.axis_size("tensor")
    embed_dev = D // tensor_count
    inner_dev = FF // tensor_count
    heads_local = HEADS // tensor_count
    token_count = tokens_in.shape[0]
    window = SEQ_LONG
    block_rows = min(512, window)
    score_scale = 1.0 / math.sqrt(HD)
    seq_length = jnp.where(long_seq[0] > 0, SEQ_LONG, SEQ_SHORT)
    positions = jnp.arange(token_count, dtype=jnp.int32)
    seq_index = positions // seq_length
    valid_rows = (segment_ids >= 0).astype(jnp.float32)
    matrices = []
    for layer_index in range(LAYERS):
        blocks = full_weights[layer_index, :, 0].astype(jnp.bfloat16).reshape(D // B, -1, B, B)
        matrices.append(unpack_layer(blocks, embed_dev, inner_dev))
    hidden_state = tokens_in
    kept_state = []
    for layer_index in range(LAYERS):
        qkv_weight, out_weight, up_weight, down_weight = matrices[layer_index]
        shared = full_shared[layer_index]
        bias_table = full_split[layer_index, 0].reshape(embed_dev, 6)
        up_bias = bias_table[:, 2:].reshape(inner_dev)
        normed = layer_norm(hidden_state, shared[0], shared[1]).astype(jnp.bfloat16)
        qkv_bias = jnp.concatenate(
            [bias_table[:, 0], jnp.zeros((embed_dev,), jnp.float32), bias_table[:, 1]]
        )
        projected = (matmul_low(normed, qkv_weight) + qkv_bias).astype(jnp.bfloat16)
        queries = projected[:, :embed_dev].reshape(token_count, heads_local, HD)
        keys_all = projected[:, embed_dev : 2 * embed_dev].reshape(token_count, heads_local, HD)
        values_all = projected[:, 2 * embed_dev :].reshape(token_count, heads_local, HD)
        attended, log_total = attention_forward(
            queries, keys_all, values_all, seq_index, segment_ids, block_rows, score_scale
        )
        attended = attended.reshape(token_count, embed_dev).astype(jnp.bfloat16)
        attn_branch = lax.psum(
            matmul_low(attended, out_weight).astype(jnp.bfloat16), "tensor"
        ).astype(jnp.float32)
        middle = hidden_state + attn_branch + shared[4]
        normed_mid = layer_norm(middle, shared[2], shared[3]).astype(jnp.bfloat16)
        pre_act = matmul_low(normed_mid, up_weight) + up_bias
        activation = gelu_exact(pre_act).astype(jnp.bfloat16)
        mlp_branch = lax.psum(
            matmul_low(activation, down_weight).astype(jnp.bfloat16), "tensor"
        ).astype(jnp.float32)
        kept_state.append(
            (
                hidden_state,
                normed,
                queries,
                keys_all,
                values_all,
                attended,
                log_total,
                middle,
                normed_mid,
                pre_act,
                activation,
            )
        )
        hidden_state = middle + mlp_branch + shared[5]
    grad_state = cotangent * valid_rows[:, None]
    layer_grads = [None] * LAYERS
    for layer_index in reversed(range(LAYERS)):
        (
            hidden_in,
            normed,
            queries,
            keys_all,
            values_all,
            attended,
            log_total,
            middle,
            normed_mid,
            pre_act,
            activation,
        ) = kept_state[layer_index]
        qkv_weight, out_weight, up_weight, down_weight = matrices[layer_index]
        shared = full_shared[layer_index]
        down_bias_grad = jnp.sum(grad_state, axis=0)
        grad_low = grad_state.astype(jnp.bfloat16)
        down_grad = inner_rows(activation, grad_low)
        act_grad = times_trans(grad_low, down_weight)
        gelu_pull = jax.vjp(gelu_exact, pre_act)[1]
        pre_grad = gelu_pull(act_grad)[0].astype(jnp.bfloat16)
        up_bias_grad = jnp.sum(pre_grad, axis=0, dtype=jnp.float32)
        up_grad = inner_rows(normed_mid, pre_grad)
        normed_mid_grad = lax.psum(times_trans(pre_grad, up_weight), "tensor")
        norm_pull = jax.vjp(layer_norm, middle, shared[2], shared[3])[1]
        middle_ln, gain_two_grad, shift_two_grad = norm_pull(normed_mid_grad)
        middle_grad = grad_state + middle_ln
        out_bias_grad = jnp.sum(middle_grad, axis=0)
        middle_low = middle_grad.astype(jnp.bfloat16)
        out_grad = inner_rows(attended, middle_low)
        attended_grad = (
            times_trans(middle_low, out_weight)
            .astype(jnp.bfloat16)
            .reshape(token_count, heads_local, HD)
        )
        query_grad, key_grad, value_grad = attention_backward(
            queries,
            keys_all,
            values_all,
            attended_grad,
            log_total,
            seq_index,
            segment_ids,
            block_rows,
            score_scale,
        )
        proj_grad = jnp.concatenate(
            [
                query_grad.reshape(token_count, embed_dev),
                key_grad.reshape(token_count, embed_dev),
                value_grad.reshape(token_count, embed_dev),
            ],
            axis=1,
        ).astype(jnp.bfloat16)
        query_bias_grad = jnp.sum(proj_grad[:, :embed_dev], axis=0, dtype=jnp.float32)
        value_bias_grad = jnp.sum(proj_grad[:, 2 * embed_dev :], axis=0, dtype=jnp.float32)
        qkv_grad = inner_rows(normed, proj_grad)
        normed_grad = lax.psum(times_trans(proj_grad, qkv_weight), "tensor")
        input_pull = jax.vjp(layer_norm, hidden_in, shared[0], shared[1])[1]
        hidden_ln, gain_one_grad, shift_one_grad = input_pull(normed_grad)
        grad_state = middle_grad + hidden_ln
        block_grads = pack_layer(qkv_grad, out_grad, up_grad, down_grad, B).reshape(-1, 1, B * B)
        split_vec = jnp.concatenate(
            [
                query_bias_grad[:, None],
                value_bias_grad[:, None],
                up_bias_grad.reshape(embed_dev, 4),
            ],
            axis=1,
        ).reshape(1, -1)
        shared_vec = jnp.stack(
            [
                gain_one_grad,
                shift_one_grad,
                gain_two_grad,
                shift_two_grad,
                out_bias_grad,
                down_bias_grad,
            ]
        )
        layer_grads[layer_index] = (block_grads, split_vec, shared_vec)
    weight_grad, split_grad, shared_grad = (
        lax.psum_scatter(
            jnp.stack([entry[0] for entry in layer_grads]), "dp", scatter_dimension=1, tiled=True
        ),
        lax.psum_scatter(
            jnp.stack([entry[1] for entry in layer_grads]), "dp", scatter_dimension=2, tiled=True
        ),
        lax.psum_scatter(
            jnp.stack([entry[2] for entry in layer_grads]), "dp", scatter_dimension=2, tiled=True
        ),
    )
    dp_index = lax.axis_index("dp")
    lead_shard = (lax.axis_index("tensor") == 0).astype(jnp.float32)
    slice_len = split_grad.shape[-1]
    global_pos = dp_index * slice_len + jnp.arange(slice_len, dtype=jnp.int32)
    table_column = global_pos % 6
    segment_of = (table_column >= 1).astype(jnp.int32) + (table_column >= 2).astype(jnp.int32)
    selector = (segment_of[:, None] == jnp.arange(3, dtype=jnp.int32)[None, :]).astype(jnp.float32)
    split_sq = split_grad[:, 0] * split_grad[:, 0]
    split_rows = jnp.dot(split_sq, selector, precision=highest)
    shared_sq = shared_grad * shared_grad
    shared_rows = jnp.sum(shared_sq, axis=-1) * lead_shard
    local_total = (
        jnp.sum(weight_grad * weight_grad) + jnp.sum(split_sq) + lead_shard * jnp.sum(shared_sq)
    )
    total_sq, split_rows, shared_rows = lax.psum(
        (local_total, split_rows, shared_rows), ("dp", "tensor")
    )
    grad_norm = jnp.sqrt(total_sq)
    factor = clip_limit / jnp.maximum(grad_norm, clip_limit)
    squared = factor * factor
    block_shape = weight_grad.shape[:-1] + (B, B)
    left_mats = left_roots.reshape(block_shape)
    right_mats = right_roots.reshape(block_shape)
    clipped = weight_grad * factor
    clipped_mats = clipped.reshape(block_shape)
    new_left = decay * left_stats + (1.0 - decay) * jnp.einsum(
        "...ij,...kj->...ik", clipped_mats, clipped_mats, precision=highest
    ).reshape(left_stats.shape)
    new_right = decay * right_stats + (1.0 - decay) * jnp.einsum(
        "...ji,...jk->...ik", clipped_mats, clipped_mats, precision=highest
    ).reshape(right_stats.shape)
    partial_dir = jnp.einsum("...ij,...jk->...ik", left_mats, clipped_mats, precision=highest)
    direction = jnp.einsum("...ij,...jk->...ik", partial_dir, right_mats, precision=highest)
    mean_sq = jnp.mean(direction * direction, axis=(-2, -1), keepdims=True)
    step_mats = direction * lax.rsqrt(mean_sq + eps_norm)
    new_weights = weights - rate_matrix * step_mats.reshape(weights.shape)
    vector_sizes = jnp.array([D, D, FF], jnp.float32)
    split_mean = jnp.dot(split_rows / vector_sizes[None, :], selector.T, precision=highest)
    split_clip = split_grad * factor
    new_split = split_params - rate_vector * split_clip * lax.rsqrt(
        squared * split_mean[:, None, :] + eps_norm
    )
    shared_clip = shared_grad * factor
    shared_mean = shared_rows / D
    new_shared = shared_params - rate_vector * shared_clip * lax.rsqrt(
        squared * shared_mean[..., None] + eps_norm
    )
    return (
        hidden_state,
        grad_state,
        clipped,
        new_weights,
        new_left,
        new_right,
        split_clip,
        new_split,
        shared_clip,
        new_shared,
        grad_norm,
    )


F32 = jnp.float32
BF16 = jnp.bfloat16
MESH = pl.DeviceIdType.MESH
CHUNKS = 4
HALF = 128
CHUNK = 2 * HALF
ROWS = CHUNKS * CHUNK
HEADS_DEV = 3
GROUPS = D // B
GROUP = 24
PARTS = ((0, 1, 2, 3, 4, 5, 14, 15), tuple(range(6, 14)), tuple(range(16, 24)))
TRANSPOSED = (frozenset((14, 15)), frozenset(), frozenset(range(16, 24)))


def dot_nn(left_mat, right_mat):
    return lax.dot_general(left_mat, right_mat, (((1,), (0,)), ((), ())), preferred_element_type=F32)


def dot_nt(left_mat, right_mat):
    return lax.dot_general(left_mat, right_mat, (((1,), (1,)), ((), ())), preferred_element_type=F32)


def dot_tn(left_mat, right_mat):
    return lax.dot_general(left_mat, right_mat, (((0,), (0,)), ((), ())), preferred_element_type=F32)


def lanes_of(shape):
    return lax.broadcasted_iota(jnp.int32, shape, len(shape) - 1)


def norm_rows(rows):
    mean = jnp.mean(rows, axis=-1, keepdims=True)
    centered = rows - mean
    var = jnp.mean(centered * centered, axis=-1, keepdims=True)
    inv = lax.rsqrt(var + eps_layer)
    return centered * inv, inv


def norm_back(grad, rows, gain):
    hat, inv = norm_rows(rows)
    scaled = grad * gain
    mean_one = jnp.mean(scaled, axis=-1, keepdims=True)
    mean_two = jnp.mean(scaled * hat, axis=-1, keepdims=True)
    d_rows = inv * (scaled - mean_one - hat * mean_two)
    return d_rows, jnp.sum(grad * hat, axis=0, keepdims=True), jnp.sum(grad, axis=0, keepdims=True)


def table_selector(shape):
    row = lax.broadcasted_iota(jnp.int32, shape, 0)
    col = lax.broadcasted_iota(jnp.int32, shape, 1)
    up_row = 6 * (col >> 2) + 2 + (col & 3)
    hit = (col < B) & (row == up_row)
    hit = hit | ((col >= 128) & (col < 152) & (row == 6 * (col - 128)))
    hit = hit | ((col >= 152) & (col < 176) & (row == 6 * (col - 152) + 1))
    return hit.astype(F32)


def flat_rows(ref):
    x_zero, x_one, x_two = [ref[pl.ds(m, 24, stride=3), :] for m in range(3)]
    lane = lanes_of((24, 128))
    x_half = pltpu.roll(x_two, 64, 1)
    return (
        x_zero,
        jnp.where(lane < 32, pltpu.roll(x_zero, 32, 1), pltpu.roll(x_one, 32, 1)),
        jnp.where(lane < 64, pltpu.roll(x_one, 64, 1), x_half),
        pltpu.roll(x_two, 96, 1),
    )


def flat_to_square(ref, place):
    for m, rows in enumerate(flat_rows(ref)):
        place[pl.ds(m, 24, stride=4), :] = rows
    return place[...][:, :B]


def split_rows(square, place):
    place[:, 0:B] = square
    return jnp.concatenate([place[pl.ds(m, 24, stride=4), :] for m in range(4)], axis=0)[:, :B]


def store_flat(ref, stacked):
    lane = lanes_of((24, 128))
    wide = jnp.concatenate([stacked, jnp.zeros((B, 128 - B), F32)], axis=1)
    m_zero, m_one, m_two, m_three = [wide[24 * m : 24 * m + 24] for m in range(4)]
    one_back = pltpu.roll(m_one, 96, 1)
    two_back = pltpu.roll(m_two, 64, 1)
    ref[pl.ds(0, 24, stride=3), :] = jnp.where(lane < 96, m_zero, one_back)
    ref[pl.ds(1, 24, stride=3), :] = jnp.where(lane < 64, one_back, two_back)
    ref[pl.ds(2, 24, stride=3), :] = jnp.where(lane < 32, two_back, pltpu.roll(m_three, 32, 1))


def train_kernel(
    n_y,
    x_hbm,
    ct_hbm,
    seg_ref,
    long_ref,
    w_hbm,
    lr_hbm,
    rr_hbm,
    split_ref,
    shared_ref,
    bo_hbm,
    ig_hbm,
    gf_hbm,
    lf_hbm,
    rf_hbm,
    pf_hbm,
    sg_ref,
    nm_ref,
    wt,
    a_all,
    c_all,
    q_all,
    k_all,
    v_all,
    v_tr,
    o_all,
    lse_all,
    z_all,
    gp_all,
    res,
    y_own,
    y_all,
    g_all,
    du_all,
    dx_all,
    dk_acc,
    dv_acc,
    stage,
    core_in,
    x_in,
    side_in,
    dw,
    rs_one,
    rs_two,
    place,
    flat,
    g_acc,
    kid_col,
    kid_row,
    vecs,
    bias_row,
    gvecs,
    gbias,
    sib_in,
    msg_in,
    gmsg_out,
    nb_out,
    nb_in,
    nd_in,
    g_s,
    g_r,
    c_s,
    c_r,
    x_s,
    x_r,
    a_s,
    a_r,
    p_s,
    p_r,
    t_s,
    t_r,
    load_sem,
    land_sem,
    ct_sem,
    y_s,
    y_r,
    out_sem,
    far_s,
    far_r,
    gout_sem,
    root_sem,
    m_s,
    m_r,
    gm_s,
    gm_r,
    sib_s,
    sib_r,
    nb_s,
    nb_r,
    nd_s,
    nd_r,
):
    n_dp = GROUPS
    n_z = n_dp // n_y
    me = lax.axis_index("dp")
    ten = lax.axis_index("tensor")
    my_z, my_y = me // n_y, lax.rem(me, n_y)
    my_x, my_c = ten // 2, lax.rem(ten, 2)
    other_c = 1 - my_c
    sibling = (me, 2 * my_x + other_c)
    across = (me, 2 * (1 - my_x) + my_c)
    scale = 1.0 / math.sqrt(HD)

    def dp_dev(index):
        return (index, ten)

    def z_peer(step):
        return lax.rem(my_z + step, n_z)

    def remote(src, dst, send, recv, dev):
        return pltpu.make_async_remote_copy(
            src_ref=src, dst_ref=dst, send_sem=send, recv_sem=recv, device_id=dev, device_id_type=MESH
        )

    def at(cond, func):
        @pl.when(cond)
        def _():
            func()

    def load_rows(j, which):
        half = my_c if which == 0 else other_c
        return pltpu.make_async_copy(x_hbm.at[j, half], res.at[which, j], load_sem.at[which, j])

    def load_blocks(l):
        return pltpu.make_async_copy(
            w_hbm.at[l], flat.at[pl.ds(l * GROUP, GROUP)], land_sem.at[l]
        )

    def load_cot(j):
        return pltpu.make_async_copy(ct_hbm.at[j, my_c], y_own.at[j], ct_sem.at[j])

    for l in range(LAYERS):
        load_blocks(l).start()
    for j in range(CHUNKS):
        load_rows(j, 0).start()
        load_rows(j, 1).start()
    for j in range(CHUNKS):
        load_cot(j).start()

    barrier = pltpu.get_barrier_semaphore()
    for step in range(1, n_dp):
        pl.semaphore_signal(
            barrier, inc=1, device_id=dp_dev(lax.rem(me + step, n_dp)), device_id_type=MESH
        )
    pl.semaphore_signal(barrier, inc=1, device_id=sibling, device_id_type=MESH)
    pl.semaphore_signal(barrier, inc=1, device_id=across, device_id_type=MESH)

    sel = table_selector((144, 256))
    for l in range(LAYERS):
        row = lax.dot_general(
            jnp.broadcast_to(split_ref[l], (8, 144)),
            sel,
            (((1,), (0,)), ((), ())),
            precision=highest,
            preferred_element_type=F32,
        )
        msg_in[me, 8 * l : 8 * l + 8, :] = row
        for r in range(6):
            msg_in[me, 8 * l + r : 8 * l + r + 1, 0:B] = shared_ref[r, l : l + 1, :]

    pl.semaphore_wait(barrier, n_dp + 1)

    def msg_copy(step):
        return remote(
            msg_in.at[me], msg_in.at[me], m_s.at[step - 1], m_r.at[me],
            dp_dev(lax.rem(me + step, n_dp)),
        )

    def msg_from(step):
        src = lax.rem(me + step, n_dp)
        return remote(msg_in.at[src], msg_in.at[src], m_s.at[step - 1], m_r.at[src], dp_dev(src))

    for step in range(1, n_dp):
        msg_copy(step).start()

    def gather_send(l, p, slab, k, dev):
        return remote(
            wt.at[l, p, slab], wt.at[l, p, slab], g_s.at[l, p, k], g_r.at[l, p, slab], dp_dev(dev)
        )

    def y_peers():
        return [my_z * n_y + lax.rem(my_y + s, n_y) for s in range(1, n_y)]

    def own_send(l, p):
        @pl.when(my_z < n_z - 1)
        def _():
            gather_send(l, p, me, 0, me + n_y).start()

        @pl.when(my_z > 0)
        def _():
            gather_send(l, p, me, 1, me - n_y).start()

    def own_beside(l, p):
        gather_send(l, p, me, 2, y_peers()[0]).start()

    def wave(l, p, hop):
        @pl.when(my_z >= hop)
        def _():
            slab = me - hop * n_y
            gather_send(l, p, slab, 0, slab).wait_recv()

            @pl.when(my_z < n_z - 1)
            def _():
                gather_send(l, p, slab, 2 + hop, me + n_y).start()

            gather_send(l, p, slab, n_z + 1 + hop, y_peers()[0]).start()

        @pl.when(my_z + hop < n_z)
        def _():
            slab = me + hop * n_y
            gather_send(l, p, slab, 0, slab).wait_recv()

            @pl.when(my_z > 0)
            def _():
                gather_send(l, p, slab, 2 * n_z + hop, me - n_y).start()

            gather_send(l, p, slab, 3 * n_z - 1 + hop, y_peers()[0]).start()

    def gather_finish(l, p):
        for s in range(0, n_z):
            slab = z_peer(s) * n_y + lax.rem(my_y + 1, n_y)
            gather_send(l, p, slab, 0, slab).wait_recv()

    def gather_drain(l, p):
        def sent(k):
            gather_send(l, p, me, k, me).wait_send()

        up, down = my_z < n_z - 1, my_z > 0
        at(up, lambda: sent(0))
        at(down, lambda: sent(1))
        sent(2)
        for hop in range(1, n_z):
            low, high = my_z >= hop, my_z + hop < n_z
            at(jnp.logical_and(low, up), lambda: sent(2 + hop))
            at(low, lambda: sent(n_z + 1 + hop))
            at(jnp.logical_and(high, down), lambda: sent(2 * n_z + hop))
            at(high, lambda: sent(3 * n_z - 1 + hop))

    def relayout(l, p):
        cols = []
        for b in range(8):
            blk = PARTS[p][b]
            square = flat_to_square(flat.at[l * GROUP + blk], place.at[b % 6])
            cols.append(jnp.transpose(square) if blk in TRANSPOSED[p] else square)
        wt[l, p, me] = jnp.concatenate(cols, axis=1).astype(BF16)

    def relayout_layer(l, carry):
        load_blocks(l).wait()
        for p in range(3):
            relayout(l, p)
            if p < 2:

                @pl.when(l == 0)
                def _():
                    if p == 0:
                        own_send(0, 0)
                    own_beside(0, p)

        return carry

    lax.fori_loop(0, LAYERS, relayout_layer, 0)

    seq_shift = jnp.where(long_ref[0, 0] > 0, 0, 1)
    seg = seg_ref[...]
    pos = lax.broadcasted_iota(jnp.int32, (8, 128), 0) * 128 + lax.broadcasted_iota(
        jnp.int32, (8, 128), 1
    )
    seq = (pos >> 8) * seq_shift
    kid = jnp.where(seg >= 0, seq * 64 + seg, -1 - seq).astype(F32)
    for r in range(8):
        kid_row[r // 2, 0:1, 128 * (r % 2) : 128 * (r % 2) + 128] = kid[r : r + 1, :]
        kid_col[r] = jnp.transpose(
            jnp.broadcast_to(kid[r : r + 1, :], (128, 128))
        )

    gvecs[...] = jnp.zeros_like(gvecs)
    gbias[...] = jnp.zeros_like(gbias)

    for step in range(1, n_dp):
        msg_from(step).wait_recv()
    for l in range(LAYERS):
        vecs[l] = jnp.concatenate(
            [msg_in[s, 8 * l : 8 * l + 8, 0:B] for s in range(n_dp)], axis=1
        )
        rows = [msg_in[s, 8 * l : 8 * l + 8, 128:256] for s in range(n_dp)]
        pad = jnp.zeros((8, D // 4), F32)
        bias_row[l] = jnp.concatenate(
            [r[:, 0:24] for r in rows]
            + [pad]
            + [r[:, 24:48] for r in rows]
            + [jnp.zeros((8, 64), F32)],
            axis=1,
        )

    low_half = lanes_of((CHUNK, 128)) < 64

    def vec(l, k):
        return vecs[l, k : k + 1, :]

    def core_copy(j):
        return remote(stage.at[j, other_c], core_in.at[j], c_s.at[j], c_r.at[j], sibling)

    def x_copy(j, par):
        if par == 2:
            return remote(stage.at[j, my_c], side_in.at[j], x_s.at[2, j], x_r.at[2, j], across)
        return remote(stage.at[j, my_c], x_in.at[par, j], x_s.at[par, j], x_r.at[par, j], across)

    def own_copy(ref, j):
        return remote(ref.at[j, my_c], ref.at[j, my_c], a_s.at[j], a_r.at[j], sibling)

    def send_partial(j, value):
        stage[j] = value.astype(BF16).reshape(2, HALF, D)
        core_copy(j).start()

    def pass_on(j, par):
        core_copy(j).wait()
        mine = stage[j, my_c].astype(F32) + core_in[j].astype(F32)
        stage[j, my_c] = mine.astype(BF16)
        x_copy(j, par).start()

    def total(j, par):
        x_copy(j, par).wait()
        came = side_in[j] if par == 2 else x_in[par, j]
        return stage[j, my_c].astype(F32) + came.astype(F32)

    def project(l, j):
        rows = a_all[l, j].reshape(CHUNK, D)
        weight = wt[l, 0].reshape(D, D)[:, 0:640]
        out = dot_nn(rows, weight) + bias_row[l, 0:1, :]
        tiles = [out[:, 128 * t : 128 * t + 128] for t in range(5)]
        q_roll = pltpu.roll(tiles[0], 64, 1)
        v_roll = pltpu.roll(tiles[3], 64, 1)
        zero = jnp.zeros((CHUNK, 128), F32)
        q_val = [
            jnp.where(low_half, zero, q_roll),
            jnp.where(low_half, q_roll, pltpu.roll(tiles[1], 64, 1)),
        ]
        k_val = [jnp.where(low_half, zero, tiles[1]), tiles[2]]
        v_val = [
            jnp.where(low_half, zero, v_roll),
            jnp.where(low_half, v_roll, pltpu.roll(tiles[4], 64, 1)),
        ]
        q_all[l, j] = jnp.concatenate(q_val, axis=1).astype(BF16)
        k_all[l, j] = jnp.concatenate(k_val, axis=1).astype(BF16)
        v_mat = jnp.concatenate(v_val, axis=1)
        v_all[l, j] = v_mat.astype(BF16)
        v_tr[:, pl.ds(pl.multiple_of(j * CHUNK, CHUNK), CHUNK)] = jnp.transpose(v_mat).astype(BF16)

    def head_tile(mat, h):
        if h == 0:
            return mat[:, 0:128]
        keep = low_half if h == 1 else jnp.logical_not(low_half)
        return jnp.where(keep, mat[:, 128:256], jnp.zeros((), mat.dtype))

    def tile_of(ref, l, h):
        full = ref[l].reshape(ROWS, 256)
        return full[:, 0:128] if h == 0 else full[:, 128:256]

    def allowed_of(j):
        col = kid_col[...].reshape(ROWS, 128)
        return jnp.concatenate([col, col], axis=1) == kid_row[j, 0:1, :]

    def attend_chunk(l, j):
        allowed = allowed_of(j)
        q_mat = q_all[l, j]
        outs = [jnp.zeros((64, CHUNK), F32)]
        for h in range(HEADS_DEV):
            scores = dot_nt(tile_of(k_all, l, h), head_tile(q_mat, h)) * scale
            scores = jnp.where(allowed, scores, big_negative)
            top = jnp.max(scores, axis=0, keepdims=True)
            expo = jnp.exp(scores - top)
            tot = jnp.sum(expo, axis=0, keepdims=True)
            lse_all[l, j, h : h + 1, :] = top + jnp.log(tot)
            out = dot_nn(v_tr[64 + 64 * h : 128 + 64 * h, :], expo.astype(BF16))
            outs.append(out / tot)
        o_mat = jnp.transpose(jnp.concatenate(outs, axis=0)).astype(BF16)
        o_all[l, j] = o_mat
        send_partial(j, dot_nt(o_mat, wt[l, 0].reshape(D, D)[:, 512:768]))

    def middle(l, j):
        mid = res[2 * l, j] + total(j, 0) + vec(l, 4)
        res[2 * l + 1, j] = mid
        hat, _ = norm_rows(mid)
        c_all[l, j, my_c] = (hat * vec(l, 2) + vec(l, 3)).astype(BF16)
        own_copy(c_all.at[l], j).start()

    def mlp(l, j):
        own_copy(c_all.at[l], j).wait()
        rows = c_all[l, j].reshape(CHUNK, D)
        pre = dot_nn(rows, wt[l, 1].reshape(D, D)) + vec(l, 6)
        cdf = 0.5 * (1.0 + lax.erf(pre * (1.0 / math.sqrt(2.0))))
        pdf = jnp.exp(-0.5 * pre * pre) * (1.0 / math.sqrt(2.0 * math.pi))
        act = (pre * cdf).astype(BF16)
        z_all[l, j] = act
        gp_all[l, j] = (cdf + pre * pdf).astype(BF16)

        @pl.when(l < LAYERS - 1)
        def _():
            at(j == 0, lambda: gather_finish(0, 2))
            send_partial(j, dot_nt(z_all[l, j], wt[l, 2].reshape(D, D)))

        @pl.when(l == LAYERS - 1)
        def _():
            y_copy(j).wait()
            mlp_back(LAYERS - 1, j)

    def y_copy(j):
        return remote(y_all.at[j, my_c], y_all.at[j, my_c], y_s.at[j], y_r.at[j], sibling)

    def near_copy(ref, hbm, which, j):
        return pltpu.make_async_copy(ref.at[j], hbm.at[j, my_c], out_sem.at[which, j])

    def far_copy(ref, hbm, which, j):
        return remote(ref.at[j], hbm.at[j, my_c], far_s.at[which, j], far_r.at[which, j], sibling)

    def layer_end(l, j):
        new = res[2 * l + 1, j] + total(j, 1) + vec(l, 5)
        res[2 * l + 2, j] = new
        hat, _ = norm_rows(new)
        a_all[l + 1, j, my_c] = (hat * vec(l + 1, 0) + vec(l + 1, 1)).astype(BF16)
        own_copy(a_all.at[l + 1], j).start()

    def last_send(slot, j):
        send_partial(slot, dot_nt(z_all[LAYERS - 1, j], wt[LAYERS - 1, 2].reshape(D, D)))

    def last_end(slot, j):
        last = res.at[2 * LAYERS - 1]
        last[j] = last[j] + total(slot, 2) + vec(LAYERS - 1, 5)
        near_copy(last, bo_hbm, 0, j).start()
        far_copy(last, bo_hbm, 0, j).start()

    def when_chunk(tick, offset, func):
        @pl.when(jnp.logical_and(tick >= offset, tick < offset + CHUNKS))
        def _():
            func(tick - offset)

    def add_vec(l, k, value):
        gvecs[l, k : k + 1, :] += value

    def mlp_back(l, j):
        d_act = dot_nn(y_all[j].reshape(CHUNK, D), wt[l, 2].reshape(D, D))
        d_pre = (d_act * gp_all[l, j].astype(F32)).astype(BF16)
        du_all[j] = d_pre
        add_vec(l, 6, jnp.sum(d_pre.astype(F32), axis=0, keepdims=True))
        send_partial(j, dot_nt(du_all[j], wt[l, 1].reshape(D, D)))

    def middle_back(l, j):
        grad = total(j, 1)
        d_rows, d_gain, d_shift = norm_back(grad, res[2 * l + 1, j], vec(l, 2))
        y_rows = y_own[j]
        add_vec(l, 5, jnp.sum(y_rows, axis=0, keepdims=True))
        g_rows = y_rows + d_rows
        add_vec(l, 2, d_gain)
        add_vec(l, 3, d_shift)
        add_vec(l, 4, jnp.sum(g_rows, axis=0, keepdims=True))
        y_own[j] = g_rows
        g_all[j, my_c] = g_rows.astype(BF16)
        own_copy(g_all, j).start()

    def attend_back(l, j):
        own_copy(g_all, j).wait()
        d_out = dot_nn(g_all[j].reshape(CHUNK, D), wt[l, 0].reshape(D, D)[:, 512:768])
        do_mat = d_out.astype(BF16)
        prod = jnp.transpose(do_mat.astype(F32) * o_all[l, j].astype(F32))
        allowed = allowed_of(j)
        q_mat = q_all[l, j]
        dq_parts = []
        for h in range(HEADS_DEV):
            q_h = head_tile(q_mat, h)
            do_h = head_tile(do_mat, h)
            scores = dot_nt(tile_of(k_all, l, h), q_h) * scale
            scores = jnp.where(allowed, scores, big_negative)
            probs = jnp.exp(scores - lse_all[l, j, h : h + 1, :])
            delta = jnp.sum(prod[64 + 64 * h : 128 + 64 * h, :], axis=0, keepdims=True)
            d_probs = dot_nt(tile_of(v_all, l, h), do_h)
            d_scores = (probs * (d_probs - delta)).astype(BF16)
            t = 0 if h == 0 else 128
            dv_acc[:, t : t + 128] += dot_nn(probs.astype(BF16), do_h)
            dk_acc[:, t : t + 128] += dot_nn(d_scores, q_h)
            dq_parts.append(dot_nn(v_tr[64 + 64 * h : 128 + 64 * h, :], d_scores))
        dq_parts.append(jnp.zeros((64, CHUNK), F32))
        dq_mat = jnp.transpose(jnp.concatenate(dq_parts, axis=0) * scale)
        dx_all[j, :, 0:256] = dq_mat.astype(BF16)

    def project_back(l, j):
        rows = pl.ds(pl.multiple_of(j * CHUNK, CHUNK), CHUNK)
        dk_mat = dk_acc[rows, :] * scale
        dv_mat = dv_acc[rows, :]
        zero = jnp.zeros((CHUNK, 128), F32)
        roll_zero = pltpu.roll(dv_mat[:, 0:128], 64, 1)
        roll_one = pltpu.roll(dv_mat[:, 128:256], 64, 1)
        tile_one = jnp.where(low_half, dx_all[j, :, 128:256].astype(F32), dk_mat[:, 0:128])
        dx_all[j, :, 128:640] = jnp.concatenate(
            [
                tile_one,
                dk_mat[:, 128:256],
                jnp.where(low_half, roll_zero, roll_one),
                jnp.where(low_half, roll_one, zero),
            ],
            axis=1,
        ).astype(BF16)
        dx_mat = dx_all[j]
        gbias[l, 0:1, :] += jnp.sum(dx_mat.astype(F32), axis=0, keepdims=True)
        send_partial(j, dot_nt(dx_mat, wt[l, 0].reshape(D, D)[:, 0:640]))

    def layer_begin(l, j):
        grad = total(j, 0)
        d_rows, d_gain, d_shift = norm_back(grad, res[2 * l, j], vec(l, 0))
        add_vec(l, 0, d_gain)
        add_vec(l, 1, d_shift)
        new = y_own[j] + d_rows
        y_own[j] = new

        @pl.when(l > 0)
        def _():
            y_all[j, my_c] = new.astype(BF16)
            own_copy(y_all, j).start()

        @pl.when(l == 0)
        def _():
            near_copy(y_own, ig_hbm, 1, j).start()
            far_copy(y_own, ig_hbm, 1, j).start()

    def slab(ref, p, owner):
        return ref.at[p, pl.ds(pl.multiple_of(owner * B, B), B)]

    def pair_copy(l, p, z):
        dest = y_peers()[0]
        return remote(
            slab(dw, p, z * n_y + lax.rem(my_y + 1, n_y)),
            rs_one.at[l, p, z],
            p_s.at[l, p, z],
            p_r.at[l, p, z],
            dp_dev(dest),
        )

    def line_copy(l, p, s):
        dest = z_peer(s)
        return remote(
            slab(dw, p, dest * n_y + my_y),
            rs_two.at[l, p, n_z - 1 - s],
            t_s.at[l, p, s - 1],
            t_r.at[l, p, n_z - 1 - s],
            dp_dev(dest * n_y + my_y),
        )

    def line_from(l, p, s):
        return remote(
            slab(dw, p, me),
            rs_two.at[l, p, s - 1],
            t_s.at[l, p, s - 1],
            t_r.at[l, p, s - 1],
            dp_dev(z_peer(s) * n_y + my_y),
        )

    def scatter_drain(l, p):
        for z in range(n_z):
            pair_copy(l, p, z).wait_send()
        for s in range(1, n_z):
            line_copy(l, p, s).wait_send()

    def scatter_begin(l, p):
        for s in list(range(1, n_z)) + [0]:
            pair_copy(l, p, z_peer(s)).start()

    def scatter_middle(l, p, steps=(1, 2, 3, 0)):
        for s in steps:
            z = z_peer(s)
            pair_copy(l, p, z).wait_recv()
            ref = slab(dw, p, z * n_y + my_y)
            both = (ref[...].astype(F32) + rs_one[l, p, z].astype(F32)).astype(BF16)
            if s:
                ref[...] = both
                line_copy(l, p, s).start()
            else:
                rs_one[l, p, my_z] = both

    def runs_of(p):
        return ((0, 0, 6), (6, 14, 2)) if p == 0 else ((0, PARTS[p][0], 8),)

    def block_copies(l, p):
        return [
            pltpu.make_async_copy(
                flat.at[pl.ds(16 + 8 * k + here, count)],
                hbm.at[l, pl.ds(there, count)],
                gout_sem.at[k, n],
            )
            for k, hbm in enumerate((gf_hbm, lf_hbm, rf_hbm, pf_hbm))
            for n, (here, there, count) in enumerate(runs_of(p))
        ]

    def root_copies(l, p):
        return [
            pltpu.make_async_copy(
                hbm.at[l, pl.ds(there, count)],
                flat.at[pl.ds(8 * k + here, count)],
                root_sem.at[k, n],
            )
            for k, hbm in enumerate((lr_hbm, rr_hbm))
            for n, (here, there, count) in enumerate(runs_of(p))
        ]

    def scatter_end(l, p):
        acc = rs_one[l, p, my_z].astype(F32)
        for s in range(1, n_z):
            line_from(l, p, s).wait_recv()
            acc = acc + rs_two[l, p, s - 1].astype(F32)
        nm_ref[0:1, 0:1] += jnp.sum(acc * acc, keepdims=True)
        g_acc[...] = acc

    def block_update(l, p):
        acc = g_acc[...]
        for copy in root_copies(l, p):
            copy.wait()
        if p < 2:
            for copy in block_copies(l, p + 1):
                copy.wait()
        else:
            @pl.when(l < LAYERS - 1)
            def _():
                for copy in block_copies(LAYERS - 1, 0):
                    copy.wait()

        for b in range(8):
            square = acc[:, B * b : B * b + B]
            turned = jnp.transpose(square)
            if PARTS[p][b] in TRANSPOSED[p]:
                square, turned = turned, square
            slot = 3 * (b % 2)
            low = square.astype(BF16)
            rows = split_rows(square, place.at[slot])
            cols = split_rows(turned, place.at[slot + 1])
            right = flat_to_square(flat.at[8 + b], place.at[slot + 2])
            left = jnp.concatenate(flat_rows(flat.at[b]), axis=0)[:, :B]
            store_flat(flat.at[16 + b], rows)
            store_flat(flat.at[24 + b], dot_nt(rows.astype(BF16), low))
            store_flat(flat.at[32 + b], dot_nn(cols.astype(BF16), low))
            half = dot_nn(left.astype(BF16), low).astype(BF16)
            store_flat(flat.at[40 + b], dot_nn(half, right.astype(BF16)))
        for copy in block_copies(l, p):
            copy.start()
        if p > 0:
            for copy in root_copies(l, p - 1):
                copy.start()
        else:
            @pl.when(l > 0)
            def _():
                for copy in root_copies(0, 2):
                    copy.start()

    nm_ref[...] = jnp.zeros_like(nm_ref)

    def weight_grad(l, p, func):
        at(l < LAYERS - 1, lambda: scatter_drain(LAYERS - 1, p))

        def piece(m, carry):
            cols = pl.ds(pl.multiple_of(m * 256, 256), 256)
            dw[p, cols, :] = func(cols).astype(BF16)
            return carry

        lax.fori_loop(0, D // 256, piece, 0)
        scatter_begin(l, p)

    def down_grad(l):
        def func(cols):
            return dot_tn(
                y_all[:, :, :, cols].reshape(ROWS, 256), z_all[l].reshape(ROWS, D)
            )

        weight_grad(l, 2, func)

    def up_grad(l):
        def func(cols):
            return dot_tn(
                c_all[l, :, :, :, cols].reshape(ROWS, 256), du_all[...].reshape(ROWS, D)
            )

        weight_grad(l, 1, func)

    def qkv_grad(l):
        def func(cols):
            first = dot_tn(
                a_all[l, :, :, :, cols].reshape(ROWS, 256), dx_all[...].reshape(ROWS, 640)
            )
            second = dot_tn(
                g_all[:, :, :, cols].reshape(ROWS, 256), o_all[l].reshape(ROWS, 256)
            )
            return jnp.concatenate(
                [first[:, 0:512], first[:, 512:640] + second[:, 0:128], second[:, 128:256]], axis=1
            )

        weight_grad(l, 0, func)

    def first_norm(j, carry):
        load_rows(j, 0).wait()
        load_rows(j, 1).wait()
        hat, _ = norm_rows(res[0, j])
        a_all[0, j, my_c] = (hat * vec(0, 0) + vec(0, 1)).astype(BF16)
        hat, _ = norm_rows(res[1, j])
        a_all[0, j, other_c] = (hat * vec(0, 0) + vec(0, 1)).astype(BF16)
        return carry

    def first_grad(j, carry):
        load_cot(j).wait()
        rows = jnp.where(kid_col[2 * j + my_c][:, 0:1] >= 0.0, y_own[j], 0.0)
        y_own[j] = rows
        y_all[j, my_c] = rows.astype(BF16)
        y_copy(j).start()
        return carry

    def first_project(j, carry):
        project(0, j)
        return carry

    for copy in root_copies(LAYERS - 1, 2):
        copy.start()
    wave(0, 0, 1)
    own_send(0, 1)
    own_beside(0, 2)
    lax.fori_loop(0, CHUNKS // 2, first_norm, 0)
    wave(0, 0, 2)
    lax.fori_loop(CHUNKS // 2, CHUNKS, first_norm, 0)
    wave(0, 0, 3)
    wave(0, 1, 1)
    lax.fori_loop(0, CHUNKS, first_grad, 0)
    own_send(0, 2)
    gather_finish(0, 0)
    wave(0, 1, 2)
    own_beside(1, 0)
    lax.fori_loop(0, CHUNKS, first_project, 0)

    def prepare_back(l):
        for j in range(CHUNKS):
            v_tr[:, j * CHUNK : j * CHUNK + CHUNK] = jnp.transpose(k_all[l, j].astype(F32)).astype(
                BF16
            )
        dk_acc[...] = jnp.zeros_like(dk_acc)
        dv_acc[...] = jnp.zeros_like(dv_acc)

    def forward_layer(l, carry):
        def step(tick, inner):
            when_chunk(tick, 1, lambda j: pass_on(j, 0))
            when_chunk(tick, 5, lambda j: pass_on(j, 1))

            when_chunk(tick, 3, lambda j: middle(l, j))

            @pl.when(l < LAYERS - 1)
            def _():
                when_chunk(tick, 7, lambda j: layer_end(0, j))

            @pl.when(l == 0)
            def _():
                @pl.when(tick == 0)
                def _():
                    wave(0, 1, 3)

                @pl.when(tick == 1)
                def _():
                    wave(0, 2, 1)

                @pl.when(tick == 2)
                def _():
                    wave(0, 2, 2)
                    own_send(1, 0)
                    own_beside(1, 1)

                @pl.when(tick == 3)
                def _():
                    wave(0, 2, 3)

                @pl.when(tick == 4)
                def _():
                    gather_finish(0, 1)
                    wave(1, 0, 1)

                @pl.when(tick == 5)
                def _():
                    wave(1, 0, 2)
                    own_send(1, 1)
                    own_beside(1, 2)

                @pl.when(tick == 6)
                def _():
                    wave(1, 0, 3)
                    wave(1, 1, 1)

                @pl.when(tick == 7)
                def _():
                    wave(1, 1, 2)
                    own_send(1, 2)

                @pl.when(tick == 8)
                def _():
                    gather_finish(1, 0)
                    wave(1, 1, 3)
                    wave(1, 2, 1)

                @pl.when(tick == 9)
                def _():
                    wave(1, 2, 2)

                @pl.when(tick == 10)
                def _():
                    wave(1, 2, 3)

            @pl.when(l == 1)
            def _():
                @pl.when(tick == 4)
                def _():
                    gather_finish(1, 1)
                    gather_finish(1, 2)

            when_chunk(tick, 0, lambda j: attend_chunk(l, j))

            def next_project(j):
                own_copy(a_all.at[LAYERS - 1], j).wait()
                project(LAYERS - 1, j)

            when_chunk(tick, 4, lambda j: mlp(l, j))

            @pl.when(l == 0)
            def _():
                when_chunk(tick, 8, next_project)

            at(jnp.logical_and(l == LAYERS - 1, tick == 8), lambda: prepare_back(LAYERS - 1))
            return inner

        lax.fori_loop(0, 12, step, 0)
        return carry

    lax.fori_loop(0, LAYERS, forward_layer, 0)
    for step in range(1, n_dp):
        msg_copy(step).wait_send()

    def finish_part(l, p):
        scatter_end(l, p)
        block_update(l, p)

    def backward_layer(n, carry):
        l = LAYERS - 1 - n
        upper = l == LAYERS - 1
        lower = l < LAYERS - 1
        down_grad(l)

        @pl.when(lower)
        def _():
            scatter_middle(LAYERS - 1, 0)

        def step(tick, inner):
            @pl.when(upper)
            def _():
                at(tick == 1, lambda: last_send(0, 0))

                @pl.when(tick == 2)
                def _():
                    last_send(1, 1)
                    pass_on(0, 2)

                at(tick == 3, lambda: pass_on(1, 2))

            middle_back(l, tick)
            at(tick == 2, lambda: up_grad(l))

            at(tick == 3, lambda: scatter_middle(l, 2))
            attend_back(l, tick)
            return inner

        lax.fori_loop(0, CHUNKS, step, 0)

        def step_two(tick, inner):
            when_chunk(tick, 1, lambda j: pass_on(j, 0))

            @pl.when(upper)
            def _():
                when_chunk(tick, 6, lambda j: pass_on(j, 1))

            when_chunk(tick, 4, lambda j: layer_begin(l, j))
            at(jnp.logical_and(upper, tick < 2), lambda: last_end(tick, tick))
            when_chunk(tick, 0, lambda j: project_back(l, j))
            at(tick == 3, lambda: qkv_grad(l))

            @pl.when(lower)
            def _():
                @pl.when(tick == 5)
                def _():
                    far_copy(y_own, ig_hbm, 1, 0).wait_recv()
                    last_send(0, 2)

                @pl.when(tick == 6)
                def _():
                    pass_on(0, 2)
                    far_copy(y_own, ig_hbm, 1, 1).wait_recv()
                    last_send(1, 3)

                at(tick == 7, lambda: pass_on(1, 2))

                @pl.when(tick == 4)
                def _():
                    scatter_middle(0, 1)
                    finish_part(LAYERS - 1, 1)

                at(tick == 5, lambda: scatter_middle(0, 0, (1,)))
                at(tick == 6, lambda: scatter_middle(0, 0, (2,)))
                at(tick == 7, lambda: scatter_middle(0, 0, (3,)))

            def next_back(j):
                own_copy(y_all, j).wait()
                mlp_back(l - 1, j)

            @pl.when(upper)
            def _():
                at(tick == 4, lambda: prepare_back(l - 1))
                when_chunk(tick, 5, next_back)

            @pl.when(upper)
            def _():
                at(tick == 4, lambda: scatter_middle(l, 1))
                at(tick == 6, lambda: finish_part(l, 2))

            return inner

        lax.fori_loop(0, 10, step_two, 0)
        return carry

    lax.fori_loop(0, LAYERS, backward_layer, 0)

    sib = remote(gvecs, sib_in, sib_s.at[0], sib_r.at[0], sibling)
    sib.start()
    sib.wait()
    row_at = lax.broadcasted_iota(jnp.int32, (8, D), 0)
    for l in range(LAYERS):
        mat = gvecs[l] + jnp.where(row_at < 6, sib_in[l], 0.0)
        extra = gbias[l]
        for s in range(n_dp):
            gmsg_out[s, 8 * l : 8 * l + 8, 0:B] = mat[:, B * s : B * s + B]
            gmsg_out[s, 8 * l : 8 * l + 8, 128:152] = extra[:, 24 * s : 24 * s + 24]
            gmsg_out[s, 8 * l : 8 * l + 8, 152:176] = extra[:, 384 + 24 * s : 384 + 24 * s + 24]
            gmsg_out[s, 8 * l : 8 * l + 8, B:128] = jnp.zeros((8, 128 - B), F32)
            gmsg_out[s, 8 * l : 8 * l + 8, 176:256] = jnp.zeros((8, 80), F32)

    def gmsg_copy(step):
        dest = lax.rem(me + step, n_dp)
        return remote(
            gmsg_out.at[dest], msg_in.at[me], gm_s.at[step - 1], gm_r.at[me], dp_dev(dest)
        )

    def gmsg_from(step):
        src = lax.rem(me + step, n_dp)
        return remote(gmsg_out.at[src], msg_in.at[src], gm_s.at[step - 1], gm_r.at[src], dp_dev(src))

    for step in range(1, n_dp):
        gmsg_copy(step).start()
    msg_in[me] = gmsg_out[me]
    scatter_middle(0, 0, (0,))
    finish_part(LAYERS - 1, 0)
    finish_part(0, 2)
    finish_part(0, 1)
    for step in range(1, n_dp):
        gmsg_from(step).wait_recv()
    summed = msg_in[0]
    for s in range(1, n_dp):
        summed = summed + msg_in[s]
    sg_ref[...] = summed

    scatter_end(0, 0)
    squares = summed * summed
    lane = lanes_of((1, 128))
    packed = jnp.where(lane == 0, nm_ref[0:1, :], 0.0)
    shared_sums = jnp.zeros((1, 128), F32)
    for l in range(LAYERS):
        base = 8 * l
        up = jnp.sum(squares[base + 6 : base + 7, 0:B], keepdims=True)
        query = jnp.sum(squares[base : base + 1, 128:152], keepdims=True)
        value = jnp.sum(squares[base : base + 1, 152:176], keepdims=True)
        for k, item in enumerate((query, value, up)):
            packed = packed + jnp.where(lane == 1 + 3 * l + k, item, 0.0)
        for r in range(6):
            item = jnp.sum(squares[base + r : base + r + 1, 0:B], keepdims=True)
            shared_sums = shared_sums + jnp.where(lane == 6 * l + r, item, 0.0)

    for hop, dev in enumerate((sibling, across)):
        nb_out[hop] = jnp.broadcast_to(packed, (8, 128))
        swap = remote(nb_out.at[hop], nb_in.at[hop], nb_s.at[hop], nb_r.at[hop], dev)
        swap.start()
        swap.wait()
        packed = packed + nb_in[hop, 0:1, :]
    row8 = lax.broadcasted_iota(jnp.int32, (8, 128), 0)
    nd_in[me] = jnp.where(row8 == 0, packed, jnp.where(row8 == 1, shared_sums, 0.0))

    def nd_copy(step):
        dest = lax.rem(me + step, n_dp)
        return remote(nd_in.at[me], nd_in.at[me], nd_s.at[step - 1], nd_r.at[me], dp_dev(dest))

    def nd_from(step):
        src = lax.rem(me + step, n_dp)
        return remote(nd_in.at[src], nd_in.at[src], nd_s.at[step - 1], nd_r.at[src], dp_dev(src))

    for step in range(1, n_dp):
        nd_copy(step).start()
    last_end(0, 2)
    last_end(1, 3)
    block_update(0, 0)
    for step in range(1, n_dp):
        nd_from(step).wait_recv()
    acc = nd_in[0]
    for s in range(1, n_dp):
        acc = acc + nd_in[s]
    nm_ref[...] = acc

    for p in range(3):
        scatter_drain(0, p)
        for l in range(LAYERS):
            gather_drain(l, p)
    for copy in block_copies(0, 0):
        copy.wait()
    for step in range(1, n_dp):
        gmsg_copy(step).wait_send()
        nd_copy(step).wait_send()
    for j in range(CHUNKS):
        near_copy(res.at[2 * LAYERS - 1], bo_hbm, 0, j).wait()
        far_copy(res.at[2 * LAYERS - 1], bo_hbm, 0, j).wait()
        near_copy(y_own, ig_hbm, 1, j).wait()
        if j < 2:
            far_copy(y_own, ig_hbm, 1, j).wait_send()
        else:
            far_copy(y_own, ig_hbm, 1, j).wait()


def train_call(n_y, x_rows, ct_rows, seg, long_flag, blocks, left, right, split, shared):
    hbm = pl.BlockSpec(memory_space=pl.ANY)
    vmem = pl.BlockSpec(memory_space=pltpu.VMEM)
    smem = pl.BlockSpec(memory_space=pltpu.SMEM)
    dma = pltpu.SemaphoreType.DMA
    n_dp = GROUPS
    n_z = n_dp // n_y

    def buf(shape, dtype=BF16):
        return pltpu.VMEM(shape, dtype)

    scratch = [
        buf((LAYERS, 3, n_dp, B, D)),
        buf((LAYERS, CHUNKS, 2, HALF, D)),
        buf((LAYERS, CHUNKS, 2, HALF, D)),
        buf((LAYERS, CHUNKS, CHUNK, 256)),
        buf((LAYERS, CHUNKS, CHUNK, 256)),
        buf((LAYERS, CHUNKS, CHUNK, 256)),
        buf((256, ROWS)),
        buf((LAYERS, CHUNKS, CHUNK, 256)),
        buf((LAYERS, CHUNKS, 8, CHUNK), F32),
        buf((LAYERS, CHUNKS, CHUNK, D)),
        buf((LAYERS, CHUNKS, CHUNK, D)),
        buf((2 * LAYERS, CHUNKS, HALF, D), F32),
        buf((CHUNKS, HALF, D), F32),
        buf((CHUNKS, 2, HALF, D)),
        buf((CHUNKS, 2, HALF, D)),
        buf((CHUNKS, CHUNK, D)),
        buf((CHUNKS, CHUNK, 640)),
        buf((ROWS, 256), F32),
        buf((ROWS, 256), F32),
        buf((CHUNKS, 2, HALF, D)),
        buf((CHUNKS, HALF, D)),
        buf((2, CHUNKS, HALF, D)),
        buf((2, HALF, D)),
        buf((3, D, D)),
        buf((LAYERS, 3, n_z, B, D)),
        buf((LAYERS, 3, n_z - 1, B, D)),
        buf((6, B, 128), F32),
        buf((LAYERS * GROUP, 72, 128), F32),
        buf((B, D), F32),
        buf((8, HALF, 128), F32),
        buf((CHUNKS, 8, CHUNK), F32),
        buf((LAYERS, 8, D), F32),
        buf((LAYERS, 8, 640), F32),
        buf((LAYERS, 8, D), F32),
        buf((LAYERS, 8, 640), F32),
        buf((LAYERS, 8, D), F32),
        buf((n_dp, 16, 256), F32),
        buf((n_dp, 16, 256), F32),
        buf((2, 8, 128), F32),
        buf((2, 8, 128), F32),
        buf((n_dp, 8, 128), F32),
        dma((LAYERS, 3, 4 * n_z)),
        dma((LAYERS, 3, n_dp)),
        dma((CHUNKS,)),
        dma((CHUNKS,)),
        dma((3, CHUNKS)),
        dma((3, CHUNKS)),
        dma((CHUNKS,)),
        dma((CHUNKS,)),
        dma((LAYERS, 3, n_z)),
        dma((LAYERS, 3, n_z)),
        dma((LAYERS, 3, n_z - 1)),
        dma((LAYERS, 3, n_z - 1)),
        dma((2, CHUNKS)),
        dma((LAYERS,)),
        dma((CHUNKS,)),
        dma((CHUNKS,)),
        dma((CHUNKS,)),
        dma((2, CHUNKS)),
        dma((2, CHUNKS)),
        dma((2, CHUNKS)),
        dma((4, 2)),
        dma((2, 2)),
        dma((n_dp - 1,)),
        dma((n_dp,)),
        dma((n_dp - 1,)),
        dma((n_dp,)),
        dma((1,)),
        dma((1,)),
        dma((2,)),
        dma((2,)),
        dma((n_dp - 1,)),
        dma((n_dp,)),
    ]
    rows_shape = jax.ShapeDtypeStruct((CHUNKS, 2, HALF, D), F32)
    return pl.pallas_call(
        functools.partial(train_kernel, n_y),
        out_shape=(
            rows_shape,
            rows_shape,
            *[jax.ShapeDtypeStruct((LAYERS, GROUP, 72, 128), F32)] * 4,
            jax.ShapeDtypeStruct((16, 256), F32),
            jax.ShapeDtypeStruct((8, 128), F32),
        ),
        in_specs=[hbm, hbm, vmem, smem, hbm, hbm, hbm, vmem, vmem],
        out_specs=(hbm, hbm, hbm, hbm, hbm, hbm, vmem, vmem),
        scratch_shapes=scratch,
        compiler_params=pltpu.CompilerParams(
            collective_id=0, has_side_effects=True, vmem_limit_bytes=61 * 1024 * 1024
        ),
        cost_estimate=pl.CostEstimate(
            flops=30_000_000_000, bytes_accessed=30_000_000, transcendentals=20_000_000
        ),
        name="train",
    )(x_rows, ct_rows, seg, long_flag, blocks, left, right, split, shared)


def update_kernel(
    g_ref,
    lg_ref,
    rg_ref,
    p_ref,
    w_ref,
    l_ref,
    r_ref,
    sg_ref,
    nm_ref,
    sp_ref,
    sh_ref,
    bo_ref,
    ig_ref,
    gout_ref,
    nw_ref,
    nl_ref,
    nr_ref,
    sgo_ref,
    nsp_ref,
    shg_ref,
    nsh_ref,
    norm_ref,
    bo_out,
    ig_out,
):
    step_at = pl.program_id(0)
    bo_out[...] = bo_ref[...]
    ig_out[...] = ig_ref[...]
    lane = lanes_of((1, 128))
    row_zero = nm_ref[0:1, :]
    row_one = nm_ref[1:2, :]
    total_sq = jnp.sum(jnp.where(lane < 7, row_zero, 0.0), keepdims=True) + jnp.sum(
        jnp.where(lane < 12, row_one, 0.0), keepdims=True
    )
    norm = jnp.sqrt(total_sq)
    factor = clip_limit / jnp.maximum(norm, clip_limit)
    squared = factor * factor
    gram_weight = (1.0 - decay) * squared

    for b in range(g_ref.shape[0]):
        gout_ref[b] = g_ref[b] * factor
        nl_ref[b] = decay * l_ref[b] + gram_weight * lg_ref[b]
        nr_ref[b] = decay * r_ref[b] + gram_weight * rg_ref[b]
        direction = p_ref[b] * factor
        mean_sq = jnp.sum(direction * direction, keepdims=True) / (B * B)
        nw_ref[b] = w_ref[b] - direction * (rate_matrix * lax.rsqrt(mean_sq + eps_norm))

    @pl.when(step_at == 0)
    def _():
        norm_ref[...] = norm
        sel = table_selector((144, 256))
        col = lanes_of((1, 256))
        for l in range(LAYERS):
            sums = [row_zero[:, 1 + 3 * l + k : 2 + 3 * l + k] for k in range(3)]
            means = [sums[0] / D, sums[1] / D, sums[2] / FF]
            scales = [lax.rsqrt(squared * m + eps_norm) for m in means]
            src = sg_ref[8 * l : 8 * l + 8, :]
            line = jnp.where(col < 128, src[6:7, :], src[0:1, :]) * factor
            step = line * jnp.where(col < 128, scales[2], jnp.where(col < 152, scales[0], scales[1]))
            both = jnp.concatenate([line, step, jnp.zeros((6, 256), F32)], axis=0)
            table = lax.dot_general(
                both, sel, (((1,), (1,)), ((), ())), precision=highest, preferred_element_type=F32
            )
            sgo_ref[l] = table[0:1, :]
            nsp_ref[l] = sp_ref[l] - rate_vector * table[1:2, :]
            for r in range(6):
                mean = row_one[:, 6 * l + r : 6 * l + r + 1] / D
                grad = src[r : r + 1, 0:B] * factor
                shg_ref[r, l : l + 1, :] = grad
                nsh_ref[r, l : l + 1, :] = sh_ref[r, l : l + 1, :] - rate_vector * grad * lax.rsqrt(
                    squared * mean + eps_norm
                )


def update_call(grads, lefts, rights, dirs, weights, left, right, sums, norms, split, shared, outs):
    per = GROUP
    count = LAYERS * GROUP
    flat = pl.BlockSpec((per, 72, 128), lambda i: (i, 0, 0))
    rows = pl.BlockSpec((2 * HALF * CHUNKS * per // count, D), lambda i: (i, 0))

    def whole(shape):
        return pl.BlockSpec(shape, lambda i: (0,) * len(shape))

    flat_shape = jax.ShapeDtypeStruct((count, 72, 128), F32)
    split_shape, shared_shape = (LAYERS, 1, 144), (6, LAYERS, B)
    return pl.pallas_call(
        update_kernel,
        grid=(count // per,),
        out_shape=(
            *[flat_shape] * 4,
            *[jax.ShapeDtypeStruct(split_shape, F32)] * 2,
            *[jax.ShapeDtypeStruct(shared_shape, F32)] * 2,
            jax.ShapeDtypeStruct((1, 1), F32),
            *[jax.ShapeDtypeStruct(o.shape, F32) for o in outs],
        ),
        in_specs=[flat] * 7
        + [whole((16, 256)), whole((8, 128)), whole(split_shape), whole(shared_shape), rows, rows],
        out_specs=(
            *[flat] * 4,
            *[whole(split_shape)] * 2,
            *[whole(shared_shape)] * 2,
            whole((1, 1)),
            rows,
            rows,
        ),
        compiler_params=pltpu.CompilerParams(vmem_limit_bytes=60 * 1024 * 1024),
        name="update",
    )(grads, lefts, rights, dirs, weights, left, right, sums, norms, split, shared, *outs)


def fast_body(
    n_y,
    tokens_in,
    cotangent,
    segment_ids,
    long_seq,
    weights,
    left_stats,
    right_stats,
    left_roots,
    right_roots,
    split_params,
    shared_params,
):
    rows = (CHUNKS, 2, HALF, D)
    flat = (LAYERS, GROUP, 72, 128)
    blocks = (LAYERS * GROUP, 72, 128)
    split = split_params
    shared = jnp.transpose(shared_params, (1, 0, 2))
    out_rows, in_grad, grads, lefts, rights, dirs, sums, norms = train_call(
        n_y,
        tokens_in.reshape(rows),
        cotangent.reshape(rows),
        segment_ids.reshape(8, 128),
        long_seq.reshape(1, 1),
        weights.reshape(flat),
        left_roots.reshape(flat),
        right_roots.reshape(flat),
        split,
        shared,
    )
    res = update_call(
        *[m.reshape(blocks) for m in (grads, lefts, rights, dirs, weights, left_stats, right_stats)],
        sums,
        norms,
        split,
        shared,
        (out_rows.reshape(tokens_in.shape), in_grad.reshape(tokens_in.shape)),
    )
    mats = [r.reshape(weights.shape) for r in res[:4]]
    return (
        res[9],
        res[10],
        *mats,
        res[4],
        res[5],
        jnp.transpose(res[6], (1, 0, 2)),
        jnp.transpose(res[7], (1, 0, 2)),
        res[8].reshape(()),
    )


def solution(mesh):
    in_specs = (
        P("dp", None),
        P("dp", None),
        P("dp"),
        P("dp"),
        P(None, "dp", "tensor", None),
        P(None, "dp", "tensor", None),
        P(None, "dp", "tensor", None),
        P(None, "dp", "tensor", None),
        P(None, "dp", "tensor", None),
        P(None, "tensor", "dp"),
        P(None, None, "dp"),
    )
    out_specs = (
        P("dp", None),
        P("dp", None),
        P(None, "dp", "tensor", None),
        P(None, "dp", "tensor", None),
        P(None, "dp", "tensor", None),
        P(None, "dp", "tensor", None),
        P(None, "tensor", "dp"),
        P(None, "tensor", "dp"),
        P(None, None, "dp"),
        P(None, None, "dp"),
        P(),
    )
    plan = body
    if mesh.shape["dp"] == GROUPS and mesh.shape["tensor"] == 4:
        plan = functools.partial(fast_body, 2)
    return jax.shard_map(plan, mesh=mesh, in_specs=in_specs, out_specs=out_specs, check_vma=False)
```
